128 devices in a mesh: dp: 4 (over x), seq: 4 (over y), mp: 8 (over z, core).
Axes of the slice: x: 4, y: 4, z: 4, core: 2. Of those that a mesh axis runs over, the one named last changes fastest.
Arguments:
- inputs: bfloat16 [8, 1024, 2048], P('dp', 'seq'), may hold values from -6 to 6
- cotangent: bfloat16 [8, 1024, 2048], P('dp', 'seq'), may hold values from -6 to 6
- parents: int32 [8, 8], P('dp'), may hold values from -1 to 7, as said below
- weight_attend: bfloat16 [2048, 3072], P(None, 'mp'), may hold values from -0.125 to 0.125
- weight_merge: bfloat16 [2048, 2048], P('mp'), may hold values from -0.5 to 0.5
- weight_expand: bfloat16 [2048, 2, 8192], P(None, None, 'mp'), may hold values from -0.125 to 0.125
- weight_reduce: bfloat16 [8192, 2048], P('mp'), may hold values from -0.0625 to 0.0625
- gains: bfloat16 [2, 2048], replicated, may hold values from 0.5 to 1.5
- master_attend: float32 [2048, 3072], P(('dp', 'seq'), 'mp'), may hold values from -0.125 to 0.125
- master_merge: float32 [2048, 2048], P('mp', ('dp', 'seq')), may hold values from -0.072 to 0.072
- master_expand: float32 [2048, 2, 8192], P(('dp', 'seq'), None, 'mp'), may hold values from -0.125 to 0.125
- master_reduce: float32 [8192, 2048], P('mp', ('dp', 'seq')), may hold values from -0.0625 to 0.0625
- master_gains: float32 [2, 2048], P(None, ('dp', 'seq')), may hold values from 0.004 to 0.02
- first_attend: float32 [2048, 3072], P(('dp', 'seq'), 'mp'), may hold values from -120 to 120
- first_merge: float32 [2048, 2048], P('mp', ('dp', 'seq')), may hold values from -120 to 120
- first_expand: float32 [2048, 2, 8192], P(('dp', 'seq'), None, 'mp'), may hold values from -120 to 120
- first_reduce: float32 [8192, 2048], P('mp', ('dp', 'seq')), may hold values from -120 to 120
- first_gains: float32 [2, 2048], P(None, ('dp', 'seq')), may hold values from -600 to 600
- second_attend: float32 [2048, 3072], P(('dp', 'seq'), 'mp'), may hold values from 100 to 5000
- second_merge: float32 [2048, 2048], P('mp', ('dp', 'seq')), may hold values from 100 to 5000
- second_expand: float32 [2048, 2, 8192], P(('dp', 'seq'), None, 'mp'), may hold values from 100 to 5000
- second_reduce: float32 [8192, 2048], P('mp', ('dp', 'seq')), may hold values from 100 to 5000
- second_gains: float32 [2, 2048], P(None, ('dp', 'seq')), may hold values from 1000 to 100000
Outputs:
- output: bfloat16 [8, 1024, 2048], P('dp', 'seq')
- input_grad: bfloat16 [8, 1024, 2048], P('dp', 'seq')
- renewed_attend: float32 [2048, 3072], P(('dp', 'seq'), 'mp')
- renewed_merge: float32 [2048, 2048], P('mp', ('dp', 'seq'))
- renewed_expand: float32 [2048, 2, 8192], P(('dp', 'seq'), None, 'mp')
- renewed_reduce: float32 [8192, 2048], P('mp', ('dp', 'seq'))
- renewed_gains: float32 [2, 2048], P(None, ('dp', 'seq'))
- momentum_attend: float32 [2048, 3072], P(('dp', 'seq'), 'mp')
- momentum_merge: float32 [2048, 2048], P('mp', ('dp', 'seq'))
- momentum_expand: float32 [2048, 2, 8192], P(('dp', 'seq'), None, 'mp')
- momentum_reduce: float32 [8192, 2048], P('mp', ('dp', 'seq'))
- momentum_gains: float32 [2, 2048], P(None, ('dp', 'seq'))
- variance_attend: float32 [2048, 3072], P(('dp', 'seq'), 'mp')
- variance_merge: float32 [2048, 2048], P('mp', ('dp', 'seq'))
- variance_expand: float32 [2048, 2, 8192], P(('dp', 'seq'), None, 'mp')
- variance_reduce: float32 [8192, 2048], P('mp', ('dp', 'seq'))
- variance_gains: float32 [2, 2048], P(None, ('dp', 'seq'))
- rounded_attend: bfloat16 [2048, 3072], P(None, 'mp')
- rounded_merge: bfloat16 [2048, 2048], P('mp')
- rounded_expand: bfloat16 [2048, 2, 8192], P(None, None, 'mp')
- rounded_reduce: bfloat16 [8192, 2048], P('mp')
- rounded_gains: bfloat16 [2, 2048], replicated
The draws below stay inside these ranges and needn't reach their ends.
Inputs may be any that keep to these rules, and one draw needn't show every extreme that they name: `parents`: each row is one tree of 8 blocks of 128 tokens: a chain of 2 trunk blocks from the root (parent -1), 2 branch blocks hanging from the trunk's last block, and two leaf blocks hanging from each branch block; the blocks stand in the row in any order.
All inputs are finite; a program needn't handle non-finite values.
Results may differ from the reference program's by a relative error of at most 0.03.
Values may be sent and summed in bfloat16 or wider, within the bound.
A program may use at most 192 MiB of HBM per device.

```python
import math
import jax
import jax.numpy as jnp
from jax import lax

D = 2048
H = 32
KVH = 8
HD = 64
FF = 8192
G = 4
QKV = 3072
TRUNK = 2
BRANCHES = 2
NB = 8
TREE_LEN = 1024
STEP = 5
TREES = 8


def draw_parents(key, part):
    key = jax.random.fold_in(key, 11)
    canonical = jnp.arange(NB, dtype=jnp.int32)
    leaf_parent = TRUNK + (canonical - TRUNK - BRANCHES) // 2
    canon_parent = jnp.where(canonical < TRUNK, canonical - 1, jnp.where(canonical < TRUNK + BRANCHES, TRUNK - 1, leaf_parent))

    def one_tree(tree_key):
        layout = jax.random.permutation(tree_key, NB).astype(jnp.int32)
        position_of = jnp.zeros((NB,), jnp.int32).at[layout].set(canonical)
        parent_canon = canon_parent[layout]
        return jnp.where(parent_canon < 0, -1, position_of[jnp.maximum(parent_canon, 0)])
    return jax.vmap(one_tree)(jax.random.split(key, TREES)).astype(jnp.int32)


def block_scale(stream_key, extent, shards, smallest, high):
    gain, own = 1.0, jax.random.fold_in(stream_key, 6)
    for axis_at, shards_of in shards:
        steps = jnp.exp(jax.random.uniform(jax.random.fold_in(own, axis_at), (shards_of,), jnp.float32, smallest / len(shards), high / len(shards)))
        gain = gain * jnp.repeat(steps, extent[axis_at] // shards_of).reshape([-1 if axis == axis_at else 1 for axis in range(len(extent))])
    return gain


def scatter_about(rng, extent, width, reach, shards=(), kind=jnp.bfloat16):
    factor_of = block_scale(rng, extent, shards, -0.22, 0.18) if shards else 1.0
    drawn = jax.random.normal(rng, extent, jnp.float32) * width * factor_of
    return jnp.minimum(jnp.maximum(drawn, -reach), reach).astype(kind)


def setup_inputs(seed: int = 0) -> dict:
    key_of = jax.random.split(jax.random.key(seed), 24)
    inputs = scatter_about(key_of[0], (TREES, TREE_LEN, D), 1.0, 6.0, ((0, 4), (1, 4)))
    cotangent = scatter_about(key_of[1], (TREES, TREE_LEN, D), 1.0, 6.0, ((0, 4), (1, 4)))
    parents = draw_parents(jax.random.fold_in(key_of[23], 71), 0)
    weight_attend = scatter_about(key_of[3], (D, QKV), D ** -0.5, 0.125, ((1, 8),))
    weight_merge = scatter_about(key_of[4], (H * HD, D), (H * HD // 16) ** -0.5, 0.5, ((0, 8),))
    weight_expand = scatter_about(key_of[5], (D, 2, FF), D ** -0.5, 0.125, ((2, 8),))
    weight_reduce = scatter_about(key_of[6], (FF, D), FF ** -0.5, 0.0625, ((0, 8),))
    gains = jnp.clip(1.0 + 0.1 * jax.random.normal(key_of[7], (2, D), jnp.float32), 0.5, 1.5).astype(jnp.bfloat16)
    master_attend = scatter_about(key_of[8], (D, QKV), D ** -0.5, 0.125, ((0, 16), (1, 8)), jnp.float32)
    master_merge = scatter_about(key_of[9], (H * HD, D), 0.012, 0.072, ((0, 8), (1, 16)), jnp.float32)
    master_expand = scatter_about(key_of[10], (D, 2, FF), D ** -0.5, 0.125, ((0, 16), (2, 8)), jnp.float32)
    master_reduce = scatter_about(key_of[11], (FF, D), FF ** -0.5, 0.0625, ((0, 8), (1, 16)), jnp.float32)
    master_gains = jnp.clip(0.004 + 0.015999999 * jax.random.uniform(key_of[12], (2, D), jnp.float32) ** block_scale(key_of[12], (2, D), ((1, 16),), -0.2, 0.2), 0.004, 0.02)
    first_attend = scatter_about(key_of[13], (D, QKV), 20.0, 120.0, ((0, 16), (1, 8)), jnp.float32)
    first_merge = scatter_about(key_of[14], (H * HD, D), 20.0, 120.0, ((0, 8), (1, 16)), jnp.float32)
    first_expand = scatter_about(key_of[15], (D, 2, FF), 20.0, 120.0, ((0, 16), (2, 8)), jnp.float32)
    first_reduce = scatter_about(key_of[16], (FF, D), 20.0, 120.0, ((0, 8), (1, 16)), jnp.float32)
    first_gains = scatter_about(key_of[17], (2, D), 100.0, 600.0, ((1, 16),), jnp.float32)
    second_attend = jnp.clip(jnp.exp(math.log(5000.0) - 3.912023 * jax.random.uniform(key_of[18], (D, QKV), jnp.float32) ** block_scale(key_of[18], (D, QKV), ((0, 16), (1, 8)), -0.2, 0.2)), 100.0, 5000.0)
    second_merge = jnp.clip(jnp.exp(math.log(5000.0) - 3.912023 * jax.random.uniform(key_of[19], (H * HD, D), jnp.float32) ** block_scale(key_of[19], (H * HD, D), ((0, 8), (1, 16)), -0.2, 0.2)), 100.0, 5000.0)
    second_expand = jnp.clip(jnp.exp(math.log(5000.0) - 3.912023 * jax.random.uniform(key_of[20], (D, 2, FF), jnp.float32) ** block_scale(key_of[20], (D, 2, FF), ((0, 16), (2, 8)), -0.2, 0.2)), 100.0, 5000.0)
    second_reduce = jnp.clip(jnp.exp(math.log(5000.0) - 3.912023 * jax.random.uniform(key_of[21], (FF, D), jnp.float32) ** block_scale(key_of[21], (FF, D), ((0, 8), (1, 16)), -0.2, 0.2)), 100.0, 5000.0)
    second_gains = jnp.clip(jnp.exp(math.log(100000.0) - 4.6051702 * jax.random.uniform(key_of[22], (2, D), jnp.float32) ** block_scale(key_of[22], (2, D), ((1, 16),), -0.2, 0.2)), 1000.0, 100000.0)
    return {"inputs": inputs, "cotangent": cotangent, "parents": parents, "weight_attend": weight_attend, "weight_merge": weight_merge, "weight_expand": weight_expand, "weight_reduce": weight_reduce, "gains": gains, "master_attend": master_attend, "master_merge": master_merge, "master_expand": master_expand, "master_reduce": master_reduce, "master_gains": master_gains, "first_attend": first_attend, "first_merge": first_merge, "first_expand": first_expand, "first_reduce": first_reduce, "first_gains": first_gains, "second_attend": second_attend, "second_merge": second_merge, "second_expand": second_expand, "second_reduce": second_reduce, "second_gains": second_gains}


NORM_EPS = 1e-05
ROPE_BASE = 500000.0
MASK_FILL = -1e+30
BETA_ONE = 0.5
BETA_TWO = 0.5
ADAM_EPS = 1e-08
LEARN_RATE = 0.005
DECAY_RATE = 0.1
PRECISE = lax.Precision.HIGHEST

@jax.custom_vjp
def low(v):
    return lax.optimization_barrier(v.astype(jnp.bfloat16)).astype(jnp.float32)

@jax.custom_vjp
def low_back(v):
    return v

def low_keep(v):
    return (low(v), None)

def low_pass(kept, grad):
    return (grad,)

def back_keep(v):
    return (v, None)

def back_low(kept, grad):
    return (low(grad),)
low.defvjp(low_keep, low_pass)
low_back.defvjp(back_keep, back_low)

def tree_geometry(parent_row):
    blocks = parent_row.shape[0]
    block_ids = jnp.arange(blocks, dtype=jnp.int32)

    def extend(loop_index, state):
        reach_table, ancestor = state
        marked = (ancestor[:, None] == block_ids[None, :]).astype(jnp.float32)
        reach_table = jnp.maximum(reach_table, marked)
        ancestor = jnp.where(ancestor >= 0, parent_row[jnp.maximum(ancestor, 0)], -1).astype(jnp.int32)
        return (reach_table, ancestor)
    start = (jnp.zeros((blocks, blocks), jnp.float32), block_ids)
    reach_table, ancestor = lax.fori_loop(0, blocks, extend, start)
    depth_table = lax.optimization_barrier(jnp.sum(reach_table, axis=1)) - 1.0
    return (reach_table, depth_table)

def rotate(values, cosine, sine_table):
    half_width = values.shape[-1] // 2
    lower_half = values[..., :half_width]
    upper_half = values[..., half_width:]
    return jnp.concatenate([lower_half * cosine - upper_half * sine_table, upper_half * cosine + lower_half * sine_table], axis=-1)

def layer(x_rows, w_attend, w_merge, w_expand, w_reduce, gain_rows, cosine, sine_table, visible):
    length = x_rows.shape[0]
    rms_one = lax.rsqrt(lax.optimization_barrier(jnp.mean(x_rows * x_rows, axis=-1, keepdims=True)) + NORM_EPS)
    normed_one = low(x_rows * rms_one * gain_rows[0])
    packed = low_back(jnp.dot(normed_one, w_attend, precision=PRECISE)).reshape(length, KVH, G + 2, HD)
    queries = low(rotate(packed[:, :, :G], cosine[:, None, None, :], sine_table[:, None, None, :]))
    keys = low(rotate(packed[:, :, G], cosine[:, None, :], sine_table[:, None, :]))
    values = low(packed[:, :, G + 1])
    scores = low_back(jnp.einsum('tkgd,skd->kgts', queries, keys, precision=PRECISE) * HD ** (-0.5))
    scores = jnp.where(visible[None, None], scores, MASK_FILL)
    probs = jax.nn.softmax(scores, axis=-1)
    attended = jnp.einsum('kgts,skd->tkgd', low(probs), values, precision=PRECISE).reshape(length, H * HD)
    attended = low_back(low(attended))
    middle = x_rows + low_back(jnp.dot(attended, w_merge, precision=PRECISE))
    rms_two = lax.rsqrt(lax.optimization_barrier(jnp.mean(middle * middle, axis=-1, keepdims=True)) + NORM_EPS)
    normed_two = low(middle * rms_two * gain_rows[1])
    expanded = jnp.dot(normed_two, w_expand.reshape(D, 2 * FF), precision=PRECISE)
    gate_pre = low_back(expanded[:, :FF])
    up_pre = low_back(expanded[:, FF:])
    hidden = low(jax.nn.silu(gate_pre) * up_pre)
    return middle + jnp.dot(hidden, w_reduce, precision=PRECISE)

def adamw(master, first, second, grad_vals, fix_one, fix_two):
    momentum = BETA_ONE * first + (1.0 - BETA_ONE) * grad_vals
    variance = BETA_TWO * second + (1.0 - BETA_TWO) * grad_vals * grad_vals
    direction = momentum / fix_one / (jnp.sqrt(variance / fix_two) + ADAM_EPS)
    renewed = master - LEARN_RATE * (direction + DECAY_RATE * master)
    return (renewed, momentum, variance)

def reference(inputs, cotangent, parents, weight_attend, weight_merge, weight_expand, weight_reduce, gains, master_attend, master_merge, master_expand, master_reduce, master_gains, first_attend, first_merge, first_expand, first_reduce, first_gains, second_attend, second_merge, second_expand, second_reduce, second_gains):
    weights = tuple((w.astype(jnp.float32) for w in (weight_attend, weight_merge, weight_expand, weight_reduce, gains)))
    blocks = parents.shape[1]
    length = inputs.shape[1]
    block_len = length // blocks
    tokens = jnp.arange(length, dtype=jnp.int32)
    tok_block = tokens // block_len
    tok_offset = tokens % block_len
    inv_freq = ROPE_BASE ** (-2.0 * jnp.arange(HD // 2, dtype=jnp.float32) / HD)

    def one_tree(totals, items):
        x_rows, cot_rows, parent_row = items
        reach_table, depth_table = tree_geometry(parent_row)
        positions = depth_table[tok_block] * block_len + tok_offset.astype(jnp.float32)
        angles = positions[:, None] * inv_freq[None, :]
        cosine = jnp.cos(angles)
        sine_table = jnp.sin(angles)
        same_block = tok_block[:, None] == tok_block[None, :]
        visible = (reach_table[tok_block[:, None], tok_block[None, :]] > 0.5) & (~same_block | (tok_offset[None, :] <= tok_offset[:, None]))

        def forward(x_vals, w_attend, w_merge, w_expand, w_reduce, gain_rows):
            return layer(x_vals, w_attend, w_merge, w_expand, w_reduce, gain_rows, cosine, sine_table, visible)
        result, pullback = jax.vjp(forward, x_rows.astype(jnp.float32), *weights)
        grad_vals = pullback(cot_rows.astype(jnp.float32))
        totals = tuple((a + b for a, b in zip(totals, grad_vals[1:])))
        return (totals, (result.astype(jnp.bfloat16), grad_vals[0].astype(jnp.bfloat16)))
    zeros_init = tuple((jnp.zeros(w.shape, jnp.float32) for w in weights))
    totals, (output, input_grad) = lax.scan(one_tree, zeros_init, (inputs, cotangent, parents))
    fix_one = 1.0 - BETA_ONE ** STEP
    fix_two = 1.0 - BETA_TWO ** STEP
    masters = (master_attend, master_merge, master_expand, master_reduce, master_gains)
    firsts = (first_attend, first_merge, first_expand, first_reduce, first_gains)
    seconds = (second_attend, second_merge, second_expand, second_reduce, second_gains)
    updated = [adamw(mw, fw, sw, gw, fix_one, fix_two) for mw, fw, sw, gw in zip(masters, firsts, seconds, totals)]
    return (output, input_grad, updated[0][0], updated[1][0], updated[2][0], updated[3][0], updated[4][0], updated[0][1], updated[1][1], updated[2][1], updated[3][1], updated[4][1], updated[0][2], updated[1][2], updated[2][2], updated[3][2], updated[4][2], updated[0][0].astype(jnp.bfloat16), updated[1][0].astype(jnp.bfloat16), updated[2][0].astype(jnp.bfloat16), updated[3][0].astype(jnp.bfloat16), updated[4][0].astype(jnp.bfloat16))
```

```python
import jax
import jax.numpy as jnp
from jax import lax
from jax.experimental import pallas as pl
from jax.experimental.pallas import tpu as pltpu
from jax.sharding import PartitionSpec as P

HD = 64
G = 4
STEP = 5


NORM_EPS = 1e-05
ROPE_BASE = 500000.0
MASK_FILL = -1e30
BETA_ONE = 0.5
BETA_TWO = 0.5
ADAM_EPS = 1e-08
LEARN_RATE = 0.005
DECAY_RATE = 0.1
PRECISE = lax.Precision.HIGHEST
MESH = pl.DeviceIdType.MESH
R = 3840
HB = R // 2
QB = R // 4
LOOP = 32

def dev(axis, delta):
    n = 4
    return {axis: lax.rem(lax.axis_index(axis) + (delta + n), n)}

def barrier4():
    sem = pltpu.get_barrier_semaphore()
    for axis in ("dp", "seq"):
        for d in (1, -1):
            pl.semaphore_signal(sem, inc=1, device_id=dev(axis, d), device_id_type=MESH)
    pl.semaphore_wait(sem, 4)

class Net:
    def __init__(self, send, recv):
        self.send, self.recv = send, recv
        self.started = []
    def put(self, k, src, dst, axis, d):
        c = pltpu.make_async_remote_copy(src_ref=src, dst_ref=dst, send_sem=self.send.at[k], recv_sem=self.recv.at[k], device_id=dev(axis, d), device_id_type=MESH)
        c.start()
        self.started.append(c)
    def got(self, k, dst):
        pltpu.make_async_remote_copy(src_ref=dst, dst_ref=dst, send_sem=self.send.at[k], recv_sem=self.recv.at[k], device_id=dev("dp", 1), device_id_type=MESH).wait_recv()
    def drain(self):
        for c in self.started:
            c.wait_send()
        self.started = []

def ag_kernel(own_ref, out_ref, send, recv, loc):
    net = Net(send, recv)
    co = {"dp": lax.axis_index("dp"), "seq": lax.axis_index("seq")}
    barrier4()
    me = co["dp"] * 4 + co["seq"]
    lc = pltpu.make_async_copy(own_ref, out_ref.at[me], loc)
    lc.start()
    halves = []
    for h, (fa, sa) in enumerate((("dp", "seq"), ("seq", "dp"))):
        def idx(da, db, fa=fa, sa=sa):
            c = {fa: lax.rem(co[fa] + da + 4, 4), sa: lax.rem(co[sa] + db + 4, 4)}
            return c["dp"] * 4 + c["seq"]
        halves.append((h * 20, h * HB, fa, sa, idx))
    def part(idx, lo, n):
        return out_ref.at[idx, pl.ds(lo, n)]
    pieces = (0, -1, 1, 2)
    for base, lo, fa, sa, idx in halves:
        src = own_ref.at[pl.ds(lo, HB)]
        net.put(base + 0, src, part(idx(0, 0), lo, HB), fa, 1)
        net.put(base + 1, src, part(idx(0, 0), lo, HB), fa, -1)
    for base, lo, fa, sa, idx in halves:
        src = own_ref.at[pl.ds(lo, HB)]
        net.put(base + 4, src, part(idx(0, 0), lo, HB), sa, 1)
        net.put(base + 5, src, part(idx(0, 0), lo, HB), sa, -1)
    for base, lo, fa, sa, idx in halves:
        p = part(idx(-1, 0), lo, HB)
        net.got(base + 0, p)
        a = part(idx(-1, 0), lo, QB)
        net.put(base + 2, a, a, fa, 1)
        p2 = part(idx(1, 0), lo, HB)
        net.got(base + 1, p2)
        b = part(idx(1, 0), lo + QB, QB)
        net.put(base + 3, b, b, fa, -1)
        for k, q in ((1, p), (2, p2)):
            net.put(base + 4 + 4 * k, q, q, sa, 1)
            net.put(base + 5 + 4 * k, q, q, sa, -1)
    for k in range(4):
        for base, lo, fa, sa, idx in halves:
            if k == 2:
                net.got(base + 2, part(idx(2, 0), lo, QB))
                net.got(base + 3, part(idx(2, 0), lo + QB, QB))
                q = part(idx(2, 0), lo, HB)
                net.put(base + 4 + 12, q, q, sa, 1)
                net.put(base + 5 + 12, q, q, sa, -1)
            net.got(base + 4 + 4 * k, part(idx(pieces[k], -1), lo, HB))
            a = part(idx(pieces[k], -1), lo, QB)
            net.put(base + 6 + 4 * k, a, a, sa, 1)
            net.got(base + 5 + 4 * k, part(idx(pieces[k], 1), lo, HB))
            b = part(idx(pieces[k], 1), lo + QB, QB)
            net.put(base + 7 + 4 * k, b, b, sa, -1)
    for k in range(4):
        for base, lo, fa, sa, idx in halves:
            net.got(base + 6 + 4 * k, part(idx(pieces[k], 2), lo, QB))
            net.got(base + 7 + 4 * k, part(idx(pieces[k], 2), lo + QB, QB))
    net.drain()
    lc.wait()

def all_gather(own, cid=1):
    return pl.pallas_call(
        ag_kernel,
        out_shape=jax.ShapeDtypeStruct((16, R, 128), jnp.bfloat16),
        in_specs=[pl.BlockSpec(memory_space=pl.ANY)],
        out_specs=pl.BlockSpec(memory_space=pl.ANY),
        scratch_shapes=[pltpu.SemaphoreType.DMA((40,)), pltpu.SemaphoreType.DMA((40,)), pltpu.SemaphoreType.DMA],
        compiler_params=pltpu.CompilerParams(collective_id=cid, has_side_effects=True),
    )(own)

def add_into(dst, srcs, n, dtype=None, out=None):
    out = dst if out is None else out
    @pl.loop(0, n // LOOP)
    def _(i):
        s = pl.ds(pl.multiple_of(i * LOOP, LOOP), LOOP)
        v = dst[s].astype(jnp.float32)
        for r in srcs:
            v = v + r[s].astype(jnp.float32)
        out[s] = v.astype(out.dtype)

def rs_kernel(g_ref, out_ref, own, r1, r2, send, recv, loc):
    net = Net(send, recv)
    co = {"dp": lax.axis_index("dp"), "seq": lax.axis_index("seq")}
    halves = []
    for h, (fa, sa) in enumerate((("dp", "seq"), ("seq", "dp"))):
        def idx(da, db, fa=fa, sa=sa):
            c = {fa: lax.rem(co[fa] + da + 4, 4), sa: lax.rem(co[sa] + db + 4, 4)}
            return c["dp"] * 4 + c["seq"]
        halves.append((h, h * HB, fa, sa, idx))
    order = (2, 1, -1, 0)
    loads = {}
    for da in (2, 1, -1, 0):
        for db in order:
            for h, lo, fa, sa, idx in halves:
                c = pltpu.make_async_copy(g_ref.at[idx(da, db), pl.ds(lo, HB)], own.at[idx(da, db), pl.ds(lo, HB)], loc.at[h, (da + 4) % 4, (db + 4) % 4])
                c.start()
                loads[h, da, db] = c
    barrier4()
    def part(idx, lo, n=QB):
        return own.at[idx, pl.ds(lo, n)]
    for t, db in enumerate(order):
        for h, lo, fa, sa, idx in halves:
            base = h * 30 + t * 6
            loads[h, 2, db].wait()
            net.put(base + 0, part(idx(2, db), lo), r1.at[h, t, 0], fa, 1)
            net.put(base + 1, part(idx(2, db), lo + QB), r1.at[h, t, 1], fa, -1)
        for h, lo, fa, sa, idx in halves:
            base = h * 30 + t * 6
            loads[h, 1, db].wait()
            net.put(base + 2, part(idx(1, db), lo + QB), r1.at[h, t, 2], fa, 1)
            loads[h, -1, db].wait()
            net.put(base + 3, part(idx(-1, db), lo), r1.at[h, t, 3], fa, -1)
    for t, db in enumerate(order):
        for h, lo, fa, sa, idx in halves:
            base = h * 30 + t * 6
            net.got(base + 0, r1.at[h, t, 0])
            add_into(part(idx(1, db), lo), [r1.at[h, t, 0]], QB)
            net.put(base + 4, part(idx(1, db), lo), r1.at[h, t, 4], fa, 1)
            net.got(base + 1, r1.at[h, t, 1])
            add_into(part(idx(-1, db), lo + QB), [r1.at[h, t, 1]], QB)
            net.put(base + 5, part(idx(-1, db), lo + QB), r1.at[h, t, 5], fa, -1)
    for t, db in enumerate(order):
        for h, lo, fa, sa, idx in halves:
            base = h * 30 + t * 6
            loads[h, 0, db].wait()
            net.got(base + 3, r1.at[h, t, 3])
            net.got(base + 4, r1.at[h, t, 4])
            add_into(part(idx(0, db), lo), [r1.at[h, t, 3], r1.at[h, t, 4]], QB)
            net.got(base + 2, r1.at[h, t, 2])
            net.got(base + 5, r1.at[h, t, 5])
            add_into(part(idx(0, db), lo + QB), [r1.at[h, t, 2], r1.at[h, t, 5]], QB)
            base = h * 30 + 24
            if db == 2:
                net.put(base + 0, part(idx(0, 2), lo), r2.at[h, 0], sa, 1)
                net.put(base + 1, part(idx(0, 2), lo + QB), r2.at[h, 1], sa, -1)
            if db == 1:
                net.put(base + 2, part(idx(0, 1), lo + QB), r2.at[h, 2], sa, 1)
            if db == -1:
                net.put(base + 3, part(idx(0, -1), lo), r2.at[h, 3], sa, -1)
    for h, lo, fa, sa, idx in halves:
        base = h * 30 + 24
        net.got(base + 0, r2.at[h, 0])
        add_into(part(idx(0, 1), lo), [r2.at[h, 0]], QB)
        net.put(base + 4, part(idx(0, 1), lo), r2.at[h, 4], sa, 1)
        net.got(base + 1, r2.at[h, 1])
        add_into(part(idx(0, -1), lo + QB), [r2.at[h, 1]], QB)
        net.put(base + 5, part(idx(0, -1), lo + QB), r2.at[h, 5], sa, -1)
    for h, lo, fa, sa, idx in halves:
        base = h * 30 + 24
        net.got(base + 3, r2.at[h, 3])
        net.got(base + 4, r2.at[h, 4])
        add_into(part(idx(0, 0), lo), [r2.at[h, 3], r2.at[h, 4]], QB, out=out_ref.at[pl.ds(lo, QB)])
        net.got(base + 2, r2.at[h, 2])
        net.got(base + 5, r2.at[h, 5])
        add_into(part(idx(0, 0), lo + QB), [r2.at[h, 2], r2.at[h, 5]], QB, out=out_ref.at[pl.ds(lo + QB, QB)])
    net.drain()

def reduce_scatter(g, cid=2):
    return pl.pallas_call(
        rs_kernel,
        out_shape=jax.ShapeDtypeStruct((R, 128), jnp.float32),
        in_specs=[pl.BlockSpec(memory_space=pl.ANY)],
        out_specs=pl.BlockSpec(memory_space=pltpu.VMEM),
        scratch_shapes=[pltpu.VMEM((16, R, 128), jnp.bfloat16), pltpu.VMEM((2, 4, 6, QB, 128), jnp.bfloat16), pltpu.VMEM((2, 6, QB, 128), jnp.bfloat16),
            pltpu.SemaphoreType.DMA((60,)), pltpu.SemaphoreType.DMA((60,)), pltpu.SemaphoreType.DMA((2, 4, 4))],
        compiler_params=pltpu.CompilerParams(collective_id=cid, has_side_effects=True, vmem_limit_bytes=50 * 2**20),
    )(g)


def tree_geometry(parent_row):
    blocks = parent_row.shape[0]
    block_ids = jnp.arange(blocks, dtype=jnp.int32)

    link = (parent_row[:, None] == block_ids[None, :]).astype(jnp.float32)
    unit = (block_ids[:, None] == block_ids[None, :]).astype(jnp.float32)
    two = jnp.sum(link[:, :, None] * link[None], axis=1)
    three = jnp.sum(two[:, :, None] * link[None], axis=1)
    reach_table = unit + link + two + three
    depth_table = jnp.sum(reach_table, axis=1) - 1.0
    return (reach_table, depth_table)


def rotate(values, cosine, sine_table):
    half_width = values.shape[-1] // 2
    lower_half = values[..., :half_width]
    upper_half = values[..., half_width:]
    return jnp.concatenate(
        [
            lower_half * cosine - upper_half * sine_table,
            upper_half * cosine + lower_half * sine_table,
        ],
        axis=-1,
    )


def unrotate(values, cosine, sine_table):
    half_width = values.shape[-1] // 2
    lower_half = values[..., :half_width]
    upper_half = values[..., half_width:]
    return jnp.concatenate(
        [
            lower_half * cosine + upper_half * sine_table,
            upper_half * cosine - lower_half * sine_table,
        ],
        axis=-1,
    )


def norm_back(grad_normed, values, rms_vals, gain_row):
    weighted = grad_normed * gain_row
    gain_part = jnp.sum(grad_normed * values * rms_vals, axis=0)
    grad_values = rms_vals * weighted - values * rms_vals**3 * jnp.mean(
        weighted * values, axis=-1, keepdims=True
    )
    return (grad_values, gain_part)


def adamw(master, first, second, grad_vals, fix_one, fix_two):
    momentum = BETA_ONE * first + (1.0 - BETA_ONE) * grad_vals
    variance = BETA_TWO * second + (1.0 - BETA_TWO) * grad_vals * grad_vals
    direction = momentum / fix_one / (jnp.sqrt(variance / fix_two) + ADAM_EPS)
    renewed = master - LEARN_RATE * (direction + DECAY_RATE * master)
    return (renewed, momentum, variance)


def on_device(
    inputs,
    cotangent,
    parents,
    weight_attend,
    weight_merge,
    weight_expand,
    weight_reduce,
    gains,
    master_attend,
    master_merge,
    master_expand,
    master_reduce,
    master_gains,
    first_attend,
    first_merge,
    first_expand,
    first_reduce,
    first_gains,
    second_attend,
    second_merge,
    second_expand,
    second_reduce,
    second_gains,
):
    micro_count = inputs.shape[0]
    local_len = inputs.shape[1]
    full_len = local_len * lax.axis_size("seq")
    blocks = parents.shape[1]
    block_len = full_len // blocks
    kv_local = weight_attend.shape[1] // ((G + 2) * HD)
    att_scale = HD ** (-0.5)
    first_row = lax.axis_index("seq") * local_len
    key_tokens = jnp.arange(full_len, dtype=jnp.int32)
    query_tokens = first_row + jnp.arange(local_len, dtype=jnp.int32)
    block_ids = jnp.arange(blocks, dtype=jnp.int32)
    key_onehot = (key_tokens[:, None] // block_len == block_ids[None, :]).astype(jnp.float32)
    query_onehot = (query_tokens[:, None] // block_len == block_ids[None, :]).astype(jnp.float32)
    same_block = query_tokens[:, None] // block_len == key_tokens[None, :] // block_len
    causal = key_tokens[None, :] % block_len <= query_tokens[:, None] % block_len
    offsets = (query_tokens % block_len).astype(jnp.float32)
    inv_freq = ROPE_BASE ** (-2.0 * jnp.arange(HD // 2, dtype=jnp.float32) / HD)
    gain_one = gains[0].astype(jnp.float32)
    gain_two = gains[1].astype(jnp.float32)
    template = (weight_attend, weight_merge, weight_expand, weight_reduce, gains)
    running = tuple((jnp.zeros(w.shape, jnp.float32) for w in template))
    outputs_list = []
    grads_list = []
    for tree_index in range(micro_count):
        reach_table, depth_table = tree_geometry(parents[tree_index])
        positions = jnp.dot(query_onehot, depth_table, precision=PRECISE) * block_len + offsets
        angles = positions[:, None] * inv_freq[None, :]
        cosine = jnp.cos(angles)
        sine_table = jnp.sin(angles)
        cos_four = cosine[:, None, None, :]
        sin_four = sine_table[:, None, None, :]
        cos_three = cosine[:, None, :]
        sin_three = sine_table[:, None, :]
        reach_rows = jnp.einsum(
            "qb,kb->qk",
            jnp.dot(query_onehot, reach_table, precision=PRECISE),
            key_onehot,
            precision=PRECISE,
        )
        visible = (reach_rows > 0.5) & (~same_block | causal)
        x_rows = inputs[tree_index].astype(jnp.float32)
        rms_one = lax.rsqrt(jnp.mean(x_rows * x_rows, axis=-1, keepdims=True) + NORM_EPS)
        normed_one = (x_rows * rms_one * gain_one).astype(jnp.bfloat16)
        packed = jnp.dot(normed_one, weight_attend, preferred_element_type=jnp.float32).reshape(
            local_len, kv_local, G + 2, HD
        )
        queries = rotate(packed[:, :, :G], cos_four, sin_four).astype(jnp.bfloat16)
        key_own = rotate(packed[:, :, G], cos_three, sin_three).astype(jnp.bfloat16)
        value_own = packed[:, :, G + 1].astype(jnp.bfloat16)
        pair_own = jnp.stack([key_own, value_own], axis=2).reshape(local_len, kv_local * 2 * HD)
        pair_all = lax.all_gather(pair_own, "seq", axis=0, tiled=True).reshape(
            full_len, kv_local, 2, HD
        )
        key_all = pair_all[:, :, 0]
        value_all = pair_all[:, :, 1]

        def masked_scores():
            raw_scores = (
                jnp.einsum("tkgd,skd->kgts", queries, key_all, preferred_element_type=jnp.float32)
                * att_scale
            )
            return jnp.where(visible[None, None], raw_scores, MASK_FILL)

        scores = masked_scores()
        row_max = jnp.max(scores, axis=-1, keepdims=True)
        exp_scores = jnp.exp(scores - row_max)
        row_total = jnp.sum(exp_scores, axis=-1, keepdims=True)
        log_total = row_max + jnp.log(row_total)
        probs_low = (exp_scores / row_total).astype(jnp.bfloat16)
        attended = jnp.einsum(
            "kgts,skd->tkgd", probs_low, value_all, preferred_element_type=jnp.float32
        )
        attended = attended.reshape(local_len, kv_local * G * HD).astype(jnp.bfloat16)
        attn_part = jnp.dot(attended, weight_merge, preferred_element_type=jnp.float32)
        middle = x_rows + lax.psum(attn_part, "mp")
        rms_two = lax.rsqrt(jnp.mean(middle * middle, axis=-1, keepdims=True) + NORM_EPS)
        normed_two = (middle * rms_two * gain_two).astype(jnp.bfloat16)
        expanded = jnp.einsum(
            "tc,cjf->tjf", normed_two, weight_expand, preferred_element_type=jnp.float32
        )
        gate_pre = expanded[:, 0]
        up_pre = expanded[:, 1]
        sigmoid_gate = jax.nn.sigmoid(gate_pre)
        silu_gate = gate_pre * sigmoid_gate
        hidden = (silu_gate * up_pre).astype(jnp.bfloat16)
        reduce_part = jnp.dot(hidden, weight_reduce, preferred_element_type=jnp.float32)
        result = middle + lax.psum(reduce_part.astype(jnp.bfloat16), "mp").astype(jnp.float32)
        outputs_list.append(result.astype(jnp.bfloat16))
        cot_low = cotangent[tree_index]
        grad_reduce = jnp.einsum("tf,td->fd", hidden, cot_low, preferred_element_type=jnp.float32)
        grad_hidden = jnp.einsum(
            "td,fd->tf", cot_low, weight_reduce, preferred_element_type=jnp.float32
        )
        grad_gate = grad_hidden * up_pre * sigmoid_gate * (1.0 + gate_pre * (1.0 - sigmoid_gate))
        grad_upper = grad_hidden * silu_gate
        grad_pair_ff = jnp.stack([grad_gate, grad_upper], axis=1).astype(jnp.bfloat16)
        grad_expand = jnp.einsum(
            "tc,tjf->cjf", normed_two, grad_pair_ff, preferred_element_type=jnp.float32
        )
        normed_two_part = jnp.einsum(
            "tjf,cjf->tc", grad_pair_ff, weight_expand, preferred_element_type=jnp.float32
        )
        grad_normed_two = lax.psum(normed_two_part.astype(jnp.bfloat16), "mp").astype(jnp.float32)
        grad_middle, gain_part_two = norm_back(grad_normed_two, middle, rms_two, gain_two)
        grad_middle = grad_middle + cot_low.astype(jnp.float32)
        grad_branch = grad_middle.astype(jnp.bfloat16)
        grad_merge = jnp.einsum(
            "tc,td->cd", attended, grad_branch, preferred_element_type=jnp.float32
        )
        grad_attended = jnp.einsum(
            "td,cd->tc", grad_branch, weight_merge, preferred_element_type=jnp.float32
        )
        grad_attended = grad_attended.astype(jnp.bfloat16).reshape(local_len, kv_local, G, HD)
        probs_full = jnp.exp(masked_scores() - log_total)
        probs_again = probs_full.astype(jnp.bfloat16)
        grad_probs = jnp.einsum(
            "tkgd,skd->kgts", grad_attended, value_all, preferred_element_type=jnp.float32
        )
        inner_sum = jnp.sum(probs_full * grad_probs, axis=-1, keepdims=True)
        grad_scores = (probs_full * (grad_probs - inner_sum)).astype(jnp.bfloat16)
        grad_queries = (
            jnp.einsum("kgts,skd->tkgd", grad_scores, key_all, preferred_element_type=jnp.float32)
            * att_scale
        )
        grad_keys = (
            jnp.einsum("kgts,tkgd->skd", grad_scores, queries, preferred_element_type=jnp.float32)
            * att_scale
        )
        grad_values = jnp.einsum(
            "kgts,tkgd->skd", probs_again, grad_attended, preferred_element_type=jnp.float32
        )
        grad_kv = jnp.stack([grad_keys, grad_values], axis=2).reshape(full_len, kv_local * 2 * HD)
        grad_kv = (
            lax.psum_scatter(grad_kv.astype(jnp.bfloat16), "seq", scatter_dimension=0, tiled=True)
            .astype(jnp.float32)
            .reshape(local_len, kv_local, 2, HD)
        )
        grad_packed = jnp.concatenate(
            [
                unrotate(grad_queries, cos_four, sin_four),
                unrotate(grad_kv[:, :, 0], cos_three, sin_three)[:, :, None],
                grad_kv[:, :, 1:2],
            ],
            axis=2,
        )
        grad_packed = grad_packed.reshape(local_len, kv_local * (G + 2) * HD).astype(jnp.bfloat16)
        grad_attend = jnp.einsum(
            "tc,tq->cq", normed_one, grad_packed, preferred_element_type=jnp.float32
        )
        normed_one_part = jnp.einsum(
            "tq,cq->tc", grad_packed, weight_attend, preferred_element_type=jnp.float32
        )
        grad_normed_one = lax.psum(normed_one_part.astype(jnp.bfloat16), "mp").astype(jnp.float32)
        grad_input, gain_part_one = norm_back(grad_normed_one, x_rows, rms_one, gain_one)
        grads_list.append((grad_middle + grad_input).astype(jnp.bfloat16))
        tree_grads = (
            grad_attend,
            grad_merge,
            grad_expand,
            grad_reduce,
            jnp.stack([gain_part_one, gain_part_two]),
        )
        running = tuple((a + b for a, b in zip(running, tree_grads)))
    low = [g.astype(jnp.bfloat16) for g in running]
    gain_part = jnp.pad(low[4].reshape(2, 16, 128).transpose(1, 0, 2), ((0, 0), (0, 126), (0, 0)))
    packs = jnp.concatenate(
        [
            low[0].reshape(16, 384, 128),
            low[1].reshape(256, 16, 128).transpose(1, 0, 2),
            low[2].reshape(16, 2048, 128),
            low[3].reshape(1024, 16, 128).transpose(1, 0, 2),
            gain_part,
        ],
        axis=1,
    )
    total = reduce_scatter(packs)
    shard_grads = (
        total[:384].reshape(128, 384),
        total[384:640],
        total[640:2688].reshape(128, 2, 1024),
        total[2688:3712],
        total[3712:3714],
    )
    fix_one = 1.0 - BETA_ONE**STEP
    fix_two = 1.0 - BETA_TWO**STEP
    masters = (master_attend, master_merge, master_expand, master_reduce, master_gains)
    firsts = (first_attend, first_merge, first_expand, first_reduce, first_gains)
    seconds = (second_attend, second_merge, second_expand, second_reduce, second_gains)
    updated = [
        adamw(mw, fw, sw, gw, fix_one, fix_two)
        for mw, fw, sw, gw in zip(masters, firsts, seconds, shard_grads)
    ]
    fresh = [u[0].astype(jnp.bfloat16) for u in updated]
    own = jnp.concatenate(
        [
            fresh[0].reshape(384, 128),
            fresh[1],
            fresh[2].reshape(2048, 128),
            fresh[3],
            jnp.pad(fresh[4], ((0, 126), (0, 0))),
        ],
        axis=0,
    )
    every = all_gather(own)
    rounded_full = (
        every[:, :384].reshape(2048, 384),
        every[:, 384:640].transpose(1, 0, 2).reshape(256, 2048),
        every[:, 640:2688].reshape(2048, 2, 1024),
        every[:, 2688:3712].transpose(1, 0, 2).reshape(1024, 2048),
        every[:, 3712:3714].transpose(1, 0, 2).reshape(2, 2048),
    )
    return (
        jnp.stack(outputs_list),
        jnp.stack(grads_list),
        updated[0][0],
        updated[1][0],
        updated[2][0],
        updated[3][0],
        updated[4][0],
        updated[0][1],
        updated[1][1],
        updated[2][1],
        updated[3][1],
        updated[4][1],
        updated[0][2],
        updated[1][2],
        updated[2][2],
        updated[3][2],
        updated[4][2],
        rounded_full[0],
        rounded_full[1],
        rounded_full[2],
        rounded_full[3],
        rounded_full[4],
    )


def solution(mesh):
    return jax.shard_map(
        on_device,
        mesh=mesh,
        in_specs=(
            P("dp", "seq", None),
            P("dp", "seq", None),
            P("dp", None),
            P(None, "mp"),
            P("mp", None),
            P(None, None, "mp"),
            P("mp", None),
            P(),
            P(("dp", "seq"), "mp"),
            P("mp", ("dp", "seq")),
            P(("dp", "seq"), None, "mp"),
            P("mp", ("dp", "seq")),
            P(None, ("dp", "seq")),
            P(("dp", "seq"), "mp"),
            P("mp", ("dp", "seq")),
            P(("dp", "seq"), None, "mp"),
            P("mp", ("dp", "seq")),
            P(None, ("dp", "seq")),
            P(("dp", "seq"), "mp"),
            P("mp", ("dp", "seq")),
            P(("dp", "seq"), None, "mp"),
            P("mp", ("dp", "seq")),
            P(None, ("dp", "seq")),
        ),
        out_specs=(
            P("dp", "seq", None),
            P("dp", "seq", None),
            P(("dp", "seq"), "mp"),
            P("mp", ("dp", "seq")),
            P(("dp", "seq"), None, "mp"),
            P("mp", ("dp", "seq")),
            P(None, ("dp", "seq")),
            P(("dp", "seq"), "mp"),
            P("mp", ("dp", "seq")),
            P(("dp", "seq"), None, "mp"),
            P("mp", ("dp", "seq")),
            P(None, ("dp", "seq")),
            P(("dp", "seq"), "mp"),
            P("mp", ("dp", "seq")),
            P(("dp", "seq"), None, "mp"),
            P("mp", ("dp", "seq")),
            P(None, ("dp", "seq")),
            P(None, "mp"),
            P("mp", None),
            P(None, None, "mp"),
            P("mp", None),
            P(),
        ),
        check_vma=False,
    )
```

```python
import functools

import jax
import jax.numpy as jnp
import numpy as np
from jax import lax
from jax.experimental import pallas as pl
from jax.experimental.pallas import tpu as pltpu
from jax.sharding import PartitionSpec as P

MESH = pl.DeviceIdType.MESH
F32 = jnp.float32
BF16 = jnp.bfloat16
D = 2048
HD = 64
STEP = 5
NORM_EPS = 1e-05
ROPE_BASE = 500000.0
MASK_FILL = -1e30
BETA_ONE = 0.5
BETA_TWO = 0.5
ADAM_EPS = 1e-08
LEARN_RATE = 0.005
DECAY_RATE = 0.1
FIX_ONE = 1.0 - BETA_ONE**STEP
FIX_TWO = 1.0 - BETA_TWO**STEP
SIZES = {"dp": 4, "seq": 4, "mp": 8}


def adamw(master, first, second, grad_vals):
    momentum = BETA_ONE * first + (1.0 - BETA_ONE) * grad_vals
    variance = BETA_TWO * second + (1.0 - BETA_TWO) * grad_vals * grad_vals
    direction = momentum / FIX_ONE / (jnp.sqrt(variance / FIX_TWO) + ADAM_EPS)
    renewed = master - LEARN_RATE * (direction + DECAY_RATE * master)
    return (renewed, momentum, variance)


def dot(a, b):
    return lax.dot_general(a, b, (((1,), (0,)), ((), ())), preferred_element_type=F32)


def dot_nt(a, b):
    return lax.dot_general(a, b, (((1,), (1,)), ((), ())), preferred_element_type=F32)


def dot_tn(a, b):
    return lax.dot_general(a, b, (((0,), (0,)), ((), ())), preferred_element_type=F32)


def shifted(axis, delta):
    n = SIZES[axis]
    return lax.rem(lax.axis_index(axis) + (delta + n), n)


def sibling():
    m = lax.axis_index("mp")
    return m + 1 - 2 * lax.rem(m, 2)


def rows(start, n):
    return pl.ds(pl.multiple_of(start, 16), n)


class Net:
    def __init__(self, send, recv, count):
        self.send, self.recv, self.count = send, recv, count
        self.used = 0
        self.started = {}

    def ids(self, n):
        first = self.used
        self.used += n
        assert self.used <= self.count
        return first

    def put(self, k, src, dst, axis, index):
        c = pltpu.make_async_remote_copy(
            src_ref=src,
            dst_ref=dst,
            send_sem=self.send.at[k],
            recv_sem=self.recv.at[k],
            device_id={axis: index},
            device_id_type=MESH,
        )
        c.start()
        self.started[k] = c

    def got(self, k, dst):
        pltpu.make_async_remote_copy(
            src_ref=dst,
            dst_ref=dst,
            send_sem=self.send.at[k],
            recv_sem=self.recv.at[k],
            device_id={"dp": shifted("dp", 1)},
            device_id_type=MESH,
        ).wait_recv()

    def sent(self, k):
        self.started.pop(k).wait_send()

    def drain(self):
        for k in sorted(self.started):
            self.started[k].wait_send()
        self.started = {}


def hello(peers):
    sem = pltpu.get_barrier_semaphore()
    for axis, index in peers:
        pl.semaphore_signal(sem, inc=1, device_id={axis: index}, device_id_type=MESH)


def hello_wait(n):
    pl.semaphore_wait(pltpu.get_barrier_semaphore(), n)


class Spread:
    def __init__(self, net, own, first, second):
        self.net, self.own, self.r1, self.r2 = net, own, first, second
        self.size, self.cols = own.shape[2], own.shape[3]
        self.q = self.size // 4
        self.base = net.ids(24)
        self.chunk = min(self.q, max(16, 16384 // self.cols))

    def axes(self, h):
        return (("dp", "seq"), ("seq", "dp"))[h]

    def row(self, h, da):
        a = shifted(self.axes(h)[0], da)
        return (lambda b: (a, b)) if h == 0 else (lambda b: (b, a))

    def block(self, h, db):
        a, b = lax.axis_index(self.axes(h)[0]), shifted(self.axes(h)[1], db)
        return (a, b) if h == 0 else (b, a)

    def view(self, h, da, lo):
        a = shifted(self.axes(h)[0], da)
        if h == 0:
            return self.own.at[a, pl.ds(0, 4), pl.ds(lo, self.q)]
        return self.own.at[pl.ds(0, 4), a, pl.ds(lo, self.q)]

    def one(self, h, db, lo):
        a, b = self.block(h, db)
        return self.own.at[a, b, pl.ds(lo, self.q)]

    def add(self, index_of, count, lo, sources, out=None):
        steps = self.q // self.chunk

        @pl.loop(0, count * steps)
        def _(k):
            b = k // steps
            r = (k % steps) * self.chunk
            at = (*index_of(b), rows(lo + r, self.chunk))
            v = self.own[at].astype(F32)
            for ref, lead in sources:
                if count > 1:
                    v = v + ref[(*lead, b, rows(r, self.chunk))].astype(F32)
                else:
                    v = v + ref[(*lead, rows(r, self.chunk))].astype(F32)
            if out is None:
                self.own[at] = v.astype(BF16)
            else:
                out[rows(lo + r, self.chunk)] = v

    def step0(self):
        q = self.q
        for h in (0, 1):
            fa, lo, base = self.axes(h)[0], 2 * h * q, self.base + 12 * h
            self.net.put(base + 0, self.view(h, 2, lo), self.r1.at[h, 0], fa, shifted(fa, 1))
            self.net.put(base + 1, self.view(h, 2, lo + q), self.r1.at[h, 1], fa, shifted(fa, -1))
        for h in (0, 1):
            fa, lo, base = self.axes(h)[0], 2 * h * q, self.base + 12 * h
            self.net.put(base + 2, self.view(h, 1, lo + q), self.r1.at[h, 2], fa, shifted(fa, 1))
            self.net.put(base + 3, self.view(h, -1, lo), self.r1.at[h, 3], fa, shifted(fa, -1))

    def step1(self):
        q = self.q
        for h in (0, 1):
            fa, lo, base = self.axes(h)[0], 2 * h * q, self.base + 12 * h
            self.net.got(base + 0, self.r1.at[h, 0])
            self.add(self.row(h, 1), 4, lo, [(self.r1, (h, 0))])
            self.net.put(base + 4, self.view(h, 1, lo), self.r1.at[h, 4], fa, shifted(fa, 1))
            self.net.got(base + 1, self.r1.at[h, 1])
            self.add(self.row(h, -1), 4, lo + q, [(self.r1, (h, 1))])
            self.net.put(base + 5, self.view(h, -1, lo + q), self.r1.at[h, 5], fa, shifted(fa, -1))

    def step2(self):
        q = self.q
        for h in (0, 1):
            sa, lo, base = self.axes(h)[1], 2 * h * q, self.base + 12 * h
            for k in (3, 4):
                self.net.got(base + k, self.r1.at[h, k])
            self.add(self.row(h, 0), 4, lo, [(self.r1, (h, 3)), (self.r1, (h, 4))])
            for k in (2, 5):
                self.net.got(base + k, self.r1.at[h, k])
            self.add(self.row(h, 0), 4, lo + q, [(self.r1, (h, 2)), (self.r1, (h, 5))])
            base += 6
            self.net.put(base + 0, self.one(h, 2, lo), self.r2.at[h, 0], sa, shifted(sa, 1))
            self.net.put(base + 1, self.one(h, 2, lo + q), self.r2.at[h, 1], sa, shifted(sa, -1))
            self.net.put(base + 2, self.one(h, 1, lo + q), self.r2.at[h, 2], sa, shifted(sa, 1))
            self.net.put(base + 3, self.one(h, -1, lo), self.r2.at[h, 3], sa, shifted(sa, -1))

    def step3(self):
        q = self.q
        for h in (0, 1):
            sa, lo, base = self.axes(h)[1], 2 * h * q, self.base + 12 * h + 6
            self.net.got(base + 0, self.r2.at[h, 0])
            at = self.block(h, 1)
            self.add(lambda b: at, 1, lo, [(self.r2, (h, 0))])
            self.net.put(base + 4, self.one(h, 1, lo), self.r2.at[h, 4], sa, shifted(sa, 1))
            self.net.got(base + 1, self.r2.at[h, 1])
            at2 = self.block(h, -1)
            self.add(lambda b: at2, 1, lo + q, [(self.r2, (h, 1))])
            self.net.put(base + 5, self.one(h, -1, lo + q), self.r2.at[h, 5], sa, shifted(sa, -1))

    def step4(self, out):
        q = self.q
        for h in (0, 1):
            lo, base = 2 * h * q, self.base + 12 * h + 6
            at = self.block(h, 0)
            for k in (3, 4):
                self.net.got(base + k, self.r2.at[h, k])
            self.add(lambda b: at, 1, lo, [(self.r2, (h, 3)), (self.r2, (h, 4))], out)
            for k in (2, 5):
                self.net.got(base + k, self.r2.at[h, k])
            self.add(lambda b: at, 1, lo + q, [(self.r2, (h, 2)), (self.r2, (h, 5))], out)


class Fold:
    def __init__(self, net, acc, rsib, zsend, zrec):
        self.net, self.acc, self.rsib, self.zsend, self.zrec = net, acc, rsib, zsend, zrec
        self.base = net.ids(10)

    def quarter(self, d):
        return 64 * lax.rem(lax.axis_index("mp") // 2 + (d + 4), 4)

    def right(self):
        return shifted("mp", 2)

    def left(self):
        return shifted("mp", -2)

    def send_columns(self, k, src):
        cols = pl.ds(512 * k, 512)
        self.net.put(self.base + k, src.at[:, cols], self.rsib.at[:, cols], "mp", sibling())

    def columns_here(self):
        for k in range(4):
            self.net.got(self.base + k, self.rsib.at[:, pl.ds(512 * k, 512)])

    def send_rows(self, src):
        for k, d in enumerate((2, 1, -1, 0)):
            at = rows(self.quarter(d), 64)
            self.net.put(self.base + k, src.at[at], self.rsib.at[at], "mp", sibling())

    def total(self, d, own, store):
        start = self.quarter(d)

        @pl.loop(0, 4)
        def _(i):
            at = rows(start + 16 * i, 16)
            v = own[at].astype(F32) + self.rsib[at].astype(F32)
            self.acc[at] = v
            if store:
                self.zsend[at] = v.astype(BF16)

    def begin(self, own, by_rows):
        put, base = self.net.put, self.base + 4

        def arrived(k, d):
            if by_rows:
                at = rows(self.quarter(d), 64)
                self.net.got(self.base + k, self.rsib.at[at])

        if not by_rows:
            self.columns_here()
        arrived(0, 2)
        self.total(2, own, True)
        s = self.quarter(2)
        put(base + 0, self.zsend.at[rows(s, 32)], self.zrec.at[0], "mp", self.right())
        put(base + 1, self.zsend.at[rows(s + 32, 32)], self.zrec.at[1], "mp", self.left())
        arrived(1, 1)
        self.total(1, own, True)
        put(base + 2, self.zsend.at[rows(self.quarter(1) + 32, 32)], self.zrec.at[2], "mp", self.right())
        arrived(2, -1)
        self.total(-1, own, True)
        put(base + 3, self.zsend.at[rows(self.quarter(-1), 32)], self.zrec.at[3], "mp", self.left())
        arrived(3, 0)
        self.total(0, own, False)

    def middle(self):
        base = self.base + 4
        for k, d, off, way in ((0, 1, 0, self.right()), (1, -1, 32, self.left())):
            self.net.got(base + k, self.zrec.at[k])
            start = self.quarter(d) + off

            @pl.loop(0, 2)
            def _(i):
                at = rows(start + 16 * i, 16)
                v = self.acc[at] + self.zrec[k, rows(16 * i, 16)].astype(F32)
                self.zsend[at] = v.astype(BF16)

            self.net.put(base + 4 + k, self.zsend.at[rows(start, 32)], self.zrec.at[4 + k], "mp", way)

    def finish(self, use):
        base = self.base + 4
        for part, pair in ((0, (3, 4)), (1, (2, 5))):
            for k in pair:
                self.net.got(base + k, self.zrec.at[k])
            start = self.quarter(0) + 32 * part

            @pl.loop(0, 2)
            def _(i):
                v = self.acc[rows(start + 16 * i, 16)]
                for k in pair:
                    v = v + self.zrec[k, rows(16 * i, 16)].astype(F32)
                use(32 * part + 16 * i, v)

    def release(self):
        for k in range(10):
            if self.base + k in self.net.started:
                self.net.sent(self.base + k)


class Share:
    def __init__(self, net, out):
        self.net, self.out = net, out
        self.base = net.ids(8)

    def at(self, d, other=False, lo=0, n=64):
        m = lax.axis_index("mp")
        core = lax.rem(m, 2)
        if other:
            core = 1 - core
        return self.out.at[core, lax.rem(m // 2 + (d + 4), 4), pl.ds(lo, n)]

    def begin(self, src=None):
        src = self.at(0) if src is None else src
        put, base = self.net.put, self.base
        put(base + 0, src, self.at(0), "mp", shifted("mp", 2))
        put(base + 1, src, self.at(0), "mp", shifted("mp", -2))
        put(base + 4, src, self.at(0), "mp", sibling())

    def middle(self):
        put, base = self.net.put, self.base
        self.net.got(base + 0, self.at(-1))
        put(base + 2, self.at(-1, False, 0, 32), self.at(-1, False, 0, 32), "mp", shifted("mp", 2))
        self.net.got(base + 1, self.at(1))
        put(base + 3, self.at(1, False, 32, 32), self.at(1, False, 32, 32), "mp", shifted("mp", -2))
        put(base + 5, self.at(-1), self.at(-1), "mp", sibling())
        put(base + 6, self.at(1), self.at(1), "mp", sibling())

    def later(self):
        self.net.got(self.base + 2, self.at(2, False, 0, 32))
        self.net.got(self.base + 3, self.at(2, False, 32, 32))
        self.net.put(self.base + 7, self.at(2), self.at(2), "mp", sibling())

    def finish(self):
        for k, d in ((4, 0), (5, -1), (6, 1), (7, 2)):
            self.net.got(self.base + k, self.at(d, True))

    def release(self):
        for k in range(8):
            self.net.sent(self.base + k)


class Stream:
    def __init__(self, make):
        self.make = make

    def start(self, j):
        for c in self.make(j, j % 2):
            c.start()

    def wait(self, j):
        for c in self.make(j, j % 2):
            c.wait()

    def run(self, count, body, first=0):
        @pl.loop(0, count)
        def _(i):
            self.wait(first + i)
            body(i, (first + i) % 2)

            @pl.when(i + 2 < count)
            def _():
                self.start(first + i + 2)


def lanes(shape):
    return lax.broadcasted_iota(jnp.int32, shape, len(shape) - 1)


def swap_halves(v):
    lane = lanes(v.shape)
    return jnp.where(lane % HD < HD // 2, pltpu.roll(v, 96, 1), pltpu.roll(v, 32, 1))


def main_kernel(
    x_hbm, cot_hbm, parents, wa_hbm, wm_hbm, we_hbm, wr_hbm, gains, table,
    y2_hbm, y4_hbm, spill, mid, dmid, gpart, o_att, o_mrg, o_gate, o_up, o_red,
    g_red, g_gate, g_up, g_mrg, g_att,
    ra_red, ra_gate, ra_up, ra_mrg, ra_att,
    rb_red, rb_gate, rb_up, rb_mrg, rb_att,
    sa, sb, wa, wm, xd, cot, n1, tt, n2, hid, hid_t,
    acc, sib, rsib, zrec, probs, kv, q, att, datt, dkv, dkv_low, dkv_in, dpack,
    send, recv, loc, wsem,
):
    net = Net(send, recv, send.shape[0])
    m = lax.axis_index("mp")
    core, z = lax.rem(m, 2), m // 2
    seq = lax.axis_index("seq")
    other = 1 - core
    hello(
        [("dp", shifted("dp", 1)), ("dp", shifted("dp", -1))]
        + [("seq", shifted("seq", d)) for d in (1, 2, 3)]
        + [("mp", shifted("mp", 2)), ("mp", shifted("mp", -2)), ("mp", sibling())]
    )
    base_kv, base_dkv = net.ids(3), net.ids(3)
    fold = Fold(net, acc, rsib, sib, zrec)
    share_one, share_two = Share(net, n2), Share(net, xd)
    s_red = Spread(net, g_red, ra_red, rb_red)
    s_gate = Spread(net, g_gate, ra_gate, rb_gate)
    s_up = Spread(net, g_up, ra_up, rb_up)
    s_mrg = Spread(net, g_mrg, ra_mrg, rb_mrg)
    s_att = Spread(net, g_att, ra_att, rb_att)

    def bring(k, src, dst):
        c = pltpu.make_async_copy(src, dst, loc.at[k])
        c.start()
        return c

    c_x = [bring(t, x_hbm.at[t], xd.at[t]) for t in (0, 1)]
    c_wa = bring(2, wa_hbm, wa)
    c_cot = bring(3, cot_hbm, cot)
    c_wm = bring(4, wm_hbm, wm)
    down = Stream(lambda j, s: [pltpu.make_async_copy(wr_hbm.at[rows(256 * j, 256)], sb.at[s], wsem.at[0, s])])
    down.start(0)
    down.start(1)

    gain_one, gain_two = gains[0:1, :], gains[1:2, :]
    flat = xd
    for t in (0, 1):
        c_x[t].wait()

        @pl.loop(0, 16)
        def _(i):
            v = flat[t, i // 4, rows(16 * (i % 4), 16)].astype(F32)
            r = lax.rsqrt(jnp.mean(v * v, axis=-1, keepdims=True) + NORM_EPS)
            n1[t, rows(16 * i, 16)] = (v * r * gain_one).astype(BF16)

    c_wa.wait()

    def ancestors(t, b):
        p1 = parents[t, b]
        p2 = jnp.where(p1 >= 0, parents[t, jnp.maximum(p1, 0)], -1)
        p3 = jnp.where(p2 >= 0, parents[t, jnp.maximum(p2, 0)], -1)
        return p1, p2, p3

    def turns(t, i):
        ps = ancestors(t, 2 * seq + i)
        depth = sum(jnp.where(p >= 0, 1, 0) for p in ps)
        return table[0, depth], table[1, depth]

    lower = lanes((128, 128)) < HD
    for t in (0, 1):
        packed = dot(n1[t], wa[...])
        for i in (0, 1):
            c, s = turns(t, i)
            part = packed[128 * i : 128 * i + 128]
            for g in (0, 1):
                v = part[:, 128 * g : 128 * g + 128]
                q[t, i, g] = (v * c + swap_halves(v) * s).astype(BF16)
            v = part[:, 256:384]
            kv[t, 2 * seq + i] = jnp.where(lower, v * c + swap_halves(v) * s, v).astype(BF16)
    hello_wait(8)
    own_kv = kv.at[pl.ds(0, 2), pl.ds(2 * seq, 2)]
    for d in (1, 2, 3):
        net.put(base_kv + d - 1, own_kv, own_kv, "seq", shifted("seq", d))

    def transpose_into(src_of, dst):
        @pl.loop(0, 16)
        def _(j):
            cols = pl.ds(pl.multiple_of(128 * j, 128), 128)
            for t in (0, 1):
                dst[rows(128 * j, 128), 256 * t : 256 * t + 256] = src_of(t, cols).T

    transpose_into(lambda t, cols: n1[t, :, cols], tt)
    c_spill = bring(5, tt, spill)
    c_cot.wait()

    def hidden_grad(j, s):
        v = dot_nt(cot[...].reshape(512, D), sb[s])
        high = v.astype(BF16)
        low = (v - high.astype(F32)).astype(BF16)
        cols = pl.ds(pl.multiple_of(256 * j, 256), 256)
        g_gate[0, :, :, cols] = high.reshape(4, 128, 256)
        g_gate[1, :, :, cols] = low.reshape(4, 128, 256)

    down.run(4, hidden_grad)

    for d in (1, 2, 3):
        net.got(base_kv + d - 1, kv.at[pl.ds(0, 2), pl.ds(2 * shifted("seq", -d), 2)])

    low_lane = lanes((512, 128)) < HD
    key_col = lanes((128, 512))
    query_row = lax.broadcasted_iota(jnp.int32, (128, 512), 0)

    def key_views(t, ids):
        both = jnp.concatenate([kv[t, jnp.maximum(c, 0)] for c in ids], axis=0).astype(F32)
        turned = pltpu.roll(both, HD, 1)
        zero = jnp.zeros_like(both)
        keys = [jnp.where(low_lane, both, zero).astype(BF16), jnp.where(low_lane, zero, turned).astype(BF16)]
        values = [jnp.where(low_lane, turned, zero).astype(BF16), jnp.where(low_lane, zero, both).astype(BF16)]
        return keys, values

    c_wm.wait()

    @pl.loop(0, 4)
    def _(u):
        t, i = u // 2, u % 2
        b = 2 * seq + i
        ps = ancestors(t, b)
        keys, values = key_views(t, (b, *ps))
        seen = (key_col < 128) & (key_col <= query_row)
        for k, p in enumerate(ps):
            inside = (key_col >= 128 * (k + 1)) & (key_col < 128 * (k + 2))
            seen = seen | (inside & (p >= 0))
        for g in (0, 1):
            total = jnp.zeros((128, 128), F32)
            for h in (0, 1):
                scores = dot_nt(q[t, i, g], keys[h]) * HD**-0.5
                scores = jnp.where(seen, scores, MASK_FILL)
                e = jnp.exp(scores - jnp.max(scores, axis=-1, keepdims=True))
                p = (e / jnp.sum(e, axis=-1, keepdims=True)).astype(BF16)
                probs[u, 2 * g + h] = p
                total = total + dot(p, values[h])
            att[t, rows(128 * i, 128), 128 * g : 128 * g + 128] = total.astype(BF16)

    for k in range(4):
        cols = pl.ds(512 * k, 512)
        sib[:, cols] = dot(att[other], wm[:, cols]).astype(BF16)
        fold.send_columns(k, sib)
    for k in range(4):
        cols = pl.ds(512 * k, 512)
        acc[:, cols] = dot(att[core], wm[:, cols])
    expand = Stream(
        lambda j, s: [
            pltpu.make_async_copy(
                we_hbm.at[w, :, pl.ds(pl.multiple_of(128 * j, 128), 128)], sa.at[s, :, pl.ds(128 * w, 128)], wsem.at[1 + w, s]
            )
            for w in (0, 1)
        ]
    )
    expand.start(0)
    expand.start(1)
    for k in range(4):
        net.sent(fold.base + k)
    fold.begin(acc, False)
    fold.middle()

    def to_normed(r, v):
        x_own = flat[core, z, rows(r, 16)].astype(F32)
        total = x_own + v
        mid[rows(r, 16)] = total
        rms = lax.rsqrt(jnp.mean(total * total, axis=-1, keepdims=True) + NORM_EPS)
        n2[core, z, rows(r, 16)] = (total * rms * gain_two).astype(BF16)

    fold.finish(to_normed)
    share_one.begin()
    share_one.middle()
    share_one.later()
    share_one.finish()
    fold.release()

    dgu = n1

    def feed(j, s):
        both = dot(n2[...].reshape(512, D), sa[s])
        acc[:, 0:256] = both[0:256]
        acc[:, 256:512] = both[256:512]
        cols = pl.ds(pl.multiple_of(128 * j, 128), 128)
        cols_up = pl.ds(pl.multiple_of(1024 + 128 * j, 128), 128)
        for t in (0, 1):

            @pl.loop(0, 4)
            def _(i):
                at = rows(64 * i, 64)
                gate = acc[at, 256 * t : 256 * t + 128]
                up = acc[at, 256 * t + 128 : 256 * t + 256]
                blk, off = 2 * t + i // 2, rows(64 * (i % 2), 64)
                dh = g_gate[0, blk, off, cols].astype(F32) + g_gate[1, blk, off, cols].astype(F32)
                sig = 1.0 / (1.0 + jnp.exp(-gate))
                act = gate * sig
                hid[t, at, cols] = (act * up).astype(BF16)
                n1[t, at, cols] = (dh * up * sig * (1.0 + gate * (1.0 - sig))).astype(BF16)
                n1[t, at, cols_up] = (dh * act).astype(BF16)

            hid_t[rows(128 * j, 128), 256 * t : 256 * t + 256] = hid[t, :, cols].T

    expand.run(8, feed)

    back = Stream(
        lambda j, s: [
            pltpu.make_async_copy(we_hbm.at[w, rows(256 * j, 256)], sb.at[s, :, pl.ds(1024 * w, 1024)], wsem.at[3 + w, s])
            for w in (0, 1)
        ]
    )
    back.start(0)
    back.start(1)

    @pl.loop(0, 8)
    def _(j):
        cols = pl.ds(pl.multiple_of(256 * j, 256), 256)
        v = dot(hid_t[...], cot[:, :, :, cols].reshape(512, 256))
        g_red[j // 2, 2 * (j % 2)] = v[:, 0:128].astype(BF16)
        g_red[j // 2, 2 * (j % 2) + 1] = v[:, 128:256].astype(BF16)

    s_red.step0()

    for k in range(4):
        for w in (0, 1):
            j = 2 * k + w
            back.wait(j)
            cols = pl.ds(256 * j, 256)
            sib[:, cols] = dot_nt(dgu[other], sb[j % 2]).astype(BF16)
            acc[:, cols] = dot_nt(dgu[core], sb[j % 2])
            if j + 2 < 8:
                back.start(j + 2)
        fold.send_columns(k, sib)

    c_spill.wait()
    transpose_into(lambda t, cols: n2[t, :, :, cols].reshape(256, 128), tt)
    for k in range(4):
        net.sent(fold.base + k)
    fold.begin(acc, False)

    def expand_grad(dst, first):
        @pl.loop(0, 16)
        def _(k):
            a, j = k // 4, k % 4
            cols = pl.ds(pl.multiple_of(first + 256 * j, 256), 256)
            v = dot(tt[rows(512 * a, 512)], dgu[:, :, cols].reshape(512, 256))
            dst[a, :, :, pl.ds(pl.multiple_of(256 * j, 256), 256)] = v.astype(BF16).reshape(4, 128, 256)

    expand_grad(g_gate, 0)
    s_gate.step0()
    fold.middle()
    expand_grad(g_up, 1024)
    s_up.step0()
    c_tt = pltpu.make_async_copy(spill, tt, loc.at[6])
    c_tt.start()
    s_red.step1()

    def to_branch(r, v):
        at = rows(r, 16)
        total = mid[at]
        rms = lax.rsqrt(jnp.mean(total * total, axis=-1, keepdims=True) + NORM_EPS)
        u = v * gain_two
        back_vals = rms * u - total * (rms * rms * rms) * jnp.mean(u * total, axis=-1, keepdims=True)
        full = cot[core, z, at].astype(F32) + back_vals
        dmid[at] = full
        xd[core, z, at] = full.astype(BF16)
        gpart[0:1, :] = gpart[0:1, :] + jnp.sum(v * total * rms, axis=0, keepdims=True)

    gpart[...] = jnp.zeros_like(gpart)
    fold.finish(to_branch)
    share_two.begin()

    down_out = Stream(
        lambda j, s: [
            pltpu.make_async_copy(
                wr_hbm.at[:, pl.ds(pl.multiple_of(256 * j, 256), 256)], sa.at[s, pl.ds(0, 1024)], wsem.at[5, s]
            )
        ]
    )
    down_out.start(0)
    down_out.start(1)

    def part_out(j, s):
        v = dot(hid[...].reshape(512, 1024), sa[s, 0:1024])
        n1[:, :, pl.ds(pl.multiple_of(256 * j, 256), 256)] = v.astype(BF16).reshape(2, 256, 256)

    down_out.run(8, part_out)
    c_y2 = bring(7, n1, y2_hbm)
    share_two.middle()
    s_gate.step1()
    share_two.later()
    share_two.finish()

    dbr = xd
    v = dot_nt(dbr[...].reshape(512, D), wm[...]).astype(BF16)
    datt[...] = v.reshape(2, 256, 256)

    @pl.loop(0, 8)
    def _(j):
        cols = pl.ds(pl.multiple_of(256 * j, 256), 256)
        v = dot_tn(att[...].reshape(512, 256), dbr[:, :, :, cols].reshape(512, 256))
        g_mrg[j // 2, 2 * (j % 2)] = v[:, 0:128].astype(BF16)
        g_mrg[j // 2, 2 * (j % 2) + 1] = v[:, 128:256].astype(BF16)

    s_mrg.step0()
    dkv[...] = jnp.zeros_like(dkv)

    @pl.loop(0, 4)
    def _(u):
        t, i = u // 2, u % 2
        b = 2 * seq + i
        ps = ancestors(t, b)
        keys, values = key_views(t, (b, *ps))
        c, s = turns(t, i)
        at = rows(128 * i, 128)
        dk = [jnp.zeros((512, 128), F32), jnp.zeros((512, 128), F32)]
        dv = [jnp.zeros((512, 128), F32), jnp.zeros((512, 128), F32)]
        for g in (0, 1):
            dq = jnp.zeros((128, 128), F32)
            da = datt[t, at, 128 * g : 128 * g + 128]
            for h in (0, 1):
                p = probs[u, 2 * g + h]
                pf = p.astype(F32)
                dp = dot_nt(da, values[h])
                inner = jnp.sum(pf * dp, axis=-1, keepdims=True)
                ds = (pf * (dp - inner)).astype(BF16)
                dq = dq + dot(ds, keys[h])
                dk[h] = dk[h] + dot_tn(ds, q[t, i, g])
                dv[h] = dv[h] + dot_tn(p, da)
            dq = dq * HD**-0.5
            dpack[t, at, 128 * g : 128 * g + 128] = (dq * c - swap_halves(dq) * s).astype(BF16)
        both = jnp.where(
            low_lane, (dk[0] + pltpu.roll(dk[1], HD, 1)) * HD**-0.5, pltpu.roll(dv[0], HD, 1) + dv[1]
        )
        dkv[t, b] = dkv[t, b] + both[0:128]
        for k, p in enumerate(ps):
            piece = both[128 * (k + 1) : 128 * (k + 2)]

            @pl.loop(0, 8)
            def _(blk):
                dkv[t, blk] = dkv[t, blk] + piece * jnp.where(p == blk, 1.0, 0.0)

    dkv_low[...] = dkv[...].astype(BF16)
    for d in (1, 2, 3):
        peer = shifted("seq", d)
        net.put(base_dkv + d - 1, dkv_low.at[pl.ds(0, 2), pl.ds(2 * peer, 2)], dkv_in.at[d - 1], "seq", peer)
    s_up.step1()
    s_red.step2()
    for d in (1, 2, 3):
        net.got(base_dkv + d - 1, dkv_in.at[d - 1])
    for t in (0, 1):
        for i in (0, 1):
            v = dkv[t, 2 * seq + i]
            for d in (0, 1, 2):
                v = v + dkv_in[d, t, i].astype(F32)
            c, s = turns(t, i)
            v = jnp.where(lower, v * c - swap_halves(v) * s, v)
            dpack[t, 128 * i : 128 * i + 128, 256:384] = v.astype(BF16)
    c_tt.wait()

    @pl.loop(0, 4)
    def _(a):
        v = dot(tt[rows(512 * a, 512)], dpack[...].reshape(512, 384))
        g_att[a] = v.astype(BF16).reshape(4, 128, 384)

    s_att.step0()
    s_mrg.step1()
    share_one.release()

    @pl.loop(0, 8)
    def _(j):
        v = dot_nt(dpack[...].reshape(512, 384), wa[rows(256 * j, 256)])
        n2[:, :, :, pl.ds(pl.multiple_of(256 * j, 256), 256)] = v.astype(BF16).reshape(2, 4, 64, 256)

    c_y4 = bring(8, n2, y4_hbm)
    s_gate.step2()
    s_red.step3()
    s_att.step1()
    s_up.step2()
    s_gate.step3()
    s_red.step4(o_red)
    s_mrg.step2()
    s_att.step2()
    s_up.step3()
    s_gate.step4(o_gate)
    s_mrg.step3()
    s_att.step3()
    s_up.step4(o_up)
    s_mrg.step4(o_mrg)
    s_att.step4(o_att)
    c_y2.wait()
    c_y4.wait()
    net.drain()


def any_space(n):
    return [pl.BlockSpec(memory_space=pl.ANY)] * n


def main_call(x, cot, parents, wa, wm, we, wr, gains, table):
    def grads(size, cols):
        q = size // 4
        return (size, cols, q)

    kinds = [grads(1024, 128), grads(128, 1024), grads(128, 1024), grads(256, 128), grads(128, 384)]
    vm = pltpu.VMEM
    scratch = (
        [vm((4, 4, s, c), BF16) for s, c, q in kinds]
        + [vm((2, 6, 4, q, c), BF16) for s, c, q in kinds]
        + [vm((2, 6, q, c), BF16) for s, c, q in kinds]
        + [
            vm((2, 2048, 256), BF16),
            vm((2, 256, 2048), BF16),
            vm((2048, 384), BF16),
            vm((256, 2048), BF16),
            vm((2, 4, 64, D), BF16),
            vm((2, 4, 64, D), BF16),
            vm((2, 256, D), BF16),
            vm((D, 512), BF16),
            vm((2, 4, 64, D), BF16),
            vm((2, 256, 1024), BF16),
            vm((1024, 512), BF16),
            vm((256, D), F32),
            vm((256, D), BF16),
            vm((256, D), BF16),
            vm((6, 32, D), BF16),
            vm((4, 4, 128, 512), BF16),
            vm((2, 8, 128, 128), BF16),
            vm((2, 2, 2, 128, 128), BF16),
            vm((2, 256, 256), BF16),
            vm((2, 256, 256), BF16),
            vm((2, 8, 128, 128), F32),
            vm((2, 8, 128, 128), BF16),
            vm((3, 2, 2, 128, 128), BF16),
            vm((2, 256, 384), BF16),
            pltpu.SemaphoreType.DMA((160,)),
            pltpu.SemaphoreType.DMA((160,)),
            pltpu.SemaphoreType.DMA((10,)),
            pltpu.SemaphoreType.DMA((6, 2)),
        ]
    )
    sds = jax.ShapeDtypeStruct
    out_shape = [
        sds((2, 256, D), BF16),
        sds((2, 4, 64, D), BF16),
        sds((D, 512), BF16),
        sds((64, D), F32),
        sds((64, D), F32),
        sds((8, D), F32),
        sds((128, 384), F32),
        sds((256, 128), F32),
        sds((128, 1024), F32),
        sds((128, 1024), F32),
        sds((1024, 128), F32),
    ]
    vspec = pl.BlockSpec(memory_space=pltpu.VMEM)
    hbm = pl.BlockSpec(memory_space=pl.ANY)
    return pl.pallas_call(
        main_kernel,
        out_shape=out_shape,
        in_specs=[hbm, hbm, pl.BlockSpec(memory_space=pltpu.SMEM), hbm, hbm, hbm, hbm, vspec, vspec],
        out_specs=[hbm] * 3 + [vspec] * 8,
        scratch_shapes=scratch,
        compiler_params=pltpu.CompilerParams(
            collective_id=1, has_side_effects=True, vmem_limit_bytes=64 * 2**20 - 65536
        ),
    )(x, cot, parents, wa, wm, we, wr, gains, table)


class Gather:
    def __init__(self, net, own, size, region):
        self.net, self.own, self.size, self.region = net, own, size, region
        self.base = net.ids(40)
        self.half, self.quarter = size // 2, size // 4

    def idx(self, h, da, db):
        fa, sa = (("dp", "seq"), ("seq", "dp"))[h]
        c = {fa: shifted(fa, da), sa: shifted(sa, db)}
        return c["dp"] * 4 + c["seq"]

    def both(self, k, src, dst, axis):
        self.net.put(k, src, dst, axis, shifted(axis, 1))
        self.net.put(k + 1, src, dst, axis, shifted(axis, -1))

    def begin(self):
        for stage in (0, 1):
            for h in (0, 1):
                axis = ("dp", "seq")[(h + stage) % 2]
                lo = h * self.half
                src = self.own.at[pl.ds(lo, self.half)]
                self.both(self.base + 20 * h + 4 * stage, src, self.region(self.idx(h, 0, 0), lo, self.half), axis)

    def near(self):
        for h in (0, 1):
            fa, sa = (("dp", "seq"), ("seq", "dp"))[h]
            base, lo = self.base + 20 * h, h * self.half
            for k, d in ((0, -1), (1, 1)):
                p = self.region(self.idx(h, d, 0), lo, self.half)
                self.net.got(base + k, p)
                part = self.region(self.idx(h, d, 0), lo + k * self.quarter, self.quarter)
                self.net.put(base + 2 + k, part, part, fa, shifted(fa, -d))
                self.both(base + 8 + 4 * k, p, p, sa)

    def far(self):
        for h in (0, 1):
            fa, sa = (("dp", "seq"), ("seq", "dp"))[h]
            base, lo = self.base + 20 * h, h * self.half
            at = self.idx(h, 2, 0)
            for k in (0, 1):
                self.net.got(base + 2 + k, self.region(at, lo + k * self.quarter, self.quarter))
            p = self.region(at, lo, self.half)
            self.both(base + 16, p, p, sa)

    def cross(self, k):
        d = (0, -1, 1, 2)[k]
        for h in (0, 1):
            sa = (("dp", "seq"), ("seq", "dp"))[h][1]
            base, lo = self.base + 20 * h + 4 + 4 * k, h * self.half
            for w, db in ((0, -1), (1, 1)):
                at = self.idx(h, d, db)
                self.net.got(base + w, self.region(at, lo, self.half))
                part = self.region(at, lo + w * self.quarter, self.quarter)
                self.net.put(base + 2 + w, part, part, sa, shifted(sa, -db))

    def finish(self):
        for k, d in enumerate((0, -1, 1, 2)):
            for h in (0, 1):
                base, lo = self.base + 20 * h + 4 + 4 * k, h * self.half
                at = self.idx(h, d, 2)
                for w in (0, 1):
                    self.net.got(base + 2 + w, self.region(at, lo + w * self.quarter, self.quarter))


def last_kernel(
    w_att, w_mrg, w_exp, w_red, y2, y4, mid, dmid, x_hbm, gains, gpart, mg, fg, sg,
    out, grad, f_att, f_mrg, f_exp, f_red, n_gain, m_gain, v_gain, f_gain,
    own, acc, rsib2, zs2, zrec2, rsib4, zs4, zrec4, x_own, rows2, rows4,
    gbuf, gs1, gs2, gs3, gs4, gs5, gtot, gtwo, gnew,
    send, recv, loc,
):
    net = Net(send, recv, send.shape[0])
    m = lax.axis_index("mp")
    core, z = lax.rem(m, 2), m // 2
    other = 1 - core
    dp, seq = lax.axis_index("dp"), lax.axis_index("seq")
    me = dp * 4 + seq
    peers = [("dp", shifted("dp", d)) for d in (1, 2, 3)] + [("seq", shifted("seq", d)) for d in (1, 2, 3)]
    peers += [("mp", shifted("mp", d)) for d in range(1, 8)]
    hello(peers)

    def bring(k, src, dst):
        c = pltpu.make_async_copy(src, dst, loc.at[k])
        c.start()
        return c

    by_row = lambda ref, n: (lambda i, lo, k: ref.at[rows(i * n + lo, k)])
    by_col = lambda ref: (lambda i, lo, k: ref.at[pl.ds(lo, k), pl.ds(pl.multiple_of(128 * i, 128), 128)])
    exp_at = lambda i, lo, k: f_exp.at[pl.ds(128 * i + lo, k)]
    sets = [
        Gather(net, w_exp, 128, exp_at),
        Gather(net, w_red, 1024, by_col(f_red)),
        Gather(net, w_att, 128, by_row(f_att, 128)),
        Gather(net, w_mrg, 256, by_col(f_mrg)),
    ]
    fold4, fold2 = Fold(net, acc, rsib4, zs4, zrec4), Fold(net, acc, rsib2, zs2, zrec2)
    share4, share2 = Share(net, grad), Share(net, out)
    b1, b2, b3, b4, b5 = net.ids(7), net.ids(3), net.ids(3), net.ids(3), net.ids(3)
    local = [
        bring(0, w_att, f_att.at[rows(128 * me, 128)]),
        bring(1, w_mrg, f_mrg.at[:, pl.ds(pl.multiple_of(128 * me, 128), 128)]),
        bring(2, w_exp, f_exp.at[pl.ds(128 * me, 128)]),
        bring(3, w_red, f_red.at[:, pl.ds(pl.multiple_of(128 * me, 128), 128)]),
    ]
    c_own = bring(4, y4.at[core], own)
    c_x = bring(5, x_hbm.at[core, z], x_own)
    hello_wait(13)
    fold4.send_rows(y4.at[other])
    for g in sets:
        g.begin()
    gain_one = gains[0:1, :]
    c_own.wait()
    fold4.begin(own, True)
    c_own = bring(4, y2.at[core], own)
    fold2.send_rows(y2.at[other])
    fold4.middle()
    gbuf[...] = jnp.zeros_like(gbuf)
    gbuf[1:2, :] = gpart[0:1, :]
    c_x.wait()

    def to_grad(r, v):
        at = rows(r, 16)
        x = x_own[at].astype(F32)
        rms = lax.rsqrt(jnp.mean(x * x, axis=-1, keepdims=True) + NORM_EPS)
        u = v * gain_one
        back = rms * u - x * (rms * rms * rms) * jnp.mean(u * x, axis=-1, keepdims=True)
        rows4[at] = (dmid[at] + back).astype(BF16)
        gbuf[0:1, :] = gbuf[0:1, :] + jnp.sum(v * x * rms, axis=0, keepdims=True)

    fold4.finish(to_grad)
    share4.begin(rows4)
    l4 = bring(6, rows4, grad.at[core, z])
    gs1[m] = gbuf[...]
    for d in range(1, 8):
        net.put(b1 + d - 1, gbuf, gs1.at[m], "mp", shifted("mp", d))
    for g in sets:
        g.near()
    c_own.wait()
    fold2.begin(own, True)
    fold2.middle()
    for d in range(1, 8):
        net.got(b1 + d - 1, gs1.at[shifted("mp", -d)])
    total = gs1[0]
    for k in range(1, 8):
        total = total + gs1[k]
    gtot[...] = total
    piece = lambda i, n: pl.ds(pl.multiple_of(i * n, 128), n)
    gs2[dp] = gtot[:, piece(dp, 512)]
    for d in (1, 2, 3):
        net.put(b2 + d - 1, gtot.at[:, piece(shifted("dp", d), 512)], gs2.at[dp], "dp", shifted("dp", d))
    share4.middle()

    def to_out(r, v):
        at = rows(r, 16)
        rows2[at] = (mid[at] + v).astype(BF16)

    fold2.finish(to_out)
    share2.begin(rows2)
    l2 = bring(7, rows2, out.at[core, z])
    for g in sets:
        g.far()
    for d in (1, 2, 3):
        net.got(b2 + d - 1, gs2.at[shifted("dp", -d)])
    gtwo[...] = gs2[0] + gs2[1] + gs2[2] + gs2[3]
    gs3[seq] = gtwo[:, piece(seq, 128)]
    for d in (1, 2, 3):
        net.put(b3 + d - 1, gtwo.at[:, piece(shifted("seq", d), 128)], gs3.at[seq], "seq", shifted("seq", d))
    share4.later()
    for g in sets:
        g.cross(0)
    for d in (1, 2, 3):
        net.got(b3 + d - 1, gs3.at[shifted("seq", -d)])
    shard = gs3[0] + gs3[1] + gs3[2] + gs3[3]
    new, mom, var = adamw(mg[...], fg[...], sg[...], shard[0:2])
    n_gain[...] = new
    m_gain[...] = mom
    v_gain[...] = var
    gnew[...] = jnp.zeros_like(gnew)
    gnew[0:2, :] = new
    gs4[seq] = gnew[...]
    for d in (1, 2, 3):
        net.put(b4 + d - 1, gnew, gs4.at[seq], "seq", shifted("seq", d))
    share2.middle()
    for g in sets:
        g.cross(1)
    for d in (1, 2, 3):
        net.got(b4 + d - 1, gs4.at[shifted("seq", -d)])
    gs5[dp] = gs4[...]
    for d in (1, 2, 3):
        net.put(b5 + d - 1, gs4, gs5.at[dp], "dp", shifted("dp", d))
    share2.later()
    for k in (2, 3):
        for g in sets:
            g.cross(k)
    for d in (1, 2, 3):
        net.got(b5 + d - 1, gs5.at[shifted("dp", -d)])
    for a in range(4):
        for b in range(4):
            lo = 128 * (4 * a + b)
            f_gain[:, lo : lo + 128] = gs5[a, b, 0:2].astype(BF16)
    share4.finish()
    share2.finish()
    for g in sets:
        g.finish()
    for c in local + [l4, l2]:
        c.wait()
    net.drain()


def last_call(w_att, w_mrg, w_exp, w_red, y2, y4, mid, dmid, x, gains, gpart, mg, fg, sg):
    vm, sds = pltpu.VMEM, jax.ShapeDtypeStruct
    hbm = pl.BlockSpec(memory_space=pl.ANY)
    vspec = pl.BlockSpec(memory_space=pltpu.VMEM)
    out_shape = [
        sds((2, 4, 64, D), BF16),
        sds((2, 4, 64, D), BF16),
        sds((D, 384), BF16),
        sds((256, D), BF16),
        sds((D, 2, 1024), BF16),
        sds((1024, D), BF16),
        sds((2, 128), F32),
        sds((2, 128), F32),
        sds((2, 128), F32),
        sds((2, D), BF16),
    ]
    scratch = [
        vm((256, D), BF16),
        vm((256, D), F32),
        vm((256, D), BF16),
        vm((256, D), BF16),
        vm((6, 32, D), BF16),
        vm((256, D), BF16),
        vm((256, D), BF16),
        vm((6, 32, D), BF16),
        vm((64, D), BF16),
        vm((64, D), BF16),
        vm((64, D), BF16),
        vm((8, D), F32),
        vm((8, 8, D), F32),
        vm((4, 8, 512), F32),
        vm((4, 8, 128), F32),
        vm((4, 8, 128), F32),
        vm((4, 4, 8, 128), F32),
        vm((8, D), F32),
        vm((8, 512), F32),
        vm((8, 128), F32),
        pltpu.SemaphoreType.DMA((240,)),
        pltpu.SemaphoreType.DMA((240,)),
        pltpu.SemaphoreType.DMA((10,)),
    ]
    return pl.pallas_call(
        last_kernel,
        out_shape=out_shape,
        in_specs=[hbm] * 6 + [vspec] * 2 + [hbm] + [vspec] * 5,
        out_specs=[hbm] * 6 + [vspec] * 4,
        scratch_shapes=scratch,
        compiler_params=pltpu.CompilerParams(
            collective_id=2, has_side_effects=True, vmem_limit_bytes=32 * 2**20
        ),
    )(w_att, w_mrg, w_exp, w_red, y2, y4, mid, dmid, x, gains, gpart, mg, fg, sg)


def rotary_table():
    inv = ROPE_BASE ** (-2.0 * np.arange(HD // 2, dtype=np.float32) / HD)
    angle = np.arange(512, dtype=np.float32)[:, None] * inv.astype(np.float32)[None, :]
    c, s = np.cos(angle), np.sin(angle)
    both = np.stack([np.concatenate([c, c, c, c], 1), np.concatenate([-s, s, -s, s], 1)])
    return both.reshape(2, 4, 128, 128).astype(np.float32)


def on_device(
    inputs, cotangent, parents, weight_attend, weight_merge, weight_expand, weight_reduce, gains,
    master_attend, master_merge, master_expand, master_reduce, master_gains,
    first_attend, first_merge, first_expand, first_reduce, first_gains,
    second_attend, second_merge, second_expand, second_reduce, second_gains,
):
    x = inputs.reshape(2, 4, 64, D)
    cot = cotangent.reshape(2, 4, 64, D)
    we = weight_expand.transpose(1, 0, 2)
    gain_rows = gains.astype(F32)
    y2, y4, _, mid, dmid, gpart, g_att, g_mrg, g_gate, g_up, g_red = main_call(
        x, cot, parents, weight_attend, weight_merge, we, weight_reduce, gain_rows, jnp.asarray(rotary_table())
    )
    n_att, m_att, v_att = adamw(master_attend, first_attend, second_attend, g_att)
    n_mrg, m_mrg, v_mrg = adamw(master_merge, first_merge, second_merge, g_mrg)
    g_exp = jnp.stack([g_gate, g_up], axis=1)
    n_exp, m_exp, v_exp = adamw(master_expand, first_expand, second_expand, g_exp)
    n_red, m_red, v_red = adamw(master_reduce, first_reduce, second_reduce, g_red)
    out, grad, f_att, f_mrg, f_exp, f_red, n_gain, m_gain, v_gain, f_gain = last_call(
        n_att.astype(BF16), n_mrg.astype(BF16), n_exp.astype(BF16), n_red.astype(BF16),
        y2, y4.reshape(2, 256, D), mid, dmid, x, gain_rows, gpart, master_gains, first_gains, second_gains,
    )
    return (
        out.reshape(2, 256, D), grad.reshape(2, 256, D),
        n_att, n_mrg, n_exp, n_red, n_gain,
        m_att, m_mrg, m_exp, m_red, m_gain,
        v_att, v_mrg, v_exp, v_red, v_gain,
        f_att, f_mrg, f_exp, f_red, f_gain,
    )


def solution(mesh):
    both = ("dp", "seq")
    states = (P(both, "mp"), P("mp", both), P(both, None, "mp"), P("mp", both), P(None, both))
    weights = (P(None, "mp"), P("mp", None), P(None, None, "mp"), P("mp", None), P())
    tokens = P("dp", "seq", None)
    return jax.shard_map(
        on_device,
        mesh=mesh,
        in_specs=(tokens, tokens, P("dp", None), *weights, *states, *states, *states),
        out_specs=(tokens, tokens, *states, *states, *states, *weights),
        check_vma=False,
    )
```

```python
import functools

import jax
import jax.numpy as jnp
import numpy as np
from jax import lax
from jax.experimental import pallas as pl
from jax.experimental.pallas import tpu as pltpu
from jax.sharding import PartitionSpec as P

MESH = pl.DeviceIdType.MESH
F32 = jnp.float32
BF16 = jnp.bfloat16
D = 2048
HD = 64
STEP = 5
NORM_EPS = 1e-05
ROPE_BASE = 500000.0
MASK_FILL = -1e30
BETA_ONE = 0.5
BETA_TWO = 0.5
ADAM_EPS = 1e-08
LEARN_RATE = 0.005
DECAY_RATE = 0.1
FIX_ONE = 1.0 - BETA_ONE**STEP
FIX_TWO = 1.0 - BETA_TWO**STEP
SIZES = {"dp": 4, "seq": 4, "mp": 8}


def adamw(master, first, second, grad_vals):
    momentum = BETA_ONE * first + (1.0 - BETA_ONE) * grad_vals
    variance = BETA_TWO * second + (1.0 - BETA_TWO) * grad_vals * grad_vals
    direction = momentum / FIX_ONE / (jnp.sqrt(variance / FIX_TWO) + ADAM_EPS)
    renewed = master - LEARN_RATE * (direction + DECAY_RATE * master)
    return (renewed, momentum, variance)


def dot(a, b):
    return lax.dot_general(a, b, (((1,), (0,)), ((), ())), preferred_element_type=F32)


def dot_nt(a, b):
    return lax.dot_general(a, b, (((1,), (1,)), ((), ())), preferred_element_type=F32)


def dot_tn(a, b):
    return lax.dot_general(a, b, (((0,), (0,)), ((), ())), preferred_element_type=F32)


def shifted(axis, delta):
    n = SIZES[axis]
    return lax.rem(lax.axis_index(axis) + (delta + n), n)


def sibling():
    m = lax.axis_index("mp")
    return m + 1 - 2 * lax.rem(m, 2)


def rows(start, n):
    return pl.ds(pl.multiple_of(start, 16), n)


class Net:
    def __init__(self, send, recv, count):
        self.send, self.recv, self.count = send, recv, count
        self.used = 0
        self.started = {}

    def ids(self, n):
        first = self.used
        self.used += n
        assert self.used <= self.count
        return first

    def put(self, k, src, dst, axis, index):
        c = pltpu.make_async_remote_copy(
            src_ref=src,
            dst_ref=dst,
            send_sem=self.send.at[k],
            recv_sem=self.recv.at[k],
            device_id={axis: index},
            device_id_type=MESH,
        )
        c.start()
        self.started[k] = c

    def got(self, k, dst):
        pltpu.make_async_remote_copy(
            src_ref=dst,
            dst_ref=dst,
            send_sem=self.send.at[k],
            recv_sem=self.recv.at[k],
            device_id={"dp": shifted("dp", 1)},
            device_id_type=MESH,
        ).wait_recv()

    def sent(self, k):
        self.started.pop(k).wait_send()

    def drain(self):
        for k in sorted(self.started):
            self.started[k].wait_send()
        self.started = {}


def hello(peers):
    sem = pltpu.get_barrier_semaphore()
    for axis, index in peers:
        pl.semaphore_signal(sem, inc=1, device_id={axis: index}, device_id_type=MESH)


def hello_wait(n):
    pl.semaphore_wait(pltpu.get_barrier_semaphore(), n)


class Spread:
    def __init__(self, net, own, first, second):
        self.net, self.own, self.r1, self.r2 = net, own, first, second
        self.size, self.cols = own.shape[2], own.shape[3]
        self.q = self.size // 4
        self.base = net.ids(24)
        self.chunk = min(self.q, max(16, 16384 // self.cols))

    def axes(self, h):
        return (("dp", "seq"), ("seq", "dp"))[h]

    def row(self, h, da):
        a = shifted(self.axes(h)[0], da)
        return (lambda b: (a, b)) if h == 0 else (lambda b: (b, a))

    def block(self, h, db):
        a, b = lax.axis_index(self.axes(h)[0]), shifted(self.axes(h)[1], db)
        return (a, b) if h == 0 else (b, a)

    def view(self, h, da, lo):
        a = shifted(self.axes(h)[0], da)
        if h == 0:
            return self.own.at[a, pl.ds(0, 4), pl.ds(lo, self.q)]
        return self.own.at[pl.ds(0, 4), a, pl.ds(lo, self.q)]

    def one(self, h, db, lo):
        a, b = self.block(h, db)
        return self.own.at[a, b, pl.ds(lo, self.q)]

    def add(self, index_of, count, lo, sources, out=None):
        steps = self.q // self.chunk

        @pl.loop(0, count * steps)
        def _(k):
            b = k // steps
            r = (k % steps) * self.chunk
            at = (*index_of(b), rows(lo + r, self.chunk))
            v = self.own[at].astype(F32)
            for ref, lead in sources:
                if count > 1:
                    v = v + ref[(*lead, b, rows(r, self.chunk))].astype(F32)
                else:
                    v = v + ref[(*lead, rows(r, self.chunk))].astype(F32)
            if out is None:
                self.own[at] = v.astype(BF16)
            else:
                out[rows(lo + r, self.chunk)] = v

    def step0(self):
        q = self.q
        for h in (0, 1):
            fa, lo, base = self.axes(h)[0], 2 * h * q, self.base + 12 * h
            self.net.put(base + 0, self.view(h, 2, lo), self.r1.at[h, 0], fa, shifted(fa, 1))
            self.net.put(base + 1, self.view(h, 2, lo + q), self.r1.at[h, 1], fa, shifted(fa, -1))
        for h in (0, 1):
            fa, lo, base = self.axes(h)[0], 2 * h * q, self.base + 12 * h
            self.net.put(base + 2, self.view(h, 1, lo + q), self.r1.at[h, 2], fa, shifted(fa, 1))
            self.net.put(base + 3, self.view(h, -1, lo), self.r1.at[h, 3], fa, shifted(fa, -1))

    def step1(self):
        q = self.q
        for h in (0, 1):
            fa, lo, base = self.axes(h)[0], 2 * h * q, self.base + 12 * h
            self.net.got(base + 0, self.r1.at[h, 0])
            self.add(self.row(h, 1), 4, lo, [(self.r1, (h, 0))])
            self.net.put(base + 4, self.view(h, 1, lo), self.r1.at[h, 4], fa, shifted(fa, 1))
            self.net.got(base + 1, self.r1.at[h, 1])
            self.add(self.row(h, -1), 4, lo + q, [(self.r1, (h, 1))])
            self.net.put(base + 5, self.view(h, -1, lo + q), self.r1.at[h, 5], fa, shifted(fa, -1))

    def step2(self):
        q = self.q
        for h in (0, 1):
            sa, lo, base = self.axes(h)[1], 2 * h * q, self.base + 12 * h
            for k in (3, 4):
                self.net.got(base + k, self.r1.at[h, k])
            self.add(self.row(h, 0), 4, lo, [(self.r1, (h, 3)), (self.r1, (h, 4))])
            for k in (2, 5):
                self.net.got(base + k, self.r1.at[h, k])
            self.add(self.row(h, 0), 4, lo + q, [(self.r1, (h, 2)), (self.r1, (h, 5))])
            base += 6
            self.net.put(base + 0, self.one(h, 2, lo), self.r2.at[h, 0], sa, shifted(sa, 1))
            self.net.put(base + 1, self.one(h, 2, lo + q), self.r2.at[h, 1], sa, shifted(sa, -1))
            self.net.put(base + 2, self.one(h, 1, lo + q), self.r2.at[h, 2], sa, shifted(sa, 1))
            self.net.put(base + 3, self.one(h, -1, lo), self.r2.at[h, 3], sa, shifted(sa, -1))

    def step3(self):
        q = self.q
        for h in (0, 1):
            sa, lo, base = self.axes(h)[1], 2 * h * q, self.base + 12 * h + 6
            self.net.got(base + 0, self.r2.at[h, 0])
            at = self.block(h, 1)
            self.add(lambda b: at, 1, lo, [(self.r2, (h, 0))])
            self.net.put(base + 4, self.one(h, 1, lo), self.r2.at[h, 4], sa, shifted(sa, 1))
            self.net.got(base + 1, self.r2.at[h, 1])
            at2 = self.block(h, -1)
            self.add(lambda b: at2, 1, lo + q, [(self.r2, (h, 1))])
            self.net.put(base + 5, self.one(h, -1, lo + q), self.r2.at[h, 5], sa, shifted(sa, -1))

    def step4(self, out, column=None):
        q = self.q
        if column is not None:
            out = out.at[:, column, :]
        for h in (0, 1):
            lo, base = 2 * h * q, self.base + 12 * h + 6
            at = self.block(h, 0)
            for k in (3, 4):
                self.net.got(base + k, self.r2.at[h, k])
            self.add(lambda b: at, 1, lo, [(self.r2, (h, 3)), (self.r2, (h, 4))], out)
            for k in (2, 5):
                self.net.got(base + k, self.r2.at[h, k])
            self.add(lambda b: at, 1, lo + q, [(self.r2, (h, 2)), (self.r2, (h, 5))], out)


class Fold:
    def __init__(self, net, acc, rsib, zsend, zrec):
        self.net, self.acc, self.rsib, self.zsend, self.zrec = net, acc, rsib, zsend, zrec
        self.base = net.ids(16)

    def quarter(self, d):
        return 64 * lax.rem(lax.axis_index("mp") // 2 + (d + 4), 4)

    def right(self):
        return shifted("mp", 2)

    def left(self):
        return shifted("mp", -2)

    def send_columns(self, k, src):
        cols = pl.ds(512 * k, 512)
        self.net.put(self.base + k, src.at[:, cols], self.rsib.at[:, cols], "mp", sibling())

    def columns_here(self):
        for k in range(4):
            self.net.got(self.base + k, self.rsib.at[:, pl.ds(512 * k, 512)])

    def send_rows(self, src):
        for k, d in enumerate((2, 1, -1, 0)):
            at = rows(self.quarter(d), 64)
            self.net.put(self.base + k, src.at[at], self.rsib.at[at], "mp", sibling())

    def total(self, d, p, own, store):
        start = self.quarter(d) + 32 * p
        for i in (0, 1):
            at = rows(start + 16 * i, 16)
            v = own[at].astype(F32) + self.rsib[at].astype(F32)
            self.acc[at] = v
            if store:
                self.zsend[at] = v.astype(BF16)

    def begin(self, p, own, by_rows):
        put, base = self.net.put, self.base + 4 + 6 * p

        def arrived(k, d):
            if by_rows and p == 0:
                self.net.got(self.base + k, self.rsib.at[rows(self.quarter(d), 64)])

        if p == 0 and not by_rows:
            self.columns_here()
        arrived(0, 2)
        self.total(2, p, own, True)
        s = self.quarter(2) + 32 * p
        put(base + 0, self.zsend.at[rows(s, 16)], self.zrec.at[p, 0], "mp", self.right())
        put(base + 1, self.zsend.at[rows(s + 16, 16)], self.zrec.at[p, 1], "mp", self.left())
        arrived(1, 1)
        self.total(1, p, own, True)
        s = self.quarter(1) + 32 * p
        put(base + 2, self.zsend.at[rows(s + 16, 16)], self.zrec.at[p, 2], "mp", self.right())
        arrived(2, -1)
        self.total(-1, p, own, True)
        s = self.quarter(-1) + 32 * p
        put(base + 3, self.zsend.at[rows(s, 16)], self.zrec.at[p, 3], "mp", self.left())
        arrived(3, 0)
        self.total(0, p, own, False)

    def middle(self, p):
        base = self.base + 4 + 6 * p
        for k, d, off, way in ((0, 1, 0, self.right()), (1, -1, 16, self.left())):
            self.net.got(base + k, self.zrec.at[p, k])
            at = rows(self.quarter(d) + 32 * p + off, 16)
            self.zsend[at] = (self.acc[at] + self.zrec[p, k].astype(F32)).astype(BF16)
            self.net.put(base + 4 + k, self.zsend.at[at], self.zrec.at[p, 4 + k], "mp", way)

    def finish(self, p, use):
        base = self.base + 4 + 6 * p
        for part, pair in ((0, (3, 4)), (1, (2, 5))):
            for k in pair:
                self.net.got(base + k, self.zrec.at[p, k])
            r = 32 * p + 16 * part
            v = self.acc[rows(self.quarter(0) + r, 16)]
            for k in pair:
                v = v + self.zrec[p, k].astype(F32)
            use(r, v)

    def release(self):
        for k in range(16):
            if self.base + k in self.net.started:
                self.net.sent(self.base + k)


class Share:
    def __init__(self, net, out):
        self.net, self.out = net, out
        self.base = net.ids(16)

    def at(self, p, d, other=False, lo=0, n=32):
        m = lax.axis_index("mp")
        core = lax.rem(m, 2)
        if other:
            core = 1 - core
        return self.out.at[core, lax.rem(m // 2 + (d + 4), 4), pl.ds(32 * p + lo, n)]

    def begin(self, p, src=None):
        src = self.at(p, 0) if src is None else src.at[pl.ds(32 * p, 32)]
        put, base = self.net.put, self.base + 8 * p
        put(base + 0, src, self.at(p, 0), "mp", shifted("mp", 2))
        put(base + 1, src, self.at(p, 0), "mp", shifted("mp", -2))
        put(base + 4, src, self.at(p, 0), "mp", sibling())

    def middle(self, p):
        put, base = self.net.put, self.base + 8 * p
        self.net.got(base + 0, self.at(p, -1))
        half = self.at(p, -1, False, 0, 16)
        put(base + 2, half, half, "mp", shifted("mp", 2))
        self.net.got(base + 1, self.at(p, 1))
        half = self.at(p, 1, False, 16, 16)
        put(base + 3, half, half, "mp", shifted("mp", -2))
        put(base + 5, self.at(p, -1), self.at(p, -1), "mp", sibling())
        put(base + 6, self.at(p, 1), self.at(p, 1), "mp", sibling())

    def later(self, p):
        base = self.base + 8 * p
        self.net.got(base + 2, self.at(p, 2, False, 0, 16))
        self.net.got(base + 3, self.at(p, 2, False, 16, 16))
        self.net.put(base + 7, self.at(p, 2), self.at(p, 2), "mp", sibling())

    def finish(self, p):
        for k, d in ((4, 0), (5, -1), (6, 1), (7, 2)):
            self.net.got(self.base + 8 * p + k, self.at(p, d, True))

    def release(self):
        for k in range(16):
            self.net.sent(self.base + k)


class Stream:
    def __init__(self, make):
        self.make = make

    def start(self, j):
        for c in self.make(j, j % 2):
            c.start()

    def wait(self, j):
        for c in self.make(j, j % 2):
            c.wait()

    def start_slot(self, j, s):
        for c in self.make(j, s):
            c.start()

    def wait_slot(self, s):
        for c in self.make(0, s):
            c.wait()

    def run(self, count, body, first=0):
        @pl.loop(0, count)
        def _(i):
            self.wait(first + i)
            body(i, (first + i) % 2)

            @pl.when(i + 2 < count)
            def _():
                self.start(first + i + 2)


def lanes(shape):
    return lax.broadcasted_iota(jnp.int32, shape, len(shape) - 1)


def swap_halves(v):
    lane = lanes(v.shape)
    return jnp.where(lane % HD < HD // 2, pltpu.roll(v, 96, 1), pltpu.roll(v, 32, 1))


def main_kernel(
    x_hbm, cot_hbm, parents, wa_hbm, wm_hbm, we_hbm, wr_hbm, gains, table,
    y2_hbm, y4_hbm, spill, mid, dmid, gpart, o_att, o_mrg, o_exp, o_red,
    g_red, g_gate, g_up, g_mrg, g_att,
    ra_red, ra_gate, ra_up, ra_mrg, ra_att,
    rb_red, rb_gate, rb_up, rb_mrg, rb_att,
    sa, sb, wa, wm, xd, cot, n1, tt, n2, hid, hid_t,
    acc, sib, rsib, zrec, probs, kv, q, att, datt, dkv, dkv_low, dkv_in, dpack,
    send, recv, loc, wsem,
):
    net = Net(send, recv, send.shape[0])
    m = lax.axis_index("mp")
    core, z = lax.rem(m, 2), m // 2
    seq = lax.axis_index("seq")
    other = 1 - core
    hello(
        [("dp", shifted("dp", 1)), ("dp", shifted("dp", -1))]
        + [("seq", shifted("seq", d)) for d in (1, 2, 3)]
        + [("mp", shifted("mp", 2)), ("mp", shifted("mp", -2)), ("mp", sibling())]
    )
    base_kv, base_dkv = net.ids(6), net.ids(3)
    fold = Fold(net, acc, rsib, sib, zrec)
    share_one, share_two = Share(net, n2), Share(net, xd)
    s_red = Spread(net, g_red, ra_red, rb_red)
    s_gate = Spread(net, g_gate, ra_gate, rb_gate)
    s_up = Spread(net, g_up, ra_up, rb_up)
    s_mrg = Spread(net, g_mrg, ra_mrg, rb_mrg)
    s_att = Spread(net, g_att, ra_att, rb_att)

    def bring(k, src, dst):
        c = pltpu.make_async_copy(src, dst, loc.at[k])
        c.start()
        return c

    c_x = [bring(t, x_hbm.at[t], xd.at[t]) for t in (0, 1)]
    c_wa = bring(2, wa_hbm, wa)
    c_cot = bring(3, cot_hbm, cot)
    c_wm = bring(4, wm_hbm, wm)
    down = Stream(lambda j, s: [pltpu.make_async_copy(wr_hbm.at[rows(256 * j, 256)], sb.at[s], wsem.at[0, s])])
    down.start(0)
    down.start(1)

    both_gains = gains[...].astype(F32)
    gain_one, gain_two = both_gains[0:1, :], both_gains[1:2, :]
    flat = xd
    for t in (0, 1):
        c_x[t].wait()

        @pl.loop(0, 16, unroll=4)
        def _(i):
            v = flat[t, i // 4, rows(16 * (i % 4), 16)].astype(F32)
            r = lax.rsqrt(jnp.mean(v * v, axis=-1, keepdims=True) + NORM_EPS)
            n1[t, rows(16 * i, 16)] = (v * r * gain_one).astype(BF16)

    c_wa.wait()

    def ancestors(t, b):
        p1 = parents[t, b]
        p2 = jnp.where(p1 >= 0, parents[t, jnp.maximum(p1, 0)], -1)
        p3 = jnp.where(p2 >= 0, parents[t, jnp.maximum(p2, 0)], -1)
        return p1, p2, p3

    def turns(t, i):
        ps = ancestors(t, 2 * seq + i)
        depth = sum(jnp.where(p >= 0, 1, 0) for p in ps)
        return table[0, depth], table[1, depth]

    lower = lanes((128, 128)) < HD

    def own_kv(t, at):
        return kv.at[t, pl.ds(2 * at, 2)]

    for t in (0, 1):
        packed = dot(n1[t], wa[...])
        for i in (0, 1):
            c, s = turns(t, i)
            part = packed[128 * i : 128 * i + 128]
            for g in (0, 1):
                v = part[:, 128 * g : 128 * g + 128]
                q[t, i, g] = (v * c + swap_halves(v) * s).astype(BF16)
            v = part[:, 256:384]
            kv[t, 2 * seq + i] = jnp.where(lower, v * c + swap_halves(v) * s, v).astype(BF16)
        if t == 0:
            hello_wait(8)
        for d in (1, 2, 3):
            net.put(base_kv + 3 * t + d - 1, own_kv(t, seq), own_kv(t, seq), "seq", shifted("seq", d))

    def transpose_into(src_of, dst):
        @pl.loop(0, 16, unroll=4)
        def _(j):
            cols = pl.ds(pl.multiple_of(128 * j, 128), 128)
            for t in (0, 1):
                dst[rows(128 * j, 128), 256 * t : 256 * t + 256] = src_of(t, cols).T

    transpose_into(lambda t, cols: n1[t, :, cols], tt)
    c_spill = bring(5, tt, spill)

    def hidden_grad(j):
        down.wait(j)
        v = dot_nt(cot[...].reshape(512, D), sb[j % 2])
        high = v.astype(BF16)
        low = (v - high.astype(F32)).astype(BF16)
        cols = pl.ds(256 * j, 256)
        g_gate[0, :, :, cols] = high.reshape(4, 128, 256)
        g_gate[1, :, :, cols] = low.reshape(4, 128, 256)
        if j < 2:
            down.start(j + 2)

    c_wm.wait()
    for t in (0, 1):
        for d in (1, 2, 3):
            net.got(base_kv + 3 * t + d - 1, own_kv(t, shifted("seq", -d)))

    low_lane = lanes((512, 128)) < HD
    key_col = lanes((128, 512))
    query_row = lax.broadcasted_iota(jnp.int32, (128, 512), 0)

    def key_views(t, ids):
        both = jnp.concatenate([kv[t, jnp.maximum(c, 0)] for c in ids], axis=0).astype(F32)
        turned = pltpu.roll(both, HD, 1)
        zero = jnp.zeros_like(both)
        keys = [jnp.where(low_lane, both, zero).astype(BF16), jnp.where(low_lane, zero, turned).astype(BF16)]
        values = [jnp.where(low_lane, turned, zero).astype(BF16), jnp.where(low_lane, zero, both).astype(BF16)]
        return keys, values

    @pl.loop(0, 4, unroll=2)
    def _(u):
        t, i = u // 2, u % 2
        b = 2 * seq + i
        ps = ancestors(t, b)
        keys, values = key_views(t, (b, *ps))
        seen = (key_col < 128) & (key_col <= query_row)
        for k, p in enumerate(ps):
            inside = (key_col >= 128 * (k + 1)) & (key_col < 128 * (k + 2))
            seen = seen | (inside & (p >= 0))
        for g in (0, 1):
            total = jnp.zeros((128, 128), F32)
            for h in (0, 1):
                scores = dot_nt(q[t, i, g], keys[h]) * HD**-0.5
                scores = jnp.where(seen, scores, MASK_FILL)
                e = jnp.exp(scores - jnp.max(scores, axis=-1, keepdims=True))
                p = (e / jnp.sum(e, axis=-1, keepdims=True)).astype(BF16)
                probs[u, 2 * g + h] = p
                total = total + dot(p, values[h])
            att[t, rows(128 * i, 128), 128 * g : 128 * g + 128] = total.astype(BF16)

    for k in range(4):
        cols = pl.ds(512 * k, 512)
        sib[:, cols] = dot(att[other], wm[:, cols]).astype(BF16)
    fold.send_rows(sib)
    for k in range(4):
        cols = pl.ds(512 * k, 512)
        acc[:, cols] = dot(att[core], wm[:, cols])
    expand = Stream(
        lambda j, s: [
            pltpu.make_async_copy(
                we_hbm.at[w, :, pl.ds(pl.multiple_of(128 * j, 128), 128)], sa.at[s, :, pl.ds(128 * w, 128)], wsem.at[1 + w, s]
            )
            for w in (0, 1)
        ]
    )
    expand.start(0)
    expand.start(1)
    c_cot.wait()
    for k in range(4):
        net.sent(fold.base + k)
    fold.begin(0, acc, True)
    fold.begin(1, acc, True)
    hidden_grad(0)
    fold.middle(0)
    hidden_grad(1)
    fold.middle(1)
    hidden_grad(2)
    hidden_grad(3)

    def to_normed(r, v):
        x_own = flat[core, z, rows(r, 16)].astype(F32)
        total = x_own + v
        mid[rows(r, 16)] = total
        rms = lax.rsqrt(jnp.mean(total * total, axis=-1, keepdims=True) + NORM_EPS)
        n2[core, z, rows(r, 16)] = (total * rms * gain_two).astype(BF16)

    for p in (0, 1):
        fold.finish(p, to_normed)
        share_one.begin(p)
    for p in (0, 1):
        share_one.middle(p)
    for p in (0, 1):
        share_one.later(p)
    for p in (0, 1):
        share_one.finish(p)
    fold.release()

    dgu = n1

    def feed_dot(s):
        both = dot(n2[...].reshape(512, D), sa[s])
        dkv[s, 0:4] = both[:, 0:128].reshape(4, 128, 128)
        dkv[s, 4:8] = both[:, 128:256].reshape(4, 128, 128)

    def feed_rest(j, s):
        cols = pl.ds(pl.multiple_of(128 * j, 128), 128)
        cols_up = pl.ds(pl.multiple_of(1024 + 128 * j, 128), 128)
        for k in range(8):
            t, blk, lo = k // 4, k // 2, 64 * (k % 2)
            at = pl.ds(64 * (k % 4), 64)
            gate = dkv[s, blk, lo : lo + 64]
            up = dkv[s, 4 + blk, lo : lo + 64]
            dh = g_gate[0, blk, lo : lo + 64, cols].astype(F32) + g_gate[1, blk, lo : lo + 64, cols].astype(F32)
            sig = 1.0 / (1.0 + jnp.exp(-gate))
            act = gate * sig
            h = (act * up).astype(BF16)
            hid[t, at, cols] = h
            hid_t[rows(128 * j, 128), 64 * k : 64 * k + 64] = h.T
            dup = dh * act
            n1[t, at, cols] = (dh * up * (sig + act * (1.0 - sig))).astype(BF16)
            n1[t, at, cols_up] = dup.astype(BF16)

    expand.wait(0)
    feed_dot(0)
    expand.start(2)

    @pl.loop(0, 3)
    def _(i):
        expand.wait_slot(1)
        feed_dot(1)
        feed_rest(2 * i, 0)
        expand.start_slot(2 * i + 3, 1)
        expand.wait_slot(0)
        feed_dot(0)
        feed_rest(2 * i + 1, 1)

        @pl.when(i < 2)
        def _():
            expand.start_slot(2 * i + 4, 0)

    expand.wait(7)
    feed_dot(1)
    feed_rest(6, 0)
    feed_rest(7, 1)

    back = Stream(
        lambda j, s: [
            pltpu.make_async_copy(we_hbm.at[w, rows(256 * j, 256)], sb.at[s, :, pl.ds(1024 * w, 1024)], wsem.at[3 + w, s])
            for w in (0, 1)
        ]
    )
    back.start(0)
    back.start(1)

    @pl.loop(0, 8)
    def _(j):
        cols = pl.ds(pl.multiple_of(256 * j, 256), 256)
        v = dot(hid_t[...], cot[:, :, :, cols].reshape(512, 256))
        g_red[j // 2, 2 * (j % 2)] = v[:, 0:128].astype(BF16)
        g_red[j // 2, 2 * (j % 2) + 1] = v[:, 128:256].astype(BF16)

    s_red.step0()
    c_spill.wait()
    transpose_into(lambda t, cols: n2[t, :, :, cols].reshape(256, 128), tt)

    def expand_grad(dst, first):
        @pl.loop(0, 16)
        def _(k):
            a, j = k // 4, k % 4
            cols = pl.ds(pl.multiple_of(first + 256 * j, 256), 256)
            v = dot(tt[rows(512 * a, 512)], dgu[:, :, cols].reshape(512, 256))
            dst[a, :, :, pl.ds(pl.multiple_of(256 * j, 256), 256)] = v.astype(BF16).reshape(4, 128, 256)

    expand_grad(g_gate, 0)
    s_gate.step0()

    for k in range(4):
        for w in (0, 1):
            j = 2 * k + w
            back.wait(j)
            cols = pl.ds(256 * j, 256)
            v = dot_nt(dgu[...].reshape(512, D), sb[j % 2])
            first, second = v[0:256], v[256:512]
            sib[:, cols] = jnp.where(core == 0, second, first).astype(BF16)
            acc[:, cols] = jnp.where(core == 0, first, second)
            if j + 2 < 8:
                back.start(j + 2)
        fold.send_columns(k, sib)
    s_red.step1()
    for k in range(4):
        net.sent(fold.base + k)
    fold.begin(0, acc, False)
    fold.begin(1, acc, False)
    expand_grad(g_up, 1024)
    s_up.step0()
    c_tt = pltpu.make_async_copy(spill, tt, loc.at[6])
    c_tt.start()
    fold.middle(0)
    fold.middle(1)
    s_gate.step1()

    def to_branch(r, v):
        at = rows(r, 16)
        total = mid[at]
        rms = lax.rsqrt(jnp.mean(total * total, axis=-1, keepdims=True) + NORM_EPS)
        u = v * gain_two
        back_vals = rms * u - total * (rms * rms * rms) * jnp.mean(u * total, axis=-1, keepdims=True)
        full = cot[core, z, at].astype(F32) + back_vals
        dmid[at] = full
        xd[core, z, at] = full.astype(BF16)
        gpart[0:1, :] = gpart[0:1, :] + jnp.sum(v * total * rms, axis=0, keepdims=True)

    gpart[...] = jnp.zeros_like(gpart)
    for p in (0, 1):
        fold.finish(p, to_branch)
        share_two.begin(p)

    down_out = Stream(
        lambda j, s: [
            pltpu.make_async_copy(
                wr_hbm.at[:, pl.ds(pl.multiple_of(256 * j, 256), 256)], sa.at[s, pl.ds(0, 1024)], wsem.at[5, s]
            )
        ]
    )
    down_out.start(0)
    down_out.start(1)

    def part_out(j, s):
        v = dot(hid[...].reshape(512, 1024), sa[s, 0:1024])
        n1[:, :, pl.ds(pl.multiple_of(256 * j, 256), 256)] = v.astype(BF16).reshape(2, 256, 256)

    down_out.run(8, part_out)
    c_y2 = bring(7, n1, y2_hbm)
    s_red.step2()
    for p in (0, 1):
        share_two.middle(p)
    s_up.step1()
    for p in (0, 1):
        share_two.later(p)
    for p in (0, 1):
        share_two.finish(p)

    dbr = xd
    v = dot_nt(dbr[...].reshape(512, D), wm[...]).astype(BF16)
    datt[...] = v.reshape(2, 256, 256)

    dkv[...] = jnp.zeros_like(dkv)

    @pl.loop(0, 4, unroll=2)
    def _(u):
        t, i = u // 2, u % 2
        b = 2 * seq + i
        ps = ancestors(t, b)
        keys, values = key_views(t, (b, *ps))
        c, s = turns(t, i)
        at = rows(128 * i, 128)
        dk = [jnp.zeros((512, 128), F32), jnp.zeros((512, 128), F32)]
        dv = [jnp.zeros((512, 128), F32), jnp.zeros((512, 128), F32)]
        for g in (0, 1):
            dq = jnp.zeros((128, 128), F32)
            da = datt[t, at, 128 * g : 128 * g + 128]
            for h in (0, 1):
                p = probs[u, 2 * g + h]
                pf = p.astype(F32)
                dp = dot_nt(da, values[h])
                inner = jnp.sum(pf * dp, axis=-1, keepdims=True)
                ds = (pf * (dp - inner)).astype(BF16)
                dq = dq + dot(ds, keys[h])
                dk[h] = dk[h] + dot_tn(ds, q[t, i, g])
                dv[h] = dv[h] + dot_tn(p, da)
            dq = dq * HD**-0.5
            dpack[t, at, 128 * g : 128 * g + 128] = (dq * c - swap_halves(dq) * s).astype(BF16)
        both = jnp.where(
            low_lane, (dk[0] + pltpu.roll(dk[1], HD, 1)) * HD**-0.5, pltpu.roll(dv[0], HD, 1) + dv[1]
        )
        dkv[t, b] = dkv[t, b] + both[0:128]
        for blk in range(8):
            v = dkv[t, blk]
            for k, p in enumerate(ps):
                v = v + both[128 * (k + 1) : 128 * (k + 2)] * jnp.where(p == blk, 1.0, 0.0)
            dkv[t, blk] = v

    dkv_low[...] = dkv[...].astype(BF16)
    for d in (1, 2, 3):
        peer = shifted("seq", d)
        net.put(base_dkv + d - 1, dkv_low.at[pl.ds(0, 2), pl.ds(2 * peer, 2)], dkv_in.at[d - 1], "seq", peer)

    @pl.loop(0, 8)
    def _(j):
        cols = pl.ds(pl.multiple_of(256 * j, 256), 256)
        v = dot_tn(att[...].reshape(512, 256), dbr[:, :, :, cols].reshape(512, 256))
        g_mrg[j // 2, 2 * (j % 2)] = v[:, 0:128].astype(BF16)
        g_mrg[j // 2, 2 * (j % 2) + 1] = v[:, 128:256].astype(BF16)

    s_mrg.step0()
    s_gate.step2()
    s_red.step3()
    for d in (1, 2, 3):
        net.got(base_dkv + d - 1, dkv_in.at[d - 1])
    for t in (0, 1):
        for i in (0, 1):
            v = dkv[t, 2 * seq + i]
            for d in (0, 1, 2):
                v = v + dkv_in[d, t, i].astype(F32)
            c, s = turns(t, i)
            v = jnp.where(lower, v * c - swap_halves(v) * s, v)
            dpack[t, 128 * i : 128 * i + 128, 256:384] = v.astype(BF16)
    c_tt.wait()

    @pl.loop(0, 4)
    def _(a):
        v = dot(tt[rows(512 * a, 512)], dpack[...].reshape(512, 384))
        g_att[a] = v.astype(BF16).reshape(4, 128, 384)

    s_att.step0()
    s_mrg.step1()
    share_one.release()

    @pl.loop(0, 8)
    def _(j):
        v = dot_nt(dpack[...].reshape(512, 384), wa[rows(256 * j, 256)])
        n2[:, :, :, pl.ds(pl.multiple_of(256 * j, 256), 256)] = v.astype(BF16).reshape(2, 4, 64, 256)

    c_y4 = bring(8, n2, y4_hbm)
    s_up.step2()
    s_gate.step3()
    s_att.step1()
    s_red.step4(o_red)
    s_mrg.step2()
    s_up.step3()
    s_att.step2()
    s_gate.step4(o_exp, 0)
    s_mrg.step3()
    s_att.step3()
    s_up.step4(o_exp, 1)
    s_mrg.step4(o_mrg)
    s_att.step4(o_att)
    c_y2.wait()
    c_y4.wait()
    net.drain()


def any_space(n):
    return [pl.BlockSpec(memory_space=pl.ANY)] * n


def main_call(x, cot, parents, wa, wm, we, wr, gains, table):
    def grads(size, cols):
        q = size // 4
        return (size, cols, q)

    kinds = [grads(1024, 128), grads(128, 1024), grads(128, 1024), grads(256, 128), grads(128, 384)]
    vm = pltpu.VMEM
    scratch = (
        [vm((4, 4, s, c), BF16) for s, c, q in kinds]
        + [vm((2, 6, 4, q, c), BF16) for s, c, q in kinds]
        + [vm((2, 6, q, c), BF16) for s, c, q in kinds]
        + [
            vm((2, 2048, 256), BF16),
            vm((2, 256, 2048), BF16),
            vm((2048, 384), BF16),
            vm((256, 2048), BF16),
            vm((2, 4, 64, D), BF16),
            vm((2, 4, 64, D), BF16),
            vm((2, 256, D), BF16),
            vm((D, 512), BF16),
            vm((2, 4, 64, D), BF16),
            vm((2, 256, 1024), BF16),
            vm((1024, 512), BF16),
            vm((256, D), F32),
            vm((256, D), BF16),
            vm((256, D), BF16),
            vm((2, 6, 16, D), BF16),
            vm((4, 4, 128, 512), BF16),
            vm((2, 8, 128, 128), BF16),
            vm((2, 2, 2, 128, 128), BF16),
            vm((2, 256, 256), BF16),
            vm((2, 256, 256), BF16),
            vm((2, 8, 128, 128), F32),
            vm((2, 8, 128, 128), BF16),
            vm((3, 2, 2, 128, 128), BF16),
            vm((2, 256, 384), BF16),
            pltpu.SemaphoreType.DMA((192,)),
            pltpu.SemaphoreType.DMA((192,)),
            pltpu.SemaphoreType.DMA((10,)),
            pltpu.SemaphoreType.DMA((6, 2)),
        ]
    )
    sds = jax.ShapeDtypeStruct
    out_shape = [
        sds((2, 256, D), BF16),
        sds((2, 4, 64, D), BF16),
        sds((D, 512), BF16),
        sds((64, D), F32),
        sds((64, D), F32),
        sds((8, D), F32),
        sds((128, 384), F32),
        sds((256, 128), F32),
        sds((128, 2, 1024), F32),
        sds((1024, 128), F32),
    ]
    vspec = pl.BlockSpec(memory_space=pltpu.VMEM)
    hbm = pl.BlockSpec(memory_space=pl.ANY)
    return pl.pallas_call(
        main_kernel,
        out_shape=out_shape,
        in_specs=[hbm, hbm, pl.BlockSpec(memory_space=pltpu.SMEM), hbm, hbm, hbm, hbm, vspec, vspec],
        out_specs=[hbm] * 3 + [vspec] * 7,
        scratch_shapes=scratch,
        compiler_params=pltpu.CompilerParams(
            collective_id=1, has_side_effects=True, vmem_limit_bytes=64 * 2**20 - 65536
        ),
    )(x, cot, parents, wa, wm, we, wr, gains, table)


class Gather:
    def __init__(self, net, own, size, region):
        self.net, self.own, self.size, self.region = net, own, size, region
        self.base = net.ids(40)
        self.half, self.quarter = size // 2, size // 4

    def idx(self, h, da, db):
        fa, sa = (("dp", "seq"), ("seq", "dp"))[h]
        c = {fa: shifted(fa, da), sa: shifted(sa, db)}
        return c["dp"] * 4 + c["seq"]

    def both(self, k, src, dst, axis):
        self.net.put(k, src, dst, axis, shifted(axis, 1))
        self.net.put(k + 1, src, dst, axis, shifted(axis, -1))

    def begin(self):
        for stage in (0, 1):
            for h in (0, 1):
                axis = ("dp", "seq")[(h + stage) % 2]
                lo = h * self.half
                src = self.own.at[pl.ds(lo, self.half)]
                self.both(self.base + 20 * h + 4 * stage, src, self.region(self.idx(h, 0, 0), lo, self.half), axis)

    def near(self):
        for h in (0, 1):
            fa, sa = (("dp", "seq"), ("seq", "dp"))[h]
            base, lo = self.base + 20 * h, h * self.half
            for k, d in ((0, -1), (1, 1)):
                p = self.region(self.idx(h, d, 0), lo, self.half)
                self.net.got(base + k, p)
                part = self.region(self.idx(h, d, 0), lo + k * self.quarter, self.quarter)
                self.net.put(base + 2 + k, part, part, fa, shifted(fa, -d))
                self.both(base + 8 + 4 * k, p, p, sa)

    def far(self):
        for h in (0, 1):
            fa, sa = (("dp", "seq"), ("seq", "dp"))[h]
            base, lo = self.base + 20 * h, h * self.half
            at = self.idx(h, 2, 0)
            for k in (0, 1):
                self.net.got(base + 2 + k, self.region(at, lo + k * self.quarter, self.quarter))
            p = self.region(at, lo, self.half)
            self.both(base + 16, p, p, sa)

    def cross(self, k):
        d = (0, -1, 1, 2)[k]
        for h in (0, 1):
            sa = (("dp", "seq"), ("seq", "dp"))[h][1]
            base, lo = self.base + 20 * h + 4 + 4 * k, h * self.half
            for w, db in ((0, -1), (1, 1)):
                at = self.idx(h, d, db)
                self.net.got(base + w, self.region(at, lo, self.half))
                part = self.region(at, lo + w * self.quarter, self.quarter)
                self.net.put(base + 2 + w, part, part, sa, shifted(sa, -db))

    def finish(self):
        for k, d in enumerate((0, -1, 1, 2)):
            for h in (0, 1):
                base, lo = self.base + 20 * h + 4 + 4 * k, h * self.half
                at = self.idx(h, d, 2)
                for w in (0, 1):
                    self.net.got(base + 2 + w, self.region(at, lo + w * self.quarter, self.quarter))


def last_kernel(
    w_att, w_mrg, w_exp, w_red, y2, y4, mid, dmid, x_hbm, gains, gpart, mg, fg, sg,
    out, grad, f_att, f_mrg, f_exp, f_red, n_gain, m_gain, v_gain, f_gain,
    own, acc, rsib2, zs2, zrec2, rsib4, zs4, zrec4, x_own, rows2, rows4,
    gbuf, gs1, gs2, gs3, gs4, gs5, gtot, gtwo, gnew,
    send, recv, loc,
):
    net = Net(send, recv, send.shape[0])
    m = lax.axis_index("mp")
    core, z = lax.rem(m, 2), m // 2
    other = 1 - core
    dp, seq = lax.axis_index("dp"), lax.axis_index("seq")
    me = dp * 4 + seq
    peers = [("dp", shifted("dp", d)) for d in (1, 2, 3)] + [("seq", shifted("seq", d)) for d in (1, 2, 3)]
    peers += [("mp", shifted("mp", d)) for d in range(1, 8)]
    hello(peers)

    def bring(k, src, dst):
        c = pltpu.make_async_copy(src, dst, loc.at[k])
        c.start()
        return c

    by_row = lambda ref, n: (lambda i, lo, k: ref.at[rows(i * n + lo, k)])
    by_col = lambda ref: (lambda i, lo, k: ref.at[pl.ds(lo, k), pl.ds(pl.multiple_of(128 * i, 128), 128)])
    exp_at = lambda i, lo, k: f_exp.at[pl.ds(128 * i + lo, k)]
    sets = [
        Gather(net, w_exp, 128, exp_at),
        Gather(net, w_red, 1024, by_col(f_red)),
        Gather(net, w_att, 128, by_row(f_att, 128)),
        Gather(net, w_mrg, 256, by_col(f_mrg)),
    ]
    fold4, fold2 = Fold(net, acc, rsib4, zs4, zrec4), Fold(net, acc, rsib2, zs2, zrec2)
    share4, share2 = Share(net, grad), Share(net, out)
    b1, b2, b3, b4, b5 = net.ids(7), net.ids(3), net.ids(3), net.ids(3), net.ids(3)
    local = [
        bring(0, w_att, f_att.at[rows(128 * me, 128)]),
        bring(1, w_mrg, f_mrg.at[:, pl.ds(pl.multiple_of(128 * me, 128), 128)]),
        bring(2, w_exp, f_exp.at[pl.ds(128 * me, 128)]),
        bring(3, w_red, f_red.at[:, pl.ds(pl.multiple_of(128 * me, 128), 128)]),
    ]
    c_own = bring(4, y4.at[core], own)
    c_x = bring(5, x_hbm.at[core, z], x_own)
    hello_wait(13)
    fold4.send_rows(y4.at[other])
    for g in sets:
        g.begin()
    gain_one = gains[...].astype(F32)[0:1, :]
    c_own.wait()
    fold4.begin(0, own, True)
    fold4.begin(1, own, True)
    c_own = bring(4, y2.at[core], own)
    fold2.send_rows(y2.at[other])
    fold4.middle(0)
    fold4.middle(1)
    gbuf[...] = jnp.zeros_like(gbuf)
    gbuf[1:2, :] = gpart[0:1, :]
    c_x.wait()

    def to_grad(r, v):
        at = rows(r, 16)
        x = x_own[at].astype(F32)
        rms = lax.rsqrt(jnp.mean(x * x, axis=-1, keepdims=True) + NORM_EPS)
        u = v * gain_one
        back = rms * u - x * (rms * rms * rms) * jnp.mean(u * x, axis=-1, keepdims=True)
        rows4[at] = (dmid[at] + back).astype(BF16)
        gbuf[0:1, :] = gbuf[0:1, :] + jnp.sum(v * x * rms, axis=0, keepdims=True)

    for p in (0, 1):
        fold4.finish(p, to_grad)
        share4.begin(p, rows4)
    l4 = bring(6, rows4, grad.at[core, z])
    gs1[m] = gbuf[...]
    for d in range(1, 8):
        net.put(b1 + d - 1, gbuf, gs1.at[m], "mp", shifted("mp", d))
    for g in sets:
        g.near()
    c_own.wait()
    fold2.begin(0, own, True)
    fold2.begin(1, own, True)
    fold2.middle(0)
    fold2.middle(1)
    for d in range(1, 8):
        net.got(b1 + d - 1, gs1.at[shifted("mp", -d)])
    total = gs1[0]
    for k in range(1, 8):
        total = total + gs1[k]
    gtot[...] = total
    piece = lambda i, n: pl.ds(pl.multiple_of(i * n, 128), n)
    gs2[dp] = gtot[:, piece(dp, 512)]
    for d in (1, 2, 3):
        net.put(b2 + d - 1, gtot.at[:, piece(shifted("dp", d), 512)], gs2.at[dp], "dp", shifted("dp", d))
    share4.middle(0)
    share4.middle(1)

    def to_out(r, v):
        at = rows(r, 16)
        rows2[at] = (mid[at] + v).astype(BF16)

    for p in (0, 1):
        fold2.finish(p, to_out)
        share2.begin(p, rows2)
    l2 = bring(7, rows2, out.at[core, z])
    for g in sets:
        g.far()
    for d in (1, 2, 3):
        net.got(b2 + d - 1, gs2.at[shifted("dp", -d)])
    gtwo[...] = gs2[0] + gs2[1] + gs2[2] + gs2[3]
    gs3[seq] = gtwo[:, piece(seq, 128)]
    for d in (1, 2, 3):
        net.put(b3 + d - 1, gtwo.at[:, piece(shifted("seq", d), 128)], gs3.at[seq], "seq", shifted("seq", d))
    share4.later(0)
    share4.later(1)
    for g in sets:
        g.cross(0)
    for d in (1, 2, 3):
        net.got(b3 + d - 1, gs3.at[shifted("seq", -d)])
    shard = gs3[0] + gs3[1] + gs3[2] + gs3[3]
    new, mom, var = adamw(mg[...], fg[...], sg[...], shard[0:2])
    n_gain[...] = new
    m_gain[...] = mom
    v_gain[...] = var
    gnew[...] = jnp.zeros_like(gnew)
    gnew[0:2, :] = new
    gs4[seq] = gnew[...]
    for d in (1, 2, 3):
        net.put(b4 + d - 1, gnew, gs4.at[seq], "seq", shifted("seq", d))
    share2.middle(0)
    share2.middle(1)
    for g in sets:
        g.cross(1)
    for d in (1, 2, 3):
        net.got(b4 + d - 1, gs4.at[shifted("seq", -d)])
    gs5[dp] = gs4[...]
    for d in (1, 2, 3):
        net.put(b5 + d - 1, gs4, gs5.at[dp], "dp", shifted("dp", d))
    share2.later(0)
    share2.later(1)
    for k in (2, 3):
        for g in sets:
            g.cross(k)
    for d in (1, 2, 3):
        net.got(b5 + d - 1, gs5.at[shifted("dp", -d)])
    for a in range(4):
        for b in range(4):
            lo = 128 * (4 * a + b)
            f_gain[:, lo : lo + 128] = gs5[a, b, 0:2].astype(BF16)
    share4.finish(0)
    share4.finish(1)
    share2.finish(0)
    share2.finish(1)
    for g in sets:
        g.finish()
    for c in local + [l4, l2]:
        c.wait()
    net.drain()


def last_call(w_att, w_mrg, w_exp, w_red, y2, y4, mid, dmid, x, gains, gpart, mg, fg, sg):
    vm, sds = pltpu.VMEM, jax.ShapeDtypeStruct
    hbm = pl.BlockSpec(memory_space=pl.ANY)
    vspec = pl.BlockSpec(memory_space=pltpu.VMEM)
    out_shape = [
        sds((2, 4, 64, D), BF16),
        sds((2, 4, 64, D), BF16),
        sds((D, 384), BF16),
        sds((256, D), BF16),
        sds((D, 2, 1024), BF16),
        sds((1024, D), BF16),
        sds((2, 128), F32),
        sds((2, 128), F32),
        sds((2, 128), F32),
        sds((2, D), BF16),
    ]
    scratch = [
        vm((256, D), BF16),
        vm((256, D), F32),
        vm((256, D), BF16),
        vm((256, D), BF16),
        vm((2, 6, 16, D), BF16),
        vm((256, D), BF16),
        vm((256, D), BF16),
        vm((2, 6, 16, D), BF16),
        vm((64, D), BF16),
        vm((64, D), BF16),
        vm((64, D), BF16),
        vm((8, D), F32),
        vm((8, 8, D), F32),
        vm((4, 8, 512), F32),
        vm((4, 8, 128), F32),
        vm((4, 8, 128), F32),
        vm((4, 4, 8, 128), F32),
        vm((8, D), F32),
        vm((8, 512), F32),
        vm((8, 128), F32),
        pltpu.SemaphoreType.DMA((256,)),
        pltpu.SemaphoreType.DMA((256,)),
        pltpu.SemaphoreType.DMA((10,)),
    ]
    return pl.pallas_call(
        last_kernel,
        out_shape=out_shape,
        in_specs=[hbm] * 6 + [vspec] * 2 + [hbm] + [vspec] * 5,
        out_specs=[hbm] * 6 + [vspec] * 4,
        scratch_shapes=scratch,
        compiler_params=pltpu.CompilerParams(
            collective_id=2, has_side_effects=True, vmem_limit_bytes=32 * 2**20
        ),
    )(w_att, w_mrg, w_exp, w_red, y2, y4, mid, dmid, x, gains, gpart, mg, fg, sg)


def rotary_table():
    inv = ROPE_BASE ** (-2.0 * np.arange(HD // 2, dtype=np.float32) / HD)
    angle = np.arange(512, dtype=np.float32)[:, None] * inv.astype(np.float32)[None, :]
    c, s = np.cos(angle), np.sin(angle)
    both = np.stack([np.concatenate([c, c, c, c], 1), np.concatenate([-s, s, -s, s], 1)])
    return both.reshape(2, 4, 128, 128).astype(np.float32)


def on_device(
    inputs, cotangent, parents, weight_attend, weight_merge, weight_expand, weight_reduce, gains,
    master_attend, master_merge, master_expand, master_reduce, master_gains,
    first_attend, first_merge, first_expand, first_reduce, first_gains,
    second_attend, second_merge, second_expand, second_reduce, second_gains,
):
    x = inputs.reshape(2, 4, 64, D)
    cot = cotangent.reshape(2, 4, 64, D)
    we = weight_expand.transpose(1, 0, 2)
    y2, y4, _, mid, dmid, gpart, g_att, g_mrg, g_exp, g_red = main_call(
        x, cot, parents, weight_attend, weight_merge, we, weight_reduce, gains, jnp.asarray(rotary_table())
    )
    n_att, m_att, v_att = adamw(master_attend, first_attend, second_attend, g_att)
    n_mrg, m_mrg, v_mrg = adamw(master_merge, first_merge, second_merge, g_mrg)
    n_exp, m_exp, v_exp = adamw(master_expand, first_expand, second_expand, g_exp)
    n_red, m_red, v_red = adamw(master_reduce, first_reduce, second_reduce, g_red)
    out, grad, f_att, f_mrg, f_exp, f_red, n_gain, m_gain, v_gain, f_gain = last_call(
        n_att.astype(BF16), n_mrg.astype(BF16), n_exp.astype(BF16), n_red.astype(BF16),
        y2, y4.reshape(2, 256, D), mid, dmid, x, gains, gpart, master_gains, first_gains, second_gains,
    )
    return (
        out.reshape(2, 256, D), grad.reshape(2, 256, D),
        n_att, n_mrg, n_exp, n_red, n_gain,
        m_att, m_mrg, m_exp, m_red, m_gain,
        v_att, v_mrg, v_exp, v_red, v_gain,
        f_att, f_mrg, f_exp, f_red, f_gain,
    )


def solution(mesh):
    both = ("dp", "seq")
    states = (P(both, "mp"), P("mp", both), P(both, None, "mp"), P("mp", both), P(None, both))
    weights = (P(None, "mp"), P("mp", None), P(None, None, "mp"), P("mp", None), P())
    tokens = P("dp", "seq", None)
    return jax.shard_map(
        on_device,
        mesh=mesh,
        in_specs=(tokens, tokens, P("dp", None), *weights, *states, *states, *states),
        out_specs=(tokens, tokens, *states, *states, *states, *weights),
        check_vma=False,
    )
```

```python
import functools

import jax
import jax.numpy as jnp
import numpy as np
from jax import lax
from jax.experimental import pallas as pl
from jax.experimental.pallas import tpu as pltpu
from jax.sharding import PartitionSpec as P

MESH = pl.DeviceIdType.MESH
F32 = jnp.float32
BF16 = jnp.bfloat16
D = 2048
HD = 64
STEP = 5
NORM_EPS = 1e-05
ROPE_BASE = 500000.0
MASK_FILL = -1e30
BETA_ONE = 0.5
BETA_TWO = 0.5
ADAM_EPS = 1e-08
LEARN_RATE = 0.005
DECAY_RATE = 0.1
FIX_ONE = 1.0 - BETA_ONE**STEP
FIX_TWO = 1.0 - BETA_TWO**STEP
SIZES = {"dp": 4, "seq": 4, "mp": 8}


def adamw(master, first, second, grad_vals):
    momentum = BETA_ONE * first + (1.0 - BETA_ONE) * grad_vals
    variance = BETA_TWO * second + (1.0 - BETA_TWO) * grad_vals * grad_vals
    direction = momentum / FIX_ONE / (jnp.sqrt(variance / FIX_TWO) + ADAM_EPS)
    renewed = master - LEARN_RATE * (direction + DECAY_RATE * master)
    return (renewed, momentum, variance)


def dot(a, b):
    return lax.dot_general(a, b, (((1,), (0,)), ((), ())), preferred_element_type=F32)


def dot_nt(a, b):
    return lax.dot_general(a, b, (((1,), (1,)), ((), ())), preferred_element_type=F32)


def dot_tn(a, b):
    return lax.dot_general(a, b, (((0,), (0,)), ((), ())), preferred_element_type=F32)


def shifted(axis, delta):
    n = SIZES[axis]
    return lax.rem(lax.axis_index(axis) + (delta + n), n)


def sibling():
    m = lax.axis_index("mp")
    return m + 1 - 2 * lax.rem(m, 2)


def rows(start, n):
    return pl.ds(pl.multiple_of(start, 16), n)


class Net:
    def __init__(self, send, recv, count):
        self.send, self.recv, self.count = send, recv, count
        self.used = 0
        self.started = {}

    def ids(self, n):
        first = self.used
        self.used += n
        assert self.used <= self.count
        return first

    def put(self, k, src, dst, axis, index):
        c = pltpu.make_async_remote_copy(
            src_ref=src,
            dst_ref=dst,
            send_sem=self.send.at[k],
            recv_sem=self.recv.at[k],
            device_id={axis: index},
            device_id_type=MESH,
        )
        c.start()
        self.started[k] = c

    def got(self, k, dst):
        pltpu.make_async_remote_copy(
            src_ref=dst,
            dst_ref=dst,
            send_sem=self.send.at[k],
            recv_sem=self.recv.at[k],
            device_id={"dp": shifted("dp", 1)},
            device_id_type=MESH,
        ).wait_recv()

    def sent(self, k):
        self.started.pop(k).wait_send()

    def drain(self):
        for k in sorted(self.started):
            self.started[k].wait_send()
        self.started = {}


def hello(peers):
    sem = pltpu.get_barrier_semaphore()
    for axis, index in peers:
        pl.semaphore_signal(sem, inc=1, device_id={axis: index}, device_id_type=MESH)


def hello_wait(n):
    pl.semaphore_wait(pltpu.get_barrier_semaphore(), n)


class Spread:
    def __init__(self, net, own, first, second):
        self.net, self.own, self.r1, self.r2 = net, own, first, second
        self.size, self.cols = own.shape[2], own.shape[3]
        self.q = self.size // 4
        self.base = net.ids(24)
        self.chunk = min(self.q, max(16, 16384 // self.cols))

    def axes(self, h):
        return (("dp", "seq"), ("seq", "dp"))[h]

    def row(self, h, da):
        a = shifted(self.axes(h)[0], da)
        return (lambda b: (a, b)) if h == 0 else (lambda b: (b, a))

    def block(self, h, db):
        a, b = lax.axis_index(self.axes(h)[0]), shifted(self.axes(h)[1], db)
        return (a, b) if h == 0 else (b, a)

    def view(self, h, da, lo):
        a = shifted(self.axes(h)[0], da)
        if h == 0:
            return self.own.at[a, pl.ds(0, 4), pl.ds(lo, self.q)]
        return self.own.at[pl.ds(0, 4), a, pl.ds(lo, self.q)]

    def one(self, h, db, lo):
        a, b = self.block(h, db)
        return self.own.at[a, b, pl.ds(lo, self.q)]

    def add(self, index_of, count, lo, sources, out=None):
        steps = self.q // self.chunk

        @pl.loop(0, count * steps)
        def _(k):
            b = k // steps
            r = (k % steps) * self.chunk
            at = (*index_of(b), rows(lo + r, self.chunk))
            v = self.own[at].astype(F32)
            for ref, lead in sources:
                if count > 1:
                    v = v + ref[(*lead, b, rows(r, self.chunk))].astype(F32)
                else:
                    v = v + ref[(*lead, rows(r, self.chunk))].astype(F32)
            if out is None:
                self.own[at] = v.astype(BF16)
            else:
                out[rows(lo + r, self.chunk)] = v

    def step0(self):
        q = self.q
        for h in (0, 1):
            fa, lo, base = self.axes(h)[0], 2 * h * q, self.base + 12 * h
            self.net.put(base + 0, self.view(h, 2, lo), self.r1.at[h, 0], fa, shifted(fa, 1))
            self.net.put(base + 1, self.view(h, 2, lo + q), self.r1.at[h, 1], fa, shifted(fa, -1))
        for h in (0, 1):
            fa, lo, base = self.axes(h)[0], 2 * h * q, self.base + 12 * h
            self.net.put(base + 2, self.view(h, 1, lo + q), self.r1.at[h, 2], fa, shifted(fa, 1))
            self.net.put(base + 3, self.view(h, -1, lo), self.r1.at[h, 3], fa, shifted(fa, -1))

    def step1(self):
        q = self.q
        for h in (0, 1):
            fa, lo, base = self.axes(h)[0], 2 * h * q, self.base + 12 * h
            self.net.got(base + 0, self.r1.at[h, 0])
            self.add(self.row(h, 1), 4, lo, [(self.r1, (h, 0))])
            self.net.put(base + 4, self.view(h, 1, lo), self.r1.at[h, 4], fa, shifted(fa, 1))
            self.net.got(base + 1, self.r1.at[h, 1])
            self.add(self.row(h, -1), 4, lo + q, [(self.r1, (h, 1))])
            self.net.put(base + 5, self.view(h, -1, lo + q), self.r1.at[h, 5], fa, shifted(fa, -1))

    def step2(self):
        q = self.q
        for h in (0, 1):
            sa, lo, base = self.axes(h)[1], 2 * h * q, self.base + 12 * h
            for k in (3, 4):
                self.net.got(base + k, self.r1.at[h, k])
            self.add(self.row(h, 0), 4, lo, [(self.r1, (h, 3)), (self.r1, (h, 4))])
            for k in (2, 5):
                self.net.got(base + k, self.r1.at[h, k])
            self.add(self.row(h, 0), 4, lo + q, [(self.r1, (h, 2)), (self.r1, (h, 5))])
            base += 6
            self.net.put(base + 0, self.one(h, 2, lo), self.r2.at[h, 0], sa, shifted(sa, 1))
            self.net.put(base + 1, self.one(h, 2, lo + q), self.r2.at[h, 1], sa, shifted(sa, -1))
            self.net.put(base + 2, self.one(h, 1, lo + q), self.r2.at[h, 2], sa, shifted(sa, 1))
            self.net.put(base + 3, self.one(h, -1, lo), self.r2.at[h, 3], sa, shifted(sa, -1))

    def step3(self):
        q = self.q
        for h in (0, 1):
            sa, lo, base = self.axes(h)[1], 2 * h * q, self.base + 12 * h + 6
            self.net.got(base + 0, self.r2.at[h, 0])
            at = self.block(h, 1)
            self.add(lambda b: at, 1, lo, [(self.r2, (h, 0))])
            self.net.put(base + 4, self.one(h, 1, lo), self.r2.at[h, 4], sa, shifted(sa, 1))
            self.net.got(base + 1, self.r2.at[h, 1])
            at2 = self.block(h, -1)
            self.add(lambda b: at2, 1, lo + q, [(self.r2, (h, 1))])
            self.net.put(base + 5, self.one(h, -1, lo + q), self.r2.at[h, 5], sa, shifted(sa, -1))

    def step4(self, out, column=None):
        q = self.q
        if column is not None:
            out = out.at[:, column, :]
        for h in (0, 1):
            lo, base = 2 * h * q, self.base + 12 * h + 6
            at = self.block(h, 0)
            for k in (3, 4):
                self.net.got(base + k, self.r2.at[h, k])
            self.add(lambda b: at, 1, lo, [(self.r2, (h, 3)), (self.r2, (h, 4))], out)
            for k in (2, 5):
                self.net.got(base + k, self.r2.at[h, k])
            self.add(lambda b: at, 1, lo + q, [(self.r2, (h, 2)), (self.r2, (h, 5))], out)


class Fold:
    def __init__(self, net, acc, rsib, zsend, zrec):
        self.net, self.acc, self.rsib, self.zsend, self.zrec = net, acc, rsib, zsend, zrec
        self.base = net.ids(20)

    def quarter(self, d):
        return 32 * lax.rem(lax.axis_index("mp") // 2 + (d + 4), 4)

    def right(self):
        return shifted("mp", 2)

    def left(self):
        return shifted("mp", -2)

    def send_columns(self, p, k, src):
        cols = pl.ds(512 * k, 512)
        self.net.put(self.base + 10 * p + k, src.at[:, cols], self.rsib.at[p, :, cols], "mp", sibling())

    def send_rows(self, p, src):
        for k, d in enumerate((2, 1, -1, 0)):
            at = rows(self.quarter(d), 32)
            self.net.put(self.base + 10 * p + k, src.at[at], self.rsib.at[p, at], "mp", sibling())

    def sent(self, p):
        for k in range(4):
            self.net.sent(self.base + 10 * p + k)

    def total(self, d, p, own, store):
        for i in (0, 1):
            at = rows(self.quarter(d) + 16 * i, 16)
            v = own[p, at].astype(F32) + self.rsib[p, at].astype(F32)
            self.acc[p, at] = v
            if store:
                self.zsend[p, at] = v.astype(BF16)

    def begin(self, p, own, by_rows):
        put, base = self.net.put, self.base + 10 * p + 4

        def arrived(k, d):
            if by_rows:
                self.net.got(base - 4 + k, self.rsib.at[p, rows(self.quarter(d), 32)])

        if not by_rows:
            for k in range(4):
                self.net.got(base - 4 + k, self.rsib.at[p, :, pl.ds(512 * k, 512)])
        arrived(0, 2)
        self.total(2, p, own, True)
        s = self.quarter(2)
        put(base + 0, self.zsend.at[p, rows(s, 16)], self.zrec.at[p, 0], "mp", self.right())
        put(base + 1, self.zsend.at[p, rows(s + 16, 16)], self.zrec.at[p, 1], "mp", self.left())
        arrived(1, 1)
        self.total(1, p, own, True)
        put(base + 2, self.zsend.at[p, rows(self.quarter(1) + 16, 16)], self.zrec.at[p, 2], "mp", self.right())
        arrived(2, -1)
        self.total(-1, p, own, True)
        put(base + 3, self.zsend.at[p, rows(self.quarter(-1), 16)], self.zrec.at[p, 3], "mp", self.left())
        arrived(3, 0)
        self.total(0, p, own, False)

    def middle(self, p):
        base = self.base + 10 * p + 4
        for k, d, off, way in ((0, 1, 0, self.right()), (1, -1, 16, self.left())):
            self.net.got(base + k, self.zrec.at[p, k])
            at = rows(self.quarter(d) + off, 16)
            self.zsend[p, at] = (self.acc[p, at] + self.zrec[p, k].astype(F32)).astype(BF16)
            self.net.put(base + 4 + k, self.zsend.at[p, at], self.zrec.at[p, 4 + k], "mp", way)

    def finish(self, p, use):
        base = self.base + 10 * p + 4
        for part, pair in ((0, (3, 4)), (1, (2, 5))):
            for k in pair:
                self.net.got(base + k, self.zrec.at[p, k])
            v = self.acc[p, rows(self.quarter(0) + 16 * part, 16)]
            for k in pair:
                v = v + self.zrec[p, k].astype(F32)
            use(p, 16 * part, v)

    def release(self):
        for k in range(20):
            if self.base + k in self.net.started:
                self.net.sent(self.base + k)


class Share:
    def __init__(self, net, out):
        self.net, self.out = net, out
        self.base = net.ids(16)

    def at(self, p, d, other=False, lo=0, n=32):
        m = lax.axis_index("mp")
        core = lax.rem(m, 2)
        if other:
            core = 1 - core
        return self.out.at[p, core, lax.rem(m // 2 + (d + 4), 4), pl.ds(lo, n)]

    def begin(self, p, src=None):
        src = self.at(p, 0) if src is None else src.at[pl.ds(32 * p, 32)]
        put, base = self.net.put, self.base + 8 * p
        put(base + 0, src, self.at(p, 0), "mp", shifted("mp", 2))
        put(base + 1, src, self.at(p, 0), "mp", shifted("mp", -2))
        put(base + 4, src, self.at(p, 0), "mp", sibling())

    def middle(self, p):
        put, base = self.net.put, self.base + 8 * p
        self.net.got(base + 0, self.at(p, -1))
        half = self.at(p, -1, False, 0, 16)
        put(base + 2, half, half, "mp", shifted("mp", 2))
        self.net.got(base + 1, self.at(p, 1))
        half = self.at(p, 1, False, 16, 16)
        put(base + 3, half, half, "mp", shifted("mp", -2))
        put(base + 5, self.at(p, -1), self.at(p, -1), "mp", sibling())
        put(base + 6, self.at(p, 1), self.at(p, 1), "mp", sibling())

    def later(self, p):
        base = self.base + 8 * p
        self.net.got(base + 2, self.at(p, 2, False, 0, 16))
        self.net.got(base + 3, self.at(p, 2, False, 16, 16))
        self.net.put(base + 7, self.at(p, 2), self.at(p, 2), "mp", sibling())

    def finish(self, p):
        for k, d in ((4, 0), (5, -1), (6, 1), (7, 2)):
            self.net.got(self.base + 8 * p + k, self.at(p, d, True))

    def release(self):
        for k in range(16):
            self.net.sent(self.base + k)


def lanes(shape):
    return lax.broadcasted_iota(jnp.int32, shape, len(shape) - 1)


def swap_halves(v):
    lane = lanes(v.shape)
    return jnp.where(lane % HD < HD // 2, pltpu.roll(v, 96, 1), pltpu.roll(v, 32, 1))


def main_kernel(
    x_hbm, cot_hbm, parents, wa_hbm, wm_hbm, we_hbm, wr_hbm, gains, table_hbm,
    y2_hbm, y4_hbm, spill, mid, dmid, gpart, o_att, o_mrg, o_exp, o_red,
    g_red, g_gate, g_up, g_mrg, g_att,
    ra_red, ra_gate, ra_up, ra_mrg, ra_att,
    rb_red, rb_gate, rb_up, rb_mrg, rb_att,
    sa, table, wa, wm, xd, cot, n1, tt, n2, hid, hid_t,
    acc, sib, rsib, zrec, probs, kv_a, kv_b, q, att, datt, dkv, dkv_low, dkv_in, dpack,
    send, recv, loc,
):
    net = Net(send, recv, send.shape[0])
    m = lax.axis_index("mp")
    core, z = lax.rem(m, 2), m // 2
    seq = lax.axis_index("seq")
    other = 1 - core
    hello(
        [("dp", shifted("dp", 1)), ("dp", shifted("dp", -1))]
        + [("seq", shifted("seq", d)) for d in (1, 2, 3)]
        + [("mp", shifted("mp", 2)), ("mp", shifted("mp", -2)), ("mp", sibling())]
    )
    kv = (kv_a, kv_b)
    base_kv, base_dkv = net.ids(6), net.ids(6)
    fold = Fold(net, acc, rsib, sib, zrec)
    share_one, share_two = Share(net, n2), Share(net, xd)
    s_red = Spread(net, g_red, ra_red, rb_red)
    s_gate = Spread(net, g_gate, ra_gate, rb_gate)
    s_up = Spread(net, g_up, ra_up, rb_up)
    s_mrg = Spread(net, g_mrg, ra_mrg, rb_mrg)
    s_att = Spread(net, g_att, ra_att, rb_att)

    def bring(k, src, dst):
        c = pltpu.make_async_copy(src, dst, loc.at[k])
        c.start()
        return c

    c_x = [bring(t, x_hbm.at[t], xd.at[t]) for t in (0, 1)]
    c_wa = bring(2, wa_hbm, wa)
    c_table = bring(9, table_hbm, table)

    def all_here(ref, k):
        pltpu.make_async_copy(ref, ref, loc.at[k]).wait()

    both_gains = gains[...].astype(F32)
    gain_one, gain_two = both_gains[0:1, :], both_gains[1:2, :]

    def ancestors(t, b):
        p1 = parents[t, b]
        p2 = jnp.where(p1 >= 0, parents[t, jnp.maximum(p1, 0)], -1)
        p3 = jnp.where(p2 >= 0, parents[t, jnp.maximum(p2, 0)], -1)
        return p1, p2, p3

    def turns(t, i):
        ps = ancestors(t, 2 * seq + i)
        depth = sum(jnp.where(p >= 0, 1, 0) for p in ps)
        return table[0, depth], table[1, depth]

    lower = lanes((128, 128)) < HD

    def own_kv(t, at):
        return kv[t].at[pl.ds(2 * at, 2)]

    for t in (0, 1):
        c_x[t].wait()
        if t == 0:
            c_wa.wait()
            c_table.wait()
        else:
            c_wm = bring(4, wm_hbm, wm)
            c_cot = bring(3, cot_hbm, cot)
            for k in range(16):
                pltpu.make_async_copy(wr_hbm.at[:, pl.ds(128 * k, 128)], g_red.at[k // 4, k % 4], loc.at[10]).start()
            for k in range(4):
                pltpu.make_async_copy(we_hbm.at[0, :, pl.ds(256 * k, 256)], sa.at[k], loc.at[11]).start()
            for k in range(16):
                pltpu.make_async_copy(we_hbm.at[1, pl.ds(128 * k, 128)], g_up.at[k // 4, k % 4], loc.at[12]).start()

        @pl.loop(0, 16, unroll=4)
        def _(i):
            v = xd[t, i // 8, (i // 2) % 4, rows(16 * (i % 2), 16)].astype(F32)
            r = lax.rsqrt(jnp.mean(v * v, axis=-1, keepdims=True) + NORM_EPS)
            n1[t, rows(16 * i, 16)] = (v * r * gain_one).astype(BF16)

        packed = dot(n1[t], wa[...])
        for i in (0, 1):
            c, s = turns(t, i)
            part = packed[128 * i : 128 * i + 128]
            for g in (0, 1):
                v = part[:, 128 * g : 128 * g + 128]
                q[t, i, g] = (v * c + swap_halves(v) * s).astype(BF16)
            v = part[:, 256:384]
            kv[t][2 * seq + i] = jnp.where(lower, v * c + swap_halves(v) * s, v).astype(BF16)
        if t == 0:
            hello_wait(8)
        for d in (1, 2, 3):
            net.put(base_kv + 3 * t + d - 1, own_kv(t, seq), own_kv(t, seq), "seq", shifted("seq", d))

    def transpose_into(src_of, dst):
        @pl.loop(0, 16, unroll=4)
        def _(j):
            cols = pl.ds(pl.multiple_of(128 * j, 128), 128)
            for t in (0, 1):
                dst[rows(128 * j, 128), 256 * t : 256 * t + 256] = src_of(t, cols).T

    transpose_into(lambda t, cols: n1[t, :, cols], tt)
    c_spill = bring(5, tt, spill)

    def hidden_grad(j):
        w = jnp.concatenate([g_red[k // 4, k % 4, 256 * j : 256 * j + 256] for k in range(16)], axis=1)
        v = dot_nt(cot[...].reshape(512, D), w)
        high = v.astype(BF16)
        low = (v - high.astype(F32)).astype(BF16)
        cols = pl.ds(256 * j, 256)
        g_gate[0, :, :, cols] = high.reshape(4, 128, 256)
        g_gate[1, :, :, cols] = low.reshape(4, 128, 256)

    low_lane = lanes((512, 128)) < HD
    key_col = lanes((128, 512))
    query_row = lax.broadcasted_iota(jnp.int32, (128, 512), 0)

    def key_views(t, ids):
        both = jnp.concatenate([kv[t][jnp.maximum(c, 0)] for c in ids], axis=0).astype(F32)
        turned = pltpu.roll(both, HD, 1)
        zero = jnp.zeros_like(both)
        keys = [jnp.where(low_lane, both, zero).astype(BF16), jnp.where(low_lane, zero, turned).astype(BF16)]
        values = [jnp.where(low_lane, turned, zero).astype(BF16), jnp.where(low_lane, zero, both).astype(BF16)]
        return keys, values

    def attention(t):
        for d in (1, 2, 3):
            net.got(base_kv + 3 * t + d - 1, own_kv(t, shifted("seq", -d)))
        for i in (0, 1):
            b = 2 * seq + i
            ps = ancestors(t, b)
            keys, values = key_views(t, (b, *ps))
            seen = (key_col < 128) & (key_col <= query_row)
            for k, p in enumerate(ps):
                inside = (key_col >= 128 * (k + 1)) & (key_col < 128 * (k + 2))
                seen = seen | (inside & (p >= 0))
            for g in (0, 1):
                total = jnp.zeros((128, 128), F32)
                for h in (0, 1):
                    scores = dot_nt(q[t, i, g], keys[h]) * HD**-0.5
                    scores = jnp.where(seen, scores, MASK_FILL)
                    e = jnp.exp(scores - jnp.max(scores, axis=-1, keepdims=True))
                    p = (e / jnp.sum(e, axis=-1, keepdims=True)).astype(BF16)
                    probs[2 * t + i, 2 * g + h] = p
                    total = total + dot(p, values[h])
                att[t, 128 * i : 128 * i + 128, 128 * g : 128 * g + 128] = total.astype(BF16)

    def merge(p):
        for k in range(4):
            cols = pl.ds(512 * k, 512)
            sib[p, :, cols] = dot(att[p, rows(128 * other, 128)], wm[:, cols]).astype(BF16)
        fold.send_rows(p, sib.at[p])
        for k in range(4):
            cols = pl.ds(512 * k, 512)
            acc[p, :, cols] = dot(att[p, rows(128 * core, 128)], wm[:, cols])

    def to_normed(p, r, v):
        x_own = xd[p, core, z, r : r + 16].astype(F32)
        total = x_own + v
        mid[p, r : r + 16] = total
        rms = lax.rsqrt(jnp.mean(total * total, axis=-1, keepdims=True) + NORM_EPS)
        n2[p, core, z, r : r + 16] = (total * rms * gain_two).astype(BF16)

    dgu = n1

    def feed_dot(p, j):
        lo = 1024 * (j % 2)
        for k, w in ((0, sa[j]), (1, g_up[:, :, :, 256 * j : 256 * j + 256].reshape(D, 256))):
            v = dot(n2[p].reshape(256, D), w)
            acc[p, :, lo + 256 * k : lo + 256 * k + 256] = v[0:128]
            acc[p, :, lo + 512 + 256 * k : lo + 768 + 256 * k] = v[128:256]

    def feed_rest(p, j):
        cols, cols_up = pl.ds(256 * j, 256), pl.ds(1024 + 256 * j, 256)
        for half in (0, 1):
            lo = 1024 * (j % 2) + 512 * half
            for i in range(4):
                at = pl.ds(32 * i, 32)
                gate, up = acc[p, at, lo : lo + 256], acc[p, at, lo + 256 : lo + 512]
                dh = g_gate[0, 2 * p + half, at, cols].astype(F32) + g_gate[1, 2 * p + half, at, cols].astype(F32)
                sig = 0.5 + 0.5 * jnp.tanh(0.5 * gate)
                act = gate * sig
                to = pl.ds(128 * half + 32 * i, 32)
                hid[p, to, cols] = (act * up).astype(BF16)
                n1[p, to, cols] = (dh * up * (sig + act * (1.0 - sig))).astype(BF16)
                n1[p, to, cols_up] = (dh * act).astype(BF16)
        hid_t[256 * j : 256 * j + 256, 256 * p : 256 * p + 256] = hid[p, :, cols].T

    def feed(p, between):
        feed_dot(p, 0)
        for j in (1, 2, 3):
            feed_dot(p, j)
            feed_rest(p, j - 1)
            if j == 1:
                between()
        feed_rest(p, 3)

    attention(0)
    c_wm.wait()
    merge(0)
    attention(1)
    fold.sent(0)
    fold.begin(0, acc, True)
    merge(1)
    c_cot.wait()
    all_here(g_red, 10)
    hidden_grad(0)
    fold.middle(0)
    fold.sent(1)
    fold.begin(1, acc, True)
    hidden_grad(1)
    fold.finish(0, to_normed)
    share_one.begin(0)
    fold.middle(1)
    hidden_grad(2)
    share_one.middle(0)
    fold.finish(1, to_normed)
    share_one.begin(1)
    hidden_grad(3)
    all_here(sa, 11)
    all_here(g_up, 12)
    share_one.later(0)
    share_one.middle(1)
    share_one.finish(0)
    feed(0, lambda: share_one.later(1))
    share_one.finish(1)
    fold.release()
    feed(1, lambda: None)

    @pl.loop(0, 8)
    def _(j):
        cols = pl.ds(pl.multiple_of(256 * j, 256), 256)
        v = dot(hid_t[...], cot[:, :, :, :, cols].reshape(512, 256))
        g_red[j // 2, 2 * (j % 2)] = v[:, 0:128].astype(BF16)
        g_red[j // 2, 2 * (j % 2) + 1] = v[:, 128:256].astype(BF16)

    s_red.step0()
    c_spill.wait()
    transpose_into(lambda t, cols: n2[t, :, :, :, cols].reshape(256, 128), tt)

    def expand_grad(dst, first):
        @pl.loop(0, 16)
        def _(k):
            a, j = k // 4, k % 4
            cols = pl.ds(pl.multiple_of(first + 256 * j, 256), 256)
            v = dot(tt[rows(512 * a, 512)], dgu[:, :, cols].reshape(512, 256))
            dst[a, :, :, pl.ds(pl.multiple_of(256 * j, 256), 256)] = v.astype(BF16).reshape(4, 128, 256)

    expand_grad(g_gate, 0)
    s_gate.step0()

    def norm_grad(p):
        for k in range(4):
            for j in (2 * k, 2 * k + 1):
                cols = pl.ds(256 * j, 256)
                w_gate = jnp.concatenate([sa[i, 256 * j : 256 * j + 256] for i in range(4)], axis=1)
                w_up = g_up[j // 2, 2 * (j % 2) : 2 * (j % 2) + 2].reshape(256, 1024)
                v = dot_nt(dgu[p], jnp.concatenate([w_gate, w_up], axis=1))
                first, second = v[0:128], v[128:256]
                sib[p, :, cols] = jnp.where(core == 0, second, first).astype(BF16)
                acc[p, :, cols] = jnp.where(core == 0, first, second)
            fold.send_columns(p, k, sib.at[p])

    def to_branch(p, r, v):
        total = mid[p, r : r + 16]
        rms = lax.rsqrt(jnp.mean(total * total, axis=-1, keepdims=True) + NORM_EPS)
        u = v * gain_two
        back_vals = rms * u - total * (rms * rms * rms) * jnp.mean(u * total, axis=-1, keepdims=True)
        full = cot[p, core, z, r : r + 16].astype(F32) + back_vals
        dmid[p, r : r + 16] = full
        xd[p, core, z, r : r + 16] = full.astype(BF16)
        gpart[0:1, :] = gpart[0:1, :] + jnp.sum(v * total * rms, axis=0, keepdims=True)

    gpart[...] = jnp.zeros_like(gpart)
    norm_grad(0)
    s_red.step1()
    fold.sent(0)
    fold.begin(0, acc, False)
    norm_grad(1)
    for k in range(8):
        half = sa.at[k // 2, pl.ds(1024 * (k % 2), 1024)]
        pltpu.make_async_copy(wr_hbm.at[:, pl.ds(256 * k, 256)], half, loc.at[13]).start()
    expand_grad(g_up, 1024)
    s_up.step0()
    c_tt = pltpu.make_async_copy(spill, tt, loc.at[6])
    c_tt.start()
    fold.middle(0)
    fold.sent(1)
    fold.begin(1, acc, False)
    s_gate.step1()
    fold.finish(0, to_branch)
    share_two.begin(0)
    fold.middle(1)

    all_here(sa, 13)

    @pl.loop(0, 8)
    def _(j):
        v = dot(hid[...].reshape(512, 1024), sa[j // 2, rows(1024 * (j % 2), 1024)])
        n1[:, :, pl.ds(pl.multiple_of(256 * j, 256), 256)] = v.astype(BF16).reshape(2, 256, 256)

    c_y2 = bring(7, n1, y2_hbm)
    fold.finish(1, to_branch)
    share_two.begin(1)
    share_two.middle(0)
    s_up.step1()
    share_two.middle(1)
    share_two.later(0)
    s_red.step2()
    share_two.finish(0)

    dbr = xd

    def branch_back(t):
        datt[t] = dot_nt(dbr[t].reshape(256, D), wm[...]).astype(BF16)

    branch_back(0)
    share_two.later(1)
    dkv[...] = jnp.zeros_like(dkv)

    def attention_back(t, i):
        u = 2 * t + i
        b = 2 * seq + i
        ps = ancestors(t, b)
        keys, values = key_views(t, (b, *ps))
        c, s = turns(t, i)
        at = rows(128 * i, 128)
        dk = [jnp.zeros((512, 128), F32), jnp.zeros((512, 128), F32)]
        dv = [jnp.zeros((512, 128), F32), jnp.zeros((512, 128), F32)]
        for g in (0, 1):
            dq = jnp.zeros((128, 128), F32)
            da = datt[t, at, 128 * g : 128 * g + 128]
            for h in (0, 1):
                p = probs[u, 2 * g + h]
                pf = p.astype(F32)
                dp = dot_nt(da, values[h])
                inner = jnp.sum(pf * dp, axis=-1, keepdims=True)
                ds = (pf * (dp - inner)).astype(BF16)
                dq = dq + dot(ds, keys[h])
                dk[h] = dk[h] + dot_tn(ds, q[t, i, g])
                dv[h] = dv[h] + dot_tn(p, da)
            dq = dq * HD**-0.5
            dpack[t, at, 128 * g : 128 * g + 128] = (dq * c - swap_halves(dq) * s).astype(BF16)
        both = jnp.where(
            low_lane, (dk[0] + pltpu.roll(dk[1], HD, 1)) * HD**-0.5, pltpu.roll(dv[0], HD, 1) + dv[1]
        )
        dkv[t, b] = dkv[t, b] + both[0:128]
        for blk in range(8):
            v = dkv[t, blk]
            for k, p in enumerate(ps):
                v = v + both[128 * (k + 1) : 128 * (k + 2)] * jnp.where(p == blk, 1.0, 0.0)
            dkv[t, blk] = v

    def send_dkv(t):
        dkv_low[t] = dkv[t].astype(BF16)
        for d in (1, 2, 3):
            peer = shifted("seq", d)
            net.put(base_dkv + 3 * t + d - 1, dkv_low.at[t, pl.ds(2 * peer, 2)], dkv_in.at[d - 1, t], "seq", peer)

    def add_dkv(t):
        for d in (1, 2, 3):
            net.got(base_dkv + 3 * t + d - 1, dkv_in.at[d - 1, t])
        for i in (0, 1):
            v = dkv[t, 2 * seq + i]
            for d in (0, 1, 2):
                v = v + dkv_in[d, t, i].astype(F32)
            c, s = turns(t, i)
            v = jnp.where(lower, v * c - swap_halves(v) * s, v)
            dpack[t, 128 * i : 128 * i + 128, 256:384] = v.astype(BF16)

    for i in (0, 1):
        attention_back(0, i)
    send_dkv(0)
    share_two.finish(1)
    branch_back(1)
    for i in (0, 1):
        attention_back(1, i)
    send_dkv(1)

    @pl.loop(0, 8)
    def _(j):
        cols = pl.ds(pl.multiple_of(256 * j, 256), 256)
        v = dot_tn(att[...].reshape(512, 256), dbr[:, :, :, :, cols].reshape(512, 256))
        g_mrg[j // 2, 2 * (j % 2)] = v[:, 0:128].astype(BF16)
        g_mrg[j // 2, 2 * (j % 2) + 1] = v[:, 128:256].astype(BF16)

    s_mrg.step0()
    s_gate.step2()
    add_dkv(0)
    add_dkv(1)
    c_tt.wait()

    @pl.loop(0, 4)
    def _(a):
        v = dot(tt[rows(512 * a, 512)], dpack[...].reshape(512, 384))
        g_att[a] = v.astype(BF16).reshape(4, 128, 384)

    s_att.step0()
    s_red.step3()
    s_mrg.step1()
    share_one.release()

    @pl.loop(0, 8)
    def _(j):
        v = dot_nt(dpack[...].reshape(512, 384), wa[rows(256 * j, 256)])
        n2[:, :, :, :, pl.ds(pl.multiple_of(256 * j, 256), 256)] = v.astype(BF16).reshape(2, 2, 4, 32, 256)

    c_y4 = bring(8, n2, y4_hbm)
    s_up.step2()
    s_gate.step3()
    s_att.step1()
    s_red.step4(o_red)
    s_mrg.step2()
    s_up.step3()
    s_att.step2()
    s_gate.step4(o_exp, 0)
    s_mrg.step3()
    s_att.step3()
    s_up.step4(o_exp, 1)
    s_mrg.step4(o_mrg)
    s_att.step4(o_att)
    c_y2.wait()
    c_y4.wait()
    net.drain()


def any_space(n):
    return [pl.BlockSpec(memory_space=pl.ANY)] * n


def main_call(x, cot, parents, wa, wm, we, wr, gains, table):
    def grads(size, cols):
        q = size // 4
        return (size, cols, q)

    kinds = [grads(1024, 128), grads(128, 1024), grads(128, 1024), grads(256, 128), grads(128, 384)]
    vm = pltpu.VMEM
    scratch = (
        [vm((4, 4, s, c), BF16) for s, c, q in kinds]
        + [vm((2, 6, 4, q, c), BF16) for s, c, q in kinds]
        + [vm((2, 6, q, c), BF16) for s, c, q in kinds]
        + [
            vm((4, 2048, 256), BF16),
            vm((2, 4, 128, 128), F32),
            vm((2048, 384), BF16),
            vm((256, 2048), BF16),
            vm((2, 2, 4, 32, D), BF16),
            vm((2, 2, 4, 32, D), BF16),
            vm((2, 256, D), BF16),
            vm((D, 512), BF16),
            vm((2, 2, 4, 32, D), BF16),
            vm((2, 256, 1024), BF16),
            vm((1024, 512), BF16),
            vm((2, 128, D), F32),
            vm((2, 128, D), BF16),
            vm((2, 128, D), BF16),
            vm((2, 6, 16, D), BF16),
            vm((4, 4, 128, 512), BF16),
            vm((8, 128, 128), BF16),
            vm((8, 128, 128), BF16),
            vm((2, 2, 2, 128, 128), BF16),
            vm((2, 256, 256), BF16),
            vm((2, 256, 256), BF16),
            vm((2, 8, 128, 128), F32),
            vm((2, 8, 128, 128), BF16),
            vm((3, 2, 2, 128, 128), BF16),
            vm((2, 256, 384), BF16),
            pltpu.SemaphoreType.DMA((192,)),
            pltpu.SemaphoreType.DMA((192,)),
            pltpu.SemaphoreType.DMA((16,)),
        ]
    )
    sds = jax.ShapeDtypeStruct
    out_shape = [
        sds((2, 256, D), BF16),
        sds((2, 2, 4, 32, D), BF16),
        sds((D, 512), BF16),
        sds((2, 32, D), F32),
        sds((2, 32, D), F32),
        sds((8, D), F32),
        sds((128, 384), F32),
        sds((256, 128), F32),
        sds((128, 2, 1024), F32),
        sds((1024, 128), F32),
    ]
    vspec = pl.BlockSpec(memory_space=pltpu.VMEM)
    hbm = pl.BlockSpec(memory_space=pl.ANY)
    return pl.pallas_call(
        main_kernel,
        out_shape=out_shape,
        in_specs=[hbm, hbm, pl.BlockSpec(memory_space=pltpu.SMEM), hbm, hbm, hbm, hbm, vspec, hbm],
        out_specs=[hbm] * 3 + [vspec] * 7,
        scratch_shapes=scratch,
        compiler_params=pltpu.CompilerParams(
            collective_id=1, has_side_effects=True, vmem_limit_bytes=64 * 2**20 - 65536
        ),
    )(x, cot, parents, wa, wm, we, wr, gains, table)


class Gather:
    def __init__(self, net, own, size, region):
        self.net, self.own, self.size, self.region = net, own, size, region
        self.base = net.ids(40)
        self.half, self.quarter = size // 2, size // 4

    def idx(self, h, da, db):
        fa, sa = (("dp", "seq"), ("seq", "dp"))[h]
        c = {fa: shifted(fa, da), sa: shifted(sa, db)}
        return c["dp"] * 4 + c["seq"]

    def both(self, k, src, dst, axis):
        self.net.put(k, src, dst, axis, shifted(axis, 1))
        self.net.put(k + 1, src, dst, axis, shifted(axis, -1))

    def begin(self):
        for stage in (0, 1):
            for h in (0, 1):
                axis = ("dp", "seq")[(h + stage) % 2]
                lo = h * self.half
                src = self.own.at[pl.ds(lo, self.half)]
                self.both(self.base + 20 * h + 4 * stage, src, self.region(self.idx(h, 0, 0), lo, self.half), axis)

    def near(self):
        for h in (0, 1):
            fa, sa = (("dp", "seq"), ("seq", "dp"))[h]
            base, lo = self.base + 20 * h, h * self.half
            for k, d in ((0, -1), (1, 1)):
                p = self.region(self.idx(h, d, 0), lo, self.half)
                self.net.got(base + k, p)
                part = self.region(self.idx(h, d, 0), lo + k * self.quarter, self.quarter)
                self.net.put(base + 2 + k, part, part, fa, shifted(fa, -d))
                self.both(base + 8 + 4 * k, p, p, sa)

    def far(self):
        for h in (0, 1):
            fa, sa = (("dp", "seq"), ("seq", "dp"))[h]
            base, lo = self.base + 20 * h, h * self.half
            at = self.idx(h, 2, 0)
            for k in (0, 1):
                self.net.got(base + 2 + k, self.region(at, lo + k * self.quarter, self.quarter))
            p = self.region(at, lo, self.half)
            self.both(base + 16, p, p, sa)

    def cross(self, k):
        d = (0, -1, 1, 2)[k]
        for h in (0, 1):
            sa = (("dp", "seq"), ("seq", "dp"))[h][1]
            base, lo = self.base + 20 * h + 4 + 4 * k, h * self.half
            for w, db in ((0, -1), (1, 1)):
                at = self.idx(h, d, db)
                self.net.got(base + w, self.region(at, lo, self.half))
                part = self.region(at, lo + w * self.quarter, self.quarter)
                self.net.put(base + 2 + w, part, part, sa, shifted(sa, -db))

    def finish(self):
        for k, d in enumerate((0, -1, 1, 2)):
            for h in (0, 1):
                base, lo = self.base + 20 * h + 4 + 4 * k, h * self.half
                at = self.idx(h, d, 2)
                for w in (0, 1):
                    self.net.got(base + 2 + w, self.region(at, lo + w * self.quarter, self.quarter))


def last_kernel(
    w_att, w_mrg, w_exp, w_red, y2, y4, mid, dmid, x_hbm, gains, gpart, mg, fg, sg,
    out, grad, f_att, f_mrg, f_exp, f_red, n_gain, m_gain, v_gain, f_gain,
    own4, own2, acc, rsib2, zs2, zrec2, rsib4, zs4, zrec4, x_own, rows2, rows4,
    gbuf, gs1, gs2, gs3, gs4, gs5, gtot, gtwo, gnew,
    send, recv, loc,
):
    net = Net(send, recv, send.shape[0])
    m = lax.axis_index("mp")
    core, z = lax.rem(m, 2), m // 2
    other = 1 - core
    dp, seq = lax.axis_index("dp"), lax.axis_index("seq")
    me = dp * 4 + seq
    peers = [("dp", shifted("dp", d)) for d in (1, 2, 3)] + [("seq", shifted("seq", d)) for d in (1, 2, 3)]
    peers += [("mp", shifted("mp", d)) for d in range(1, 8)]
    hello(peers)

    def bring(k, src, dst):
        c = pltpu.make_async_copy(src, dst, loc.at[k])
        c.start()
        return c

    by_row = lambda ref, n: (lambda i, lo, k: ref.at[rows(i * n + lo, k)])
    by_col = lambda ref: (lambda i, lo, k: ref.at[pl.ds(lo, k), pl.ds(pl.multiple_of(128 * i, 128), 128)])
    exp_at = lambda i, lo, k: f_exp.at[pl.ds(128 * i + lo, k)]
    sets = [
        Gather(net, w_exp, 128, exp_at),
        Gather(net, w_red, 1024, by_col(f_red)),
        Gather(net, w_att, 128, by_row(f_att, 128)),
        Gather(net, w_mrg, 256, by_col(f_mrg)),
    ]
    fold4, fold2 = Fold(net, acc, rsib4, zs4, zrec4), Fold(net, acc, rsib2, zs2, zrec2)
    share4, share2 = Share(net, grad), Share(net, out)
    b1, b2, b3, b4, b5 = net.ids(7), net.ids(3), net.ids(3), net.ids(3), net.ids(3)
    local = [
        bring(0, w_att, f_att.at[rows(128 * me, 128)]),
        bring(1, w_mrg, f_mrg.at[:, pl.ds(pl.multiple_of(128 * me, 128), 128)]),
        bring(2, w_exp, f_exp.at[pl.ds(128 * me, 128)]),
        bring(3, w_red, f_red.at[:, pl.ds(pl.multiple_of(128 * me, 128), 128)]),
    ]
    c_own4 = [bring(4 + p, y4.at[p, core], own4.at[p]) for p in (0, 1)]
    c_own2 = [bring(6 + p, y2.at[p, core], own2.at[p]) for p in (0, 1)]
    c_x = [bring(8 + p, x_hbm.at[p, core, z], x_own.at[p]) for p in (0, 1)]
    hello_wait(13)
    for p in (0, 1):
        fold4.send_rows(p, y4.at[p, other])
    for g in sets:
        g.begin()
    gain_one = gains[...].astype(F32)[0:1, :]
    for c in c_own4 + c_own2 + c_x:
        c.wait()
    fold4.begin(0, own4, True)
    fold4.begin(1, own4, True)
    sets[0].near()
    for p in (0, 1):
        fold2.send_rows(p, y2.at[p, other])
    fold4.middle(0)
    fold4.middle(1)
    sets[1].near()
    gbuf[...] = jnp.zeros_like(gbuf)
    gbuf[1:2, :] = gpart[0:1, :]

    def to_grad(p, r, v):
        x = x_own[p, r : r + 16].astype(F32)
        rms = lax.rsqrt(jnp.mean(x * x, axis=-1, keepdims=True) + NORM_EPS)
        u = v * gain_one
        back = rms * u - x * (rms * rms * rms) * jnp.mean(u * x, axis=-1, keepdims=True)
        rows4[32 * p + r : 32 * p + r + 16] = (dmid[p, r : r + 16] + back).astype(BF16)
        gbuf[0:1, :] = gbuf[0:1, :] + jnp.sum(v * x * rms, axis=0, keepdims=True)

    for p in (0, 1):
        fold4.finish(p, to_grad)
        share4.begin(p, rows4)
    l4 = [bring(10 + p, rows4.at[pl.ds(32 * p, 32)], grad.at[p, core, z]) for p in (0, 1)]
    gs1[m] = gbuf[...]
    for d in range(1, 8):
        net.put(b1 + d - 1, gbuf, gs1.at[m], "mp", shifted("mp", d))
    for g in sets[2:]:
        g.near()
    sets[0].far()
    fold2.begin(0, own2, True)
    fold2.begin(1, own2, True)
    fold2.middle(0)
    fold2.middle(1)
    for d in range(1, 8):
        net.got(b1 + d - 1, gs1.at[shifted("mp", -d)])
    total = gs1[0]
    for k in range(1, 8):
        total = total + gs1[k]
    gtot[...] = total
    piece = lambda i, n: pl.ds(pl.multiple_of(i * n, 128), n)
    gs2[dp] = gtot[:, piece(dp, 512)]
    for d in (1, 2, 3):
        net.put(b2 + d - 1, gtot.at[:, piece(shifted("dp", d), 512)], gs2.at[dp], "dp", shifted("dp", d))
    share4.middle(0)
    share4.middle(1)

    def to_out(p, r, v):
        rows2[32 * p + r : 32 * p + r + 16] = (mid[p, r : r + 16] + v).astype(BF16)

    for p in (0, 1):
        fold2.finish(p, to_out)
        share2.begin(p, rows2)
    l2 = [bring(12 + p, rows2.at[pl.ds(32 * p, 32)], out.at[p, core, z]) for p in (0, 1)]
    for g in sets[1:]:
        g.far()
    for d in (1, 2, 3):
        net.got(b2 + d - 1, gs2.at[shifted("dp", -d)])
    gtwo[...] = gs2[0] + gs2[1] + gs2[2] + gs2[3]
    gs3[seq] = gtwo[:, piece(seq, 128)]
    for d in (1, 2, 3):
        net.put(b3 + d - 1, gtwo.at[:, piece(shifted("seq", d), 128)], gs3.at[seq], "seq", shifted("seq", d))
    share4.later(0)
    share4.later(1)
    for g in sets:
        g.cross(0)
    for d in (1, 2, 3):
        net.got(b3 + d - 1, gs3.at[shifted("seq", -d)])
    shard = gs3[0] + gs3[1] + gs3[2] + gs3[3]
    new, mom, var = adamw(mg[...], fg[...], sg[...], shard[0:2])
    n_gain[...] = new
    m_gain[...] = mom
    v_gain[...] = var
    gnew[...] = jnp.zeros_like(gnew)
    gnew[0:2, :] = new
    gs4[seq] = gnew[...]
    for d in (1, 2, 3):
        net.put(b4 + d - 1, gnew, gs4.at[seq], "seq", shifted("seq", d))
    share2.middle(0)
    share2.middle(1)
    for g in sets:
        g.cross(1)
    for d in (1, 2, 3):
        net.got(b4 + d - 1, gs4.at[shifted("seq", -d)])
    gs5[dp] = gs4[...]
    for d in (1, 2, 3):
        net.put(b5 + d - 1, gs4, gs5.at[dp], "dp", shifted("dp", d))
    share2.later(0)
    share2.later(1)
    for k in (2, 3):
        for g in sets:
            g.cross(k)
    for d in (1, 2, 3):
        net.got(b5 + d - 1, gs5.at[shifted("dp", -d)])
    for a in range(4):
        for b in range(4):
            lo = 128 * (4 * a + b)
            f_gain[:, lo : lo + 128] = gs5[a, b, 0:2].astype(BF16)
    share4.finish(0)
    share4.finish(1)
    share2.finish(0)
    share2.finish(1)
    for g in sets:
        g.finish()
    for c in local + l4 + l2:
        c.wait()
    net.drain()


def last_call(w_att, w_mrg, w_exp, w_red, y2, y4, mid, dmid, x, gains, gpart, mg, fg, sg):
    vm, sds = pltpu.VMEM, jax.ShapeDtypeStruct
    hbm = pl.BlockSpec(memory_space=pl.ANY)
    vspec = pl.BlockSpec(memory_space=pltpu.VMEM)
    out_shape = [
        sds((2, 2, 4, 32, D), BF16),
        sds((2, 2, 4, 32, D), BF16),
        sds((D, 384), BF16),
        sds((256, D), BF16),
        sds((D, 2, 1024), BF16),
        sds((1024, D), BF16),
        sds((2, 128), F32),
        sds((2, 128), F32),
        sds((2, 128), F32),
        sds((2, D), BF16),
    ]
    scratch = [
        vm((2, 128, D), BF16),
        vm((2, 128, D), BF16),
        vm((2, 128, D), F32),
        vm((2, 128, D), BF16),
        vm((2, 128, D), BF16),
        vm((2, 6, 16, D), BF16),
        vm((2, 128, D), BF16),
        vm((2, 128, D), BF16),
        vm((2, 6, 16, D), BF16),
        vm((2, 32, D), BF16),
        vm((64, D), BF16),
        vm((64, D), BF16),
        vm((8, D), F32),
        vm((8, 8, D), F32),
        vm((4, 8, 512), F32),
        vm((4, 8, 128), F32),
        vm((4, 8, 128), F32),
        vm((4, 4, 8, 128), F32),
        vm((8, D), F32),
        vm((8, 512), F32),
        vm((8, 128), F32),
        pltpu.SemaphoreType.DMA((256,)),
        pltpu.SemaphoreType.DMA((256,)),
        pltpu.SemaphoreType.DMA((16,)),
    ]
    return pl.pallas_call(
        last_kernel,
        out_shape=out_shape,
        in_specs=[hbm] * 6 + [vspec] * 2 + [hbm] + [vspec] * 5,
        out_specs=[hbm] * 6 + [vspec] * 4,
        scratch_shapes=scratch,
        compiler_params=pltpu.CompilerParams(
            collective_id=2, has_side_effects=True, vmem_limit_bytes=32 * 2**20
        ),
    )(w_att, w_mrg, w_exp, w_red, y2, y4, mid, dmid, x, gains, gpart, mg, fg, sg)


def adam_kernel(*refs):
    ins, outs = refs[:16], refs[16:]
    for k in range(4):
        master, first, second, grad = ins[4 * k : 4 * k + 4]
        new, mom, var, low = outs[4 * k : 4 * k + 4]
        if k < 3:
            n, m, v = adamw(master[...], first[...], second[...], grad[...])
            new[...], mom[...], var[...] = n, m, v
            low[...] = n.astype(BF16)
        else:
            both = []
            for j in (0, 1):
                n, m, v = adamw(master[:, j, :], first[:, j, :], second[:, j, :], grad[:, j, :])
                new[:, j, :], mom[:, j, :], var[:, j, :] = n, m, v
                both.append(n)
            low[...] = jnp.stack(both, axis=1).astype(BF16)


def adam_call(*args):
    shapes = [args[4 * k].shape for k in range(4)]

    def spec(shape):
        block = (shape[0] // 8, *shape[1:])
        zeros = (0,) * (len(shape) - 1)
        return pl.BlockSpec(block, lambda i: (i, *zeros))

    return pl.pallas_call(
        adam_kernel,
        grid=(8,),
        in_specs=[spec(sh) for sh in shapes for _ in range(4)],
        out_specs=[spec(sh) for sh in shapes for _ in range(4)],
        out_shape=[jax.ShapeDtypeStruct(sh, t) for sh in shapes for t in (F32, F32, F32, BF16)],
        compiler_params=pltpu.CompilerParams(vmem_limit_bytes=32 * 2**20),
    )(*args)


def rotary_table():
    inv = ROPE_BASE ** (-2.0 * np.arange(HD // 2, dtype=np.float32) / HD)
    angle = np.arange(512, dtype=np.float32)[:, None] * inv.astype(np.float32)[None, :]
    c, s = np.cos(angle), np.sin(angle)
    both = np.stack([np.concatenate([c, c, c, c], 1), np.concatenate([-s, s, -s, s], 1)])
    return both.reshape(2, 4, 128, 128).astype(np.float32)


def on_device(
    inputs, cotangent, parents, weight_attend, weight_merge, weight_expand, weight_reduce, gains,
    master_attend, master_merge, master_expand, master_reduce, master_gains,
    first_attend, first_merge, first_expand, first_reduce, first_gains,
    second_attend, second_merge, second_expand, second_reduce, second_gains,
):
    x = inputs.reshape(2, 2, 4, 32, D)
    cot = cotangent.reshape(2, 2, 4, 32, D)
    we = weight_expand.transpose(1, 0, 2)
    y2, y4, _, mid, dmid, gpart, g_att, g_mrg, g_exp, g_red = main_call(
        x, cot, parents, weight_attend, weight_merge, we, weight_reduce, gains, jnp.asarray(rotary_table())
    )
    (
        n_att, m_att, v_att, w_att, n_mrg, m_mrg, v_mrg, w_mrg, n_red, m_red, v_red, w_red, n_exp, m_exp, v_exp, w_exp
    ) = adam_call(
        master_attend, first_attend, second_attend, g_att,
        master_merge, first_merge, second_merge, g_mrg,
        master_reduce, first_reduce, second_reduce, g_red,
        master_expand, first_expand, second_expand, g_exp,
    )
    out, grad, f_att, f_mrg, f_exp, f_red, n_gain, m_gain, v_gain, f_gain = last_call(
        w_att, w_mrg, w_exp, w_red,
        y2.reshape(2, 2, 128, D), y4.reshape(2, 2, 128, D), mid, dmid, x, gains, gpart, master_gains, first_gains, second_gains,
    )
    return (
        out.reshape(2, 256, D), grad.reshape(2, 256, D),
        n_att, n_mrg, n_exp, n_red, n_gain,
        m_att, m_mrg, m_exp, m_red, m_gain,
        v_att, v_mrg, v_exp, v_red, v_gain,
        f_att, f_mrg, f_exp, f_red, f_gain,
    )


def solution(mesh):
    both = ("dp", "seq")
    states = (P(both, "mp"), P("mp", both), P(both, None, "mp"), P("mp", both), P(None, both))
    weights = (P(None, "mp"), P("mp", None), P(None, None, "mp"), P("mp", None), P())
    tokens = P("dp", "seq", None)
    return jax.shard_map(
        on_device,
        mesh=mesh,
        in_specs=(tokens, tokens, P("dp", None), *weights, *states, *states, *states),
        out_specs=(tokens, tokens, *states, *states, *states, *weights),
        check_vma=False,
    )
```

```python
import functools

import jax
import jax.numpy as jnp
import numpy as np
from jax import lax
from jax.experimental import pallas as pl
from jax.experimental.pallas import tpu as pltpu
from jax.sharding import PartitionSpec as P

MESH = pl.DeviceIdType.MESH
F32 = jnp.float32
BF16 = jnp.bfloat16
D = 2048
HD = 64
STEP = 5
NORM_EPS = 1e-05
ROPE_BASE = 500000.0
MASK_FILL = -1e30
BETA_ONE = 0.5
BETA_TWO = 0.5
ADAM_EPS = 1e-08
LEARN_RATE = 0.005
DECAY_RATE = 0.1
FIX_ONE = 1.0 - BETA_ONE**STEP
FIX_TWO = 1.0 - BETA_TWO**STEP
SIZES = {"dp": 4, "seq": 4, "mp": 8}


def adamw(master, first, second, grad_vals):
    momentum = BETA_ONE * first + (1.0 - BETA_ONE) * grad_vals
    variance = BETA_TWO * second + (1.0 - BETA_TWO) * grad_vals * grad_vals
    direction = momentum / FIX_ONE / (jnp.sqrt(variance / FIX_TWO) + ADAM_EPS)
    renewed = master - LEARN_RATE * (direction + DECAY_RATE * master)
    return (renewed, momentum, variance)


def dot(a, b):
    return lax.dot_general(a, b, (((1,), (0,)), ((), ())), preferred_element_type=F32)


def dot_nt(a, b):
    return lax.dot_general(a, b, (((1,), (1,)), ((), ())), preferred_element_type=F32)


def dot_tn(a, b):
    return lax.dot_general(a, b, (((0,), (0,)), ((), ())), preferred_element_type=F32)


def shifted(axis, delta):
    n = SIZES[axis]
    return lax.rem(lax.axis_index(axis) + (delta + n), n)


def sibling():
    m = lax.axis_index("mp")
    return m + 1 - 2 * lax.rem(m, 2)


def rows(start, n):
    return pl.ds(pl.multiple_of(start, 16), n)


class Net:
    def __init__(self, send, recv, count):
        self.send, self.recv, self.count = send, recv, count
        self.used = 0
        self.started = {}

    def ids(self, n):
        first = self.used
        self.used += n
        assert self.used <= self.count
        return first

    def put(self, k, src, dst, axis, index):
        c = pltpu.make_async_remote_copy(
            src_ref=src,
            dst_ref=dst,
            send_sem=self.send.at[k],
            recv_sem=self.recv.at[k],
            device_id={axis: index},
            device_id_type=MESH,
        )
        c.start()
        self.started[k] = c

    def got(self, k, dst):
        pltpu.make_async_remote_copy(
            src_ref=dst,
            dst_ref=dst,
            send_sem=self.send.at[k],
            recv_sem=self.recv.at[k],
            device_id={"dp": shifted("dp", 1)},
            device_id_type=MESH,
        ).wait_recv()

    def sent(self, k):
        self.started.pop(k).wait_send()

    def drain(self):
        for k in sorted(self.started):
            self.started[k].wait_send()
        self.started = {}


def hello(peers):
    sem = pltpu.get_barrier_semaphore()
    for axis, index in peers:
        pl.semaphore_signal(sem, inc=1, device_id={axis: index}, device_id_type=MESH)


def hello_wait(n):
    pl.semaphore_wait(pltpu.get_barrier_semaphore(), n)


class Spread:
    def __init__(self, net, own, first, second):
        self.net, self.own, self.r1, self.r2 = net, own, first, second
        self.size, self.cols = own.shape[2], own.shape[3]
        self.q = self.size // 4
        self.base = net.ids(24)
        self.chunk = min(self.q, max(16, 16384 // self.cols))

    def axes(self, h):
        return (("dp", "seq"), ("seq", "dp"))[h]

    def row(self, h, da):
        a = shifted(self.axes(h)[0], da)
        return (lambda b: (a, b)) if h == 0 else (lambda b: (b, a))

    def block(self, h, db):
        a, b = lax.axis_index(self.axes(h)[0]), shifted(self.axes(h)[1], db)
        return (a, b) if h == 0 else (b, a)

    def view(self, h, da, lo):
        a = shifted(self.axes(h)[0], da)
        if h == 0:
            return self.own.at[a, pl.ds(0, 4), pl.ds(lo, self.q)]
        return self.own.at[pl.ds(0, 4), a, pl.ds(lo, self.q)]

    def one(self, h, db, lo):
        a, b = self.block(h, db)
        return self.own.at[a, b, pl.ds(lo, self.q)]

    def add(self, index_of, count, lo, sources, use=None):
        steps = self.q // self.chunk

        @pl.loop(0, count * steps)
        def _(k):
            b = k // steps
            r = (k % steps) * self.chunk
            at = (*index_of(b), rows(lo + r, self.chunk))
            v = self.own[at].astype(F32)
            for ref, lead in sources:
                if count > 1:
                    v = v + ref[(*lead, b, rows(r, self.chunk))].astype(F32)
                else:
                    v = v + ref[(*lead, rows(r, self.chunk))].astype(F32)
            if use is None:
                self.own[at] = v.astype(BF16)
            else:
                use(lo + r, v)

    def step0(self):
        q = self.q
        for h in (0, 1):
            fa, lo, base = self.axes(h)[0], 2 * h * q, self.base + 12 * h
            self.net.put(base + 0, self.view(h, 2, lo), self.r1.at[h, 0], fa, shifted(fa, 1))
            self.net.put(base + 1, self.view(h, 2, lo + q), self.r1.at[h, 1], fa, shifted(fa, -1))
        for h in (0, 1):
            fa, lo, base = self.axes(h)[0], 2 * h * q, self.base + 12 * h
            self.net.put(base + 2, self.view(h, 1, lo + q), self.r1.at[h, 2], fa, shifted(fa, 1))
            self.net.put(base + 3, self.view(h, -1, lo), self.r1.at[h, 3], fa, shifted(fa, -1))

    def step1(self):
        q = self.q
        for h in (0, 1):
            fa, lo, base = self.axes(h)[0], 2 * h * q, self.base + 12 * h
            self.net.got(base + 0, self.r1.at[h, 0])
            self.add(self.row(h, 1), 4, lo, [(self.r1, (h, 0))])
            self.net.put(base + 4, self.view(h, 1, lo), self.r1.at[h, 4], fa, shifted(fa, 1))
            self.net.got(base + 1, self.r1.at[h, 1])
            self.add(self.row(h, -1), 4, lo + q, [(self.r1, (h, 1))])
            self.net.put(base + 5, self.view(h, -1, lo + q), self.r1.at[h, 5], fa, shifted(fa, -1))

    def step2(self):
        q = self.q
        for h in (0, 1):
            sa, lo, base = self.axes(h)[1], 2 * h * q, self.base + 12 * h
            for k in (3, 4):
                self.net.got(base + k, self.r1.at[h, k])
            self.add(self.row(h, 0), 4, lo, [(self.r1, (h, 3)), (self.r1, (h, 4))])
            for k in (2, 5):
                self.net.got(base + k, self.r1.at[h, k])
            self.add(self.row(h, 0), 4, lo + q, [(self.r1, (h, 2)), (self.r1, (h, 5))])
            base += 6
            self.net.put(base + 0, self.one(h, 2, lo), self.r2.at[h, 0], sa, shifted(sa, 1))
            self.net.put(base + 1, self.one(h, 2, lo + q), self.r2.at[h, 1], sa, shifted(sa, -1))
            self.net.put(base + 2, self.one(h, 1, lo + q), self.r2.at[h, 2], sa, shifted(sa, 1))
            self.net.put(base + 3, self.one(h, -1, lo), self.r2.at[h, 3], sa, shifted(sa, -1))

    def step3(self):
        q = self.q
        for h in (0, 1):
            sa, lo, base = self.axes(h)[1], 2 * h * q, self.base + 12 * h + 6
            self.net.got(base + 0, self.r2.at[h, 0])
            at = self.block(h, 1)
            self.add(lambda b: at, 1, lo, [(self.r2, (h, 0))])
            self.net.put(base + 4, self.one(h, 1, lo), self.r2.at[h, 4], sa, shifted(sa, 1))
            self.net.got(base + 1, self.r2.at[h, 1])
            at2 = self.block(h, -1)
            self.add(lambda b: at2, 1, lo + q, [(self.r2, (h, 1))])
            self.net.put(base + 5, self.one(h, -1, lo + q), self.r2.at[h, 5], sa, shifted(sa, -1))

    def step4(self, h, use):
        q = self.q
        lo, base = 2 * h * q, self.base + 12 * h + 6
        at = self.block(h, 0)
        for k in (3, 4):
            self.net.got(base + k, self.r2.at[h, k])
        self.add(lambda b: at, 1, lo, [(self.r2, (h, 3)), (self.r2, (h, 4))], use)
        for k in (2, 5):
            self.net.got(base + k, self.r2.at[h, k])
        self.add(lambda b: at, 1, lo + q, [(self.r2, (h, 2)), (self.r2, (h, 5))], use)


class Fold:
    def __init__(self, net, acc, rsib, zsend, zrec):
        self.net, self.acc, self.rsib, self.zsend, self.zrec = net, acc, rsib, zsend, zrec
        self.base = net.ids(20)

    def quarter(self, d):
        return 32 * lax.rem(lax.axis_index("mp") // 2 + (d + 4), 4)

    def right(self):
        return shifted("mp", 2)

    def left(self):
        return shifted("mp", -2)

    def send_columns(self, p, k, src):
        cols = pl.ds(512 * k, 512)
        self.net.put(self.base + 10 * p + k, src.at[:, cols], self.rsib.at[p, :, cols], "mp", sibling())

    def send_rows(self, p, src):
        for k, d in enumerate((2, 1, -1, 0)):
            at = rows(self.quarter(d), 32)
            self.net.put(self.base + 10 * p + k, src(at), self.rsib.at[p, at], "mp", sibling())

    def sent(self, p):
        for k in range(4):
            self.net.sent(self.base + 10 * p + k)

    def total(self, d, p, own, store):
        for i in (0, 1):
            at = rows(self.quarter(d) + 16 * i, 16)
            v = own(p, at).astype(F32) + self.rsib[p, at].astype(F32)
            self.acc[p, at] = v
            if store:
                self.zsend[p, at] = v.astype(BF16)

    def begin(self, p, own, by_rows):
        put, base = self.net.put, self.base + 10 * p + 4

        def arrived(k, d):
            if by_rows:
                self.net.got(base - 4 + k, self.rsib.at[p, rows(self.quarter(d), 32)])

        if not by_rows:
            for k in range(4):
                self.net.got(base - 4 + k, self.rsib.at[p, :, pl.ds(512 * k, 512)])
        arrived(0, 2)
        self.total(2, p, own, True)
        s = self.quarter(2)
        put(base + 0, self.zsend.at[p, rows(s, 16)], self.zrec.at[p, 0], "mp", self.right())
        put(base + 1, self.zsend.at[p, rows(s + 16, 16)], self.zrec.at[p, 1], "mp", self.left())
        arrived(1, 1)
        self.total(1, p, own, True)
        put(base + 2, self.zsend.at[p, rows(self.quarter(1) + 16, 16)], self.zrec.at[p, 2], "mp", self.right())
        arrived(2, -1)
        self.total(-1, p, own, True)
        put(base + 3, self.zsend.at[p, rows(self.quarter(-1), 16)], self.zrec.at[p, 3], "mp", self.left())
        arrived(3, 0)
        self.total(0, p, own, False)

    def middle(self, p):
        base = self.base + 10 * p + 4
        for k, d, off, way in ((0, 1, 0, self.right()), (1, -1, 16, self.left())):
            self.net.got(base + k, self.zrec.at[p, k])
            at = rows(self.quarter(d) + off, 16)
            self.zsend[p, at] = (self.acc[p, at] + self.zrec[p, k].astype(F32)).astype(BF16)
            self.net.put(base + 4 + k, self.zsend.at[p, at], self.zrec.at[p, 4 + k], "mp", way)

    def finish(self, p, use):
        base = self.base + 10 * p + 4
        for part, pair in ((0, (3, 4)), (1, (2, 5))):
            for k in pair:
                self.net.got(base + k, self.zrec.at[p, k])
            v = self.acc[p, rows(self.quarter(0) + 16 * part, 16)]
            for k in pair:
                v = v + self.zrec[p, k].astype(F32)
            use(p, 16 * part, v)

    def release(self):
        for k in range(20):
            if self.base + k in self.net.started:
                self.net.sent(self.base + k)


class Share:
    def __init__(self, net, out):
        self.net, self.out = net, out
        self.base = net.ids(16)

    def at(self, p, d, other=False, lo=0, n=32):
        m = lax.axis_index("mp")
        core = lax.rem(m, 2)
        if other:
            core = 1 - core
        return self.out.at[p, core, lax.rem(m // 2 + (d + 4), 4), pl.ds(lo, n)]

    def begin(self, p, src=None):
        src = self.at(p, 0) if src is None else src
        put, base = self.net.put, self.base + 8 * p
        put(base + 0, src, self.at(p, 0), "mp", shifted("mp", 2))
        put(base + 1, src, self.at(p, 0), "mp", shifted("mp", -2))
        put(base + 4, src, self.at(p, 0), "mp", sibling())

    def middle(self, p):
        put, base = self.net.put, self.base + 8 * p
        self.net.got(base + 0, self.at(p, -1))
        half = self.at(p, -1, False, 0, 16)
        put(base + 2, half, half, "mp", shifted("mp", 2))
        self.net.got(base + 1, self.at(p, 1))
        half = self.at(p, 1, False, 16, 16)
        put(base + 3, half, half, "mp", shifted("mp", -2))
        put(base + 5, self.at(p, -1), self.at(p, -1), "mp", sibling())
        put(base + 6, self.at(p, 1), self.at(p, 1), "mp", sibling())

    def later(self, p):
        base = self.base + 8 * p
        self.net.got(base + 2, self.at(p, 2, False, 0, 16))
        self.net.got(base + 3, self.at(p, 2, False, 16, 16))
        self.net.put(base + 7, self.at(p, 2), self.at(p, 2), "mp", sibling())

    def finish(self, p):
        for k, d in ((4, 0), (5, -1), (6, 1), (7, 2)):
            self.net.got(self.base + 8 * p + k, self.at(p, d, True))

    def release(self):
        for k in range(16):
            self.net.sent(self.base + k)


class Gather:
    def __init__(self, net, own, size, region):
        self.net, self.own, self.size, self.region = net, own, size, region
        self.base = net.ids(40)
        self.half, self.quarter = size // 2, size // 4

    def idx(self, h, da, db):
        fa, sa = (("dp", "seq"), ("seq", "dp"))[h]
        c = {fa: shifted(fa, da), sa: shifted(sa, db)}
        return c["dp"] * 4 + c["seq"]

    def both(self, k, src, dst, axis):
        self.net.put(k, src, dst, axis, shifted(axis, 1))
        self.net.put(k + 1, src, dst, axis, shifted(axis, -1))

    def begin(self, h):
        for stage in (0, 1):
            axis = ("dp", "seq")[(h + stage) % 2]
            lo = h * self.half
            src = self.own.at[pl.ds(lo, self.half)]
            self.both(self.base + 20 * h + 4 * stage, src, self.region(self.idx(h, 0, 0), lo, self.half), axis)

    def near(self):
        for h in (0, 1):
            fa, sa = (("dp", "seq"), ("seq", "dp"))[h]
            base, lo = self.base + 20 * h, h * self.half
            for k, d in ((0, -1), (1, 1)):
                p = self.region(self.idx(h, d, 0), lo, self.half)
                self.net.got(base + k, p)
                part = self.region(self.idx(h, d, 0), lo + k * self.quarter, self.quarter)
                self.net.put(base + 2 + k, part, part, fa, shifted(fa, -d))
                self.both(base + 8 + 4 * k, p, p, sa)

    def far(self):
        for h in (0, 1):
            fa, sa = (("dp", "seq"), ("seq", "dp"))[h]
            base, lo = self.base + 20 * h, h * self.half
            at = self.idx(h, 2, 0)
            for k in (0, 1):
                self.net.got(base + 2 + k, self.region(at, lo + k * self.quarter, self.quarter))
            p = self.region(at, lo, self.half)
            self.both(base + 16, p, p, sa)

    def cross(self, k):
        d = (0, -1, 1, 2)[k]
        for h in (0, 1):
            sa = (("dp", "seq"), ("seq", "dp"))[h][1]
            base, lo = self.base + 20 * h + 4 + 4 * k, h * self.half
            for w, db in ((0, -1), (1, 1)):
                at = self.idx(h, d, db)
                self.net.got(base + w, self.region(at, lo, self.half))
                part = self.region(at, lo + w * self.quarter, self.quarter)
                self.net.put(base + 2 + w, part, part, sa, shifted(sa, -db))

    def finish(self):
        for k, d in enumerate((0, -1, 1, 2)):
            for h in (0, 1):
                base, lo = self.base + 20 * h + 4 + 4 * k, h * self.half
                at = self.idx(h, d, 2)
                for w in (0, 1):
                    self.net.got(base + 2 + w, self.region(at, lo + w * self.quarter, self.quarter))


def lanes(shape):
    return lax.broadcasted_iota(jnp.int32, shape, len(shape) - 1)


def swap_halves(v):
    lane = lanes(v.shape)
    return jnp.where(lane % HD < HD // 2, pltpu.roll(v, 96, 1), pltpu.roll(v, 32, 1))


def main_kernel(
    x_hbm, cot_hbm, parents, wa_hbm, wm_hbm, we_hbm, wr_hbm, gains, table_hbm,
    i_att, i_mrg, i_exp, i_red, mg, fg, sg,
    out, grad, o_att, o_mrg, o_exp, o_red, f_att, f_mrg, f_exp, f_red,
    n_gain, m_gain, v_gain, f_gain,
    g_red, g_gate, g_up, g_mrg, g_att,
    ra_red, ra_gate, ra_up, ra_mrg, ra_att,
    rb_red, rb_gate, rb_up, rb_mrg, rb_att,
    sa, table, wa, wm, xd, cot, n1, dgu, n2, hid,
    acc, sib, rsib, zrec, probs, kv_a, kv_b, q, att, datt, dkv, dkv_in, dpack,
    mid, dmid, stage, stage_exp, w_exp,
    gbuf, gs1, gs2, gs3, gs4, gs5, gtot, gtwo, gnew,
    send, recv, loc,
):
    net = Net(send, recv, send.shape[0])
    m = lax.axis_index("mp")
    core, z = lax.rem(m, 2), m // 2
    seq = lax.axis_index("seq")
    other = 1 - core
    dp = lax.axis_index("dp")
    me = 4 * dp + seq
    hello(
        [("dp", shifted("dp", d)) for d in (1, 2, 3)]
        + [("seq", shifted("seq", d)) for d in (1, 2, 3)]
        + [("mp", shifted("mp", d)) for d in range(1, 8)]
    )
    kv = (kv_a, kv_b)
    base_kv, base_dkv = net.ids(6), net.ids(6)
    fold = Fold(net, acc, rsib, sib, zrec)
    share_one, share_two, share_out, share_grad = Share(net, n2), Share(net, xd), Share(net, out), Share(net, grad)
    b1, b2, b3, b4, b5 = net.ids(7), net.ids(3), net.ids(3), net.ids(3), net.ids(3)

    def by_col(ref):
        return lambda i, lo, k: ref.at[pl.ds(lo, k), pl.ds(pl.multiple_of(128 * i, 128), 128)]

    all_red = Gather(net, g_red.at[dp, seq], 1024, by_col(f_red))
    all_exp = Gather(net, w_exp, 128, lambda i, lo, k: f_exp.at[pl.ds(128 * i + lo, k)])
    all_mrg = Gather(net, g_mrg.at[dp, seq], 256, by_col(f_mrg))
    all_att = Gather(net, g_att.at[dp, seq], 128, lambda i, lo, k: f_att.at[rows(128 * i + lo, k)])
    s_red = Spread(net, g_red, ra_red, rb_red)
    s_gate = Spread(net, g_gate, ra_gate, rb_gate)
    s_up = Spread(net, g_up, ra_up, rb_up)
    s_mrg = Spread(net, g_mrg, ra_mrg, rb_mrg)
    s_att = Spread(net, g_att, ra_att, rb_att)

    def bring(k, src, dst):
        c = pltpu.make_async_copy(src, dst, loc.at[k])
        c.start()
        return c

    c_x = [bring(t, x_hbm.at[t], xd.at[t]) for t in (0, 1)]
    c_wa = bring(2, wa_hbm, wa)
    c_table = bring(9, table_hbm, table)

    def all_here(ref, k):
        pltpu.make_async_copy(ref, ref, loc.at[k]).wait()

    both_gains = gains[...].astype(F32)
    gain_one, gain_two = both_gains[0:1, :], both_gains[1:2, :]

    def ancestors(t, b):
        p1 = parents[t, b]
        p2 = jnp.where(p1 >= 0, parents[t, jnp.maximum(p1, 0)], -1)
        p3 = jnp.where(p2 >= 0, parents[t, jnp.maximum(p2, 0)], -1)
        return p1, p2, p3

    def turns(t, i):
        ps = ancestors(t, 2 * seq + i)
        depth = sum(jnp.where(p >= 0, 1, 0) for p in ps)
        return table[0, depth], table[1, depth]

    lower = lanes((128, 128)) < HD

    def own_kv(t, at):
        return kv[t].at[pl.ds(2 * at, 2)]

    for t in (0, 1):
        c_x[t].wait()
        if t == 0:
            c_wa.wait()
            c_table.wait()
        else:
            c_wm = bring(4, wm_hbm, wm)
            c_cot = bring(3, cot_hbm, cot)
            for k in range(16):
                pltpu.make_async_copy(wr_hbm.at[:, pl.ds(128 * k, 128)], g_red.at[k // 4, k % 4], loc.at[10]).start()
            for k in range(4):
                pltpu.make_async_copy(we_hbm.at[0, :, pl.ds(256 * k, 256)], sa.at[k], loc.at[11]).start()
            for k in range(16):
                pltpu.make_async_copy(we_hbm.at[1, pl.ds(128 * k, 128)], g_up.at[k // 4, k % 4], loc.at[12]).start()

        @pl.loop(0, 16, unroll=4)
        def _(i):
            v = xd[t, i // 8, (i // 2) % 4, rows(16 * (i % 2), 16)].astype(F32)
            r = lax.rsqrt(jnp.mean(v * v, axis=-1, keepdims=True) + NORM_EPS)
            n1[t, rows(16 * i, 16)] = (v * r * gain_one).astype(BF16)

        packed = dot(n1[t], wa[...])
        for i in (0, 1):
            c, s = turns(t, i)
            part = packed[128 * i : 128 * i + 128]
            for g in (0, 1):
                v = part[:, 128 * g : 128 * g + 128]
                q[t, i, g] = (v * c + swap_halves(v) * s).astype(BF16)
            v = part[:, 256:384]
            kv[t][2 * seq + i] = jnp.where(lower, v * c + swap_halves(v) * s, v).astype(BF16)
        if t == 0:
            hello_wait(13)
        for d in (1, 2, 3):
            net.put(base_kv + 3 * t + d - 1, own_kv(t, seq), own_kv(t, seq), "seq", shifted("seq", d))

    def hidden_grad(j):
        w = jnp.concatenate([g_red[k // 4, k % 4, 256 * j : 256 * j + 256] for k in range(16)], axis=1)
        v = dot_nt(cot[...].reshape(512, D), w)
        high = v.astype(BF16)
        low = (v - high.astype(F32)).astype(BF16)
        cols = pl.ds(256 * j, 256)
        g_gate[0, :, :, cols] = high.reshape(4, 128, 256)
        g_gate[1, :, :, cols] = low.reshape(4, 128, 256)

    low_lane = lanes((512, 128)) < HD
    key_col = lanes((128, 512))
    query_row = lax.broadcasted_iota(jnp.int32, (128, 512), 0)

    def key_views(t, ids):
        both = jnp.concatenate([kv[t][jnp.maximum(c, 0)] for c in ids], axis=0).astype(F32)
        turned = pltpu.roll(both, HD, 1)
        zero = jnp.zeros_like(both)
        keys = [jnp.where(low_lane, both, zero).astype(BF16), jnp.where(low_lane, zero, turned).astype(BF16)]
        values = [jnp.where(low_lane, turned, zero).astype(BF16), jnp.where(low_lane, zero, both).astype(BF16)]
        return keys, values

    def attention(t):
        for d in (1, 2, 3):
            net.got(base_kv + 3 * t + d - 1, own_kv(t, shifted("seq", -d)))
        for i in (0, 1):
            b = 2 * seq + i
            ps = ancestors(t, b)
            keys, values = key_views(t, (b, *ps))
            seen = (key_col < 128) & (key_col <= query_row)
            for k, p in enumerate(ps):
                inside = (key_col >= 128 * (k + 1)) & (key_col < 128 * (k + 2))
                seen = seen | (inside & (p >= 0))
            for g in (0, 1):
                total = jnp.zeros((128, 128), F32)
                for h in (0, 1):
                    scores = dot_nt(q[t, i, g], keys[h]) * HD**-0.5
                    scores = jnp.where(seen, scores, MASK_FILL)
                    e = jnp.exp(scores - jnp.max(scores, axis=-1, keepdims=True))
                    p = (e / jnp.sum(e, axis=-1, keepdims=True)).astype(BF16)
                    probs[2 * t + i, 2 * g + h] = p
                    total = total + dot(p, values[h])
                att[t, 128 * i : 128 * i + 128, 128 * g : 128 * g + 128] = total.astype(BF16)

    def mine(p, at):
        return acc[p, at]

    def merge(p):
        for k in range(4):
            cols = pl.ds(512 * k, 512)
            sib[p, :, cols] = dot(att[p, rows(128 * other, 128)], wm[:, cols]).astype(BF16)
        fold.send_rows(p, lambda at: sib.at[p, at])
        for k in range(4):
            cols = pl.ds(512 * k, 512)
            acc[p, :, cols] = dot(att[p, rows(128 * core, 128)], wm[:, cols])

    def to_normed(p, r, v):
        x_own = xd[p, core, z, r : r + 16].astype(F32)
        total = x_own + v
        mid[p, r : r + 16] = total
        rms = lax.rsqrt(jnp.mean(total * total, axis=-1, keepdims=True) + NORM_EPS)
        n2[p, core, z, r : r + 16] = (total * rms * gain_two).astype(BF16)


    def feed_dot(p, j):
        lo = 1024 * (j % 2)
        for k, w in ((0, sa[j]), (1, g_up[:, :, :, 256 * j : 256 * j + 256].reshape(D, 256))):
            v = dot(n2[p].reshape(256, D), w)
            acc[p, :, lo + 256 * k : lo + 256 * k + 256] = v[0:128]
            acc[p, :, lo + 512 + 256 * k : lo + 768 + 256 * k] = v[128:256]

    def feed_rest(p, j):
        cols, cols_up = pl.ds(256 * j, 256), pl.ds(1024 + 256 * j, 256)
        for half in (0, 1):
            lo = 1024 * (j % 2) + 512 * half
            for i in range(4):
                at = pl.ds(32 * i, 32)
                gate, up = acc[p, at, lo : lo + 256], acc[p, at, lo + 256 : lo + 512]
                dh = g_gate[0, 2 * p + half, at, cols].astype(F32) + g_gate[1, 2 * p + half, at, cols].astype(F32)
                sig = 0.5 + 0.5 * jnp.tanh(0.5 * gate)
                act = gate * sig
                to = pl.ds(128 * half + 32 * i, 32)
                hid[p, to, cols] = (act * up).astype(BF16)
                dgu[p, to, cols] = (dh * up * (sig + act * (1.0 - sig))).astype(BF16)
                dgu[p, to, cols_up] = (dh * act).astype(BF16)

    def feed(p, between):
        feed_dot(p, 0)
        for j in (1, 2, 3):
            feed_dot(p, j)
            feed_rest(p, j - 1)
            if j == 1:
                between()
        feed_rest(p, 3)

    attention(0)
    c_wm.wait()
    merge(0)
    attention(1)
    fold.sent(0)
    fold.begin(0, mine, True)
    merge(1)
    c_cot.wait()
    all_here(g_red, 10)
    hidden_grad(0)
    fold.middle(0)
    fold.sent(1)
    fold.begin(1, mine, True)
    hidden_grad(1)
    fold.finish(0, to_normed)
    share_one.begin(0)
    fold.middle(1)
    hidden_grad(2)
    share_one.middle(0)
    fold.finish(1, to_normed)
    share_one.begin(1)
    hidden_grad(3)
    all_here(sa, 11)
    all_here(g_up, 12)
    share_one.later(0)
    share_one.middle(1)
    share_one.finish(0)
    feed(0, lambda: share_one.later(1))
    share_one.finish(1)
    fold.release()
    feed(1, lambda: None)

    @pl.loop(0, 8)
    def _(j):
        cols = pl.ds(pl.multiple_of(256 * j, 256), 256)
        v = dot_tn(hid[...].reshape(512, 1024), cot[:, :, :, :, cols].reshape(512, 256))
        g_red[j // 2, 2 * (j % 2)] = v[:, 0:128].astype(BF16)
        g_red[j // 2, 2 * (j % 2) + 1] = v[:, 128:256].astype(BF16)

    s_red.step0()
    def expand_grad(dst, first):
        @pl.loop(0, 8)
        def _(k):
            a, j = k // 2, k % 2
            cols = pl.ds(pl.multiple_of(first + 512 * j, 512), 512)
            left = n2[:, :, :, :, pl.ds(pl.multiple_of(512 * a, 512), 512)].reshape(512, 512)
            v = dot_tn(left, dgu[:, :, cols].reshape(512, 512))
            dst[a, :, :, pl.ds(pl.multiple_of(512 * j, 512), 512)] = v.astype(BF16).reshape(4, 128, 512)

    expand_grad(g_gate, 0)
    s_gate.step0()

    def norm_grad(p):
        for k in range(4):
            for j in (2 * k, 2 * k + 1):
                cols = pl.ds(256 * j, 256)
                w_gate = jnp.concatenate([sa[i, 256 * j : 256 * j + 256] for i in range(4)], axis=1)
                w_up = g_up[j // 2, 2 * (j % 2) : 2 * (j % 2) + 2].reshape(256, 1024)
                v = dot_nt(dgu[p], jnp.concatenate([w_gate, w_up], axis=1))
                first, second = v[0:128], v[128:256]
                sib[p, :, cols] = jnp.where(core == 0, second, first).astype(BF16)
                acc[p, :, cols] = jnp.where(core == 0, first, second)
            fold.send_columns(p, k, sib.at[p])

    def to_branch(p, r, v):
        total = mid[p, r : r + 16]
        rms = lax.rsqrt(jnp.mean(total * total, axis=-1, keepdims=True) + NORM_EPS)
        u = v * gain_two
        back_vals = rms * u - total * (rms * rms * rms) * jnp.mean(u * total, axis=-1, keepdims=True)
        full = cot[p, core, z, r : r + 16].astype(F32) + back_vals
        dmid[p, r : r + 16] = full
        xd[p, core, z, r : r + 16] = full.astype(BF16)
        gbuf[1:2, :] = gbuf[1:2, :] + jnp.sum(v * total * rms, axis=0, keepdims=True)

    gbuf[...] = jnp.zeros_like(gbuf)
    norm_grad(0)
    s_red.step1()
    fold.sent(0)
    fold.begin(0, mine, False)
    norm_grad(1)
    for k in range(8):
        half = sa.at[k // 2, pl.ds(1024 * (k % 2), 1024)]
        pltpu.make_async_copy(wr_hbm.at[:, pl.ds(256 * k, 256)], half, loc.at[13]).start()
    expand_grad(g_up, 1024)
    s_up.step0()
    fold.middle(0)
    fold.sent(1)
    fold.begin(1, mine, False)
    s_gate.step1()
    fold.finish(0, to_branch)
    share_two.begin(0)
    fold.middle(1)

    all_here(sa, 13)

    @pl.loop(0, 8)
    def _(j):
        v = dot(hid[...].reshape(512, 1024), sa[j // 2, rows(1024 * (j % 2), 1024)])
        dgu[:, :, pl.ds(pl.multiple_of(256 * j, 256), 256)] = v.astype(BF16).reshape(2, 256, 256)

    fold.finish(1, to_branch)
    share_two.begin(1)

    x_slot = lax.rem(z + 1, 4)
    c_xo = [bring(p, x_hbm.at[p, core, z], cot.at[p, core, x_slot]) for p in (0, 1)]
    for k in (0, 1, 2):
        pltpu.make_async_copy(i_exp[k], stage_exp.at[k], loc.at[10]).start()
        pltpu.make_async_copy(i_red[k].at[pl.ds(0, 512)], stage.at[k], loc.at[11]).start()
    share_two.middle(0)
    share_two.middle(1)
    share_two.later(0)
    s_red.step2()
    share_two.finish(0)

    dbr = xd

    def branch_back(t):
        datt[t] = dot_nt(dbr[t].reshape(256, D), wm[...]).astype(BF16)

    branch_back(0)
    share_two.later(1)
    dkv[...] = jnp.zeros_like(dkv)

    def attention_back(t, i):
        u = 2 * t + i
        b = 2 * seq + i
        ps = ancestors(t, b)
        keys, values = key_views(t, (b, *ps))
        c, s = turns(t, i)
        at = rows(128 * i, 128)
        dk = [jnp.zeros((512, 128), F32), jnp.zeros((512, 128), F32)]
        dv = [jnp.zeros((512, 128), F32), jnp.zeros((512, 128), F32)]
        for g in (0, 1):
            dq = jnp.zeros((128, 128), F32)
            da = datt[t, at, 128 * g : 128 * g + 128]
            for h in (0, 1):
                p = probs[u, 2 * g + h]
                pf = p.astype(F32)
                dp = dot_nt(da, values[h])
                inner = jnp.sum(pf * dp, axis=-1, keepdims=True)
                ds = (pf * (dp - inner)).astype(BF16)
                dq = dq + dot(ds, keys[h])
                dk[h] = dk[h] + dot_tn(ds, q[t, i, g])
                dv[h] = dv[h] + dot_tn(p, da)
            dq = dq * HD**-0.5
            dpack[t, at, 128 * g : 128 * g + 128] = (dq * c - swap_halves(dq) * s).astype(BF16)
        both = jnp.where(
            low_lane, (dk[0] + pltpu.roll(dk[1], HD, 1)) * HD**-0.5, pltpu.roll(dv[0], HD, 1) + dv[1]
        )
        dkv[t, b] = dkv[t, b] + both[0:128]
        for blk in range(8):
            v = dkv[t, blk]
            for k, p in enumerate(ps):
                v = v + both[128 * (k + 1) : 128 * (k + 2)] * jnp.where(p == blk, 1.0, 0.0)
            dkv[t, blk] = v

    def send_dkv(t):
        for c in range(8):
            probs[2 * t, c // 4, :, 128 * (c % 4) : 128 * (c % 4) + 128] = dkv[t, c].astype(BF16)
        for d in (1, 2, 3):
            peer = shifted("seq", d)
            src = probs.at[2 * t, peer // 2, :, pl.ds(pl.multiple_of(256 * lax.rem(peer, 2), 256), 256)]
            net.put(base_dkv + 3 * t + d - 1, src, dkv_in.at[d - 1, t], "seq", peer)

    def add_dkv(t):
        for d in (1, 2, 3):
            net.got(base_dkv + 3 * t + d - 1, dkv_in.at[d - 1, t])
        for i in (0, 1):
            v = dkv[t, 2 * seq + i]
            for d in (0, 1, 2):
                v = v + dkv_in[d, t, :, 128 * i : 128 * i + 128].astype(F32)
            c, s = turns(t, i)
            v = jnp.where(lower, v * c - swap_halves(v) * s, v)
            dpack[t, 128 * i : 128 * i + 128, 256:384] = v.astype(BF16)

    for i in (0, 1):
        attention_back(0, i)
    send_dkv(0)
    share_two.finish(1)
    fold.release()

    def down_rows(p, at):
        return dgu[p, pl.ds(pl.multiple_of(128 * core + at.start, 16), 16)]

    for p in (0, 1):
        fold.send_rows(p, lambda at: dgu.at[p, rows(128 * other + at.start, 32)])
    branch_back(1)
    for i in (0, 1):
        attention_back(1, i)
    send_dkv(1)
    s_up.step1()

    @pl.loop(0, 8)
    def _(j):
        cols = pl.ds(pl.multiple_of(256 * j, 256), 256)
        v = dot_tn(att[...].reshape(512, 256), dbr[:, :, :, :, cols].reshape(512, 256))
        g_mrg[j // 2, 2 * (j % 2)] = v[:, 0:128].astype(BF16)
        g_mrg[j // 2, 2 * (j % 2) + 1] = v[:, 128:256].astype(BF16)

    s_mrg.step0()
    fold.begin(0, down_rows, True)
    fold.begin(1, down_rows, True)
    s_gate.step2()
    add_dkv(0)
    add_dkv(1)

    @pl.loop(0, 4)
    def _(a):
        left = n1[:, :, pl.ds(pl.multiple_of(512 * a, 512), 512)].reshape(512, 512)
        g_att[a] = dot_tn(left, dpack[...].reshape(512, 384)).astype(BF16).reshape(4, 128, 384)

    s_att.step0()
    fold.middle(0)
    fold.middle(1)
    s_red.step3()
    for k in (0, 1, 2):
        pltpu.make_async_copy(i_mrg[k], dkv.at[0, pl.ds(2 * k, 2)], loc.at[12]).start()
    share_one.release()

    @pl.loop(0, 8)
    def _(j):
        v = dot_nt(dpack[...].reshape(512, 384), wa[rows(256 * j, 256)])
        n2[:, :, :, :, pl.ds(pl.multiple_of(256 * j, 256), 256)] = v.astype(BF16).reshape(2, 2, 4, 32, 256)

    def to_out(p, r, v):
        cot[p, core, z, r : r + 16] = (mid[p, r : r + 16] + v).astype(BF16)

    l_out = []
    for p in (0, 1):
        fold.finish(p, to_out)
        share_out.begin(p, cot.at[p, core, z])
        l_out.append(bring(2 + p, cot.at[p, core, z], out.at[p, core, z]))
    s_mrg.step1()

    def out_of(k, src, dst):
        return [bring(k + i, src(i), dst[i]) for i in (0, 1, 2)]

    def renew(state, at, grads):
        new, mom, var = adamw(state[0][at], state[1][at], state[2][at], grads)
        state[0][at], state[1][at], state[2][at] = new, mom, var
        return new

    flat_stage = [stage.at[k] for k in (0, 1, 2)]

    def use_red(h):
        def use(r, v):
            new = renew(flat_stage, rows(r - 512 * h, 128), v)
            g_red[dp, seq, rows(r, 128)] = new.astype(BF16)

        return use

    all_here(stage, 11)
    s_red.step4(0, use_red(0))
    all_red.begin(0)
    c_red = out_of(4, lambda i: stage.at[i], [o.at[pl.ds(0, 512)] for o in o_red])
    local = [bring(14, g_red.at[dp, seq, pl.ds(0, 512)], f_red.at[pl.ds(0, 512), pl.ds(pl.multiple_of(128 * me, 128), 128)])]
    s_up.step2()
    share_out.middle(0)
    share_out.middle(1)
    s_att.step1()
    s_gate.step3()
    for c in c_red:
        c.wait()
    for k in (0, 1, 2):
        pltpu.make_async_copy(i_red[k].at[pl.ds(512, 512)], stage.at[k], loc.at[11]).start()
    share_out.later(0)
    share_out.later(1)
    s_mrg.step2()
    all_here(stage, 11)
    s_red.step4(1, use_red(1))
    all_red.begin(1)
    c_red = out_of(4, lambda i: stage.at[i], [o.at[pl.ds(512, 512)] for o in o_red])
    local.append(bring(15, g_red.at[dp, seq, pl.ds(512, 512)], f_red.at[pl.ds(512, 512), pl.ds(pl.multiple_of(128 * me, 128), 128)]))
    share_out.finish(0)
    share_out.finish(1)
    fold.release()
    for p in (0, 1):
        fold.send_rows(p, lambda at: n2.at[p, other, at.start // 32])
    s_up.step3()
    s_att.step2()

    def use_gate(r, v):
        at = rows(r, 16)
        new, mom, var = adamw(stage_exp[0, at, 0, :], stage_exp[1, at, 0, :], stage_exp[2, at, 0, :], v)
        stage_exp[0, at, 0, :], stage_exp[1, at, 0, :], stage_exp[2, at, 0, :] = new, mom, var

    def use_up(r, v):
        at = rows(r, 16)
        new, mom, var = adamw(stage_exp[0, at, 1, :], stage_exp[1, at, 1, :], stage_exp[2, at, 1, :], v)
        stage_exp[0, at, 1, :], stage_exp[1, at, 1, :], stage_exp[2, at, 1, :] = new, mom, var

    all_here(stage_exp, 10)
    s_gate.step4(0, use_gate)
    s_gate.step4(1, use_gate)
    for c in c_red:
        c.wait()
    for k in (0, 1, 2):
        for a in (0, 1, 2):
            pltpu.make_async_copy(
                i_att[k].at[:, pl.ds(128 * a, 128)], stage.at[k, pl.ds(128 * a, 128)], loc.at[11]
            ).start()

    def norm_rows(p, at):
        return n2[p, core, at.start // 32, pl.ds(pl.multiple_of(at.start % 32, 16), 16)]

    def fold_begin(p):
        fold.begin(p, norm_rows, True)

    fold_begin(0)
    fold_begin(1)
    all_red.near()
    s_mrg.step3()
    s_att.step3()
    fold.middle(0)
    fold.middle(1)
    for h in (0, 1):
        s_up.step4(h, use_up)
        for i in (0, 1, 2, 3):
            at = rows(64 * h + 16 * i, 16)
            w_exp[at] = stage_exp[0, at].astype(BF16)
        all_exp.begin(h)
    c_exp = out_of(6, lambda i: stage_exp.at[i], o_exp)
    local.append(bring(9, w_exp, f_exp.at[pl.ds(128 * me, 128)]))
    for c in c_xo:
        c.wait()

    def to_grad(p, r, v):
        x = cot[p, core, x_slot, r : r + 16].astype(F32)
        rms = lax.rsqrt(jnp.mean(x * x, axis=-1, keepdims=True) + NORM_EPS)
        u = v * gain_one
        back_vals = rms * u - x * (rms * rms * rms) * jnp.mean(u * x, axis=-1, keepdims=True)
        cot[p, other, z, r : r + 16] = (dmid[p, r : r + 16] + back_vals).astype(BF16)
        gbuf[0:1, :] = gbuf[0:1, :] + jnp.sum(v * x * rms, axis=0, keepdims=True)

    for p in (0, 1):
        fold.finish(p, to_grad)
        share_grad.begin(p, cot.at[p, other, z])
    l_grad = [bring(p, cot.at[p, other, z], grad.at[p, core, z]) for p in (0, 1)]
    gs1[m] = gbuf[...]
    for d in range(1, 8):
        net.put(b1 + d - 1, gbuf, gs1.at[m], "mp", shifted("mp", d))

    def use_mrg(r, v):
        new = renew([dkv.at[0, 2 * k + r // 128] for k in (0, 1, 2)], rows(r % 128, 64), v)
        g_mrg[dp, seq, rows(r, 64)] = new.astype(BF16)

    all_here(dkv.at[0, pl.ds(0, 6)], 12)
    for h in (0, 1):
        s_mrg.step4(h, use_mrg)
        all_mrg.begin(h)
    c_mrg = [bring(16 + i, dkv.at[0, pl.ds(2 * i, 2)], o_mrg[i]) for i in (0, 1, 2)]
    local.append(bring(19, g_mrg.at[dp, seq], f_mrg.at[:, pl.ds(pl.multiple_of(128 * me, 128), 128)]))
    all_here(stage.at[:, pl.ds(0, 384)], 11)

    def use_att(r, v):
        parts = []
        for a in (0, 1, 2):
            parts.append(renew(flat_stage, rows(128 * a + r, 32), v[:, 128 * a : 128 * a + 128]))
        g_att[dp, seq, rows(r, 32)] = jnp.concatenate(parts, axis=1).astype(BF16)

    for h in (0, 1):
        s_att.step4(h, use_att)
        all_att.begin(h)
    c_att = []
    for k in (0, 1, 2):
        for a in (0, 1, 2):
            c_att.append(bring(20 + 3 * k + a, stage.at[k, pl.ds(128 * a, 128)], o_att[k].at[:, pl.ds(128 * a, 128)]))
    local.append(bring(29, g_att.at[dp, seq], f_att.at[rows(128 * me, 128)]))
    all_red.far()
    share_grad.middle(0)
    share_grad.middle(1)
    all_exp.near()
    for d in range(1, 8):
        net.got(b1 + d - 1, gs1.at[shifted("mp", -d)])
    total = gs1[0]
    for k in range(1, 8):
        total = total + gs1[k]
    gtot[...] = total

    def piece(i, n):
        return pl.ds(pl.multiple_of(i * n, 128), n)

    gs2[dp] = gtot[:, piece(dp, 512)]
    for d in (1, 2, 3):
        net.put(b2 + d - 1, gtot.at[:, piece(shifted("dp", d), 512)], gs2.at[dp], "dp", shifted("dp", d))
    all_red.cross(0)
    all_mrg.near()
    all_att.near()
    share_grad.later(0)
    share_grad.later(1)
    all_red.cross(1)
    all_exp.far()
    for d in (1, 2, 3):
        net.got(b2 + d - 1, gs2.at[shifted("dp", -d)])
    gtwo[...] = gs2[0] + gs2[1] + gs2[2] + gs2[3]
    gs3[seq] = gtwo[:, piece(seq, 128)]
    for d in (1, 2, 3):
        net.put(b3 + d - 1, gtwo.at[:, piece(shifted("seq", d), 128)], gs3.at[seq], "seq", shifted("seq", d))
    all_red.cross(2)
    all_mrg.far()
    all_att.far()
    all_exp.cross(0)
    for d in (1, 2, 3):
        net.got(b3 + d - 1, gs3.at[shifted("seq", -d)])
    shard = gs3[0] + gs3[1] + gs3[2] + gs3[3]
    new, mom, var = adamw(mg[...], fg[...], sg[...], shard)
    n_gain[...] = new
    m_gain[...] = mom
    v_gain[...] = var
    gnew[...] = new
    gs4[seq] = new
    for d in (1, 2, 3):
        net.put(b4 + d - 1, gnew, gs4.at[seq], "seq", shifted("seq", d))
    all_red.cross(3)
    all_exp.cross(1)
    all_mrg.cross(0)
    all_att.cross(0)
    for d in (1, 2, 3):
        net.got(b4 + d - 1, gs4.at[shifted("seq", -d)])
    gs5[dp] = gs4[...]
    for d in (1, 2, 3):
        net.put(b5 + d - 1, gs4, gs5.at[dp], "dp", shifted("dp", d))
    all_mrg.cross(1)
    all_att.cross(1)
    all_exp.cross(2)
    all_mrg.cross(2)
    all_att.cross(2)
    all_exp.cross(3)
    all_mrg.cross(3)
    all_att.cross(3)
    for d in (1, 2, 3):
        net.got(b5 + d - 1, gs5.at[shifted("dp", -d)])
    for a in range(4):
        for b in range(4):
            lo = 128 * (4 * a + b)
            f_gain[:, lo : lo + 128] = gs5[a, b].astype(BF16)
    share_grad.finish(0)
    share_grad.finish(1)
    for g in (all_red, all_exp, all_mrg, all_att):
        g.finish()
    for c in local + l_out + l_grad + c_exp + c_mrg + c_att:
        c.wait()
    net.drain()


def main_call(x, cot, parents, wa, wm, we, wr, gains, table, states, gain_states):
    kinds = [(1024, 128), (128, 1024), (128, 1024), (256, 128), (128, 384)]
    vm, sds = pltpu.VMEM, jax.ShapeDtypeStruct
    scratch = (
        [vm((4, 4, n, c), BF16) for n, c in kinds]
        + [vm((2, 6, 4, n // 4, c), BF16) for n, c in kinds]
        + [vm((2, 6, n // 4, c), BF16) for n, c in kinds]
        + [
            vm((4, 2048, 256), BF16),
            vm((2, 4, 128, 128), F32),
            vm((2048, 384), BF16),
            vm((256, 2048), BF16),
            vm((2, 2, 4, 32, D), BF16),
            vm((2, 2, 4, 32, D), BF16),
            vm((2, 256, D), BF16),
            vm((2, 256, D), BF16),
            vm((2, 2, 4, 32, D), BF16),
            vm((2, 256, 1024), BF16),
            vm((2, 128, D), F32),
            vm((2, 128, D), BF16),
            vm((2, 128, D), BF16),
            vm((2, 6, 16, D), BF16),
            vm((4, 4, 128, 512), BF16),
            vm((8, 128, 128), BF16),
            vm((8, 128, 128), BF16),
            vm((2, 2, 2, 128, 128), BF16),
            vm((2, 256, 256), BF16),
            vm((2, 256, 256), BF16),
            vm((2, 8, 128, 128), F32),
            vm((3, 2, 128, 256), BF16),
            vm((2, 256, 384), BF16),
            vm((2, 32, D), F32),
            vm((2, 32, D), F32),
            vm((3, 512, 128), F32),
            vm((3, 128, 2, 1024), F32),
            vm((128, 2, 1024), BF16),
            vm((2, D), F32),
            vm((8, 2, D), F32),
            vm((4, 2, 512), F32),
            vm((4, 2, 128), F32),
            vm((4, 2, 128), F32),
            vm((4, 4, 2, 128), F32),
            vm((2, D), F32),
            vm((2, 512), F32),
            vm((2, 128), F32),
            pltpu.SemaphoreType.DMA((420,)),
            pltpu.SemaphoreType.DMA((420,)),
            pltpu.SemaphoreType.DMA((32,)),
        ]
    )
    rows_out = sds((2, 2, 4, 32, D), BF16)
    shards = [sds((128, 384), F32), sds((2, 128, 128), F32), sds((128, 2, 1024), F32), sds((1024, 128), F32)]
    fulls = [sds((D, 384), BF16), sds((256, D), BF16), sds((D, 2, 1024), BF16), sds((1024, D), BF16)]
    out_shape = [rows_out, rows_out, *[[v] * 3 for v in shards], *fulls, *[sds((2, 128), F32)] * 3, sds((2, D), BF16)]
    vspec = pl.BlockSpec(memory_space=pltpu.VMEM)
    hbm = pl.BlockSpec(memory_space=pl.ANY)
    return pl.pallas_call(
        main_kernel,
        out_shape=out_shape,
        in_specs=[hbm, hbm, pl.BlockSpec(memory_space=pltpu.SMEM), hbm, hbm, hbm, hbm, vspec, hbm]
        + [[hbm] * 3] * 4
        + [vspec] * 3,
        out_specs=[hbm, hbm] + [[hbm] * 3] * 4 + [hbm] * 4 + [vspec] * 4,
        scratch_shapes=scratch,
        compiler_params=pltpu.CompilerParams(
            collective_id=1, has_side_effects=True, vmem_limit_bytes=64 * 2**20 - 65536
        ),
    )(x, cot, parents, wa, wm, we, wr, gains, table, *states, *gain_states)


def rotary_table():
    inv = ROPE_BASE ** (-2.0 * np.arange(HD // 2, dtype=np.float32) / HD)
    angle = np.arange(512, dtype=np.float32)[:, None] * inv.astype(np.float32)[None, :]
    c, s = np.cos(angle), np.sin(angle)
    both = np.stack([np.concatenate([c, c, c, c], 1), np.concatenate([-s, s, -s, s], 1)])
    return both.reshape(2, 4, 128, 128).astype(np.float32)


def on_device(
    inputs, cotangent, parents, weight_attend, weight_merge, weight_expand, weight_reduce, gains,
    master_attend, master_merge, master_expand, master_reduce, master_gains,
    first_attend, first_merge, first_expand, first_reduce, first_gains,
    second_attend, second_merge, second_expand, second_reduce, second_gains,
):
    x = inputs.reshape(2, 2, 4, 32, D)
    cot = cotangent.reshape(2, 2, 4, 32, D)
    we = weight_expand.transpose(1, 0, 2)
    out, grad, s_att, s_mrg, s_exp, s_red, f_att, f_mrg, f_exp, f_red, n_gain, m_gain, v_gain, f_gain = main_call(
        x, cot, parents, weight_attend, weight_merge, we, weight_reduce, gains, jnp.asarray(rotary_table()),
        [
            [master_attend, first_attend, second_attend],
            [v.reshape(2, 128, 128) for v in (master_merge, first_merge, second_merge)],
            [master_expand, first_expand, second_expand],
            [master_reduce, first_reduce, second_reduce],
        ],
        [master_gains, first_gains, second_gains],
    )
    s_mrg = [v.reshape(256, 128) for v in s_mrg]
    return (
        out.reshape(2, 256, D), grad.reshape(2, 256, D),
        s_att[0], s_mrg[0], s_exp[0], s_red[0], n_gain,
        s_att[1], s_mrg[1], s_exp[1], s_red[1], m_gain,
        s_att[2], s_mrg[2], s_exp[2], s_red[2], v_gain,
        f_att, f_mrg, f_exp, f_red, f_gain,
    )


def solution(mesh):
    both = ("dp", "seq")
    states = (P(both, "mp"), P("mp", both), P(both, None, "mp"), P("mp", both), P(None, both))
    weights = (P(None, "mp"), P("mp", None), P(None, None, "mp"), P("mp", None), P())
    tokens = P("dp", "seq", None)
    return jax.shard_map(
        on_device,
        mesh=mesh,
        in_specs=(tokens, tokens, P("dp", None), *weights, *states, *states, *states),
        out_specs=(tokens, tokens, *states, *states, *states, *weights),
        check_vma=False,
    )
```

```python
import functools

import jax
import jax.numpy as jnp
import numpy as np
from jax import lax
from jax.experimental import pallas as pl
from jax.experimental.pallas import tpu as pltpu
from jax.sharding import PartitionSpec as P

MESH = pl.DeviceIdType.MESH
F32 = jnp.float32
BF16 = jnp.bfloat16
D = 2048
HD = 64
STEP = 5
NORM_EPS = 1e-05
ROPE_BASE = 500000.0
MASK_FILL = -1e30
BETA_ONE = 0.5
BETA_TWO = 0.5
ADAM_EPS = 1e-08
LEARN_RATE = 0.005
DECAY_RATE = 0.1
FIX_ONE = 1.0 - BETA_ONE**STEP
FIX_TWO = 1.0 - BETA_TWO**STEP
SIZES = {"dp": 4, "seq": 4, "mp": 8}


def adamw(master, first, second, grad_vals):
    momentum = BETA_ONE * first + (1.0 - BETA_ONE) * grad_vals
    variance = BETA_TWO * second + (1.0 - BETA_TWO) * grad_vals * grad_vals
    direction = momentum / FIX_ONE / (jnp.sqrt(variance / FIX_TWO) + ADAM_EPS)
    renewed = master - LEARN_RATE * (direction + DECAY_RATE * master)
    return (renewed, momentum, variance)


def dot(a, b):
    return lax.dot_general(a, b, (((1,), (0,)), ((), ())), preferred_element_type=F32)


def dot_nt(a, b):
    return lax.dot_general(a, b, (((1,), (1,)), ((), ())), preferred_element_type=F32)


def dot_tn(a, b):
    return lax.dot_general(a, b, (((0,), (0,)), ((), ())), preferred_element_type=F32)


def shifted(axis, delta):
    n = SIZES[axis]
    return lax.rem(lax.axis_index(axis) + (delta + n), n)


def sibling():
    m = lax.axis_index("mp")
    return m + 1 - 2 * lax.rem(m, 2)


def rows(start, n):
    return pl.ds(pl.multiple_of(start, 16), n)


class Net:
    def __init__(self, send, recv):
        self.send, self.recv = send, recv
        self.sends, self.recvs = 0, 0
        self.open = {}

    def send_id(self):
        self.sends += 1
        assert self.sends <= self.send.shape[0]
        return self.sends - 1

    def recv_ids(self, n):
        self.recvs += n
        assert self.recvs <= self.recv.shape[0]
        return self.recvs - n

    def put(self, sid, whole, rid, src, dst, axis, index):
        pltpu.make_async_remote_copy(
            src_ref=src,
            dst_ref=dst,
            send_sem=self.send.at[sid],
            recv_sem=self.recv.at[rid],
            device_id={axis: index},
            device_id_type=MESH,
        ).start()
        self.open[sid] = whole

    def stub(self, sid, rid, ref):
        return pltpu.make_async_remote_copy(
            src_ref=ref,
            dst_ref=ref,
            send_sem=self.send.at[sid],
            recv_sem=self.recv.at[rid],
            device_id={"dp": shifted("dp", 1)},
            device_id_type=MESH,
        )

    def got(self, rid, ref):
        self.stub(0, rid, ref).wait_recv()

    def sent(self, sid):
        self.stub(sid, 0, self.open.pop(sid)).wait_send()

    def drain(self):
        for sid in sorted(self.open):
            self.sent(sid)


def hello(peers):
    sem = pltpu.get_barrier_semaphore()
    for axis, index in peers:
        pl.semaphore_signal(sem, inc=1, device_id={axis: index}, device_id_type=MESH)


def hello_wait(n):
    pl.semaphore_wait(pltpu.get_barrier_semaphore(), n)


class Spread:
    def __init__(self, net, own, first, second):
        self.net, self.own, self.r1, self.r2 = net, own, first, second
        self.size, self.cols = own.shape[2], own.shape[3]
        self.q = self.size // 4
        self.sid = (net.send_id(), net.send_id())
        self.rid = net.recv_ids(16)
        self.chunk = min(self.q, max(16, 16384 // self.cols))

    def put(self, stage, h, slot, src, d):
        axis = self.axes(h)[stage]
        rid = self.rid + 8 * stage + 4 * h + (0, 1, 2, 2, 3, 3)[slot]
        to = (self.r1, self.r2)[stage]
        self.net.put(self.sid[stage], to, rid, src, to.at[h, slot], axis, shifted(axis, d))

    def got(self, stage, h, k):
        ref = (self.r1, self.r2)[stage]
        ref = ref.at[h, k] if k < 2 else ref.at[h, pl.ds(2 * k - 2, 2)]
        self.net.got(self.rid + 8 * stage + 4 * h + k, ref)

    def axes(self, h):
        return (("dp", "seq"), ("seq", "dp"))[h]

    def row(self, h, da):
        a = shifted(self.axes(h)[0], da)
        return (lambda b: (a, b)) if h == 0 else (lambda b: (b, a))

    def block(self, h, db):
        a, b = lax.axis_index(self.axes(h)[0]), shifted(self.axes(h)[1], db)
        return (a, b) if h == 0 else (b, a)

    def view(self, h, da, lo):
        a = shifted(self.axes(h)[0], da)
        if h == 0:
            return self.own.at[a, pl.ds(0, 4), pl.ds(lo, self.q)]
        return self.own.at[pl.ds(0, 4), a, pl.ds(lo, self.q)]

    def one(self, h, db, lo):
        a, b = self.block(h, db)
        return self.own.at[a, b, pl.ds(lo, self.q)]

    def add(self, index_of, count, lo, sources, use=None):
        steps = self.q // self.chunk

        @pl.loop(0, count * steps)
        def _(k):
            b = k // steps
            r = (k % steps) * self.chunk
            at = (*index_of(b), rows(lo + r, self.chunk))
            v = self.own[at].astype(F32)
            for ref, lead in sources:
                if count > 1:
                    v = v + ref[(*lead, b, rows(r, self.chunk))].astype(F32)
                else:
                    v = v + ref[(*lead, rows(r, self.chunk))].astype(F32)
            if use is None:
                self.own[at] = v.astype(BF16)
            else:
                use(lo + r, v)

    def step0(self):
        q = self.q
        for h in (0, 1):
            lo = 2 * h * q
            self.put(0, h, 0, self.view(h, 2, lo), 1)
            self.put(0, h, 1, self.view(h, 2, lo + q), -1)
        for h in (0, 1):
            lo = 2 * h * q
            self.put(0, h, 4, self.view(h, 1, lo + q), 1)
            self.put(0, h, 2, self.view(h, -1, lo), -1)

    def step1(self):
        q = self.q
        for h in (0, 1):
            lo = 2 * h * q
            self.got(0, h, 0)
            self.add(self.row(h, 1), 4, lo, [(self.r1, (h, 0))])
            self.put(0, h, 3, self.view(h, 1, lo), 1)
            self.got(0, h, 1)
            self.add(self.row(h, -1), 4, lo + q, [(self.r1, (h, 1))])
            self.put(0, h, 5, self.view(h, -1, lo + q), -1)

    def step2(self):
        q = self.q
        for h in (0, 1):
            lo = 2 * h * q
            self.got(0, h, 2)
            self.add(self.row(h, 0), 4, lo, [(self.r1, (h, 2)), (self.r1, (h, 3))])
            self.got(0, h, 3)
            self.add(self.row(h, 0), 4, lo + q, [(self.r1, (h, 4)), (self.r1, (h, 5))])
            self.put(1, h, 0, self.one(h, 2, lo), 1)
            self.put(1, h, 1, self.one(h, 2, lo + q), -1)
            self.put(1, h, 4, self.one(h, 1, lo + q), 1)
            self.put(1, h, 2, self.one(h, -1, lo), -1)

    def step3(self):
        q = self.q
        for h in (0, 1):
            lo = 2 * h * q
            self.got(1, h, 0)
            at = self.block(h, 1)
            self.add(lambda b: at, 1, lo, [(self.r2, (h, 0))])
            self.put(1, h, 3, self.one(h, 1, lo), 1)
            self.got(1, h, 1)
            at2 = self.block(h, -1)
            self.add(lambda b: at2, 1, lo + q, [(self.r2, (h, 1))])
            self.put(1, h, 5, self.one(h, -1, lo + q), -1)

    def step4(self, h, use):
        q = self.q
        lo = 2 * h * q
        at = self.block(h, 0)
        self.got(1, h, 2)
        self.add(lambda b: at, 1, lo, [(self.r2, (h, 2)), (self.r2, (h, 3))], use)
        self.got(1, h, 3)
        self.add(lambda b: at, 1, lo + q, [(self.r2, (h, 4)), (self.r2, (h, 5))], use)


class Fold:
    def __init__(self, net, acc, rsib, zsend, zrec):
        self.net, self.acc, self.rsib, self.zsend, self.zrec = net, acc, rsib, zsend, zrec
        self.sib_sid = [net.send_id(), net.send_id()]
        self.z_sid = [net.send_id(), net.send_id()]
        self.rid = net.recv_ids(16)

    def quarter(self, d):
        return 32 * lax.rem(lax.axis_index("mp") // 2 + (d + 4), 4)

    def right(self):
        return shifted("mp", 2)

    def left(self):
        return shifted("mp", -2)

    def to_sibling(self, p, k, src, dst):
        self.net.put(self.sib_sid[p], self.rsib.at[p], self.rid + 8 * p + k, src, dst, "mp", sibling())

    def to_chip(self, p, slot, src, way):
        rid = self.rid + 8 * p + 4 + (0, 1, 2, 2, 3, 3)[slot]
        self.net.put(self.z_sid[p], self.zrec.at[p], rid, src, self.zrec.at[p, slot], "mp", way)

    def send_columns(self, p, k, src):
        cols = pl.ds(512 * k, 512)
        self.to_sibling(p, k, src.at[:, cols], self.rsib.at[p, :, cols])

    def send_rows(self, p, src):
        for k, d in enumerate((2, 1, -1, 0)):
            at = rows(self.quarter(d), 32)
            self.to_sibling(p, k, src(at), self.rsib.at[p, at])

    def sent(self, p):
        self.net.sent(self.sib_sid[p])

    def total(self, d, p, own, store):
        for i in (0, 1):
            at = rows(self.quarter(d) + 16 * i, 16)
            v = own(p, at).astype(F32) + self.rsib[p, at].astype(F32)
            self.acc[p, at] = v
            if store:
                self.zsend[p, at] = v.astype(BF16)

    def begin(self, p, own, by_rows):
        rid = self.rid + 8 * p

        def arrived(k, d):
            if by_rows:
                self.net.got(rid + k, self.rsib.at[p, rows(self.quarter(d), 32)])

        if not by_rows:
            for k in range(4):
                self.net.got(rid + k, self.rsib.at[p, :, pl.ds(512 * k, 512)])
        arrived(0, 2)
        self.total(2, p, own, True)
        s = self.quarter(2)
        self.to_chip(p, 0, self.zsend.at[p, rows(s, 16)], self.right())
        self.to_chip(p, 1, self.zsend.at[p, rows(s + 16, 16)], self.left())
        arrived(1, 1)
        self.total(1, p, own, True)
        self.to_chip(p, 4, self.zsend.at[p, rows(self.quarter(1) + 16, 16)], self.right())
        arrived(2, -1)
        self.total(-1, p, own, True)
        self.to_chip(p, 2, self.zsend.at[p, rows(self.quarter(-1), 16)], self.left())
        arrived(3, 0)
        self.total(0, p, own, False)

    def middle(self, p):
        for k, d, off, way in ((0, 1, 0, self.right()), (1, -1, 16, self.left())):
            self.net.got(self.rid + 8 * p + 4 + k, self.zrec.at[p, k])
            at = rows(self.quarter(d) + off, 16)
            self.zsend[p, at] = (self.acc[p, at] + self.zrec[p, k].astype(F32)).astype(BF16)
            self.to_chip(p, 3 + 2 * k, self.zsend.at[p, at], way)

    def finish(self, p, use):
        for part in (0, 1):
            self.net.got(self.rid + 8 * p + 6 + part, self.zrec.at[p, pl.ds(2 + 2 * part, 2)])
            v = self.acc[p, rows(self.quarter(0) + 16 * part, 16)]
            for k in (2 + 2 * part, 3 + 2 * part):
                v = v + self.zrec[p, k].astype(F32)
            use(p, 16 * part, v)

    def release(self):
        for sid in (*self.sib_sid, *self.z_sid):
            if sid in self.net.open:
                self.net.sent(sid)


class Share:
    def __init__(self, net, out):
        self.net, self.out = net, out
        self.sid = (net.send_id(), net.send_id())
        self.rid = net.recv_ids(8)

    def at(self, p, d, other=False, lo=0, n=32):
        m = lax.axis_index("mp")
        core = lax.rem(m, 2)
        if other:
            core = 1 - core
        return self.out.at[p, core, lax.rem(m // 2 + (d + 4), 4), pl.ds(lo, n)]

    def put(self, p, k, src, dst, index):
        own = k < 2 or (k == 3 and dst is None)
        dst = self.at(p, 0) if dst is None else dst
        whole = self.out.at[pl.ds(0, 2), 0, pl.ds(0, 3 if own else 4)]
        self.net.put(self.sid[0 if own else 1], whole, self.rid + 4 * p + k, src, dst, "mp", index)

    def got(self, p, k, ref):
        self.net.got(self.rid + 4 * p + k, ref)

    def begin(self, p, src=None):
        src = self.at(p, 0) if src is None else src
        self.put(p, 0, src, None, shifted("mp", 2))
        self.put(p, 1, src, None, shifted("mp", -2))
        self.put(p, 3, src, None, sibling())

    def middle(self, p):
        self.got(p, 0, self.at(p, -1))
        half = self.at(p, -1, False, 0, 16)
        self.put(p, 2, half, half, shifted("mp", 2))
        self.got(p, 1, self.at(p, 1))
        half = self.at(p, 1, False, 16, 16)
        self.put(p, 2, half, half, shifted("mp", -2))
        for d in (-1, 1):
            self.put(p, 3, self.at(p, d), self.at(p, d), sibling())

    def later(self, p):
        self.got(p, 2, self.at(p, 2))
        self.put(p, 3, self.at(p, 2), self.at(p, 2), sibling())

    def finish(self, p):
        self.got(p, 3, self.out.at[p, 1 - lax.rem(lax.axis_index("mp"), 2)])

    def release(self):
        for sid in self.sid:
            self.net.sent(sid)


class Gather:
    def __init__(self, net, own, size, region, whole):
        self.net, self.own, self.size, self.region, self.whole = net, own, size, region, whole
        self.sid, self.rid = net.send_id(), net.recv_ids(30)
        self.half, self.quarter = size // 2, size // 4

    def put(self, k, src, dst, axis, d):
        self.net.put(self.sid, self.whole, self.rid + k, src, dst, axis, shifted(axis, d))

    def got(self, k, ref):
        self.net.got(self.rid + k, ref)

    def idx(self, h, da, db):
        fa, sa = (("dp", "seq"), ("seq", "dp"))[h]
        c = {fa: shifted(fa, da), sa: shifted(sa, db)}
        return c["dp"] * 4 + c["seq"]

    def both(self, k, src, dst, axis):
        self.put(k, src, dst, axis, 1)
        self.put(k + 1, src, dst, axis, -1)

    def begin(self, h):
        for stage in (0, 1):
            axis = ("dp", "seq")[(h + stage) % 2]
            lo = h * self.half
            src = self.own.at[pl.ds(lo, self.half)]
            self.both(15 * h + 3 * stage, src, self.region(self.idx(h, 0, 0), lo, self.half), axis)

    def near(self):
        for h in (0, 1):
            fa, sa = (("dp", "seq"), ("seq", "dp"))[h]
            lo = h * self.half
            for k, d in ((0, -1), (1, 1)):
                p = self.region(self.idx(h, d, 0), lo, self.half)
                self.got(15 * h + k, p)
                part = self.region(self.idx(h, d, 0), lo + k * self.quarter, self.quarter)
                self.put(15 * h + 2, part, part, fa, -d)
                self.both(15 * h + 5 + 2 * k, p, p, sa)

    def far(self):
        for h in (0, 1):
            sa, lo = (("dp", "seq"), ("seq", "dp"))[h][1], h * self.half
            p = self.region(self.idx(h, 2, 0), lo, self.half)
            self.got(15 * h + 2, p)
            self.both(15 * h + 9, p, p, sa)

    def cross(self, k):
        d = (0, -1, 1, 2)[k]
        for h in (0, 1):
            sa, lo = (("dp", "seq"), ("seq", "dp"))[h][1], h * self.half
            for w, db in ((0, -1), (1, 1)):
                at = self.idx(h, d, db)
                self.got(15 * h + 3 + 2 * k + w, self.region(at, lo, self.half))
                part = self.region(at, lo + w * self.quarter, self.quarter)
                self.put(15 * h + 11 + k, part, part, sa, -db)

    def finish(self):
        for k, d in enumerate((0, -1, 1, 2)):
            for h in (0, 1):
                lo = h * self.half
                self.got(15 * h + 11 + k, self.region(self.idx(h, d, 2), lo, self.half))


def lanes(shape):
    return lax.broadcasted_iota(jnp.int32, shape, len(shape) - 1)


def swap_halves(v):
    lane = lanes(v.shape)
    return jnp.where(lane % HD < HD // 2, pltpu.roll(v, 96, 1), pltpu.roll(v, 32, 1))


def main_kernel(
    x_hbm, cot_hbm, parents, wa_hbm, wm_hbm, we_hbm, wr_hbm, gains, table_hbm,
    i_att, i_mrg, i_exp, i_red, mg, fg, sg,
    out, grad, o_att, o_mrg, o_exp, o_red, f_att, f_mrg, f_exp, f_red,
    o_gain, f_gain,
    g_red, g_gate, g_up, g_mrg, g_att,
    ra_red, ra_gate, ra_up, ra_mrg, ra_att,
    rb_red, rb_gate, rb_up, rb_mrg, rb_att,
    sa, table, wa, wm, xd, cot, n1, dgu, n2, hid,
    acc, sib, rsib, zrec, probs, kv_a, kv_b, q, att, datt, dkv, dkv_in, dpack,
    mid, dmid, stage, stage_exp, w_exp,
    gbuf, gs1, gs2, gs3, gs4, gs5, gtot, gtwo, gnew,
    send, recv, loc,
):
    net = Net(send, recv)
    m = lax.axis_index("mp")
    core, z = lax.rem(m, 2), m // 2
    seq = lax.axis_index("seq")
    other = 1 - core
    dp = lax.axis_index("dp")
    me = 4 * dp + seq
    hello(
        [("dp", shifted("dp", d)) for d in (1, 2, 3)]
        + [("seq", shifted("seq", d)) for d in (1, 2, 3)]
        + [("mp", shifted("mp", d)) for d in range(1, 8)]
    )
    kv = (kv_a, kv_b)
    kv_sid, kv_rid = (net.send_id(), net.send_id()), net.recv_ids(2)
    dkv_sid, dkv_rid = net.send_id(), net.recv_ids(2)
    fold = Fold(net, acc, rsib, sib, zrec)
    share_one, share_two, share_out, share_grad = Share(net, n2), Share(net, xd), Share(net, out), Share(net, grad)
    gain_sid, gain_rid = [net.send_id() for _ in range(5)], net.recv_ids(5)

    def gain_put(k, ref, count, src, dst, axis, d):
        net.put(gain_sid[k], ref.at[pl.ds(0, count)], gain_rid + k, src, dst, axis, shifted(axis, d))

    def gain_got(k, ref, count):
        net.got(gain_rid + k, ref.at[pl.ds(0, count)])


    def by_col(ref):
        return lambda i, lo, k: ref.at[pl.ds(lo, k), pl.ds(pl.multiple_of(128 * i, 128), 128)]

    all_red = Gather(net, g_red.at[dp, seq], 1024, by_col(f_red), f_red.at[:, pl.ds(0, 1920)])
    all_exp = Gather(net, w_exp, 128, lambda i, lo, k: f_exp.at[pl.ds(128 * i + lo, k)], f_exp.at[pl.ds(0, 1920)])
    all_mrg = Gather(net, g_mrg.at[dp, seq], 256, by_col(f_mrg), f_mrg.at[:, pl.ds(0, 1920)])
    all_att = Gather(net, g_att.at[dp, seq], 128, lambda i, lo, k: f_att.at[rows(128 * i + lo, k)], f_att.at[pl.ds(0, 1920)])
    s_red = Spread(net, g_red, ra_red, rb_red)
    s_gate = Spread(net, g_gate, ra_gate, rb_gate)
    s_up = Spread(net, g_up, ra_up, rb_up)
    s_mrg = Spread(net, g_mrg, ra_mrg, rb_mrg)
    s_att = Spread(net, g_att, ra_att, rb_att)

    def bring(k, src, dst):
        c = pltpu.make_async_copy(src, dst, loc.at[k])
        c.start()
        return c

    c_x = [bring(t, x_hbm.at[t], xd.at[t]) for t in (0, 1)]
    c_wa = bring(2, wa_hbm, wa)
    c_table = bring(9, table_hbm, table)

    def all_here(ref, k):
        pltpu.make_async_copy(ref, ref, loc.at[k]).wait()

    both_gains = gains[...].astype(F32)
    gain_one, gain_two = both_gains[0:1, :], both_gains[1:2, :]

    def ancestors(t, b):
        p1 = parents[t, b]
        p2 = jnp.where(p1 >= 0, parents[t, jnp.maximum(p1, 0)], -1)
        p3 = jnp.where(p2 >= 0, parents[t, jnp.maximum(p2, 0)], -1)
        return p1, p2, p3

    def turns(t, i):
        ps = ancestors(t, 2 * seq + i)
        depth = sum(jnp.where(p >= 0, 1, 0) for p in ps)
        return table[0, depth], table[1, depth]

    lower = lanes((128, 128)) < HD

    def own_kv(t, at):
        return kv[t].at[pl.ds(2 * at, 2)]

    for t in (0, 1):
        c_x[t].wait()
        if t == 0:
            c_wa.wait()
            c_table.wait()
        else:
            c_wm = bring(4, wm_hbm, wm)
            c_cot = bring(3, cot_hbm, cot)
            for k in range(16):
                pltpu.make_async_copy(wr_hbm.at[:, pl.ds(128 * k, 128)], g_red.at[k // 4, k % 4], loc.at[10]).start()
            for k in range(4):
                pltpu.make_async_copy(we_hbm.at[0, :, pl.ds(256 * k, 256)], sa.at[k], loc.at[11]).start()
            for k in range(16):
                pltpu.make_async_copy(we_hbm.at[1, pl.ds(128 * k, 128)], g_up.at[k // 4, k % 4], loc.at[12]).start()

        @pl.loop(0, 16, unroll=4)
        def _(i):
            v = xd[t, i // 8, (i // 2) % 4, rows(16 * (i % 2), 16)].astype(F32)
            r = lax.rsqrt(jnp.mean(v * v, axis=-1, keepdims=True) + NORM_EPS)
            n1[t, rows(16 * i, 16)] = (v * r * gain_one).astype(BF16)

        packed = dot(n1[t], wa[...])
        for i in (0, 1):
            c, s = turns(t, i)
            part = packed[128 * i : 128 * i + 128]
            for g in (0, 1):
                v = part[:, 128 * g : 128 * g + 128]
                q[t, i, g] = (v * c + swap_halves(v) * s).astype(BF16)
            v = part[:, 256:384]
            kv[t][2 * seq + i] = jnp.where(lower, v * c + swap_halves(v) * s, v).astype(BF16)
        if t == 0:
            hello_wait(13)
        for d in (1, 2, 3):
            net.put(kv_sid[t], kv[t].at[pl.ds(0, 6)], kv_rid + t, own_kv(t, seq), own_kv(t, seq), "seq", shifted("seq", d))

    def hidden_grad(j):
        w = jnp.concatenate([g_red[k // 4, k % 4, 256 * j : 256 * j + 256] for k in range(16)], axis=1)
        v = dot_nt(cot[...].reshape(512, D), w)
        high = v.astype(BF16)
        low = (v - high.astype(F32)).astype(BF16)
        cols = pl.ds(256 * j, 256)
        g_gate[0, :, :, cols] = high.reshape(4, 128, 256)
        g_gate[1, :, :, cols] = low.reshape(4, 128, 256)

    low_lane = lanes((512, 128)) < HD
    key_col = lanes((128, 512))
    query_row = lax.broadcasted_iota(jnp.int32, (128, 512), 0)

    def key_views(t, ids):
        both = jnp.concatenate([kv[t][jnp.maximum(c, 0)] for c in ids], axis=0).astype(F32)
        turned = pltpu.roll(both, HD, 1)
        zero = jnp.zeros_like(both)
        keys = [jnp.where(low_lane, both, zero).astype(BF16), jnp.where(low_lane, zero, turned).astype(BF16)]
        values = [jnp.where(low_lane, turned, zero).astype(BF16), jnp.where(low_lane, zero, both).astype(BF16)]
        return keys, values

    def attention(t):
        net.got(kv_rid + t, kv[t].at[pl.ds(0, 6)])
        for i in (0, 1):
            b = 2 * seq + i
            ps = ancestors(t, b)
            keys, values = key_views(t, (b, *ps))
            seen = (key_col < 128) & (key_col <= query_row)
            for k, p in enumerate(ps):
                inside = (key_col >= 128 * (k + 1)) & (key_col < 128 * (k + 2))
                seen = seen | (inside & (p >= 0))
            for g in (0, 1):
                total = jnp.zeros((128, 128), F32)
                for h in (0, 1):
                    scores = dot_nt(q[t, i, g], keys[h]) * HD**-0.5
                    scores = jnp.where(seen, scores, MASK_FILL)
                    e = jnp.exp(scores - jnp.max(scores, axis=-1, keepdims=True))
                    p = (e / jnp.sum(e, axis=-1, keepdims=True)).astype(BF16)
                    probs[2 * t + i, 2 * g + h] = p
                    total = total + dot(p, values[h])
                att[t, 128 * i : 128 * i + 128, 128 * g : 128 * g + 128] = total.astype(BF16)

    def mine(p, at):
        return acc[p, at]

    def merge(p):
        for k in range(4):
            cols = pl.ds(512 * k, 512)
            sib[p, :, cols] = dot(att[p, rows(128 * other, 128)], wm[:, cols]).astype(BF16)
        fold.send_rows(p, lambda at: sib.at[p, at])
        for k in range(4):
            cols = pl.ds(512 * k, 512)
            acc[p, :, cols] = dot(att[p, rows(128 * core, 128)], wm[:, cols])

    def to_normed(p, r, v):
        x_own = xd[p, core, z, r : r + 16].astype(F32)
        total = x_own + v
        mid[p, r : r + 16] = total
        rms = lax.rsqrt(jnp.mean(total * total, axis=-1, keepdims=True) + NORM_EPS)
        n2[p, core, z, r : r + 16] = (total * rms * gain_two).astype(BF16)


    def feed_dot(p, j):
        lo = 1024 * (j % 2)
        for k, w in ((0, sa[j]), (1, g_up[:, :, :, 256 * j : 256 * j + 256].reshape(D, 256))):
            v = dot(n2[p].reshape(256, D), w)
            acc[p, :, lo + 256 * k : lo + 256 * k + 256] = v[0:128]
            acc[p, :, lo + 512 + 256 * k : lo + 768 + 256 * k] = v[128:256]

    def feed_rest(p, j):
        cols, cols_up = pl.ds(256 * j, 256), pl.ds(1024 + 256 * j, 256)
        for half in (0, 1):
            lo = 1024 * (j % 2) + 512 * half
            for i in range(4):
                at = pl.ds(32 * i, 32)
                gate, up = acc[p, at, lo : lo + 256], acc[p, at, lo + 256 : lo + 512]
                dh = g_gate[0, 2 * p + half, at, cols].astype(F32) + g_gate[1, 2 * p + half, at, cols].astype(F32)
                sig = 0.5 + 0.5 * jnp.tanh(0.5 * gate)
                act = gate * sig
                to = pl.ds(128 * half + 32 * i, 32)
                hid[p, to, cols] = (act * up).astype(BF16)
                dgu[p, to, cols] = (dh * up * (sig + act * (1.0 - sig))).astype(BF16)
                dgu[p, to, cols_up] = (dh * act).astype(BF16)

    def feed(p, between):
        feed_dot(p, 0)
        for j in (1, 2, 3):
            feed_dot(p, j)
            feed_rest(p, j - 1)
            if j == 1:
                between()
        feed_rest(p, 3)

    attention(0)
    c_wm.wait()
    merge(0)
    attention(1)
    fold.sent(0)
    fold.begin(0, mine, True)
    merge(1)
    c_cot.wait()
    all_here(g_red, 10)
    hidden_grad(0)
    fold.middle(0)
    fold.sent(1)
    fold.begin(1, mine, True)
    hidden_grad(1)
    fold.finish(0, to_normed)
    share_one.begin(0)
    fold.middle(1)
    hidden_grad(2)
    share_one.middle(0)
    fold.finish(1, to_normed)
    share_one.begin(1)
    hidden_grad(3)
    all_here(sa, 11)
    all_here(g_up, 12)
    share_one.later(0)
    share_one.middle(1)
    share_one.finish(0)
    feed(0, lambda: share_one.later(1))
    share_one.finish(1)
    fold.release()
    feed(1, lambda: None)

    @pl.loop(0, 4)
    def _(a):
        cols = pl.ds(pl.multiple_of(512 * a, 512), 512)
        v = dot_tn(hid[...].reshape(512, 1024), cot[:, :, :, :, cols].reshape(512, 512)).astype(BF16)
        for b in range(4):
            g_red[a, b] = v[:, 128 * b : 128 * b + 128]

    s_red.step0()
    def expand_grad(dst, first):
        @pl.loop(0, 4)
        def _(a):
            left = n2[:, :, :, :, pl.ds(pl.multiple_of(512 * a, 512), 512)].reshape(512, 512)
            v = dot_tn(left, dgu[:, :, first : first + 1024].reshape(512, 1024))
            dst[a] = v.astype(BF16).reshape(4, 128, 1024)

    expand_grad(g_gate, 0)
    s_gate.step0()

    def norm_grad(p):
        for k in range(4):
            for j in (2 * k, 2 * k + 1):
                cols = pl.ds(256 * j, 256)
                w_gate = jnp.concatenate([sa[i, 256 * j : 256 * j + 256] for i in range(4)], axis=1)
                w_up = g_up[j // 2, 2 * (j % 2) : 2 * (j % 2) + 2].reshape(256, 1024)
                v = dot_nt(dgu[p], jnp.concatenate([w_gate, w_up], axis=1))
                first, second = v[0:128], v[128:256]
                sib[p, :, cols] = jnp.where(core == 0, second, first).astype(BF16)
                acc[p, :, cols] = jnp.where(core == 0, first, second)
            fold.send_columns(p, k, sib.at[p])

    def to_branch(p, r, v):
        total = mid[p, r : r + 16]
        rms = lax.rsqrt(jnp.mean(total * total, axis=-1, keepdims=True) + NORM_EPS)
        u = v * gain_two
        back_vals = rms * u - total * (rms * rms * rms) * jnp.mean(u * total, axis=-1, keepdims=True)
        full = cot[p, core, z, r : r + 16].astype(F32) + back_vals
        dmid[p, r : r + 16] = full
        xd[p, core, z, r : r + 16] = full.astype(BF16)
        gbuf[1:2, :] = gbuf[1:2, :] + jnp.sum(v * total * rms, axis=0, keepdims=True)

    gbuf[...] = jnp.zeros_like(gbuf)
    norm_grad(0)
    s_red.step1()
    fold.sent(0)
    fold.begin(0, mine, False)
    norm_grad(1)
    for k in range(8):
        half = sa.at[k // 2, pl.ds(1024 * (k % 2), 1024)]
        pltpu.make_async_copy(wr_hbm.at[:, pl.ds(256 * k, 256)], half, loc.at[13]).start()
    expand_grad(g_up, 1024)
    s_up.step0()
    fold.middle(0)
    fold.sent(1)
    fold.begin(1, mine, False)
    s_gate.step1()
    fold.finish(0, to_branch)
    share_two.begin(0)
    fold.middle(1)

    all_here(sa, 13)

    @pl.loop(0, 4)
    def _(j):
        for k in (0, 1):
            v = dot(hid[...].reshape(512, 1024), sa[j, 1024 * k : 1024 * k + 1024])
            dgu[:, :, pl.ds(pl.multiple_of(512 * j + 256 * k, 256), 256)] = v.astype(BF16).reshape(2, 256, 256)

    fold.finish(1, to_branch)
    share_two.begin(1)

    x_slot = lax.rem(z + 1, 4)
    c_xo = [bring(p, x_hbm.at[p, core, z], cot.at[p, core, x_slot]) for p in (0, 1)]
    for k in (0, 1, 2):
        pltpu.make_async_copy(i_exp[k], stage_exp.at[k], loc.at[10]).start()
        pltpu.make_async_copy(i_red[k].at[pl.ds(0, 512)], stage.at[k], loc.at[11]).start()
    share_two.middle(0)
    share_two.middle(1)
    share_two.later(0)
    s_red.step2()
    share_two.finish(0)

    dbr = xd

    def branch_back(t):
        datt[t] = dot_nt(dbr[t].reshape(256, D), wm[...]).astype(BF16)

    branch_back(0)
    share_two.later(1)
    dkv[...] = jnp.zeros_like(dkv)

    def attention_back(t, i):
        u = 2 * t + i
        b = 2 * seq + i
        ps = ancestors(t, b)
        keys, values = key_views(t, (b, *ps))
        c, s = turns(t, i)
        at = rows(128 * i, 128)
        dk = [jnp.zeros((512, 128), F32), jnp.zeros((512, 128), F32)]
        dv = [jnp.zeros((512, 128), F32), jnp.zeros((512, 128), F32)]
        for g in (0, 1):
            dq = jnp.zeros((128, 128), F32)
            da = datt[t, at, 128 * g : 128 * g + 128]
            for h in (0, 1):
                p = probs[u, 2 * g + h]
                pf = p.astype(F32)
                dp = dot_nt(da, values[h])
                inner = jnp.sum(pf * dp, axis=-1, keepdims=True)
                ds = (pf * (dp - inner)).astype(BF16)
                dq = dq + dot(ds, keys[h])
                dk[h] = dk[h] + dot_tn(ds, q[t, i, g])
                dv[h] = dv[h] + dot_tn(p, da)
            dq = dq * HD**-0.5
            dpack[t, at, 128 * g : 128 * g + 128] = (dq * c - swap_halves(dq) * s).astype(BF16)
        both = jnp.where(
            low_lane, (dk[0] + pltpu.roll(dk[1], HD, 1)) * HD**-0.5, pltpu.roll(dv[0], HD, 1) + dv[1]
        )
        dkv[t, b] = dkv[t, b] + both[0:128]
        for blk in range(8):
            v = dkv[t, blk]
            for k, p in enumerate(ps):
                v = v + both[128 * (k + 1) : 128 * (k + 2)] * jnp.where(p == blk, 1.0, 0.0)
            dkv[t, blk] = v

    def send_dkv(t):
        for c in range(8):
            probs[2 * t, c // 4, :, 128 * (c % 4) : 128 * (c % 4) + 128] = dkv[t, c].astype(BF16)
        for d in (1, 2, 3):
            peer = shifted("seq", d)
            src = probs.at[2 * t, peer // 2, :, pl.ds(pl.multiple_of(256 * lax.rem(peer, 2), 256), 256)]
            net.put(dkv_sid, dkv_in, dkv_rid + t, src, dkv_in.at[d - 1, t], "seq", peer)

    def add_dkv(t):
        net.got(dkv_rid + t, dkv_in.at[pl.ds(0, 3), t])
        for i in (0, 1):
            v = dkv[t, 2 * seq + i]
            for d in (0, 1, 2):
                v = v + dkv_in[d, t, :, 128 * i : 128 * i + 128].astype(F32)
            c, s = turns(t, i)
            v = jnp.where(lower, v * c - swap_halves(v) * s, v)
            dpack[t, 128 * i : 128 * i + 128, 256:384] = v.astype(BF16)

    for i in (0, 1):
        attention_back(0, i)
    send_dkv(0)
    share_two.finish(1)
    fold.release()

    def down_rows(p, at):
        return dgu[p, pl.ds(pl.multiple_of(128 * core + at.start, 16), 16)]

    for p in (0, 1):
        fold.send_rows(p, lambda at: dgu.at[p, rows(128 * other + at.start, 32)])
    branch_back(1)
    for i in (0, 1):
        attention_back(1, i)
    send_dkv(1)
    s_up.step1()

    @pl.loop(0, 8)
    def _(j):
        cols = pl.ds(pl.multiple_of(256 * j, 256), 256)
        v = dot_tn(att[...].reshape(512, 256), dbr[:, :, :, :, cols].reshape(512, 256))
        g_mrg[j // 2, 2 * (j % 2)] = v[:, 0:128].astype(BF16)
        g_mrg[j // 2, 2 * (j % 2) + 1] = v[:, 128:256].astype(BF16)

    s_mrg.step0()
    fold.begin(0, down_rows, True)
    fold.begin(1, down_rows, True)
    s_gate.step2()
    add_dkv(0)
    add_dkv(1)

    @pl.loop(0, 4)
    def _(a):
        left = n1[:, :, pl.ds(pl.multiple_of(512 * a, 512), 512)].reshape(512, 512)
        g_att[a] = dot_tn(left, dpack[...].reshape(512, 384)).astype(BF16).reshape(4, 128, 384)

    s_att.step0()
    fold.middle(0)
    fold.middle(1)
    s_red.step3()
    for k in (0, 1, 2):
        pltpu.make_async_copy(i_mrg[k], dkv.at[0, pl.ds(2 * k, 2)], loc.at[12]).start()
    share_one.release()

    @pl.loop(0, 8)
    def _(j):
        v = dot_nt(dpack[...].reshape(512, 384), wa[rows(256 * j, 256)])
        n2[:, :, :, :, pl.ds(pl.multiple_of(256 * j, 256), 256)] = v.astype(BF16).reshape(2, 2, 4, 32, 256)

    def to_out(p, r, v):
        cot[p, core, z, r : r + 16] = (mid[p, r : r + 16] + v).astype(BF16)

    l_out = []
    for p in (0, 1):
        fold.finish(p, to_out)
        share_out.begin(p, cot.at[p, core, z])
        l_out.append(bring(2 + p, cot.at[p, core, z], out.at[p, core, z]))
    s_mrg.step1()

    def renew(state, at, grads):
        new = adamw(state[0][at], state[1][at], state[2][at], grads)[0]
        state[1][at] = grads
        return new

    flat_stage = [stage.at[k] for k in (0, 1, 2)]

    def use_red(h):
        def use(r, v):
            new = renew(flat_stage, rows(r - 512 * h, 128), v)
            g_red[dp, seq, rows(r, 128)] = new.astype(BF16)

        return use

    all_here(stage, 11)
    s_red.step4(0, use_red(0))
    all_red.begin(0)
    c_red = [bring(4, stage.at[1], o_red.at[pl.ds(0, 512)])]
    local = [bring(14, g_red.at[dp, seq, pl.ds(0, 512)], f_red.at[pl.ds(0, 512), pl.ds(pl.multiple_of(128 * me, 128), 128)])]
    s_up.step2()
    share_out.middle(0)
    share_out.middle(1)
    s_att.step1()
    s_gate.step3()
    for c in c_red:
        c.wait()
    for k in (0, 1, 2):
        pltpu.make_async_copy(i_red[k].at[pl.ds(512, 512)], stage.at[k], loc.at[11]).start()
    share_out.later(0)
    share_out.later(1)
    s_mrg.step2()
    all_here(stage, 11)
    s_red.step4(1, use_red(1))
    all_red.begin(1)
    c_red = [bring(4, stage.at[1], o_red.at[pl.ds(512, 512)])]
    local.append(bring(15, g_red.at[dp, seq, pl.ds(512, 512)], f_red.at[pl.ds(512, 512), pl.ds(pl.multiple_of(128 * me, 128), 128)]))
    share_out.finish(0)
    share_out.finish(1)
    fold.release()
    for p in (0, 1):
        fold.send_rows(p, lambda at: n2.at[p, other, at.start // 32])
    s_up.step3()
    s_att.step2()

    def use_expand(j):
        def use(r, v):
            at = rows(r, 16)
            new = adamw(stage_exp[0, at, j, :], stage_exp[1, at, j, :], stage_exp[2, at, j, :], v)[0]
            stage_exp[0, at, j, :] = new
            stage_exp[1, at, j, :] = v

        return use

    all_here(stage_exp, 10)
    s_gate.step4(0, use_expand(0))
    s_gate.step4(1, use_expand(0))
    for c in c_red:
        c.wait()
    for k in (0, 1, 2):
        for a in (0, 1, 2):
            pltpu.make_async_copy(
                i_att[k].at[:, pl.ds(128 * a, 128)], stage.at[k, pl.ds(128 * a, 128)], loc.at[11]
            ).start()

    def norm_rows(p, at):
        return n2[p, core, at.start // 32, pl.ds(pl.multiple_of(at.start % 32, 16), 16)]

    def fold_begin(p):
        fold.begin(p, norm_rows, True)

    fold_begin(0)
    fold_begin(1)
    all_red.near()
    s_mrg.step3()
    s_att.step3()
    fold.middle(0)
    fold.middle(1)
    for h in (0, 1):
        s_up.step4(h, use_expand(1))
        for i in (0, 1, 2, 3):
            at = rows(64 * h + 16 * i, 16)
            w_exp[at] = stage_exp[0, at].astype(BF16)
        all_exp.begin(h)
    c_exp = [bring(6, stage_exp.at[1], o_exp)]
    local.append(bring(9, w_exp, f_exp.at[pl.ds(128 * me, 128)]))
    for c in c_xo:
        c.wait()

    def to_grad(p, r, v):
        x = cot[p, core, x_slot, r : r + 16].astype(F32)
        rms = lax.rsqrt(jnp.mean(x * x, axis=-1, keepdims=True) + NORM_EPS)
        u = v * gain_one
        back_vals = rms * u - x * (rms * rms * rms) * jnp.mean(u * x, axis=-1, keepdims=True)
        cot[p, other, z, r : r + 16] = (dmid[p, r : r + 16] + back_vals).astype(BF16)
        gbuf[0:1, :] = gbuf[0:1, :] + jnp.sum(v * x * rms, axis=0, keepdims=True)

    for p in (0, 1):
        fold.finish(p, to_grad)
        share_grad.begin(p, cot.at[p, other, z])
    l_grad = [bring(p, cot.at[p, other, z], grad.at[p, core, z]) for p in (0, 1)]
    gs1[m] = gbuf[...]
    for d in range(1, 8):
        gain_put(0, gs1, 7, gbuf, gs1.at[m], "mp", d)

    def use_mrg(r, v):
        new = renew([dkv.at[0, 2 * k + r // 128] for k in (0, 1, 2)], rows(r % 128, 64), v)
        g_mrg[dp, seq, rows(r, 64)] = new.astype(BF16)

    all_here(dkv.at[0, pl.ds(0, 6)], 12)
    for h in (0, 1):
        s_mrg.step4(h, use_mrg)
        all_mrg.begin(h)
    c_mrg = [bring(7, dkv.at[0, pl.ds(2, 2)], o_mrg)]
    local.append(bring(8, g_mrg.at[dp, seq], f_mrg.at[:, pl.ds(pl.multiple_of(128 * me, 128), 128)]))
    all_here(stage.at[:, pl.ds(0, 384)], 11)

    def use_att(r, v):
        parts = []
        for a in (0, 1, 2):
            parts.append(renew(flat_stage, rows(128 * a + r, 32), v[:, 128 * a : 128 * a + 128]))
        g_att[dp, seq, rows(r, 32)] = jnp.concatenate(parts, axis=1).astype(BF16)

    for h in (0, 1):
        s_att.step4(h, use_att)
        all_att.begin(h)
    c_att = [bring(16 + a, stage.at[1, pl.ds(128 * a, 128)], o_att.at[:, pl.ds(128 * a, 128)]) for a in (0, 1, 2)]
    local.append(bring(5, g_att.at[dp, seq], f_att.at[rows(128 * me, 128)]))
    all_red.far()
    share_grad.middle(0)
    share_grad.middle(1)
    all_exp.near()
    gain_got(0, gs1, 7)
    total = gs1[0]
    for k in range(1, 8):
        total = total + gs1[k]
    gtot[...] = total

    def piece(i, n):
        return pl.ds(pl.multiple_of(i * n, 128), n)

    gs2[dp] = gtot[:, piece(dp, 512)]
    for d in (1, 2, 3):
        gain_put(1, gs2, 3, gtot.at[:, piece(shifted("dp", d), 512)], gs2.at[dp], "dp", d)
    all_red.cross(0)
    all_mrg.near()
    all_att.near()
    share_grad.later(0)
    share_grad.later(1)
    all_red.cross(1)
    all_exp.far()
    gain_got(1, gs2, 3)
    gtwo[...] = gs2[0] + gs2[1] + gs2[2] + gs2[3]
    gs3[seq] = gtwo[:, piece(seq, 128)]
    for d in (1, 2, 3):
        gain_put(2, gs3, 3, gtwo.at[:, piece(shifted("seq", d), 128)], gs3.at[seq], "seq", d)
    all_red.cross(2)
    all_mrg.far()
    all_att.far()
    all_exp.cross(0)
    gain_got(2, gs3, 3)
    shard = gs3[0] + gs3[1] + gs3[2] + gs3[3]
    new = adamw(mg[...], fg[...], sg[...], shard)[0]
    o_gain[...] = shard
    gnew[...] = new
    gs4[seq] = new
    for d in (1, 2, 3):
        gain_put(3, gs4, 3, gnew, gs4.at[seq], "seq", d)
    all_red.cross(3)
    all_exp.cross(1)
    all_mrg.cross(0)
    all_att.cross(0)
    gain_got(3, gs4, 3)
    gs5[dp] = gs4[...]
    for d in (1, 2, 3):
        gain_put(4, gs5, 3, gs4, gs5.at[dp], "dp", d)
    all_mrg.cross(1)
    all_att.cross(1)
    all_exp.cross(2)
    all_mrg.cross(2)
    all_att.cross(2)
    all_exp.cross(3)
    all_mrg.cross(3)
    all_att.cross(3)
    gain_got(4, gs5, 3)
    for a in range(4):
        for b in range(4):
            lo = 128 * (4 * a + b)
            f_gain[:, lo : lo + 128] = gs5[a, b].astype(BF16)
    share_grad.finish(0)
    share_grad.finish(1)
    for g in (all_red, all_exp, all_mrg, all_att):
        g.finish()
    for c in local + l_out + l_grad + c_exp + c_mrg + c_att:
        c.wait()
    net.drain()


def main_call(x, cot, parents, wa, wm, we, wr, gains, table, states, gain_states):
    kinds = [(1024, 128), (128, 1024), (128, 1024), (256, 128), (128, 384)]
    vm, sds = pltpu.VMEM, jax.ShapeDtypeStruct
    scratch = (
        [vm((4, 4, n, c), BF16) for n, c in kinds]
        + [vm((2, 6, 4, n // 4, c), BF16) for n, c in kinds]
        + [vm((2, 6, n // 4, c), BF16) for n, c in kinds]
        + [
            vm((4, 2048, 256), BF16),
            vm((2, 4, 128, 128), F32),
            vm((2048, 384), BF16),
            vm((256, 2048), BF16),
            vm((2, 2, 4, 32, D), BF16),
            vm((2, 2, 4, 32, D), BF16),
            vm((2, 256, D), BF16),
            vm((2, 256, D), BF16),
            vm((2, 2, 4, 32, D), BF16),
            vm((2, 256, 1024), BF16),
            vm((2, 128, D), F32),
            vm((2, 128, D), BF16),
            vm((2, 128, D), BF16),
            vm((2, 6, 16, D), BF16),
            vm((4, 4, 128, 512), BF16),
            vm((8, 128, 128), BF16),
            vm((8, 128, 128), BF16),
            vm((2, 2, 2, 128, 128), BF16),
            vm((2, 256, 256), BF16),
            vm((2, 256, 256), BF16),
            vm((2, 8, 128, 128), F32),
            vm((3, 2, 128, 256), BF16),
            vm((2, 256, 384), BF16),
            vm((2, 32, D), F32),
            vm((2, 32, D), F32),
            vm((3, 512, 128), F32),
            vm((3, 128, 2, 1024), F32),
            vm((128, 2, 1024), BF16),
            vm((2, D), F32),
            vm((8, 2, D), F32),
            vm((4, 2, 512), F32),
            vm((4, 2, 128), F32),
            vm((4, 2, 128), F32),
            vm((4, 4, 2, 128), F32),
            vm((2, D), F32),
            vm((2, 512), F32),
            vm((2, 128), F32),
            pltpu.SemaphoreType.DMA((36,)),
            pltpu.SemaphoreType.DMA((260,)),
            pltpu.SemaphoreType.DMA((20,)),
        ]
    )
    rows_out = sds((2, 2, 4, 32, D), BF16)
    shards = [sds((128, 384), F32), sds((2, 128, 128), F32), sds((128, 2, 1024), F32), sds((1024, 128), F32)]
    fulls = [sds((D, 384), BF16), sds((256, D), BF16), sds((D, 2, 1024), BF16), sds((1024, D), BF16)]
    out_shape = [rows_out, rows_out, *shards, *fulls, sds((2, 128), F32), sds((2, D), BF16)]
    vspec = pl.BlockSpec(memory_space=pltpu.VMEM)
    hbm = pl.BlockSpec(memory_space=pl.ANY)
    return pl.pallas_call(
        main_kernel,
        out_shape=out_shape,
        in_specs=[hbm, hbm, pl.BlockSpec(memory_space=pltpu.SMEM), hbm, hbm, hbm, hbm, vspec, hbm]
        + [[hbm] * 3] * 4
        + [vspec] * 3,
        out_specs=[hbm] * 10 + [vspec] * 2,
        scratch_shapes=scratch,
        compiler_params=pltpu.CompilerParams(
            collective_id=1, has_side_effects=True, vmem_limit_bytes=64 * 2**20 - 65536
        ),
    )(x, cot, parents, wa, wm, we, wr, gains, table, *states, *gain_states)


def adam_kernel(*refs):
    ins, outs = refs[:20], refs[20:]
    for k in range(5):
        master, first, second, grads = ins[4 * k : 4 * k + 4]
        new, mom, var = outs[3 * k : 3 * k + 3]
        if k != 2:
            new[...], mom[...], var[...] = adamw(master[...], first[...], second[...], grads[...])
        else:
            for j in (0, 1):
                one = adamw(master[:, j, :], first[:, j, :], second[:, j, :], grads[:, j, :])
                new[:, j, :], mom[:, j, :], var[:, j, :] = one


def adam_call(groups):
    def spec(shape, k):
        parts = 8 if k < 4 else 1
        zeros = (0,) * (len(shape) - 1)
        return pl.BlockSpec((shape[0] // parts, *shape[1:]), lambda i: (i if k < 4 else 0, *zeros))

    shapes = [g[0].shape for g in groups]
    flat = pl.pallas_call(
        adam_kernel,
        grid=(8,),
        in_specs=[spec(n, k) for k, n in enumerate(shapes) for _ in range(4)],
        out_specs=[spec(n, k) for k, n in enumerate(shapes) for _ in range(3)],
        out_shape=[jax.ShapeDtypeStruct(n, F32) for n in shapes for _ in range(3)],
        compiler_params=pltpu.CompilerParams(vmem_limit_bytes=64 * 2**20 - 65536),
    )(*[v for g in groups for v in g])
    return [flat[3 * k : 3 * k + 3] for k in range(5)]


def rotary_table():
    inv = ROPE_BASE ** (-2.0 * np.arange(HD // 2, dtype=np.float32) / HD)
    angle = np.arange(512, dtype=np.float32)[:, None] * inv.astype(np.float32)[None, :]
    c, s = np.cos(angle), np.sin(angle)
    both = np.stack([np.concatenate([c, c, c, c], 1), np.concatenate([-s, s, -s, s], 1)])
    return both.reshape(2, 4, 128, 128).astype(np.float32)


def on_device(
    inputs, cotangent, parents, weight_attend, weight_merge, weight_expand, weight_reduce, gains,
    master_attend, master_merge, master_expand, master_reduce, master_gains,
    first_attend, first_merge, first_expand, first_reduce, first_gains,
    second_attend, second_merge, second_expand, second_reduce, second_gains,
):
    x = inputs.reshape(2, 2, 4, 32, D)
    cot = cotangent.reshape(2, 2, 4, 32, D)
    we = weight_expand.transpose(1, 0, 2)
    states = [
        [master_attend, first_attend, second_attend],
        [v.reshape(2, 128, 128) for v in (master_merge, first_merge, second_merge)],
        [master_expand, first_expand, second_expand],
        [master_reduce, first_reduce, second_reduce],
    ]
    gain_states = [master_gains, first_gains, second_gains]
    out, grad, g_att, g_mrg, g_exp, g_red, f_att, f_mrg, f_exp, f_red, g_gain, f_gain = main_call(
        x, cot, parents, weight_attend, weight_merge, we, weight_reduce, gains, jnp.asarray(rotary_table()), states, gain_states
    )
    states[1] = [master_merge, first_merge, second_merge]
    sums = (g_att, g_mrg.reshape(256, 128), g_exp, g_red, g_gain)
    s_att, s_mrg, s_exp, s_red, s_gain = adam_call([[*v, g] for v, g in zip((*states, gain_states), sums)])
    return (
        out.reshape(2, 256, D), grad.reshape(2, 256, D),
        s_att[0], s_mrg[0], s_exp[0], s_red[0], s_gain[0],
        s_att[1], s_mrg[1], s_exp[1], s_red[1], s_gain[1],
        s_att[2], s_mrg[2], s_exp[2], s_red[2], s_gain[2],
        f_att, f_mrg, f_exp, f_red, f_gain,
    )


def solution(mesh):
    both = ("dp", "seq")
    states = (P(both, "mp"), P("mp", both), P(both, None, "mp"), P("mp", both), P(None, both))
    weights = (P(None, "mp"), P("mp", None), P(None, None, "mp"), P("mp", None), P())
    tokens = P("dp", "seq", None)
    return jax.shard_map(
        on_device,
        mesh=mesh,
        in_specs=(tokens, tokens, P("dp", None), *weights, *states, *states, *states),
        out_specs=(tokens, tokens, *states, *states, *states, *weights),
        check_vma=False,
    )
```

```python
import functools

import jax
import jax.numpy as jnp
import numpy as np
from jax import lax
from jax.experimental import pallas as pl
from jax.experimental.pallas import tpu as pltpu
from jax.sharding import PartitionSpec as P

MESH = pl.DeviceIdType.MESH
F32 = jnp.float32
BF16 = jnp.bfloat16
D = 2048
HD = 64
STEP = 5
NORM_EPS = 1e-05
ROPE_BASE = 500000.0
MASK_FILL = -1e30
BETA_ONE = 0.5
BETA_TWO = 0.5
ADAM_EPS = 1e-08
LEARN_RATE = 0.005
DECAY_RATE = 0.1
FIX_ONE = 1.0 - BETA_ONE**STEP
FIX_TWO = 1.0 - BETA_TWO**STEP
SIZES = {"dp": 4, "seq": 4, "mp": 8}


def adamw(master, first, second, grad_vals):
    momentum = BETA_ONE * first + (1.0 - BETA_ONE) * grad_vals
    variance = BETA_TWO * second + (1.0 - BETA_TWO) * grad_vals * grad_vals
    direction = momentum / FIX_ONE / (jnp.sqrt(variance / FIX_TWO) + ADAM_EPS)
    renewed = master - LEARN_RATE * (direction + DECAY_RATE * master)
    return (renewed, momentum, variance)


def dot(a, b):
    return lax.dot_general(a, b, (((1,), (0,)), ((), ())), preferred_element_type=F32)


def dot_nt(a, b):
    return lax.dot_general(a, b, (((1,), (1,)), ((), ())), preferred_element_type=F32)


def dot_tn(a, b):
    return lax.dot_general(a, b, (((0,), (0,)), ((), ())), preferred_element_type=F32)


def shifted(axis, delta):
    n = SIZES[axis]
    return lax.rem(lax.axis_index(axis) + (delta + n), n)


def sibling():
    m = lax.axis_index("mp")
    return m + 1 - 2 * lax.rem(m, 2)


def rows(start, n):
    return pl.ds(pl.multiple_of(start, 16), n)


class Net:
    def __init__(self, send, recv):
        self.send, self.recv = send, recv
        self.sends, self.recvs = 0, 0
        self.open = {}

    def send_id(self):
        self.sends += 1
        assert self.sends <= self.send.shape[0]
        return self.sends - 1

    def recv_ids(self, n):
        self.recvs += n
        assert self.recvs <= self.recv.shape[0]
        return self.recvs - n

    def put(self, sid, whole, rid, src, dst, axis, index):
        pltpu.make_async_remote_copy(
            src_ref=src,
            dst_ref=dst,
            send_sem=self.send.at[sid],
            recv_sem=self.recv.at[rid],
            device_id={axis: index},
            device_id_type=MESH,
        ).start()
        self.open[sid] = whole

    def stub(self, sid, rid, ref):
        return pltpu.make_async_remote_copy(
            src_ref=ref,
            dst_ref=ref,
            send_sem=self.send.at[sid],
            recv_sem=self.recv.at[rid],
            device_id={"dp": shifted("dp", 1)},
            device_id_type=MESH,
        )

    def got(self, rid, ref):
        self.stub(0, rid, ref).wait_recv()

    def sent(self, sid):
        self.stub(sid, 0, self.open.pop(sid)).wait_send()

    def drain(self):
        for sid in sorted(self.open):
            self.sent(sid)


def hello(peers):
    sem = pltpu.get_barrier_semaphore()
    for axis, index in peers:
        pl.semaphore_signal(sem, inc=1, device_id={axis: index}, device_id_type=MESH)


def hello_wait(n):
    pl.semaphore_wait(pltpu.get_barrier_semaphore(), n)


class Spread:
    def __init__(self, net, own, first, second):
        self.net, self.own, self.r1, self.r2 = net, own, first, second
        self.size, self.cols = own.shape[2], own.shape[3]
        self.q = self.size // 4
        self.sid = (net.send_id(), net.send_id())
        self.rid = net.recv_ids(16)
        self.chunk = min(self.q, max(16, 16384 // self.cols))

    def put(self, stage, h, slot, src, d):
        axis = self.axes(h)[stage]
        rid = self.rid + 8 * stage + 4 * h + (0, 1, 2, 2, 3, 3)[slot]
        to = (self.r1, self.r2)[stage]
        self.net.put(self.sid[stage], to, rid, src, to.at[h, slot], axis, shifted(axis, d))

    def got(self, stage, h, k):
        ref = (self.r1, self.r2)[stage]
        ref = ref.at[h, k] if k < 2 else ref.at[h, pl.ds(2 * k - 2, 2)]
        self.net.got(self.rid + 8 * stage + 4 * h + k, ref)

    def axes(self, h):
        return (("dp", "seq"), ("seq", "dp"))[h]

    def row(self, h, da):
        a = shifted(self.axes(h)[0], da)
        return (lambda b: (a, b)) if h == 0 else (lambda b: (b, a))

    def block(self, h, db):
        a, b = lax.axis_index(self.axes(h)[0]), shifted(self.axes(h)[1], db)
        return (a, b) if h == 0 else (b, a)

    def view(self, h, da, lo):
        a = shifted(self.axes(h)[0], da)
        if h == 0:
            return self.own.at[a, pl.ds(0, 4), pl.ds(lo, self.q)]
        return self.own.at[pl.ds(0, 4), a, pl.ds(lo, self.q)]

    def one(self, h, db, lo):
        a, b = self.block(h, db)
        return self.own.at[a, b, pl.ds(lo, self.q)]

    def add(self, index_of, count, lo, sources, use=None):
        steps = self.q // self.chunk

        @pl.loop(0, count * steps)
        def _(k):
            b = k // steps
            r = (k % steps) * self.chunk
            at = (*index_of(b), rows(lo + r, self.chunk))
            v = self.own[at].astype(F32)
            for ref, lead in sources:
                if count > 1:
                    v = v + ref[(*lead, b, rows(r, self.chunk))].astype(F32)
                else:
                    v = v + ref[(*lead, rows(r, self.chunk))].astype(F32)
            if use is None:
                self.own[at] = v.astype(BF16)
            else:
                use(lo + r, v)

    def step0_far(self, h):
        lo = 2 * h * self.q
        self.put(0, h, 0, self.view(h, 2, lo), 1)
        self.put(0, h, 1, self.view(h, 2, lo + self.q), -1)

    def step0_near(self, h):
        lo = 2 * h * self.q
        self.put(0, h, 4, self.view(h, 1, lo + self.q), 1)
        self.put(0, h, 2, self.view(h, -1, lo), -1)

    def step0(self):
        for h in (0, 1):
            self.step0_far(h)
        for h in (0, 1):
            self.step0_near(h)

    def step1(self):
        q = self.q
        for h in (0, 1):
            lo = 2 * h * q
            self.got(0, h, 0)
            self.add(self.row(h, 1), 4, lo, [(self.r1, (h, 0))])
            self.put(0, h, 3, self.view(h, 1, lo), 1)
            self.got(0, h, 1)
            self.add(self.row(h, -1), 4, lo + q, [(self.r1, (h, 1))])
            self.put(0, h, 5, self.view(h, -1, lo + q), -1)

    def step2(self):
        q = self.q
        for h in (0, 1):
            lo = 2 * h * q
            self.got(0, h, 2)
            self.add(self.row(h, 0), 4, lo, [(self.r1, (h, 2)), (self.r1, (h, 3))])
            self.got(0, h, 3)
            self.add(self.row(h, 0), 4, lo + q, [(self.r1, (h, 4)), (self.r1, (h, 5))])
            self.put(1, h, 0, self.one(h, 2, lo), 1)
            self.put(1, h, 1, self.one(h, 2, lo + q), -1)
            self.put(1, h, 4, self.one(h, 1, lo + q), 1)
            self.put(1, h, 2, self.one(h, -1, lo), -1)

    def step3(self):
        q = self.q
        for h in (0, 1):
            lo = 2 * h * q
            self.got(1, h, 0)
            at = self.block(h, 1)
            self.add(lambda b: at, 1, lo, [(self.r2, (h, 0))])
            self.put(1, h, 3, self.one(h, 1, lo), 1)
            self.got(1, h, 1)
            at2 = self.block(h, -1)
            self.add(lambda b: at2, 1, lo + q, [(self.r2, (h, 1))])
            self.put(1, h, 5, self.one(h, -1, lo + q), -1)

    def step4(self, h, use):
        q = self.q
        lo = 2 * h * q
        at = self.block(h, 0)
        self.got(1, h, 2)
        self.add(lambda b: at, 1, lo, [(self.r2, (h, 2)), (self.r2, (h, 3))], use)
        self.got(1, h, 3)
        self.add(lambda b: at, 1, lo + q, [(self.r2, (h, 4)), (self.r2, (h, 5))], use)


class Fold:
    def __init__(self, net, acc, rsib, zsend, zrec):
        self.net, self.acc, self.rsib, self.zsend, self.zrec = net, acc, rsib, zsend, zrec
        self.sib_sid = [net.send_id(), net.send_id()]
        self.z_sid = [net.send_id(), net.send_id()]
        self.rid = net.recv_ids(16)

    def quarter(self, d):
        return 32 * lax.rem(lax.axis_index("mp") // 2 + (d + 4), 4)

    def right(self):
        return shifted("mp", 2)

    def left(self):
        return shifted("mp", -2)

    def to_sibling(self, p, k, src, dst):
        self.net.put(self.sib_sid[p], self.rsib.at[p], self.rid + 8 * p + k, src, dst, "mp", sibling())

    def to_chip(self, p, slot, src, way):
        rid = self.rid + 8 * p + 4 + (0, 1, 2, 2, 3, 3)[slot]
        self.net.put(self.z_sid[p], self.zrec.at[p], rid, src, self.zrec.at[p, slot], "mp", way)

    def send_columns(self, p, k, src):
        cols = pl.ds(512 * k, 512)
        self.to_sibling(p, k, src.at[:, cols], self.rsib.at[p, :, cols])

    def send_rows(self, p, src):
        for k, d in enumerate((2, 1, -1, 0)):
            at = rows(self.quarter(d), 32)
            self.to_sibling(p, k, src(at), self.rsib.at[p, at])

    def sent(self, p):
        self.net.sent(self.sib_sid[p])

    def total(self, d, p, own, store):
        for i in (0, 1):
            at = rows(self.quarter(d) + 16 * i, 16)
            v = own(p, at).astype(F32) + self.rsib[p, at].astype(F32)
            self.acc[p, at] = v
            if store:
                self.zsend[p, at] = v.astype(BF16)

    def begin(self, p, own, by_rows):
        rid = self.rid + 8 * p

        def arrived(k, d):
            if by_rows:
                self.net.got(rid + k, self.rsib.at[p, rows(self.quarter(d), 32)])

        if not by_rows:
            for k in range(4):
                self.net.got(rid + k, self.rsib.at[p, :, pl.ds(512 * k, 512)])
        arrived(0, 2)
        self.total(2, p, own, True)
        s = self.quarter(2)
        self.to_chip(p, 0, self.zsend.at[p, rows(s, 16)], self.right())
        self.to_chip(p, 1, self.zsend.at[p, rows(s + 16, 16)], self.left())
        arrived(1, 1)
        self.total(1, p, own, True)
        self.to_chip(p, 4, self.zsend.at[p, rows(self.quarter(1) + 16, 16)], self.right())
        arrived(2, -1)
        self.total(-1, p, own, True)
        self.to_chip(p, 2, self.zsend.at[p, rows(self.quarter(-1), 16)], self.left())
        arrived(3, 0)
        self.total(0, p, own, False)

    def middle(self, p):
        for k, d, off, way in ((0, 1, 0, self.right()), (1, -1, 16, self.left())):
            self.net.got(self.rid + 8 * p + 4 + k, self.zrec.at[p, k])
            at = rows(self.quarter(d) + off, 16)
            self.zsend[p, at] = (self.acc[p, at] + self.zrec[p, k].astype(F32)).astype(BF16)
            self.to_chip(p, 3 + 2 * k, self.zsend.at[p, at], way)

    def finish(self, p, use):
        for part in (0, 1):
            self.net.got(self.rid + 8 * p + 6 + part, self.zrec.at[p, pl.ds(2 + 2 * part, 2)])
            v = self.acc[p, rows(self.quarter(0) + 16 * part, 16)]
            for k in (2 + 2 * part, 3 + 2 * part):
                v = v + self.zrec[p, k].astype(F32)
            use(p, 16 * part, v)

    def release(self):
        for sid in (*self.sib_sid, *self.z_sid):
            if sid in self.net.open:
                self.net.sent(sid)


class Share:
    def __init__(self, net, out):
        self.net, self.out = net, out
        self.sid = (net.send_id(), net.send_id())
        self.rid = net.recv_ids(8)

    def at(self, p, d, other=False, lo=0, n=32):
        m = lax.axis_index("mp")
        core = lax.rem(m, 2)
        if other:
            core = 1 - core
        return self.out.at[p, core, lax.rem(m // 2 + (d + 4), 4), pl.ds(lo, n)]

    def put(self, p, k, src, dst, index):
        own = k < 2 or (k == 3 and dst is None)
        dst = self.at(p, 0) if dst is None else dst
        whole = self.out.at[pl.ds(0, 2), 0, pl.ds(0, 3 if own else 4)]
        self.net.put(self.sid[0 if own else 1], whole, self.rid + 4 * p + k, src, dst, "mp", index)

    def got(self, p, k, ref):
        self.net.got(self.rid + 4 * p + k, ref)

    def begin(self, p, src=None):
        src = self.at(p, 0) if src is None else src
        self.put(p, 0, src, None, shifted("mp", 2))
        self.put(p, 1, src, None, shifted("mp", -2))
        self.put(p, 3, src, None, sibling())

    def middle(self, p):
        self.got(p, 0, self.at(p, -1))
        half = self.at(p, -1, False, 0, 16)
        self.put(p, 2, half, half, shifted("mp", 2))
        self.got(p, 1, self.at(p, 1))
        half = self.at(p, 1, False, 16, 16)
        self.put(p, 2, half, half, shifted("mp", -2))
        for d in (-1, 1):
            self.put(p, 3, self.at(p, d), self.at(p, d), sibling())

    def later(self, p):
        self.got(p, 2, self.at(p, 2))
        self.put(p, 3, self.at(p, 2), self.at(p, 2), sibling())

    def finish(self, p):
        self.got(p, 3, self.out.at[p, 1 - lax.rem(lax.axis_index("mp"), 2)])

    def release(self):
        for sid in self.sid:
            self.net.sent(sid)


class Gather:
    def __init__(self, net, own, size, region, whole):
        self.net, self.own, self.size, self.region, self.whole = net, own, size, region, whole
        self.sid, self.rid = net.send_id(), net.recv_ids(30)
        self.half, self.quarter = size // 2, size // 4

    def put(self, k, src, dst, axis, d):
        self.net.put(self.sid, self.whole, self.rid + k, src, dst, axis, shifted(axis, d))

    def got(self, k, ref):
        self.net.got(self.rid + k, ref)

    def idx(self, h, da, db):
        fa, sa = (("dp", "seq"), ("seq", "dp"))[h]
        c = {fa: shifted(fa, da), sa: shifted(sa, db)}
        return c["dp"] * 4 + c["seq"]

    def both(self, k, src, dst, axis):
        self.put(k, src, dst, axis, 1)
        self.put(k + 1, src, dst, axis, -1)

    def begin(self, h):
        for stage in (0, 1):
            axis = ("dp", "seq")[(h + stage) % 2]
            lo = h * self.half
            src = self.own.at[pl.ds(lo, self.half)]
            self.both(15 * h + 3 * stage, src, self.region(self.idx(h, 0, 0), lo, self.half), axis)

    def near(self):
        for h in (0, 1):
            fa, sa = (("dp", "seq"), ("seq", "dp"))[h]
            lo = h * self.half
            for k, d in ((0, -1), (1, 1)):
                p = self.region(self.idx(h, d, 0), lo, self.half)
                self.got(15 * h + k, p)
                part = self.region(self.idx(h, d, 0), lo + k * self.quarter, self.quarter)
                self.put(15 * h + 2, part, part, fa, -d)
                self.both(15 * h + 5 + 2 * k, p, p, sa)

    def far(self):
        for h in (0, 1):
            sa, lo = (("dp", "seq"), ("seq", "dp"))[h][1], h * self.half
            p = self.region(self.idx(h, 2, 0), lo, self.half)
            self.got(15 * h + 2, p)
            self.both(15 * h + 9, p, p, sa)

    def cross(self, k):
        d = (0, -1, 1, 2)[k]
        for h in (0, 1):
            sa, lo = (("dp", "seq"), ("seq", "dp"))[h][1], h * self.half
            for w, db in ((0, -1), (1, 1)):
                at = self.idx(h, d, db)
                self.got(15 * h + 3 + 2 * k + w, self.region(at, lo, self.half))
                part = self.region(at, lo + w * self.quarter, self.quarter)
                self.put(15 * h + 11 + k, part, part, sa, -db)

    def finish(self):
        for k, d in enumerate((0, -1, 1, 2)):
            for h in (0, 1):
                lo = h * self.half
                self.got(15 * h + 11 + k, self.region(self.idx(h, d, 2), lo, self.half))


def lanes(shape):
    return lax.broadcasted_iota(jnp.int32, shape, len(shape) - 1)


def swap_halves(v):
    lane = lanes(v.shape)
    return jnp.where(lane % HD < HD // 2, pltpu.roll(v, 96, 1), pltpu.roll(v, 32, 1))


def main_kernel(
    x_hbm, cot_hbm, parents, wa_hbm, wm_hbm, we_hbm, wr_hbm, gains, table_hbm,
    i_att, i_mrg, i_exp, i_red, mg, fg, sg,
    out, grad, o_att, o_mrg, o_exp, o_red, f_att, f_mrg, f_exp, f_red,
    o_gain, f_gain,
    g_red, g_gate, g_up, g_mrg, g_att,
    ra_red, ra_gate, ra_up, ra_mrg, ra_att,
    rb_red, rb_gate, rb_up, rb_mrg, rb_att,
    sa, wa, wm, xd, cot, n1, dgu, n2, hid,
    acc, sib, rsib, zrec, probs, kv_a, kv_b, q, att, datt, dkv, dkv_in, dpack,
    mid, dmid, stage, stage_exp, w_exp,
    gbuf, gs1, gs2, gs3, gs4, gs5, gtot, gtwo, gnew,
    send, recv, loc,
):
    net = Net(send, recv)
    m = lax.axis_index("mp")
    core, z = lax.rem(m, 2), m // 2
    seq = lax.axis_index("seq")
    other = 1 - core
    dp = lax.axis_index("dp")
    me = 4 * dp + seq
    hello(
        [("dp", shifted("dp", d)) for d in (1, 2, 3)]
        + [("seq", shifted("seq", d)) for d in (1, 2, 3)]
        + [("mp", shifted("mp", d)) for d in range(1, 8)]
    )
    kv = (kv_a, kv_b)
    kv_sid, kv_rid = (net.send_id(), net.send_id()), net.recv_ids(2)
    dkv_sid, dkv_rid = net.send_id(), net.recv_ids(2)
    fold = Fold(net, acc, rsib, sib, zrec)
    share_one, share_two, share_out, share_grad = Share(net, n2), Share(net, xd), Share(net, out), Share(net, grad)
    gain_sid, gain_rid = [net.send_id() for _ in range(5)], net.recv_ids(5)

    def gain_put(k, ref, count, src, dst, axis, d):
        net.put(gain_sid[k], ref.at[pl.ds(0, count)], gain_rid + k, src, dst, axis, shifted(axis, d))

    def gain_got(k, ref, count):
        net.got(gain_rid + k, ref.at[pl.ds(0, count)])


    def by_col(ref):
        return lambda i, lo, k: ref.at[pl.ds(lo, k), pl.ds(pl.multiple_of(128 * i, 128), 128)]

    all_red = Gather(net, g_red.at[dp, seq], 1024, by_col(f_red), f_red.at[:, pl.ds(0, 1920)])
    all_exp = Gather(net, w_exp, 128, lambda i, lo, k: f_exp.at[pl.ds(128 * i + lo, k)], f_exp.at[pl.ds(0, 1920)])
    all_mrg = Gather(net, g_mrg.at[dp, seq], 256, by_col(f_mrg), f_mrg.at[:, pl.ds(0, 1920)])
    all_att = Gather(net, g_att.at[dp, seq], 128, lambda i, lo, k: f_att.at[rows(128 * i + lo, k)], f_att.at[pl.ds(0, 1920)])
    s_red = Spread(net, g_red, ra_red, rb_red)
    s_gate = Spread(net, g_gate, ra_gate, rb_gate)
    s_up = Spread(net, g_up, ra_up, rb_up)
    s_mrg = Spread(net, g_mrg, ra_mrg, rb_mrg)
    s_att = Spread(net, g_att, ra_att, rb_att)

    def bring(k, src, dst):
        c = pltpu.make_async_copy(src, dst, loc.at[k])
        c.start()
        return c

    c_x = [bring(t, x_hbm.at[t], xd.at[t]) for t in (0, 1)]
    c_wa = bring(2, wa_hbm, wa)
    c_table = bring(9, table_hbm, stage.at[pl.ds(0, 2)])

    def all_here(ref, k):
        pltpu.make_async_copy(ref, ref, loc.at[k]).wait()

    both_gains = gains[...].astype(F32)
    gain_one, gain_two = both_gains[0:1, :], both_gains[1:2, :]

    def ancestors(t, b):
        p1 = parents[t, b]
        p2 = jnp.where(p1 >= 0, parents[t, jnp.maximum(p1, 0)], -1)
        p3 = jnp.where(p2 >= 0, parents[t, jnp.maximum(p2, 0)], -1)
        return p1, p2, p3

    def turns(t, i):
        ps = ancestors(t, 2 * seq + i)
        depth = sum(jnp.where(p >= 0, 1, 0) for p in ps)

        def pick(k):
            v = stage[k, 0:128]
            for n in (1, 2, 3):
                v = jnp.where(depth == n, stage[k, 128 * n : 128 * n + 128], v)
            return v

        return pick(0), pick(1)

    lower = lanes((128, 128)) < HD

    def own_kv(t, at):
        return kv[t].at[pl.ds(2 * at, 2)]

    for t in (0, 1):
        c_x[t].wait()
        if t == 0:
            c_wa.wait()
            c_table.wait()
        else:
            c_wm = bring(4, wm_hbm, wm)
            c_cot = bring(3, cot_hbm, cot)
            for k in range(16):
                pltpu.make_async_copy(wr_hbm.at[:, pl.ds(128 * k, 128)], g_red.at[k // 4, k % 4], loc.at[10]).start()
            for k in range(4):
                pltpu.make_async_copy(we_hbm.at[0, :, pl.ds(256 * k, 256)], sa.at[k], loc.at[11]).start()
            for k in range(16):
                pltpu.make_async_copy(we_hbm.at[1, pl.ds(128 * k, 128)], g_up.at[k // 4, k % 4], loc.at[12]).start()

        @pl.loop(0, 16, unroll=4)
        def _(i):
            v = xd[t, i // 8, (i // 2) % 4, rows(16 * (i % 2), 16)].astype(F32)
            r = lax.rsqrt(jnp.mean(v * v, axis=-1, keepdims=True) + NORM_EPS)
            n1[t, rows(16 * i, 16)] = (v * r * gain_one).astype(BF16)

        packed = dot(n1[t], wa[...])
        for i in (0, 1):
            c, s = turns(t, i)
            part = packed[128 * i : 128 * i + 128]
            for g in (0, 1):
                v = part[:, 128 * g : 128 * g + 128]
                q[t, i, g] = (v * c + swap_halves(v) * s).astype(BF16)
            v = part[:, 256:384]
            kv[t][2 * seq + i] = jnp.where(lower, v * c + swap_halves(v) * s, v).astype(BF16)
        if t == 0:
            hello_wait(13)
        for d in (1, 2, 3):
            net.put(kv_sid[t], kv[t].at[pl.ds(0, 6)], kv_rid + t, own_kv(t, seq), own_kv(t, seq), "seq", shifted("seq", d))

    def hidden_grad(j):
        w = jnp.concatenate([g_red[k // 4, k % 4, 256 * j : 256 * j + 256] for k in range(16)], axis=1)
        v = dot_nt(cot[...].reshape(512, D), w)
        high = v.astype(BF16)
        low = (v - high.astype(F32)).astype(BF16)
        cols = pl.ds(256 * j, 256)
        g_gate[0, :, :, cols] = high.reshape(4, 128, 256)
        g_gate[1, :, :, cols] = low.reshape(4, 128, 256)

    low_lane = lanes((512, 128)) < HD
    key_col = lanes((128, 512))
    query_row = lax.broadcasted_iota(jnp.int32, (128, 512), 0)

    def key_views(t, ids):
        both = jnp.concatenate([kv[t][jnp.maximum(c, 0)] for c in ids], axis=0).astype(F32)
        turned = pltpu.roll(both, HD, 1)
        zero = jnp.zeros_like(both)
        keys = [jnp.where(low_lane, both, zero).astype(BF16), jnp.where(low_lane, zero, turned).astype(BF16)]
        values = [jnp.where(low_lane, turned, zero).astype(BF16), jnp.where(low_lane, zero, both).astype(BF16)]
        return keys, values

    def attention(t):
        net.got(kv_rid + t, kv[t].at[pl.ds(0, 6)])
        for i in (0, 1):
            b = 2 * seq + i
            ps = ancestors(t, b)
            keys, values = key_views(t, (b, *ps))
            seen = (key_col < 128) & (key_col <= query_row)
            for k, p in enumerate(ps):
                inside = (key_col >= 128 * (k + 1)) & (key_col < 128 * (k + 2))
                seen = seen | (inside & (p >= 0))
            for g in (0, 1):
                total = jnp.zeros((128, 128), F32)
                for h in (0, 1):
                    scores = dot_nt(q[t, i, g], keys[h]) * HD**-0.5
                    scores = jnp.where(seen, scores, MASK_FILL)
                    e = jnp.exp(scores - jnp.max(scores, axis=-1, keepdims=True))
                    p = (e / jnp.sum(e, axis=-1, keepdims=True)).astype(BF16)
                    probs[2 * t + i, 2 * g + h] = p
                    total = total + dot(p, values[h])
                att[t, 128 * i : 128 * i + 128, 128 * g : 128 * g + 128] = total.astype(BF16)

    def mine(p, at):
        return acc[p, at]

    def merge(p):
        for k in range(4):
            cols = pl.ds(512 * k, 512)
            sib[p, :, cols] = dot(att[p, rows(128 * other, 128)], wm[:, cols]).astype(BF16)
        fold.send_rows(p, lambda at: sib.at[p, at])
        for k in range(4):
            cols = pl.ds(512 * k, 512)
            acc[p, :, cols] = dot(att[p, rows(128 * core, 128)], wm[:, cols])

    def to_normed(p, r, v):
        x_own = xd[p, core, z, r : r + 16].astype(F32)
        total = x_own + v
        mid[p, r : r + 16] = total
        rms = lax.rsqrt(jnp.mean(total * total, axis=-1, keepdims=True) + NORM_EPS)
        n2[p, core, z, r : r + 16] = (total * rms * gain_two).astype(BF16)


    def feed_dot(p, j):
        lo = 1024 * (j % 2)
        for k, w in ((0, sa[j]), (1, g_up[:, :, :, 256 * j : 256 * j + 256].reshape(D, 256))):
            v = dot(n2[p].reshape(256, D), w)
            acc[p, :, lo + 256 * k : lo + 256 * k + 256] = v[0:128]
            acc[p, :, lo + 512 + 256 * k : lo + 768 + 256 * k] = v[128:256]

    def feed_rest(p, j):
        cols, cols_up = pl.ds(256 * j, 256), pl.ds(1024 + 256 * j, 256)
        for half in (0, 1):
            lo = 1024 * (j % 2) + 512 * half
            for i in range(4):
                at = pl.ds(32 * i, 32)
                gate, up = acc[p, at, lo : lo + 256], acc[p, at, lo + 256 : lo + 512]
                dh = g_gate[0, 2 * p + half, at, cols].astype(F32) + g_gate[1, 2 * p + half, at, cols].astype(F32)
                sig = 0.5 + 0.5 * jnp.tanh(0.5 * gate)
                act = gate * sig
                to = pl.ds(128 * half + 32 * i, 32)
                hid[p, to, cols] = (act * up).astype(BF16)
                dgu[p, to, cols] = (dh * up * (sig + act * (1.0 - sig))).astype(BF16)
                dgu[p, to, cols_up] = (dh * act).astype(BF16)

    def feed(p, between):
        feed_dot(p, 0)
        for j in (1, 2, 3):
            feed_dot(p, j)
            feed_rest(p, j - 1)
            if j == 1:
                between()
        feed_rest(p, 3)

    attention(0)
    c_wm.wait()
    merge(0)
    attention(1)
    fold.sent(0)
    fold.begin(0, mine, True)
    merge(1)
    c_cot.wait()
    all_here(g_red, 10)
    hidden_grad(0)
    fold.middle(0)
    fold.sent(1)
    fold.begin(1, mine, True)
    hidden_grad(1)
    fold.finish(0, to_normed)
    share_one.begin(0)
    fold.middle(1)
    hidden_grad(2)
    share_one.middle(0)
    fold.finish(1, to_normed)
    share_one.begin(1)
    hidden_grad(3)
    all_here(sa, 11)
    all_here(g_up, 12)
    share_one.later(0)
    share_one.middle(1)
    share_one.finish(0)
    feed(0, lambda: share_one.later(1))
    share_one.finish(1)
    fold.release()
    feed(1, lambda: None)

    def reduce_grad(a):
        @pl.loop(0, 2)
        def _(k):
            cols = pl.ds(pl.multiple_of(512 * a + 256 * k, 256), 256)
            v = dot_tn(hid[...].reshape(512, 1024), cot[:, :, :, :, cols].reshape(512, 256)).astype(BF16)
            g_red[a, 2 * k] = v[:, 0:128]
            g_red[a, 2 * k + 1] = v[:, 128:256]

    reduce_grad(shifted("dp", 2))
    s_red.step0_far(0)

    @pl.loop(0, 2)
    def _(k):
        reduce_grad(lax.rem(dp + 1 + 2 * k, 4))

    s_red.step0_near(0)
    reduce_grad(dp)
    s_red.step0_far(1)
    s_red.step0_near(1)
    def expand_grad(dst, first):
        @pl.loop(0, 4)
        def _(a):
            left = n2[:, :, :, :, pl.ds(pl.multiple_of(512 * a, 512), 512)].reshape(512, 512)
            for k in (0, 1):
                v = dot_tn(left, dgu[:, :, first + 512 * k : first + 512 * k + 512].reshape(512, 512))
                dst[a, :, :, 512 * k : 512 * k + 512] = v.astype(BF16).reshape(4, 128, 512)

    expand_grad(g_gate, 0)
    s_gate.step0()

    def norm_grad(p):
        for k in range(4):
            for j in (2 * k, 2 * k + 1):
                cols = pl.ds(256 * j, 256)
                w_gate = jnp.concatenate([sa[i, 256 * j : 256 * j + 256] for i in range(4)], axis=1)
                w_up = g_up[j // 2, 2 * (j % 2) : 2 * (j % 2) + 2].reshape(256, 1024)
                v = dot_nt(dgu[p], jnp.concatenate([w_gate, w_up], axis=1))
                first, second = v[0:128], v[128:256]
                sib[p, :, cols] = jnp.where(core == 0, second, first).astype(BF16)
                acc[p, :, cols] = jnp.where(core == 0, first, second)
            fold.send_columns(p, k, sib.at[p])

    def to_branch(p, r, v):
        total = mid[p, r : r + 16]
        rms = lax.rsqrt(jnp.mean(total * total, axis=-1, keepdims=True) + NORM_EPS)
        u = v * gain_two
        back_vals = rms * u - total * (rms * rms * rms) * jnp.mean(u * total, axis=-1, keepdims=True)
        full = cot[p, core, z, r : r + 16].astype(F32) + back_vals
        dmid[p, r : r + 16] = full
        xd[p, core, z, r : r + 16] = full.astype(BF16)
        gbuf[1:2, :] = gbuf[1:2, :] + jnp.sum(v * total * rms, axis=0, keepdims=True)

    gbuf[...] = jnp.zeros_like(gbuf)
    norm_grad(0)
    s_red.step1()
    fold.sent(0)
    fold.begin(0, mine, False)
    norm_grad(1)
    for k in range(8):
        half = sa.at[k // 2, pl.ds(1024 * (k % 2), 1024)]
        pltpu.make_async_copy(wr_hbm.at[:, pl.ds(256 * k, 256)], half, loc.at[13]).start()
    expand_grad(g_up, 1024)
    s_up.step0()
    fold.middle(0)
    fold.sent(1)
    fold.begin(1, mine, False)
    s_gate.step1()
    fold.finish(0, to_branch)
    share_two.begin(0)
    fold.middle(1)

    all_here(sa, 13)

    @pl.loop(0, 4)
    def _(j):
        for k in (0, 1):
            v = dot(hid[...].reshape(512, 1024), sa[j, 1024 * k : 1024 * k + 1024])
            dgu[:, :, pl.ds(pl.multiple_of(512 * j + 256 * k, 256), 256)] = v.astype(BF16).reshape(2, 256, 256)

    fold.finish(1, to_branch)
    share_two.begin(1)

    x_slot = lax.rem(z + 1, 4)
    c_xo = [bring(p, x_hbm.at[p, core, z], cot.at[p, core, x_slot]) for p in (0, 1)]
    for k in (0, 1, 2):
        pltpu.make_async_copy(i_exp[k], stage_exp.at[k], loc.at[10]).start()
    share_two.middle(0)
    share_two.middle(1)
    share_two.later(0)
    s_red.step2()
    share_two.finish(0)

    dbr = xd

    def branch_back(t):
        datt[t] = dot_nt(dbr[t].reshape(256, D), wm[...]).astype(BF16)

    branch_back(0)
    share_two.later(1)
    dkv[...] = jnp.zeros_like(dkv)

    def attention_back(t, i):
        u = 2 * t + i
        b = 2 * seq + i
        ps = ancestors(t, b)
        keys, values = key_views(t, (b, *ps))
        c, s = turns(t, i)
        at = rows(128 * i, 128)
        dk = [jnp.zeros((512, 128), F32), jnp.zeros((512, 128), F32)]
        dv = [jnp.zeros((512, 128), F32), jnp.zeros((512, 128), F32)]
        for g in (0, 1):
            dq = jnp.zeros((128, 128), F32)
            da = datt[t, at, 128 * g : 128 * g + 128]
            for h in (0, 1):
                p = probs[u, 2 * g + h]
                pf = p.astype(F32)
                dp = dot_nt(da, values[h])
                inner = jnp.sum(pf * dp, axis=-1, keepdims=True)
                ds = (pf * (dp - inner)).astype(BF16)
                dq = dq + dot(ds, keys[h])
                dk[h] = dk[h] + dot_tn(ds, q[t, i, g])
                dv[h] = dv[h] + dot_tn(p, da)
            dq = dq * HD**-0.5
            dpack[t, at, 128 * g : 128 * g + 128] = (dq * c - swap_halves(dq) * s).astype(BF16)
        both = jnp.where(
            low_lane, (dk[0] + pltpu.roll(dk[1], HD, 1)) * HD**-0.5, pltpu.roll(dv[0], HD, 1) + dv[1]
        )
        dkv[t, b] = dkv[t, b] + both[0:128]
        for blk in range(8):
            v = dkv[t, blk]
            for k, p in enumerate(ps):
                v = v + both[128 * (k + 1) : 128 * (k + 2)] * jnp.where(p == blk, 1.0, 0.0)
            dkv[t, blk] = v

    def send_dkv(t):
        for c in range(8):
            probs[2 * t, c // 4, :, 128 * (c % 4) : 128 * (c % 4) + 128] = dkv[t, c].astype(BF16)
        for d in (1, 2, 3):
            peer = shifted("seq", d)
            src = probs.at[2 * t, peer // 2, :, pl.ds(pl.multiple_of(256 * lax.rem(peer, 2), 256), 256)]
            net.put(dkv_sid, dkv_in, dkv_rid + t, src, dkv_in.at[d - 1, t], "seq", peer)

    def add_dkv(t):
        net.got(dkv_rid + t, dkv_in.at[pl.ds(0, 3), t])
        for i in (0, 1):
            v = dkv[t, 2 * seq + i]
            for d in (0, 1, 2):
                v = v + dkv_in[d, t, :, 128 * i : 128 * i + 128].astype(F32)
            c, s = turns(t, i)
            v = jnp.where(lower, v * c - swap_halves(v) * s, v)
            dpack[t, 128 * i : 128 * i + 128, 256:384] = v.astype(BF16)

    for i in (0, 1):
        attention_back(0, i)
    send_dkv(0)
    share_two.finish(1)
    fold.release()

    def down_rows(p, at):
        return dgu[p, pl.ds(pl.multiple_of(128 * core + at.start, 16), 16)]

    for p in (0, 1):
        fold.send_rows(p, lambda at: dgu.at[p, rows(128 * other + at.start, 32)])
    branch_back(1)
    for i in (0, 1):
        attention_back(1, i)
    send_dkv(1)
    s_up.step1()

    @pl.loop(0, 8)
    def _(j):
        cols = pl.ds(pl.multiple_of(256 * j, 256), 256)
        v = dot_tn(att[...].reshape(512, 256), dbr[:, :, :, :, cols].reshape(512, 256))
        g_mrg[j // 2, 2 * (j % 2)] = v[:, 0:128].astype(BF16)
        g_mrg[j // 2, 2 * (j % 2) + 1] = v[:, 128:256].astype(BF16)

    s_mrg.step0()
    fold.begin(0, down_rows, True)
    fold.begin(1, down_rows, True)
    s_gate.step2()
    add_dkv(0)
    add_dkv(1)

    @pl.loop(0, 4)
    def _(a):
        left = n1[:, :, pl.ds(pl.multiple_of(512 * a, 512), 512)].reshape(512, 512)
        g_att[a] = dot_tn(left, dpack[...].reshape(512, 384)).astype(BF16).reshape(4, 128, 384)

    s_att.step0()
    s_red.step3()
    for k in (0, 1, 2):
        pltpu.make_async_copy(i_mrg[k], dkv.at[0, pl.ds(2 * k, 2)], loc.at[12]).start()
        pltpu.make_async_copy(i_red[k].at[pl.ds(0, 512)], stage.at[k], loc.at[11]).start()
    fold.middle(0)
    fold.middle(1)
    share_one.release()

    @pl.loop(0, 8)
    def _(j):
        v = dot_nt(dpack[...].reshape(512, 384), wa[rows(256 * j, 256)])
        n2[:, :, :, :, pl.ds(pl.multiple_of(256 * j, 256), 256)] = v.astype(BF16).reshape(2, 2, 4, 32, 256)

    def to_out(p, r, v):
        cot[p, core, z, r : r + 16] = (mid[p, r : r + 16] + v).astype(BF16)

    s_mrg.step1()

    def renew(state, at, grads):
        new = adamw(state[0][at], state[1][at], state[2][at], grads)[0]
        state[1][at] = grads
        return new

    flat_stage = [stage.at[k] for k in (0, 1, 2)]

    def use_red(h):
        def use(r, v):
            new = renew(flat_stage, rows(r - 512 * h, 128), v)
            g_red[dp, seq, rows(r, 128)] = new.astype(BF16)

        return use

    all_here(stage, 11)
    s_red.step4(0, use_red(0))
    all_red.begin(0)
    c_red = [bring(4, stage.at[1], o_red.at[pl.ds(0, 512)])]
    local = [bring(14, g_red.at[dp, seq, pl.ds(0, 512)], f_red.at[pl.ds(0, 512), pl.ds(pl.multiple_of(128 * me, 128), 128)])]
    s_up.step2()
    s_att.step1()
    s_gate.step3()
    l_out = []
    for p in (0, 1):
        fold.finish(p, to_out)
        share_out.begin(p, cot.at[p, core, z])
        l_out.append(bring(2 + p, cot.at[p, core, z], out.at[p, core, z]))
    for c in c_red:
        c.wait()
    for k in (0, 1, 2):
        pltpu.make_async_copy(i_red[k].at[pl.ds(512, 512)], stage.at[k], loc.at[11]).start()
    s_mrg.step2()
    all_here(stage, 11)
    s_red.step4(1, use_red(1))
    all_red.begin(1)
    c_red = [bring(4, stage.at[1], o_red.at[pl.ds(512, 512)])]
    local.append(bring(15, g_red.at[dp, seq, pl.ds(512, 512)], f_red.at[pl.ds(512, 512), pl.ds(pl.multiple_of(128 * me, 128), 128)]))
    s_up.step3()
    s_att.step2()
    share_out.middle(0)
    share_out.middle(1)

    def use_expand(j):
        def use(r, v):
            at = rows(r, 16)
            new = adamw(stage_exp[0, at, j, :], stage_exp[1, at, j, :], stage_exp[2, at, j, :], v)[0]
            stage_exp[0, at, j, :] = new
            stage_exp[1, at, j, :] = v

        return use

    all_here(stage_exp, 10)
    s_gate.step4(0, use_expand(0))
    s_gate.step4(1, use_expand(0))
    for c in c_red:
        c.wait()
    for k in (0, 1, 2):
        for a in (0, 1, 2):
            pltpu.make_async_copy(
                i_att[k].at[:, pl.ds(128 * a, 128)], stage.at[k, pl.ds(128 * a, 128)], loc.at[11]
            ).start()

    def norm_rows(p, at):
        return n2[p, core, at.start // 32, pl.ds(pl.multiple_of(at.start % 32, 16), 16)]

    def fold_begin(p):
        fold.begin(p, norm_rows, True)

    all_red.near()
    s_mrg.step3()
    s_att.step3()
    share_out.later(0)
    share_out.later(1)
    for h in (0, 1):
        s_up.step4(h, use_expand(1))
        for i in (0, 1, 2, 3):
            at = rows(64 * h + 16 * i, 16)
            w_exp[at] = stage_exp[0, at].astype(BF16)
        all_exp.begin(h)
    c_exp = [bring(6, stage_exp.at[1], o_exp)]
    local.append(bring(9, w_exp, f_exp.at[pl.ds(128 * me, 128)]))
    def use_mrg(r, v):
        new = renew([dkv.at[0, 2 * k + r // 128] for k in (0, 1, 2)], rows(r % 128, 64), v)
        g_mrg[dp, seq, rows(r, 64)] = new.astype(BF16)

    all_here(dkv.at[0, pl.ds(0, 6)], 12)
    for h in (0, 1):
        s_mrg.step4(h, use_mrg)
        all_mrg.begin(h)
    c_mrg = [bring(7, dkv.at[0, pl.ds(2, 2)], o_mrg)]
    local.append(bring(8, g_mrg.at[dp, seq], f_mrg.at[:, pl.ds(pl.multiple_of(128 * me, 128), 128)]))
    all_here(stage.at[:, pl.ds(0, 384)], 11)

    def use_att(r, v):
        parts = []
        for a in (0, 1, 2):
            parts.append(renew(flat_stage, rows(128 * a + r, 32), v[:, 128 * a : 128 * a + 128]))
        g_att[dp, seq, rows(r, 32)] = jnp.concatenate(parts, axis=1).astype(BF16)

    for h in (0, 1):
        s_att.step4(h, use_att)
        all_att.begin(h)
    c_att = [bring(16 + a, stage.at[1, pl.ds(128 * a, 128)], o_att.at[:, pl.ds(128 * a, 128)]) for a in (0, 1, 2)]
    local.append(bring(5, g_att.at[dp, seq], f_att.at[rows(128 * me, 128)]))
    share_out.finish(0)
    share_out.finish(1)
    fold.release()
    for p in (0, 1):
        fold.send_rows(p, lambda at: n2.at[p, other, at.start // 32])
    all_red.far()
    all_exp.near()
    fold_begin(0)
    fold_begin(1)
    all_red.cross(0)
    all_red.cross(1)
    all_mrg.near()
    all_att.near()
    fold.middle(0)
    fold.middle(1)
    for c in c_xo:
        c.wait()

    def to_grad(p, r, v):
        x = cot[p, core, x_slot, r : r + 16].astype(F32)
        rms = lax.rsqrt(jnp.mean(x * x, axis=-1, keepdims=True) + NORM_EPS)
        u = v * gain_one
        back_vals = rms * u - x * (rms * rms * rms) * jnp.mean(u * x, axis=-1, keepdims=True)
        cot[p, other, z, r : r + 16] = (dmid[p, r : r + 16] + back_vals).astype(BF16)
        gbuf[0:1, :] = gbuf[0:1, :] + jnp.sum(v * x * rms, axis=0, keepdims=True)

    all_exp.far()
    all_red.cross(2)
    for p in (0, 1):
        fold.finish(p, to_grad)
        share_grad.begin(p, cot.at[p, other, z])
    l_grad = [bring(p, cot.at[p, other, z], grad.at[p, core, z]) for p in (0, 1)]
    gs1[m] = gbuf[...]
    for d in range(1, 8):
        gain_put(0, gs1, 7, gbuf, gs1.at[m], "mp", d)
    all_red.cross(3)
    all_exp.cross(0)
    all_mrg.far()
    all_att.far()
    gain_got(0, gs1, 7)
    total = gs1[0]
    for k in range(1, 8):
        total = total + gs1[k]
    gtot[...] = total

    def piece(i, n):
        return pl.ds(pl.multiple_of(i * n, 128), n)

    gs2[dp] = gtot[:, piece(dp, 512)]
    for d in (1, 2, 3):
        gain_put(1, gs2, 3, gtot.at[:, piece(shifted("dp", d), 512)], gs2.at[dp], "dp", d)
    share_grad.middle(0)
    share_grad.middle(1)
    all_exp.cross(1)
    gain_got(1, gs2, 3)
    gtwo[...] = gs2[0] + gs2[1] + gs2[2] + gs2[3]
    gs3[seq] = gtwo[:, piece(seq, 128)]
    for d in (1, 2, 3):
        gain_put(2, gs3, 3, gtwo.at[:, piece(shifted("seq", d), 128)], gs3.at[seq], "seq", d)
    share_grad.later(0)
    share_grad.later(1)
    all_mrg.cross(0)
    all_att.cross(0)
    gain_got(2, gs3, 3)
    shard = gs3[0] + gs3[1] + gs3[2] + gs3[3]
    new = adamw(mg[...], fg[...], sg[...], shard)[0]
    o_gain[...] = shard
    gnew[...] = new
    gs4[seq] = new
    for d in (1, 2, 3):
        gain_put(3, gs4, 3, gnew, gs4.at[seq], "seq", d)
    all_exp.cross(2)
    all_mrg.cross(1)
    all_att.cross(1)
    gain_got(3, gs4, 3)
    gs5[dp] = gs4[...]
    for d in (1, 2, 3):
        gain_put(4, gs5, 3, gs4, gs5.at[dp], "dp", d)
    all_exp.cross(3)
    for k in (2, 3):
        all_mrg.cross(k)
        all_att.cross(k)
    gain_got(4, gs5, 3)
    for a in range(4):
        for b in range(4):
            lo = 128 * (4 * a + b)
            f_gain[:, lo : lo + 128] = gs5[a, b].astype(BF16)
    share_grad.finish(0)
    share_grad.finish(1)
    for g in (all_red, all_exp, all_mrg, all_att):
        g.finish()
    for c in local + l_out + l_grad + c_exp + c_mrg + c_att:
        c.wait()
    net.drain()


def main_call(x, cot, parents, wa, wm, we, wr, gains, table, states, gain_states):
    kinds = [(1024, 128), (128, 1024), (128, 1024), (256, 128), (128, 384)]
    vm, sds = pltpu.VMEM, jax.ShapeDtypeStruct
    scratch = (
        [vm((4, 4, n, c), BF16) for n, c in kinds]
        + [vm((2, 6, 4, n // 4, c), BF16) for n, c in kinds]
        + [vm((2, 6, n // 4, c), BF16) for n, c in kinds]
        + [
            vm((4, 2048, 256), BF16),
            vm((2048, 384), BF16),
            vm((256, 2048), BF16),
            vm((2, 2, 4, 32, D), BF16),
            vm((2, 2, 4, 32, D), BF16),
            vm((2, 256, D), BF16),
            vm((2, 256, D), BF16),
            vm((2, 2, 4, 32, D), BF16),
            vm((2, 256, 1024), BF16),
            vm((2, 128, D), F32),
            vm((2, 128, D), BF16),
            vm((2, 128, D), BF16),
            vm((2, 6, 16, D), BF16),
            vm((4, 4, 128, 512), BF16),
            vm((8, 128, 128), BF16),
            vm((8, 128, 128), BF16),
            vm((2, 2, 2, 128, 128), BF16),
            vm((2, 256, 256), BF16),
            vm((2, 256, 256), BF16),
            vm((2, 8, 128, 128), F32),
            vm((3, 2, 128, 256), BF16),
            vm((2, 256, 384), BF16),
            vm((2, 32, D), F32),
            vm((2, 32, D), F32),
            vm((3, 512, 128), F32),
            vm((3, 128, 2, 1024), F32),
            vm((128, 2, 1024), BF16),
            vm((2, D), F32),
            vm((8, 2, D), F32),
            vm((4, 2, 512), F32),
            vm((4, 2, 128), F32),
            vm((4, 2, 128), F32),
            vm((4, 4, 2, 128), F32),
            vm((2, D), F32),
            vm((2, 512), F32),
            vm((2, 128), F32),
            pltpu.SemaphoreType.DMA((36,)),
            pltpu.SemaphoreType.DMA((260,)),
            pltpu.SemaphoreType.DMA((20,)),
        ]
    )
    rows_out = sds((2, 2, 4, 32, D), BF16)
    shards = [sds((128, 384), F32), sds((2, 128, 128), F32), sds((128, 2, 1024), F32), sds((1024, 128), F32)]
    fulls = [sds((D, 384), BF16), sds((256, D), BF16), sds((D, 2, 1024), BF16), sds((1024, D), BF16)]
    out_shape = [rows_out, rows_out, *shards, *fulls, sds((2, 128), F32), sds((2, D), BF16)]
    vspec = pl.BlockSpec(memory_space=pltpu.VMEM)
    hbm = pl.BlockSpec(memory_space=pl.ANY)
    return pl.pallas_call(
        main_kernel,
        out_shape=out_shape,
        in_specs=[hbm, hbm, pl.BlockSpec(memory_space=pltpu.SMEM), hbm, hbm, hbm, hbm, vspec, hbm]
        + [[hbm] * 3] * 4
        + [vspec] * 3,
        out_specs=[hbm] * 10 + [vspec] * 2,
        scratch_shapes=scratch,
        compiler_params=pltpu.CompilerParams(
            collective_id=1, has_side_effects=True, vmem_limit_bytes=64 * 2**20 - 65536
        ),
    )(x, cot, parents, wa, wm, we, wr, gains, table, *states, *gain_states)


PARTS = (2, 2, 1, 1, 4, 2, 1)


def tail_kernel(*refs):
    groups, copies, refs = refs[:20], refs[20:27], refs[27:]
    outs, copied, refs = refs[:15], refs[15:22], refs[22:]
    held, through, (sem_in, sem_out, sem_a, sem_b) = refs[:20], refs[20:27], refs[27:]
    reads = [pltpu.make_async_copy(src, dst, sem_a.at[k]) for k, (src, dst) in enumerate(zip(groups, held))]
    there, back = [], []
    for k, parts in enumerate(PARTS):
        size = copies[k].shape[0] // parts
        for i in range(parts):
            at, j = pl.ds(size * i, size), len(there)
            there.append(pltpu.make_async_copy(copies[k].at[at], through[k].at[at], sem_in.at[j]))
            back.append(pltpu.make_async_copy(through[k].at[at], copied[k].at[at], sem_out.at[j]))
    for c in there[:4]:
        c.start()
    for c in reads:
        c.start()
    for c in there[4:]:
        c.start()
    for c, e in zip(there[:4], back[:4]):
        c.wait()
        e.start()
    writes = []
    for k in range(5):
        for c in reads[4 * k : 4 * k + 4]:
            c.wait()
        master, first, second, grads = held[4 * k : 4 * k + 4]
        steps = 8 if k < 4 else 1
        size = master.shape[0] // steps

        @pl.loop(0, steps)
        def _(i):
            at = pl.ds(pl.multiple_of(size * i, size), size)
            master[at], first[at], second[at] = adamw(master[at], first[at], second[at], grads[at])

        for i in range(3):
            c = pltpu.make_async_copy(held[4 * k + i], outs[3 * k + i], sem_b.at[3 * k + i])
            c.start()
            writes.append(c)
    for c, e in zip(there[4:], back[4:]):
        c.wait()
        e.start()
    for c in writes + back:
        c.wait()


def tail_call(groups, results):
    flat = [v for g in groups for v in g]
    vm, sds = pltpu.VMEM, jax.ShapeDtypeStruct
    hbm = pl.BlockSpec(memory_space=pl.ANY)
    n = sum(PARTS)
    done = pl.pallas_call(
        tail_kernel,
        in_specs=[hbm] * 27,
        out_specs=[hbm] * 22,
        out_shape=[sds(g[0].shape, F32) for g in groups for _ in range(3)] + [sds(v.shape, v.dtype) for v in results],
        scratch_shapes=[vm(v.shape, F32) for v in flat]
        + [vm(v.shape, v.dtype) for v in results]
        + [pltpu.SemaphoreType.DMA((k,)) for k in (n, n, 20, 15)],
        compiler_params=pltpu.CompilerParams(vmem_limit_bytes=64 * 2**20 - 65536),
    )(*flat, *results)
    return [done[3 * k : 3 * k + 3] for k in range(5)], done[15:]


def rotary_table():
    inv = ROPE_BASE ** (-2.0 * np.arange(HD // 2, dtype=np.float32) / HD)
    angle = np.arange(512, dtype=np.float32)[:, None] * inv.astype(np.float32)[None, :]
    c, s = np.cos(angle), np.sin(angle)
    both = np.stack([np.concatenate([c, c, c, c], 1), np.concatenate([-s, s, -s, s], 1)])
    return both.astype(np.float32)


def on_device(
    inputs, cotangent, parents, weight_attend, weight_merge, weight_expand, weight_reduce, gains,
    master_attend, master_merge, master_expand, master_reduce, master_gains,
    first_attend, first_merge, first_expand, first_reduce, first_gains,
    second_attend, second_merge, second_expand, second_reduce, second_gains,
):
    x = inputs.reshape(2, 2, 4, 32, D)
    cot = cotangent.reshape(2, 2, 4, 32, D)
    we = weight_expand.transpose(1, 0, 2)
    states = [
        [master_attend, first_attend, second_attend],
        [v.reshape(2, 128, 128) for v in (master_merge, first_merge, second_merge)],
        [master_expand, first_expand, second_expand],
        [master_reduce, first_reduce, second_reduce],
    ]
    gain_states = [master_gains, first_gains, second_gains]
    out, grad, g_att, g_mrg, g_exp, g_red, f_att, f_mrg, f_exp, f_red, g_gain, f_gain = main_call(
        x, cot, parents, weight_attend, weight_merge, we, weight_reduce, gains, jnp.asarray(rotary_table()), states, gain_states
    )
    states[1] = [master_merge, first_merge, second_merge]
    sums = (g_att, g_mrg.reshape(256, 128), g_exp, g_red, g_gain)
    results = [out.reshape(512, D), grad.reshape(512, D), f_att, f_mrg, f_exp, f_red, f_gain]
    (s_att, s_mrg, s_exp, s_red, s_gain), results = tail_call(
        [[*v, g] for v, g in zip((*states, gain_states), sums)], results
    )
    out, grad, f_att, f_mrg, f_exp, f_red, f_gain = results
    return (
        out.reshape(2, 256, D), grad.reshape(2, 256, D),
        s_att[0], s_mrg[0], s_exp[0], s_red[0], s_gain[0],
        s_att[1], s_mrg[1], s_exp[1], s_red[1], s_gain[1],
        s_att[2], s_mrg[2], s_exp[2], s_red[2], s_gain[2],
        f_att, f_mrg, f_exp, f_red, f_gain,
    )


def solution(mesh):
    both = ("dp", "seq")
    states = (P(both, "mp"), P("mp", both), P(both, None, "mp"), P("mp", both), P(None, both))
    weights = (P(None, "mp"), P("mp", None), P(None, None, "mp"), P("mp", None), P())
    tokens = P("dp", "seq", None)
    return jax.shard_map(
        on_device,
        mesh=mesh,
        in_specs=(tokens, tokens, P("dp", None), *weights, *states, *states, *states),
        out_specs=(tokens, tokens, *states, *states, *states, *weights),
        check_vma=False,
    )
```

```python
import functools

import jax
import jax.numpy as jnp
import numpy as np
from jax import lax
from jax.experimental import pallas as pl
from jax.experimental.pallas import tpu as pltpu
from jax.sharding import PartitionSpec as P

MESH = pl.DeviceIdType.MESH
F32 = jnp.float32
BF16 = jnp.bfloat16
D = 2048
HD = 64
STEP = 5
NORM_EPS = 1e-05
ROPE_BASE = 500000.0
MASK_FILL = -1e30
BETA_ONE = 0.5
BETA_TWO = 0.5
ADAM_EPS = 1e-08
LEARN_RATE = 0.005
DECAY_RATE = 0.1
FIX_ONE = 1.0 - BETA_ONE**STEP
FIX_TWO = 1.0 - BETA_TWO**STEP
SIZES = {"dp": 4, "seq": 4, "mp": 8}


def adamw(master, first, second, grad_vals):
    momentum = BETA_ONE * first + (1.0 - BETA_ONE) * grad_vals
    variance = BETA_TWO * second + (1.0 - BETA_TWO) * grad_vals * grad_vals
    direction = momentum / FIX_ONE / (jnp.sqrt(variance / FIX_TWO) + ADAM_EPS)
    renewed = master - LEARN_RATE * (direction + DECAY_RATE * master)
    return (renewed, momentum, variance)


def dot(a, b):
    return lax.dot_general(a, b, (((1,), (0,)), ((), ())), preferred_element_type=F32)


def dot_nt(a, b):
    return lax.dot_general(a, b, (((1,), (1,)), ((), ())), preferred_element_type=F32)


def dot_tn(a, b):
    return lax.dot_general(a, b, (((0,), (0,)), ((), ())), preferred_element_type=F32)


def shifted(axis, delta):
    n = SIZES[axis]
    return lax.rem(lax.axis_index(axis) + (delta + n), n)


def sibling():
    m = lax.axis_index("mp")
    return m + 1 - 2 * lax.rem(m, 2)


def rows(start, n):
    return pl.ds(pl.multiple_of(start, 16), n)


class Net:
    def __init__(self, send, recv):
        self.send, self.recv = send, recv
        self.sends, self.recvs = 0, 0
        self.open = {}

    def send_id(self):
        self.sends += 1
        assert self.sends <= self.send.shape[0]
        return self.sends - 1

    def recv_ids(self, n):
        self.recvs += n
        assert self.recvs <= self.recv.shape[0]
        return self.recvs - n

    def put(self, sid, whole, rid, src, dst, axis, index):
        pltpu.make_async_remote_copy(
            src_ref=src,
            dst_ref=dst,
            send_sem=self.send.at[sid],
            recv_sem=self.recv.at[rid],
            device_id={axis: index},
            device_id_type=MESH,
        ).start()
        self.open[sid] = whole

    def stub(self, sid, rid, ref):
        return pltpu.make_async_remote_copy(
            src_ref=ref,
            dst_ref=ref,
            send_sem=self.send.at[sid],
            recv_sem=self.recv.at[rid],
            device_id={"dp": shifted("dp", 1)},
            device_id_type=MESH,
        )

    def got(self, rid, ref):
        self.stub(0, rid, ref).wait_recv()

    def sent(self, sid):
        self.stub(sid, 0, self.open.pop(sid)).wait_send()

    def drain(self):
        for sid in sorted(self.open):
            self.sent(sid)


def hello(peers):
    sem = pltpu.get_barrier_semaphore()
    for axis, index in peers:
        pl.semaphore_signal(sem, inc=1, device_id={axis: index}, device_id_type=MESH)


def hello_wait(n):
    pl.semaphore_wait(pltpu.get_barrier_semaphore(), n)


class Spread:
    def __init__(self, net, own, first, second):
        self.net, self.own, self.r1, self.r2 = net, own, first, second
        self.size, self.cols = own.shape[2], own.shape[3]
        self.q = self.size // 4
        self.sid = (net.send_id(), net.send_id())
        self.rid = net.recv_ids(16)
        self.chunk = min(self.q, max(16, 16384 // self.cols))

    def put(self, stage, h, slot, src, d):
        axis = self.axes(h)[stage]
        rid = self.rid + 8 * stage + 4 * h + (0, 1, 2, 2, 3, 3)[slot]
        to = (self.r1, self.r2)[stage]
        self.net.put(self.sid[stage], to, rid, src, to.at[h, slot], axis, shifted(axis, d))

    def got(self, stage, h, k):
        ref = (self.r1, self.r2)[stage]
        ref = ref.at[h, k] if k < 2 else ref.at[h, pl.ds(2 * k - 2, 2)]
        self.net.got(self.rid + 8 * stage + 4 * h + k, ref)

    def axes(self, h):
        return (("dp", "seq"), ("seq", "dp"))[h]

    def row(self, h, da):
        a = shifted(self.axes(h)[0], da)
        return (lambda b: (a, b)) if h == 0 else (lambda b: (b, a))

    def block(self, h, db):
        a, b = lax.axis_index(self.axes(h)[0]), shifted(self.axes(h)[1], db)
        return (a, b) if h == 0 else (b, a)

    def view(self, h, da, lo):
        a = shifted(self.axes(h)[0], da)
        if h == 0:
            return self.own.at[a, pl.ds(0, 4), pl.ds(lo, self.q)]
        return self.own.at[pl.ds(0, 4), a, pl.ds(lo, self.q)]

    def one(self, h, db, lo):
        a, b = self.block(h, db)
        return self.own.at[a, b, pl.ds(lo, self.q)]

    def add(self, index_of, count, lo, sources, use=None):
        steps = self.q // self.chunk

        @pl.loop(0, count * steps)
        def _(k):
            b = k // steps
            r = (k % steps) * self.chunk
            at = (*index_of(b), rows(lo + r, self.chunk))
            v = self.own[at].astype(F32)
            for ref, lead in sources:
                if count > 1:
                    v = v + ref[(*lead, b, rows(r, self.chunk))].astype(F32)
                else:
                    v = v + ref[(*lead, rows(r, self.chunk))].astype(F32)
            if use is None:
                self.own[at] = v.astype(BF16)
            else:
                use(lo + r, v)

    def step0_far(self, h):
        lo = 2 * h * self.q
        self.put(0, h, 0, self.view(h, 2, lo), 1)
        self.put(0, h, 1, self.view(h, 2, lo + self.q), -1)

    def step0_near(self, h):
        lo = 2 * h * self.q
        self.put(0, h, 4, self.view(h, 1, lo + self.q), 1)
        self.put(0, h, 2, self.view(h, -1, lo), -1)

    def step0(self):
        for h in (0, 1):
            self.step0_far(h)
        for h in (0, 1):
            self.step0_near(h)

    def step1(self):
        q = self.q
        for h in (0, 1):
            lo = 2 * h * q
            self.got(0, h, 0)
            self.add(self.row(h, 1), 4, lo, [(self.r1, (h, 0))])
            self.put(0, h, 3, self.view(h, 1, lo), 1)
            self.got(0, h, 1)
            self.add(self.row(h, -1), 4, lo + q, [(self.r1, (h, 1))])
            self.put(0, h, 5, self.view(h, -1, lo + q), -1)

    def step2(self):
        q = self.q
        for h in (0, 1):
            lo = 2 * h * q
            self.got(0, h, 2)
            self.add(self.row(h, 0), 4, lo, [(self.r1, (h, 2)), (self.r1, (h, 3))])
            self.got(0, h, 3)
            self.add(self.row(h, 0), 4, lo + q, [(self.r1, (h, 4)), (self.r1, (h, 5))])
            self.put(1, h, 0, self.one(h, 2, lo), 1)
            self.put(1, h, 1, self.one(h, 2, lo + q), -1)
            self.put(1, h, 4, self.one(h, 1, lo + q), 1)
            self.put(1, h, 2, self.one(h, -1, lo), -1)

    def step3(self):
        q = self.q
        for h in (0, 1):
            lo = 2 * h * q
            self.got(1, h, 0)
            at = self.block(h, 1)
            self.add(lambda b: at, 1, lo, [(self.r2, (h, 0))])
            self.put(1, h, 3, self.one(h, 1, lo), 1)
            self.got(1, h, 1)
            at2 = self.block(h, -1)
            self.add(lambda b: at2, 1, lo + q, [(self.r2, (h, 1))])
            self.put(1, h, 5, self.one(h, -1, lo + q), -1)

    def step4(self, h, use):
        q = self.q
        lo = 2 * h * q
        at = self.block(h, 0)
        self.got(1, h, 2)
        self.add(lambda b: at, 1, lo, [(self.r2, (h, 2)), (self.r2, (h, 3))], use)
        self.got(1, h, 3)
        self.add(lambda b: at, 1, lo + q, [(self.r2, (h, 4)), (self.r2, (h, 5))], use)


class Fold:
    def __init__(self, net, acc, rsib, zsend, zrec):
        self.net, self.acc, self.rsib, self.zsend, self.zrec = net, acc, rsib, zsend, zrec
        self.sib_sid = [net.send_id(), net.send_id()]
        self.z_sid = [net.send_id(), net.send_id()]
        self.rid = net.recv_ids(16)

    def quarter(self, d):
        return 32 * lax.rem(lax.axis_index("mp") // 2 + (d + 4), 4)

    def right(self):
        return shifted("mp", 2)

    def left(self):
        return shifted("mp", -2)

    def to_sibling(self, p, k, src, dst):
        self.net.put(self.sib_sid[p], self.rsib.at[p], self.rid + 8 * p + k, src, dst, "mp", sibling())

    def to_chip(self, p, slot, src, way):
        rid = self.rid + 8 * p + 4 + (0, 1, 2, 2, 3, 3)[slot]
        self.net.put(self.z_sid[p], self.zrec.at[p], rid, src, self.zrec.at[p, slot], "mp", way)

    def send_columns(self, p, k, src):
        cols = pl.ds(512 * k, 512)
        self.to_sibling(p, k, src.at[:, cols], self.rsib.at[p, :, cols])

    def send_rows(self, p, src):
        for k, d in enumerate((2, 1, -1, 0)):
            at = rows(self.quarter(d), 32)
            self.to_sibling(p, k, src(at), self.rsib.at[p, at])

    def sent(self, p):
        self.net.sent(self.sib_sid[p])

    def total(self, d, p, own, store):
        for i in (0, 1):
            at = rows(self.quarter(d) + 16 * i, 16)
            v = own(p, at).astype(F32) + self.rsib[p, at].astype(F32)
            self.acc[p, at] = v
            if store:
                self.zsend[p, at] = v.astype(BF16)

    def begin(self, p, own, by_rows):
        rid = self.rid + 8 * p

        def arrived(k, d):
            if by_rows:
                self.net.got(rid + k, self.rsib.at[p, rows(self.quarter(d), 32)])

        if not by_rows:
            for k in range(4):
                self.net.got(rid + k, self.rsib.at[p, :, pl.ds(512 * k, 512)])
        arrived(0, 2)
        self.total(2, p, own, True)
        s = self.quarter(2)
        self.to_chip(p, 0, self.zsend.at[p, rows(s, 16)], self.right())
        self.to_chip(p, 1, self.zsend.at[p, rows(s + 16, 16)], self.left())
        arrived(1, 1)
        self.total(1, p, own, True)
        self.to_chip(p, 4, self.zsend.at[p, rows(self.quarter(1) + 16, 16)], self.right())
        arrived(2, -1)
        self.total(-1, p, own, True)
        self.to_chip(p, 2, self.zsend.at[p, rows(self.quarter(-1), 16)], self.left())
        arrived(3, 0)
        self.total(0, p, own, False)

    def middle(self, p):
        for k, d, off, way in ((0, 1, 0, self.right()), (1, -1, 16, self.left())):
            self.net.got(self.rid + 8 * p + 4 + k, self.zrec.at[p, k])
            at = rows(self.quarter(d) + off, 16)
            self.zsend[p, at] = (self.acc[p, at] + self.zrec[p, k].astype(F32)).astype(BF16)
            self.to_chip(p, 3 + 2 * k, self.zsend.at[p, at], way)

    def finish(self, p, use):
        for part in (0, 1):
            self.net.got(self.rid + 8 * p + 6 + part, self.zrec.at[p, pl.ds(2 + 2 * part, 2)])
            v = self.acc[p, rows(self.quarter(0) + 16 * part, 16)]
            for k in (2 + 2 * part, 3 + 2 * part):
                v = v + self.zrec[p, k].astype(F32)
            use(p, 16 * part, v)

    def release(self):
        for sid in (*self.sib_sid, *self.z_sid):
            if sid in self.net.open:
                self.net.sent(sid)


class Share:
    def __init__(self, net, out):
        self.net, self.out = net, out
        self.sid = (net.send_id(), net.send_id())
        self.rid = net.recv_ids(8)

    def at(self, p, d, other=False, lo=0, n=32):
        m = lax.axis_index("mp")
        core = lax.rem(m, 2)
        if other:
            core = 1 - core
        return self.out.at[p, core, lax.rem(m // 2 + (d + 4), 4), pl.ds(lo, n)]

    def put(self, p, k, src, dst, index):
        own = k < 2 or (k == 3 and dst is None)
        dst = self.at(p, 0) if dst is None else dst
        whole = self.out.at[pl.ds(0, 2), 0, pl.ds(0, 3 if own else 4)]
        self.net.put(self.sid[0 if own else 1], whole, self.rid + 4 * p + k, src, dst, "mp", index)

    def got(self, p, k, ref):
        self.net.got(self.rid + 4 * p + k, ref)

    def begin(self, p, src=None):
        src = self.at(p, 0) if src is None else src
        self.put(p, 0, src, None, shifted("mp", 2))
        self.put(p, 1, src, None, shifted("mp", -2))
        self.put(p, 3, src, None, sibling())

    def middle(self, p):
        self.got(p, 0, self.at(p, -1))
        half = self.at(p, -1, False, 0, 16)
        self.put(p, 2, half, half, shifted("mp", 2))
        self.got(p, 1, self.at(p, 1))
        half = self.at(p, 1, False, 16, 16)
        self.put(p, 2, half, half, shifted("mp", -2))
        for d in (-1, 1):
            self.put(p, 3, self.at(p, d), self.at(p, d), sibling())

    def later(self, p):
        self.got(p, 2, self.at(p, 2))
        self.put(p, 3, self.at(p, 2), self.at(p, 2), sibling())

    def finish(self, p):
        self.got(p, 3, self.out.at[p, 1 - lax.rem(lax.axis_index("mp"), 2)])

    def release(self):
        for sid in self.sid:
            self.net.sent(sid)


class Gather:
    def __init__(self, net, own, size, region, whole):
        self.net, self.own, self.size, self.region, self.whole = net, own, size, region, whole
        self.sid, self.rid = net.send_id(), net.recv_ids(30)
        self.half, self.quarter = size // 2, size // 4

    def put(self, k, src, dst, axis, d):
        self.net.put(self.sid, self.whole, self.rid + k, src, dst, axis, shifted(axis, d))

    def got(self, k, ref):
        self.net.got(self.rid + k, ref)

    def idx(self, h, da, db):
        fa, sa = (("dp", "seq"), ("seq", "dp"))[h]
        c = {fa: shifted(fa, da), sa: shifted(sa, db)}
        return c["dp"] * 4 + c["seq"]

    def both(self, k, src, dst, axis):
        self.put(k, src, dst, axis, 1)
        self.put(k + 1, src, dst, axis, -1)

    def begin(self, h):
        for stage in (0, 1):
            axis = ("dp", "seq")[(h + stage) % 2]
            lo = h * self.half
            src = self.own.at[pl.ds(lo, self.half)]
            self.both(15 * h + 3 * stage, src, self.region(self.idx(h, 0, 0), lo, self.half), axis)

    def near(self):
        for h in (0, 1):
            fa, sa = (("dp", "seq"), ("seq", "dp"))[h]
            lo = h * self.half
            for k, d in ((0, -1), (1, 1)):
                p = self.region(self.idx(h, d, 0), lo, self.half)
                self.got(15 * h + k, p)
                part = self.region(self.idx(h, d, 0), lo + k * self.quarter, self.quarter)
                self.put(15 * h + 2, part, part, fa, -d)
                self.both(15 * h + 5 + 2 * k, p, p, sa)

    def far(self):
        for h in (0, 1):
            sa, lo = (("dp", "seq"), ("seq", "dp"))[h][1], h * self.half
            p = self.region(self.idx(h, 2, 0), lo, self.half)
            self.got(15 * h + 2, p)
            self.both(15 * h + 9, p, p, sa)

    def cross(self, k):
        d = (0, -1, 1, 2)[k]
        for h in (0, 1):
            sa, lo = (("dp", "seq"), ("seq", "dp"))[h][1], h * self.half
            for w, db in ((0, -1), (1, 1)):
                at = self.idx(h, d, db)
                self.got(15 * h + 3 + 2 * k + w, self.region(at, lo, self.half))
                part = self.region(at, lo + w * self.quarter, self.quarter)
                self.put(15 * h + 11 + k, part, part, sa, -db)

    def finish(self):
        for k, d in enumerate((0, -1, 1, 2)):
            for h in (0, 1):
                lo = h * self.half
                self.got(15 * h + 11 + k, self.region(self.idx(h, d, 2), lo, self.half))


def lanes(shape):
    return lax.broadcasted_iota(jnp.int32, shape, len(shape) - 1)


def swap_halves(v):
    lane = lanes(v.shape)
    return jnp.where(lane % HD < HD // 2, pltpu.roll(v, 96, 1), pltpu.roll(v, 32, 1))


def main_kernel(
    x_hbm, cot_hbm, parents, wa_hbm, wm_hbm, we_hbm, wr_hbm, gains, table_hbm,
    i_att, i_mrg, i_exp, i_red, mg, fg, sg,
    out, grad, o_att, o_mrg, o_exp, o_red, f_att, f_mrg, f_exp, f_red,
    o_gain, f_gain,
    g_red, g_gate, g_up, g_mrg, g_att,
    ra_red, ra_gate, ra_up, ra_mrg, ra_att,
    rb_red, rb_gate, rb_up, rb_mrg, rb_att,
    sa, wa, wm, xd, cot, n1, dgu, n2, hid,
    acc, sib, rsib, zrec, probs, kv_a, kv_b, q, att, datt, dkv, dkv_in, dpack,
    mid, dmid, stage, stage_exp, w_exp,
    gbuf, gs1, gs2, gs3, gs4, gs5, gtot, gtwo, gnew,
    send, recv, loc,
):
    net = Net(send, recv)
    m = lax.axis_index("mp")
    core, z = lax.rem(m, 2), m // 2
    seq = lax.axis_index("seq")
    other = 1 - core
    dp = lax.axis_index("dp")
    me = 4 * dp + seq
    hello(
        [("dp", shifted("dp", d)) for d in (1, 2, 3)]
        + [("seq", shifted("seq", d)) for d in (1, 2, 3)]
        + [("mp", shifted("mp", d)) for d in range(1, 8)]
    )
    kv = (kv_a, kv_b)
    kv_sid, kv_rid = (net.send_id(), net.send_id()), net.recv_ids(2)
    dkv_sid, dkv_rid = net.send_id(), net.recv_ids(2)
    fold = Fold(net, acc, rsib, sib, zrec)
    share_one, share_two, share_out, share_grad = Share(net, n2), Share(net, xd), Share(net, out), Share(net, grad)
    gain_sid, gain_rid = [net.send_id() for _ in range(5)], net.recv_ids(5)

    def gain_put(k, ref, count, src, dst, axis, d):
        net.put(gain_sid[k], ref.at[pl.ds(0, count)], gain_rid + k, src, dst, axis, shifted(axis, d))

    def gain_got(k, ref, count):
        net.got(gain_rid + k, ref.at[pl.ds(0, count)])


    def by_col(ref):
        return lambda i, lo, k: ref.at[pl.ds(lo, k), pl.ds(pl.multiple_of(128 * i, 128), 128)]

    all_red = Gather(net, g_red.at[dp, seq], 1024, by_col(f_red), f_red.at[:, pl.ds(0, 1920)])
    all_exp = Gather(net, w_exp, 128, lambda i, lo, k: f_exp.at[pl.ds(128 * i + lo, k)], f_exp.at[pl.ds(0, 1920)])
    all_mrg = Gather(net, g_mrg.at[dp, seq], 256, by_col(f_mrg), f_mrg.at[:, pl.ds(0, 1920)])
    all_att = Gather(net, g_att.at[dp, seq], 128, lambda i, lo, k: f_att.at[rows(128 * i + lo, k)], f_att.at[pl.ds(0, 1920)])
    s_red = Spread(net, g_red, ra_red, rb_red)
    s_gate = Spread(net, g_gate, ra_gate, rb_gate)
    s_up = Spread(net, g_up, ra_up, rb_up)
    s_mrg = Spread(net, g_mrg, ra_mrg, rb_mrg)
    s_att = Spread(net, g_att, ra_att, rb_att)

    def bring(k, src, dst):
        c = pltpu.make_async_copy(src, dst, loc.at[k])
        c.start()
        return c

    c_x = [bring(0, x_hbm.at[0], xd.at[0])]
    c_wa = bring(2, wa_hbm, wa)
    c_x.append(bring(1, x_hbm.at[1], xd.at[1]))
    c_table = bring(9, table_hbm, stage.at[pl.ds(0, 2)])

    def all_here(ref, k):
        pltpu.make_async_copy(ref, ref, loc.at[k]).wait()

    both_gains = gains[...].astype(F32)
    gain_one, gain_two = both_gains[0:1, :], both_gains[1:2, :]

    def ancestors(t, b):
        p1 = parents[t, b]
        p2 = jnp.where(p1 >= 0, parents[t, jnp.maximum(p1, 0)], -1)
        p3 = jnp.where(p2 >= 0, parents[t, jnp.maximum(p2, 0)], -1)
        return p1, p2, p3

    def turns(t, i):
        ps = ancestors(t, 2 * seq + i)
        depth = sum(jnp.where(p >= 0, 1, 0) for p in ps)

        def pick(k):
            v = stage[k, 0:128]
            for n in (1, 2, 3):
                v = jnp.where(depth == n, stage[k, 128 * n : 128 * n + 128], v)
            return v

        return pick(0), pick(1)

    lower = lanes((128, 128)) < HD

    def own_kv(t, at):
        return kv[t].at[pl.ds(2 * at, 2)]

    for t in (0, 1):
        c_x[t].wait()
        if t == 0:
            c_wa.wait()
            c_table.wait()
        else:
            c_wm = bring(4, wm_hbm, wm)
            c_cot = bring(3, cot_hbm, cot)
            for k in range(16):
                pltpu.make_async_copy(wr_hbm.at[:, pl.ds(128 * k, 128)], g_red.at[k // 4, k % 4], loc.at[10]).start()
            for k in range(4):
                pltpu.make_async_copy(we_hbm.at[0, :, pl.ds(256 * k, 256)], sa.at[k], loc.at[11]).start()
            for k in range(16):
                pltpu.make_async_copy(we_hbm.at[1, pl.ds(128 * k, 128)], g_up.at[k // 4, k % 4], loc.at[12]).start()

        @pl.loop(0, 16, unroll=4)
        def _(i):
            v = xd[t, i // 8, (i // 2) % 4, rows(16 * (i % 2), 16)].astype(F32)
            r = lax.rsqrt(jnp.mean(v * v, axis=-1, keepdims=True) + NORM_EPS)
            n1[t, rows(16 * i, 16)] = (v * r * gain_one).astype(BF16)

        packed = dot(n1[t], wa[...])
        for i in (0, 1):
            c, s = turns(t, i)
            part = packed[128 * i : 128 * i + 128]
            for g in (0, 1):
                v = part[:, 128 * g : 128 * g + 128]
                q[t, i, g] = (v * c + swap_halves(v) * s).astype(BF16)
            v = part[:, 256:384]
            kv[t][2 * seq + i] = jnp.where(lower, v * c + swap_halves(v) * s, v).astype(BF16)
        if t == 0:
            hello_wait(13)
        for d in (1, 2, 3):
            net.put(kv_sid[t], kv[t].at[pl.ds(0, 6)], kv_rid + t, own_kv(t, seq), own_kv(t, seq), "seq", shifted("seq", d))

    def hidden_grad(j):
        w = jnp.concatenate([g_red[k // 4, k % 4, 256 * j : 256 * j + 256] for k in range(16)], axis=1)
        v = dot_nt(cot[...].reshape(512, D), w)
        high = v.astype(BF16)
        low = (v - high.astype(F32)).astype(BF16)
        cols = pl.ds(256 * j, 256)
        g_gate[0, :, :, cols] = high.reshape(4, 128, 256)
        g_gate[1, :, :, cols] = low.reshape(4, 128, 256)

    low_lane = lanes((512, 128)) < HD
    key_col = lanes((128, 512))
    query_row = lax.broadcasted_iota(jnp.int32, (128, 512), 0)

    def key_views(t, ids):
        both = jnp.concatenate([kv[t][jnp.maximum(c, 0)] for c in ids], axis=0).astype(F32)
        turned = pltpu.roll(both, HD, 1)
        zero = jnp.zeros_like(both)
        keys = [jnp.where(low_lane, both, zero).astype(BF16), jnp.where(low_lane, zero, turned).astype(BF16)]
        values = [jnp.where(low_lane, turned, zero).astype(BF16), jnp.where(low_lane, zero, both).astype(BF16)]
        return keys, values

    def attention(t):
        net.got(kv_rid + t, kv[t].at[pl.ds(0, 6)])
        for i in (0, 1):
            b = 2 * seq + i
            ps = ancestors(t, b)
            keys, values = key_views(t, (b, *ps))
            seen = (key_col < 128) & (key_col <= query_row)
            for k, p in enumerate(ps):
                inside = (key_col >= 128 * (k + 1)) & (key_col < 128 * (k + 2))
                seen = seen | (inside & (p >= 0))
            for g in (0, 1):
                total = jnp.zeros((128, 128), F32)
                for h in (0, 1):
                    scores = dot_nt(q[t, i, g], keys[h]) * HD**-0.5
                    scores = jnp.where(seen, scores, MASK_FILL)
                    e = jnp.exp(scores - jnp.max(scores, axis=-1, keepdims=True))
                    p = (e / jnp.sum(e, axis=-1, keepdims=True)).astype(BF16)
                    probs[2 * t + i, 2 * g + h] = p
                    total = total + dot(p, values[h])
                att[t, 128 * i : 128 * i + 128, 128 * g : 128 * g + 128] = total.astype(BF16)

    def mine(p, at):
        return acc[p, at]

    def merge(p):
        for k in range(4):
            cols = pl.ds(512 * k, 512)
            sib[p, :, cols] = dot(att[p, rows(128 * other, 128)], wm[:, cols]).astype(BF16)
        fold.send_rows(p, lambda at: sib.at[p, at])
        for k in range(4):
            cols = pl.ds(512 * k, 512)
            acc[p, :, cols] = dot(att[p, rows(128 * core, 128)], wm[:, cols])

    def to_normed(p, r, v):
        x_own = xd[p, core, z, r : r + 16].astype(F32)
        total = x_own + v
        mid[p, r : r + 16] = total
        rms = lax.rsqrt(jnp.mean(total * total, axis=-1, keepdims=True) + NORM_EPS)
        n2[p, core, z, r : r + 16] = (total * rms * gain_two).astype(BF16)


    def feed_dot(p, j):
        lo = 1024 * (j % 2)
        for k, w in ((0, sa[j]), (1, g_up[:, :, :, 256 * j : 256 * j + 256].reshape(D, 256))):
            v = dot(n2[p].reshape(256, D), w)
            acc[p, :, lo + 256 * k : lo + 256 * k + 256] = v[0:128]
            acc[p, :, lo + 512 + 256 * k : lo + 768 + 256 * k] = v[128:256]

    def feed_rest(p, j):
        cols, cols_up = pl.ds(256 * j, 256), pl.ds(1024 + 256 * j, 256)
        for half in (0, 1):
            lo = 1024 * (j % 2) + 512 * half
            for i in range(4):
                at = pl.ds(32 * i, 32)
                gate, up = acc[p, at, lo : lo + 256], acc[p, at, lo + 256 : lo + 512]
                dh = g_gate[0, 2 * p + half, at, cols].astype(F32) + g_gate[1, 2 * p + half, at, cols].astype(F32)
                sig = 0.5 + 0.5 * jnp.tanh(0.5 * gate)
                act = gate * sig
                to = pl.ds(128 * half + 32 * i, 32)
                hid[p, to, cols] = (act * up).astype(BF16)
                dgu[p, to, cols] = (dh * up * (sig + act * (1.0 - sig))).astype(BF16)
                dgu[p, to, cols_up] = (dh * act).astype(BF16)

    def feed(p, between):
        feed_dot(p, 0)
        for j in (1, 2, 3):
            feed_dot(p, j)
            feed_rest(p, j - 1)
            if j == 1:
                between()
        feed_rest(p, 3)

    attention(0)
    c_wm.wait()
    merge(0)
    attention(1)
    fold.sent(0)
    fold.begin(0, mine, True)
    merge(1)
    c_cot.wait()
    all_here(g_red, 10)
    hidden_grad(0)
    fold.middle(0)
    fold.sent(1)
    fold.begin(1, mine, True)
    hidden_grad(1)
    fold.finish(0, to_normed)
    share_one.begin(0)
    fold.middle(1)
    hidden_grad(2)
    share_one.middle(0)
    fold.finish(1, to_normed)
    share_one.begin(1)
    hidden_grad(3)
    all_here(sa, 11)
    all_here(g_up, 12)
    share_one.later(0)
    share_one.middle(1)
    share_one.finish(0)
    feed(0, lambda: share_one.later(1))
    share_one.finish(1)
    fold.release()
    feed(1, lambda: None)

    def reduce_grad(a):
        @pl.loop(0, 2)
        def _(k):
            cols = pl.ds(pl.multiple_of(512 * a + 256 * k, 256), 256)
            v = dot_tn(hid[...].reshape(512, 1024), cot[:, :, :, :, cols].reshape(512, 256)).astype(BF16)
            g_red[a, 2 * k] = v[:, 0:128]
            g_red[a, 2 * k + 1] = v[:, 128:256]

    reduce_grad(shifted("dp", 2))
    s_red.step0_far(0)

    @pl.loop(0, 2)
    def _(k):
        reduce_grad(lax.rem(dp + 1 + 2 * k, 4))

    s_red.step0_near(0)
    reduce_grad(dp)
    s_red.step0_far(1)
    s_red.step0_near(1)
    def expand_grad(dst, first):
        @pl.loop(0, 4)
        def _(a):
            left = n2[:, :, :, :, pl.ds(pl.multiple_of(512 * a, 512), 512)].reshape(512, 512)
            for k in (0, 1):
                v = dot_tn(left, dgu[:, :, first + 512 * k : first + 512 * k + 512].reshape(512, 512))
                dst[a, :, :, 512 * k : 512 * k + 512] = v.astype(BF16).reshape(4, 128, 512)

    expand_grad(g_gate, 0)
    s_gate.step0()

    def norm_grad(p):
        for k in range(4):
            for j in (2 * k, 2 * k + 1):
                cols = pl.ds(256 * j, 256)
                w_gate = jnp.concatenate([sa[i, 256 * j : 256 * j + 256] for i in range(4)], axis=1)
                w_up = g_up[j // 2, 2 * (j % 2) : 2 * (j % 2) + 2].reshape(256, 1024)
                v = dot_nt(dgu[p], jnp.concatenate([w_gate, w_up], axis=1))
                first, second = v[0:128], v[128:256]
                sib[p, :, cols] = jnp.where(core == 0, second, first).astype(BF16)
                acc[p, :, cols] = jnp.where(core == 0, first, second)
            fold.send_columns(p, k, sib.at[p])

    def to_branch(p, r, v):
        total = mid[p, r : r + 16]
        rms = lax.rsqrt(jnp.mean(total * total, axis=-1, keepdims=True) + NORM_EPS)
        u = v * gain_two
        back_vals = rms * u - total * (rms * rms * rms) * jnp.mean(u * total, axis=-1, keepdims=True)
        full = cot[p, core, z, r : r + 16].astype(F32) + back_vals
        dmid[p, r : r + 16] = full
        xd[p, core, z, r : r + 16] = full.astype(BF16)
        gbuf[1:2, :] = gbuf[1:2, :] + jnp.sum(v * total * rms, axis=0, keepdims=True)

    gbuf[...] = jnp.zeros_like(gbuf)
    norm_grad(0)
    s_red.step1()
    fold.sent(0)
    fold.begin(0, mine, False)
    norm_grad(1)
    for k in range(8):
        half = sa.at[k // 2, pl.ds(1024 * (k % 2), 1024)]
        pltpu.make_async_copy(wr_hbm.at[:, pl.ds(256 * k, 256)], half, loc.at[13]).start()
    expand_grad(g_up, 1024)
    s_up.step0()
    fold.middle(0)
    fold.sent(1)
    fold.begin(1, mine, False)
    s_gate.step1()
    fold.finish(0, to_branch)
    share_two.begin(0)
    fold.middle(1)

    all_here(sa, 13)

    @pl.loop(0, 4)
    def _(j):
        for k in (0, 1):
            v = dot(hid[...].reshape(512, 1024), sa[j, 1024 * k : 1024 * k + 1024])
            dgu[:, :, pl.ds(pl.multiple_of(512 * j + 256 * k, 256), 256)] = v.astype(BF16).reshape(2, 256, 256)

    fold.finish(1, to_branch)
    share_two.begin(1)

    x_slot = lax.rem(z + 1, 4)
    c_xo = [bring(p, x_hbm.at[p, core, z], cot.at[p, core, x_slot]) for p in (0, 1)]
    for k in (0, 1, 2):
        pltpu.make_async_copy(i_exp[k], stage_exp.at[k], loc.at[10]).start()
    share_two.middle(0)
    share_two.middle(1)
    share_two.later(0)
    s_red.step2()
    share_two.finish(0)

    dbr = xd

    def branch_back(t):
        datt[t] = dot_nt(dbr[t].reshape(256, D), wm[...]).astype(BF16)

    branch_back(0)
    share_two.later(1)
    dkv[...] = jnp.zeros_like(dkv)

    def attention_back(t, i):
        u = 2 * t + i
        b = 2 * seq + i
        ps = ancestors(t, b)
        keys, values = key_views(t, (b, *ps))
        c, s = turns(t, i)
        at = rows(128 * i, 128)
        dk = [jnp.zeros((512, 128), F32), jnp.zeros((512, 128), F32)]
        dv = [jnp.zeros((512, 128), F32), jnp.zeros((512, 128), F32)]
        for g in (0, 1):
            dq = jnp.zeros((128, 128), F32)
            da = datt[t, at, 128 * g : 128 * g + 128]
            for h in (0, 1):
                p = probs[u, 2 * g + h]
                pf = p.astype(F32)
                dp = dot_nt(da, values[h])
                inner = jnp.sum(pf * dp, axis=-1, keepdims=True)
                ds = (pf * (dp - inner)).astype(BF16)
                dq = dq + dot(ds, keys[h])
                dk[h] = dk[h] + dot_tn(ds, q[t, i, g])
                dv[h] = dv[h] + dot_tn(p, da)
            dq = dq * HD**-0.5
            dpack[t, at, 128 * g : 128 * g + 128] = (dq * c - swap_halves(dq) * s).astype(BF16)
        both = jnp.where(
            low_lane, (dk[0] + pltpu.roll(dk[1], HD, 1)) * HD**-0.5, pltpu.roll(dv[0], HD, 1) + dv[1]
        )
        dkv[t, b] = dkv[t, b] + both[0:128]
        for blk in range(8):
            v = dkv[t, blk]
            for k, p in enumerate(ps):
                v = v + both[128 * (k + 1) : 128 * (k + 2)] * jnp.where(p == blk, 1.0, 0.0)
            dkv[t, blk] = v

    def send_dkv(t):
        for c in range(8):
            probs[2 * t, c // 4, :, 128 * (c % 4) : 128 * (c % 4) + 128] = dkv[t, c].astype(BF16)
        for d in (1, 2, 3):
            peer = shifted("seq", d)
            src = probs.at[2 * t, peer // 2, :, pl.ds(pl.multiple_of(256 * lax.rem(peer, 2), 256), 256)]
            net.put(dkv_sid, dkv_in, dkv_rid + t, src, dkv_in.at[d - 1, t], "seq", peer)

    def add_dkv(t):
        net.got(dkv_rid + t, dkv_in.at[pl.ds(0, 3), t])
        for i in (0, 1):
            v = dkv[t, 2 * seq + i]
            for d in (0, 1, 2):
                v = v + dkv_in[d, t, :, 128 * i : 128 * i + 128].astype(F32)
            c, s = turns(t, i)
            v = jnp.where(lower, v * c - swap_halves(v) * s, v)
            dpack[t, 128 * i : 128 * i + 128, 256:384] = v.astype(BF16)

    for i in (0, 1):
        attention_back(0, i)
    send_dkv(0)
    share_two.finish(1)
    fold.release()

    def down_rows(p, at):
        return dgu[p, pl.ds(pl.multiple_of(128 * core + at.start, 16), 16)]

    for p in (0, 1):
        fold.send_rows(p, lambda at: dgu.at[p, rows(128 * other + at.start, 32)])
    branch_back(1)
    for i in (0, 1):
        attention_back(1, i)
    send_dkv(1)
    s_up.step1()

    @pl.loop(0, 8)
    def _(j):
        cols = pl.ds(pl.multiple_of(256 * j, 256), 256)
        v = dot_tn(att[...].reshape(512, 256), dbr[:, :, :, :, cols].reshape(512, 256))
        g_mrg[j // 2, 2 * (j % 2)] = v[:, 0:128].astype(BF16)
        g_mrg[j // 2, 2 * (j % 2) + 1] = v[:, 128:256].astype(BF16)

    s_mrg.step0()
    fold.begin(0, down_rows, True)
    fold.begin(1, down_rows, True)
    s_gate.step2()
    add_dkv(0)
    add_dkv(1)

    @pl.loop(0, 4)
    def _(a):
        left = n1[:, :, pl.ds(pl.multiple_of(512 * a, 512), 512)].reshape(512, 512)
        g_att[a] = dot_tn(left, dpack[...].reshape(512, 384)).astype(BF16).reshape(4, 128, 384)

    s_att.step0()
    s_red.step3()
    for k in (0, 1, 2):
        pltpu.make_async_copy(i_mrg[k], dkv.at[0, pl.ds(2 * k, 2)], loc.at[12]).start()
        pltpu.make_async_copy(i_red[k].at[pl.ds(0, 512)], stage.at[k], loc.at[11]).start()
    fold.middle(0)
    fold.middle(1)
    share_one.release()

    @pl.loop(0, 8)
    def _(j):
        v = dot_nt(dpack[...].reshape(512, 384), wa[rows(256 * j, 256)])
        n2[:, :, :, :, pl.ds(pl.multiple_of(256 * j, 256), 256)] = v.astype(BF16).reshape(2, 2, 4, 32, 256)

    def to_out(p, r, v):
        cot[p, core, z, r : r + 16] = (mid[p, r : r + 16] + v).astype(BF16)

    s_mrg.step1()

    def renew(state, at, grads):
        new = adamw(state[0][at], state[1][at], state[2][at], grads)[0]
        state[1][at] = grads
        return new

    flat_stage = [stage.at[k] for k in (0, 1, 2)]

    def use_red(h):
        def use(r, v):
            new = renew(flat_stage, rows(r - 512 * h, 128), v)
            g_red[dp, seq, rows(r, 128)] = new.astype(BF16)

        return use

    all_here(stage, 11)
    s_red.step4(0, use_red(0))
    all_red.begin(0)
    c_red = [bring(4, stage.at[1], o_red.at[pl.ds(0, 512)])]
    local = [bring(14, g_red.at[dp, seq, pl.ds(0, 512)], f_red.at[pl.ds(0, 512), pl.ds(pl.multiple_of(128 * me, 128), 128)])]
    s_up.step2()
    s_att.step1()
    s_gate.step3()
    l_out = []
    for p in (0, 1):
        fold.finish(p, to_out)
        share_out.begin(p, cot.at[p, core, z])
        l_out.append(bring(2 + p, cot.at[p, core, z], out.at[p, core, z]))
    for c in c_red:
        c.wait()
    for k in (0, 1, 2):
        pltpu.make_async_copy(i_red[k].at[pl.ds(512, 512)], stage.at[k], loc.at[11]).start()
    s_mrg.step2()
    all_here(stage, 11)
    s_red.step4(1, use_red(1))
    all_red.begin(1)
    c_red = [bring(4, stage.at[1], o_red.at[pl.ds(512, 512)])]
    local.append(bring(15, g_red.at[dp, seq, pl.ds(512, 512)], f_red.at[pl.ds(512, 512), pl.ds(pl.multiple_of(128 * me, 128), 128)]))
    s_up.step3()
    s_att.step2()
    share_out.middle(0)
    share_out.middle(1)

    def use_expand(j):
        def use(r, v):
            at = rows(r, 16)
            new = adamw(stage_exp[0, at, j, :], stage_exp[1, at, j, :], stage_exp[2, at, j, :], v)[0]
            stage_exp[0, at, j, :] = new
            stage_exp[1, at, j, :] = v

        return use

    all_here(stage_exp, 10)
    s_gate.step4(0, use_expand(0))
    s_gate.step4(1, use_expand(0))
    for c in c_red:
        c.wait()
    for k in (0, 1, 2):
        for a in (0, 1, 2):
            pltpu.make_async_copy(
                i_att[k].at[:, pl.ds(128 * a, 128)], stage.at[k, pl.ds(128 * a, 128)], loc.at[11]
            ).start()

    def norm_rows(p, at):
        return n2[p, core, at.start // 32, pl.ds(pl.multiple_of(at.start % 32, 16), 16)]

    def fold_begin(p):
        fold.begin(p, norm_rows, True)

    all_red.near()
    s_mrg.step3()
    s_att.step3()
    share_out.later(0)
    share_out.later(1)
    for h in (0, 1):
        s_up.step4(h, use_expand(1))
        for i in (0, 1, 2, 3):
            at = rows(64 * h + 16 * i, 16)
            w_exp[at] = stage_exp[0, at].astype(BF16)
        all_exp.begin(h)
    c_exp = [bring(6, stage_exp.at[1], o_exp)]
    local.append(bring(9, w_exp, f_exp.at[pl.ds(128 * me, 128)]))
    def use_mrg(r, v):
        new = renew([dkv.at[0, 2 * k + r // 128] for k in (0, 1, 2)], rows(r % 128, 64), v)
        g_mrg[dp, seq, rows(r, 64)] = new.astype(BF16)

    all_here(dkv.at[0, pl.ds(0, 6)], 12)
    for h in (0, 1):
        s_mrg.step4(h, use_mrg)
        all_mrg.begin(h)
    c_mrg = [bring(7, dkv.at[0, pl.ds(2, 2)], o_mrg)]
    local.append(bring(8, g_mrg.at[dp, seq], f_mrg.at[:, pl.ds(pl.multiple_of(128 * me, 128), 128)]))
    all_here(stage.at[:, pl.ds(0, 384)], 11)

    def use_att(r, v):
        parts = []
        for a in (0, 1, 2):
            parts.append(renew(flat_stage, rows(128 * a + r, 32), v[:, 128 * a : 128 * a + 128]))
        g_att[dp, seq, rows(r, 32)] = jnp.concatenate(parts, axis=1).astype(BF16)

    for h in (0, 1):
        s_att.step4(h, use_att)
        all_att.begin(h)
    c_att = [bring(16 + a, stage.at[1, pl.ds(128 * a, 128)], o_att.at[:, pl.ds(128 * a, 128)]) for a in (0, 1, 2)]
    local.append(bring(5, g_att.at[dp, seq], f_att.at[rows(128 * me, 128)]))
    share_out.finish(0)
    share_out.finish(1)
    fold.release()
    for p in (0, 1):
        fold.send_rows(p, lambda at: n2.at[p, other, at.start // 32])
    all_red.far()
    all_exp.near()
    fold_begin(0)
    fold_begin(1)
    all_red.cross(0)
    all_red.cross(1)
    all_mrg.near()
    all_att.near()
    fold.middle(0)
    fold.middle(1)
    for c in c_xo:
        c.wait()

    def to_grad(p, r, v):
        x = cot[p, core, x_slot, r : r + 16].astype(F32)
        rms = lax.rsqrt(jnp.mean(x * x, axis=-1, keepdims=True) + NORM_EPS)
        u = v * gain_one
        back_vals = rms * u - x * (rms * rms * rms) * jnp.mean(u * x, axis=-1, keepdims=True)
        cot[p, other, z, r : r + 16] = (dmid[p, r : r + 16] + back_vals).astype(BF16)
        gbuf[0:1, :] = gbuf[0:1, :] + jnp.sum(v * x * rms, axis=0, keepdims=True)

    all_exp.far()
    all_red.cross(2)
    for p in (0, 1):
        fold.finish(p, to_grad)
        share_grad.begin(p, cot.at[p, other, z])
    l_grad = [bring(p, cot.at[p, other, z], grad.at[p, core, z]) for p in (0, 1)]
    gs1[m] = gbuf[...]
    for d in range(1, 8):
        gain_put(0, gs1, 7, gbuf, gs1.at[m], "mp", d)
    all_red.cross(3)
    all_exp.cross(0)
    all_mrg.far()
    all_att.far()
    gain_got(0, gs1, 7)
    total = gs1[0]
    for k in range(1, 8):
        total = total + gs1[k]
    gtot[...] = total

    def piece(i, n):
        return pl.ds(pl.multiple_of(i * n, 128), n)

    gs2[dp] = gtot[:, piece(dp, 512)]
    for d in (1, 2, 3):
        gain_put(1, gs2, 3, gtot.at[:, piece(shifted("dp", d), 512)], gs2.at[dp], "dp", d)
    share_grad.middle(0)
    share_grad.middle(1)
    all_exp.cross(1)
    gain_got(1, gs2, 3)
    gtwo[...] = gs2[0] + gs2[1] + gs2[2] + gs2[3]
    gs3[seq] = gtwo[:, piece(seq, 128)]
    for d in (1, 2, 3):
        gain_put(2, gs3, 3, gtwo.at[:, piece(shifted("seq", d), 128)], gs3.at[seq], "seq", d)
    share_grad.later(0)
    share_grad.later(1)
    all_mrg.cross(0)
    all_att.cross(0)
    gain_got(2, gs3, 3)
    shard = gs3[0] + gs3[1] + gs3[2] + gs3[3]
    new = adamw(mg[...], fg[...], sg[...], shard)[0]
    o_gain[...] = shard
    gnew[...] = new
    gs4[seq] = new
    for d in (1, 2, 3):
        gain_put(3, gs4, 3, gnew, gs4.at[seq], "seq", d)
    all_exp.cross(2)
    all_mrg.cross(1)
    all_att.cross(1)
    gain_got(3, gs4, 3)
    gs5[dp] = gs4[...]
    for d in (1, 2, 3):
        gain_put(4, gs5, 3, gs4, gs5.at[dp], "dp", d)
    for k in (2, 3):
        all_mrg.cross(k)
        all_att.cross(k)
    all_exp.cross(3)
    gain_got(4, gs5, 3)
    for a in range(4):
        for b in range(4):
            lo = 128 * (4 * a + b)
            f_gain[:, lo : lo + 128] = gs5[a, b].astype(BF16)
    share_grad.finish(0)
    share_grad.finish(1)
    for g in (all_red, all_exp, all_mrg, all_att):
        g.finish()
    for c in local + l_out + l_grad + c_exp + c_mrg + c_att:
        c.wait()
    net.drain()


def main_call(x, cot, parents, wa, wm, we, wr, gains, table, states, gain_states):
    kinds = [(1024, 128), (128, 1024), (128, 1024), (256, 128), (128, 384)]
    vm, sds = pltpu.VMEM, jax.ShapeDtypeStruct
    scratch = (
        [vm((4, 4, n, c), BF16) for n, c in kinds]
        + [vm((2, 6, 4, n // 4, c), BF16) for n, c in kinds]
        + [vm((2, 6, n // 4, c), BF16) for n, c in kinds]
        + [
            vm((4, 2048, 256), BF16),
            vm((2048, 384), BF16),
            vm((256, 2048), BF16),
            vm((2, 2, 4, 32, D), BF16),
            vm((2, 2, 4, 32, D), BF16),
            vm((2, 256, D), BF16),
            vm((2, 256, D), BF16),
            vm((2, 2, 4, 32, D), BF16),
            vm((2, 256, 1024), BF16),
            vm((2, 128, D), F32),
            vm((2, 128, D), BF16),
            vm((2, 128, D), BF16),
            vm((2, 6, 16, D), BF16),
            vm((4, 4, 128, 512), BF16),
            vm((8, 128, 128), BF16),
            vm((8, 128, 128), BF16),
            vm((2, 2, 2, 128, 128), BF16),
            vm((2, 256, 256), BF16),
            vm((2, 256, 256), BF16),
            vm((2, 8, 128, 128), F32),
            vm((3, 2, 128, 256), BF16),
            vm((2, 256, 384), BF16),
            vm((2, 32, D), F32),
            vm((2, 32, D), F32),
            vm((3, 512, 128), F32),
            vm((3, 128, 2, 1024), F32),
            vm((128, 2, 1024), BF16),
            vm((2, D), F32),
            vm((8, 2, D), F32),
            vm((4, 2, 512), F32),
            vm((4, 2, 128), F32),
            vm((4, 2, 128), F32),
            vm((4, 4, 2, 128), F32),
            vm((2, D), F32),
            vm((2, 512), F32),
            vm((2, 128), F32),
            pltpu.SemaphoreType.DMA((36,)),
            pltpu.SemaphoreType.DMA((260,)),
            pltpu.SemaphoreType.DMA((20,)),
        ]
    )
    rows_out = sds((2, 2, 4, 32, D), BF16)
    shards = [sds((128, 384), F32), sds((2, 128, 128), F32), sds((128, 2, 1024), F32), sds((1024, 128), F32)]
    fulls = [sds((D, 384), BF16), sds((256, D), BF16), sds((D, 2, 1024), BF16), sds((1024, D), BF16)]
    out_shape = [rows_out, rows_out, *shards, *fulls, sds((2, 128), F32), sds((2, D), BF16)]
    vspec = pl.BlockSpec(memory_space=pltpu.VMEM)
    hbm = pl.BlockSpec(memory_space=pl.ANY)
    return pl.pallas_call(
        main_kernel,
        out_shape=out_shape,
        in_specs=[hbm, hbm, pl.BlockSpec(memory_space=pltpu.SMEM), hbm, hbm, hbm, hbm, vspec, hbm]
        + [[hbm] * 3] * 4
        + [vspec] * 3,
        out_specs=[hbm] * 10 + [vspec] * 2,
        scratch_shapes=scratch,
        compiler_params=pltpu.CompilerParams(
            collective_id=1, has_side_effects=True, vmem_limit_bytes=64 * 2**20 - 65536
        ),
    )(x, cot, parents, wa, wm, we, wr, gains, table, *states, *gain_states)


PARTS = (2, 2, 1, 1, 4, 2, 1)


def tail_kernel(*refs):
    groups, copies, refs = refs[:20], refs[20:27], refs[27:]
    outs, copied, refs = refs[:15], refs[15:22], refs[22:]
    held, through, (sem_in, sem_out, sem_a, sem_b) = refs[:20], refs[20:27], refs[27:]
    reads = [pltpu.make_async_copy(src, dst, sem_a.at[k]) for k, (src, dst) in enumerate(zip(groups, held))]
    there, back = [], []
    for k, parts in enumerate(PARTS):
        size = copies[k].shape[0] // parts
        for i in range(parts):
            at, j = pl.ds(size * i, size), len(there)
            there.append(pltpu.make_async_copy(copies[k].at[at], through[k].at[at], sem_in.at[j]))
            back.append(pltpu.make_async_copy(through[k].at[at], copied[k].at[at], sem_out.at[j]))
    writes = []

    def renew(k):
        for c in reads[4 * k : 4 * k + 4]:
            c.wait()
        master, first, second, grads = held[4 * k : 4 * k + 4]
        steps = 8 if k < 4 else 1
        size = master.shape[0] // steps

        @pl.loop(0, steps)
        def _(i):
            at = pl.ds(pl.multiple_of(size * i, size), size)
            master[at], first[at], second[at] = adamw(master[at], first[at], second[at], grads[at])

        for i in range(3):
            c = pltpu.make_async_copy(held[4 * k + i], outs[3 * k + i], sem_b.at[3 * k + i])
            c.start()
            writes.append(c)

    def pass_on(first, last):
        for c, e in zip(there[first:last], back[first:last]):
            c.wait()
            e.start()

    for c in reads[8:12] + there[:4] + reads[:8] + reads[12:] + there[4:]:
        c.start()
    pass_on(0, 4)
    renew(2)
    pass_on(4, 7)
    renew(3)
    pass_on(7, len(there))
    for k in (0, 1, 4):
        renew(k)
    for c in writes + back:
        c.wait()


def tail_call(groups, results):
    flat = [v for g in groups for v in g]
    vm, sds = pltpu.VMEM, jax.ShapeDtypeStruct
    hbm = pl.BlockSpec(memory_space=pl.ANY)
    n = sum(PARTS)
    done = pl.pallas_call(
        tail_kernel,
        in_specs=[hbm] * 27,
        out_specs=[hbm] * 22,
        out_shape=[sds(g[0].shape, F32) for g in groups for _ in range(3)] + [sds(v.shape, v.dtype) for v in results],
        scratch_shapes=[vm(v.shape, F32) for v in flat]
        + [vm(v.shape, v.dtype) for v in results]
        + [pltpu.SemaphoreType.DMA((k,)) for k in (n, n, 20, 15)],
        compiler_params=pltpu.CompilerParams(vmem_limit_bytes=64 * 2**20 - 65536),
    )(*flat, *results)
    return [done[3 * k : 3 * k + 3] for k in range(5)], done[15:]


def rotary_table():
    inv = ROPE_BASE ** (-2.0 * np.arange(HD // 2, dtype=np.float32) / HD)
    angle = np.arange(512, dtype=np.float32)[:, None] * inv.astype(np.float32)[None, :]
    c, s = np.cos(angle), np.sin(angle)
    both = np.stack([np.concatenate([c, c, c, c], 1), np.concatenate([-s, s, -s, s], 1)])
    return both.astype(np.float32)


def on_device(
    inputs, cotangent, parents, weight_attend, weight_merge, weight_expand, weight_reduce, gains,
    master_attend, master_merge, master_expand, master_reduce, master_gains,
    first_attend, first_merge, first_expand, first_reduce, first_gains,
    second_attend, second_merge, second_expand, second_reduce, second_gains,
):
    x = inputs.reshape(2, 2, 4, 32, D)
    cot = cotangent.reshape(2, 2, 4, 32, D)
    we = weight_expand.transpose(1, 0, 2)
    states = [
        [master_attend, first_attend, second_attend],
        [v.reshape(2, 128, 128) for v in (master_merge, first_merge, second_merge)],
        [master_expand, first_expand, second_expand],
        [master_reduce, first_reduce, second_reduce],
    ]
    gain_states = [master_gains, first_gains, second_gains]
    out, grad, g_att, g_mrg, g_exp, g_red, f_att, f_mrg, f_exp, f_red, g_gain, f_gain = main_call(
        x, cot, parents, weight_attend, weight_merge, we, weight_reduce, gains, jnp.asarray(rotary_table()), states, gain_states
    )
    states[1] = [master_merge, first_merge, second_merge]
    sums = (g_att, g_mrg.reshape(256, 128), g_exp, g_red, g_gain)
    results = [out.reshape(512, D), grad.reshape(512, D), f_att, f_mrg, f_exp, f_red, f_gain]
    (s_att, s_mrg, s_exp, s_red, s_gain), results = tail_call(
        [[*v, g] for v, g in zip((*states, gain_states), sums)], results
    )
    out, grad, f_att, f_mrg, f_exp, f_red, f_gain = results
    return (
        out.reshape(2, 256, D), grad.reshape(2, 256, D),
        s_att[0], s_mrg[0], s_exp[0], s_red[0], s_gain[0],
        s_att[1], s_mrg[1], s_exp[1], s_red[1], s_gain[1],
        s_att[2], s_mrg[2], s_exp[2], s_red[2], s_gain[2],
        f_att, f_mrg, f_exp, f_red, f_gain,
    )


def solution(mesh):
    both = ("dp", "seq")
    states = (P(both, "mp"), P("mp", both), P(both, None, "mp"), P("mp", both), P(None, both))
    weights = (P(None, "mp"), P("mp", None), P(None, None, "mp"), P("mp", None), P())
    tokens = P("dp", "seq", None)
    return jax.shard_map(
        on_device,
        mesh=mesh,
        in_specs=(tokens, tokens, P("dp", None), *weights, *states, *states, *states),
        out_specs=(tokens, tokens, *states, *states, *states, *weights),
        check_vma=False,
    )
```

```python
import functools

import jax
import jax.numpy as jnp
import numpy as np
from jax import lax
from jax.experimental import pallas as pl
from jax.experimental.pallas import tpu as pltpu
from jax.sharding import PartitionSpec as P

MESH = pl.DeviceIdType.MESH
F32 = jnp.float32
BF16 = jnp.bfloat16
D = 2048
HD = 64
STEP = 5
NORM_EPS = 1e-05
ROPE_BASE = 500000.0
MASK_FILL = -1e30
BETA_ONE = 0.5
BETA_TWO = 0.5
ADAM_EPS = 1e-08
LEARN_RATE = 0.005
DECAY_RATE = 0.1
FIX_ONE = 1.0 - BETA_ONE**STEP
FIX_TWO = 1.0 - BETA_TWO**STEP
SIZES = {"dp": 4, "seq": 4, "mp": 8}


def adamw(master, first, second, grad_vals):
    momentum = BETA_ONE * first + (1.0 - BETA_ONE) * grad_vals
    variance = BETA_TWO * second + (1.0 - BETA_TWO) * grad_vals * grad_vals
    direction = momentum / FIX_ONE / (jnp.sqrt(variance / FIX_TWO) + ADAM_EPS)
    renewed = master - LEARN_RATE * (direction + DECAY_RATE * master)
    return (renewed, momentum, variance)


def dot(a, b):
    return lax.dot_general(a, b, (((1,), (0,)), ((), ())), preferred_element_type=F32)


def dot_nt(a, b):
    return lax.dot_general(a, b, (((1,), (1,)), ((), ())), preferred_element_type=F32)


def dot_tn(a, b):
    return lax.dot_general(a, b, (((0,), (0,)), ((), ())), preferred_element_type=F32)


def shifted(axis, delta):
    n = SIZES[axis]
    return lax.rem(lax.axis_index(axis) + (delta + n), n)


def sibling():
    m = lax.axis_index("mp")
    return m + 1 - 2 * lax.rem(m, 2)


def rows(start, n):
    return pl.ds(pl.multiple_of(start, 16), n)


class Net:
    def __init__(self, send, recv):
        self.send, self.recv = send, recv
        self.sends, self.recvs = 0, 0
        self.open = {}

    def send_id(self):
        self.sends += 1
        assert self.sends <= self.send.shape[0]
        return self.sends - 1

    def recv_ids(self, n):
        self.recvs += n
        assert self.recvs <= self.recv.shape[0]
        return self.recvs - n

    def put(self, sid, whole, rid, src, dst, axis, index):
        pltpu.make_async_remote_copy(
            src_ref=src,
            dst_ref=dst,
            send_sem=self.send.at[sid],
            recv_sem=self.recv.at[rid],
            device_id={axis: index},
            device_id_type=MESH,
        ).start()
        self.open[sid] = whole

    def stub(self, sid, rid, ref):
        return pltpu.make_async_remote_copy(
            src_ref=ref,
            dst_ref=ref,
            send_sem=self.send.at[sid],
            recv_sem=self.recv.at[rid],
            device_id={"dp": shifted("dp", 1)},
            device_id_type=MESH,
        )

    def got(self, rid, ref):
        self.stub(0, rid, ref).wait_recv()

    def sent(self, sid):
        self.stub(sid, 0, self.open.pop(sid)).wait_send()

    def drain(self):
        for sid in sorted(self.open):
            self.sent(sid)


def hello(peers):
    sem = pltpu.get_barrier_semaphore()
    for axis, index in peers:
        pl.semaphore_signal(sem, inc=1, device_id={axis: index}, device_id_type=MESH)


def hello_wait(n):
    pl.semaphore_wait(pltpu.get_barrier_semaphore(), n)


class Spread:
    def __init__(self, net, own, first, second):
        self.net, self.own, self.r1, self.r2 = net, own, first, second
        self.size, self.cols = own.shape[2], own.shape[3]
        self.q = self.size // 4
        self.sid = (net.send_id(), net.send_id())
        self.rid = net.recv_ids(16)
        self.chunk = min(self.q, max(16, 16384 // self.cols))

    def put(self, stage, h, slot, src, d):
        axis = self.axes(h)[stage]
        rid = self.rid + 8 * stage + 4 * h + (0, 1, 2, 2, 3, 3)[slot]
        to = (self.r1, self.r2)[stage]
        self.net.put(self.sid[stage], to, rid, src, to.at[h, slot], axis, shifted(axis, d))

    def got(self, stage, h, k):
        ref = (self.r1, self.r2)[stage]
        ref = ref.at[h, k] if k < 2 else ref.at[h, pl.ds(2 * k - 2, 2)]
        self.net.got(self.rid + 8 * stage + 4 * h + k, ref)

    def axes(self, h):
        return (("dp", "seq"), ("seq", "dp"))[h]

    def row(self, h, da):
        a = shifted(self.axes(h)[0], da)
        return (lambda b: (a, b)) if h == 0 else (lambda b: (b, a))

    def block(self, h, db):
        a, b = lax.axis_index(self.axes(h)[0]), shifted(self.axes(h)[1], db)
        return (a, b) if h == 0 else (b, a)

    def view(self, h, da, lo):
        a = shifted(self.axes(h)[0], da)
        if h == 0:
            return self.own.at[a, pl.ds(0, 4), pl.ds(lo, self.q)]
        return self.own.at[pl.ds(0, 4), a, pl.ds(lo, self.q)]

    def one(self, h, db, lo):
        a, b = self.block(h, db)
        return self.own.at[a, b, pl.ds(lo, self.q)]

    def add(self, index_of, count, lo, sources, use=None):
        steps = self.q // self.chunk

        @pl.loop(0, count * steps)
        def _(k):
            b = k // steps
            r = (k % steps) * self.chunk
            at = (*index_of(b), rows(lo + r, self.chunk))
            v = self.own[at].astype(F32)
            for ref, lead in sources:
                if count > 1:
                    v = v + ref[(*lead, b, rows(r, self.chunk))].astype(F32)
                else:
                    v = v + ref[(*lead, rows(r, self.chunk))].astype(F32)
            if use is None:
                self.own[at] = v.astype(BF16)
            else:
                use(lo + r, v)

    def step0_far(self, h):
        lo = 2 * h * self.q
        self.put(0, h, 0, self.view(h, 2, lo), 1)
        self.put(0, h, 1, self.view(h, 2, lo + self.q), -1)

    def step0_near(self, h):
        lo = 2 * h * self.q
        self.put(0, h, 4, self.view(h, 1, lo + self.q), 1)
        self.put(0, h, 2, self.view(h, -1, lo), -1)

    def step0(self):
        for h in (0, 1):
            self.step0_far(h)
        for h in (0, 1):
            self.step0_near(h)

    def step1(self):
        q = self.q
        for h in (0, 1):
            lo = 2 * h * q
            self.got(0, h, 0)
            self.add(self.row(h, 1), 4, lo, [(self.r1, (h, 0))])
            self.put(0, h, 3, self.view(h, 1, lo), 1)
            self.got(0, h, 1)
            self.add(self.row(h, -1), 4, lo + q, [(self.r1, (h, 1))])
            self.put(0, h, 5, self.view(h, -1, lo + q), -1)

    def step2(self):
        q = self.q
        for h in (0, 1):
            lo = 2 * h * q
            self.got(0, h, 2)
            self.add(self.row(h, 0), 4, lo, [(self.r1, (h, 2)), (self.r1, (h, 3))])
            self.got(0, h, 3)
            self.add(self.row(h, 0), 4, lo + q, [(self.r1, (h, 4)), (self.r1, (h, 5))])
            self.put(1, h, 0, self.one(h, 2, lo), 1)
            self.put(1, h, 1, self.one(h, 2, lo + q), -1)
            self.put(1, h, 4, self.one(h, 1, lo + q), 1)
            self.put(1, h, 2, self.one(h, -1, lo), -1)

    def step3(self):
        q = self.q
        for h in (0, 1):
            lo = 2 * h * q
            self.got(1, h, 0)
            at = self.block(h, 1)
            self.add(lambda b: at, 1, lo, [(self.r2, (h, 0))])
            self.put(1, h, 3, self.one(h, 1, lo), 1)
            self.got(1, h, 1)
            at2 = self.block(h, -1)
            self.add(lambda b: at2, 1, lo + q, [(self.r2, (h, 1))])
            self.put(1, h, 5, self.one(h, -1, lo + q), -1)

    def step4(self, h, use):
        q = self.q
        lo = 2 * h * q
        at = self.block(h, 0)
        self.got(1, h, 2)
        self.add(lambda b: at, 1, lo, [(self.r2, (h, 2)), (self.r2, (h, 3))], use)
        self.got(1, h, 3)
        self.add(lambda b: at, 1, lo + q, [(self.r2, (h, 4)), (self.r2, (h, 5))], use)


class Fold:
    def __init__(self, net, acc, rsib, zsend, zrec):
        self.net, self.acc, self.rsib, self.zsend, self.zrec = net, acc, rsib, zsend, zrec
        self.sib_sid = [net.send_id(), net.send_id()]
        self.z_sid = [net.send_id(), net.send_id()]
        self.rid = net.recv_ids(16)

    def quarter(self, d):
        return 32 * lax.rem(lax.axis_index("mp") // 2 + (d + 4), 4)

    def right(self):
        return shifted("mp", 2)

    def left(self):
        return shifted("mp", -2)

    def to_sibling(self, p, k, src, dst):
        self.net.put(self.sib_sid[p], self.rsib.at[p], self.rid + 8 * p + k, src, dst, "mp", sibling())

    def to_chip(self, p, slot, src, way):
        rid = self.rid + 8 * p + 4 + (0, 1, 2, 2, 3, 3)[slot]
        self.net.put(self.z_sid[p], self.zrec.at[p], rid, src, self.zrec.at[p, slot], "mp", way)

    def send_columns(self, p, k, src):
        cols = pl.ds(512 * k, 512)
        self.to_sibling(p, k, src.at[:, cols], self.rsib.at[p, :, cols])

    def send_rows(self, p, src):
        for k, d in enumerate((2, 1, -1, 0)):
            at = rows(self.quarter(d), 32)
            self.to_sibling(p, k, src(at), self.rsib.at[p, at])

    def sent(self, p):
        self.net.sent(self.sib_sid[p])

    def total(self, d, p, own, store):
        for i in (0, 1):
            at = rows(self.quarter(d) + 16 * i, 16)
            v = own(p, at).astype(F32) + self.rsib[p, at].astype(F32)
            self.acc[p, at] = v
            if store:
                self.zsend[p, at] = v.astype(BF16)

    def begin(self, p, own, by_rows):
        rid = self.rid + 8 * p

        def arrived(k, d):
            if by_rows:
                self.net.got(rid + k, self.rsib.at[p, rows(self.quarter(d), 32)])

        if not by_rows:
            for k in range(4):
                self.net.got(rid + k, self.rsib.at[p, :, pl.ds(512 * k, 512)])
        arrived(0, 2)
        self.total(2, p, own, True)
        s = self.quarter(2)
        self.to_chip(p, 0, self.zsend.at[p, rows(s, 16)], self.right())
        self.to_chip(p, 1, self.zsend.at[p, rows(s + 16, 16)], self.left())
        arrived(1, 1)
        self.total(1, p, own, True)
        self.to_chip(p, 4, self.zsend.at[p, rows(self.quarter(1) + 16, 16)], self.right())
        arrived(2, -1)
        self.total(-1, p, own, True)
        self.to_chip(p, 2, self.zsend.at[p, rows(self.quarter(-1), 16)], self.left())
        arrived(3, 0)
        self.total(0, p, own, False)

    def middle(self, p):
        for k, d, off, way in ((0, 1, 0, self.right()), (1, -1, 16, self.left())):
            self.net.got(self.rid + 8 * p + 4 + k, self.zrec.at[p, k])
            at = rows(self.quarter(d) + off, 16)
            self.zsend[p, at] = (self.acc[p, at] + self.zrec[p, k].astype(F32)).astype(BF16)
            self.to_chip(p, 3 + 2 * k, self.zsend.at[p, at], way)

    def finish(self, p, use):
        for part in (0, 1):
            self.net.got(self.rid + 8 * p + 6 + part, self.zrec.at[p, pl.ds(2 + 2 * part, 2)])
            v = self.acc[p, rows(self.quarter(0) + 16 * part, 16)]
            for k in (2 + 2 * part, 3 + 2 * part):
                v = v + self.zrec[p, k].astype(F32)
            use(p, 16 * part, v)

    def release(self):
        for sid in (*self.sib_sid, *self.z_sid):
            if sid in self.net.open:
                self.net.sent(sid)


class Share:
    def __init__(self, net, out):
        self.net, self.out = net, out
        self.sid = (net.send_id(), net.send_id())
        self.rid = net.recv_ids(8)

    def at(self, p, d, other=False, lo=0, n=32):
        m = lax.axis_index("mp")
        core = lax.rem(m, 2)
        if other:
            core = 1 - core
        return self.out.at[p, core, lax.rem(m // 2 + (d + 4), 4), pl.ds(lo, n)]

    def put(self, p, k, src, dst, index):
        own = k < 2 or (k == 3 and dst is None)
        dst = self.at(p, 0) if dst is None else dst
        whole = self.out.at[pl.ds(0, 2), 0, pl.ds(0, 3 if own else 4)]
        self.net.put(self.sid[0 if own else 1], whole, self.rid + 4 * p + k, src, dst, "mp", index)

    def got(self, p, k, ref):
        self.net.got(self.rid + 4 * p + k, ref)

    def begin(self, p, src=None):
        src = self.at(p, 0) if src is None else src
        self.put(p, 0, src, None, shifted("mp", 2))
        self.put(p, 1, src, None, shifted("mp", -2))
        self.put(p, 3, src, None, sibling())

    def middle(self, p):
        self.got(p, 0, self.at(p, -1))
        half = self.at(p, -1, False, 0, 16)
        self.put(p, 2, half, half, shifted("mp", 2))
        self.got(p, 1, self.at(p, 1))
        half = self.at(p, 1, False, 16, 16)
        self.put(p, 2, half, half, shifted("mp", -2))
        for d in (-1, 1):
            self.put(p, 3, self.at(p, d), self.at(p, d), sibling())

    def later(self, p):
        self.got(p, 2, self.at(p, 2))
        self.put(p, 3, self.at(p, 2), self.at(p, 2), sibling())

    def finish(self, p):
        self.got(p, 3, self.out.at[p, 1 - lax.rem(lax.axis_index("mp"), 2)])

    def release(self):
        for sid in self.sid:
            self.net.sent(sid)


class Gather:
    def __init__(self, net, own, size, region, whole, last):
        self.last = last
        self.net, self.own, self.size, self.region, self.whole = net, own, size, region, whole
        self.sid, self.rid = net.send_id(), net.recv_ids(24)
        self.half, self.quarter = size // 2, size // 4

    def put(self, k, src, dst, axis, d):
        self.net.put(self.sid, self.whole, self.rid + k, src, dst, axis, shifted(axis, d))

    def got(self, k, ref):
        self.net.got(self.rid + k, ref)

    def idx(self, h, da, db):
        fa, sa = (("dp", "seq"), ("seq", "dp"))[h]
        c = {fa: shifted(fa, da), sa: shifted(sa, db)}
        return c["dp"] * 4 + c["seq"]

    def both(self, k, src, dst, axis):
        self.put(k, src, dst, axis, 1)
        self.put(k + 1, src, dst, axis, -1)

    def begin(self, h):
        for stage in (0, 1):
            axis = ("dp", "seq")[(h + stage) % 2]
            lo = h * self.half
            src = self.own.at[pl.ds(lo, self.half)]
            self.both(12 * h + 3 * stage, src, self.region(self.idx(h, 0, 0), lo, self.half), axis)

    def near(self):
        for h in (0, 1):
            fa, sa = (("dp", "seq"), ("seq", "dp"))[h]
            lo = h * self.half
            for k, d in ((0, -1), (1, 1)):
                p = self.region(self.idx(h, d, 0), lo, self.half)
                self.got(12 * h + k, p)
                part = self.region(self.idx(h, d, 0), lo + k * self.quarter, self.quarter)
                self.put(12 * h + 2, part, part, fa, -d)
                self.both(12 * h + 5 + 2 * k, p, p, sa)

    def far(self):
        for h in (0, 1):
            sa, lo = (("dp", "seq"), ("seq", "dp"))[h][1], h * self.half
            p = self.region(self.idx(h, 2, 0), lo, self.half)
            self.got(12 * h + 2, p)
            self.both(12 * h + 9, p, p, sa)

    def cross(self, k):
        d = (0, -1, 1, 2)[k]
        for h in (0, 1):
            sa, lo = (("dp", "seq"), ("seq", "dp"))[h][1], h * self.half
            for w, db in ((0, -1), (1, 1)):
                at = self.idx(h, d, db)
                self.got(12 * h + 3 + 2 * k + w, self.region(at, lo, self.half))
                part = self.region(at, lo + w * self.quarter, self.quarter)
                self.put(12 * h + 11, part, part, sa, -db)

    def finish(self):
        for h in (0, 1):
            self.got(12 * h + 11, self.last)


def lanes(shape):
    return lax.broadcasted_iota(jnp.int32, shape, len(shape) - 1)


def swap_halves(v):
    lane = lanes(v.shape)
    return jnp.where(lane % HD < HD // 2, pltpu.roll(v, 96, 1), pltpu.roll(v, 32, 1))


def main_kernel(
    x_hbm, cot_hbm, parents, wa_hbm, wm_hbm, we_hbm, wr_hbm, gains, table_hbm,
    i_att, i_mrg, i_exp, i_red, mg, fg, sg,
    out, grad, o_att, o_mrg, o_exp, o_red, f_att, f_mrg, f_exp, f_red,
    o_gain, f_gain,
    g_red, g_gate, g_up, g_mrg, g_att,
    ra_red, ra_gate, ra_up, ra_mrg, ra_att,
    rb_red, rb_gate, rb_up, rb_mrg, rb_att,
    sa, wa, wm, xd, cot, n1, dgu, n2, hid,
    acc, sib, rsib, zrec, probs, kv_a, kv_b, q, att, datt, dkv, dkv_in, dpack,
    mid, dmid, stage, stage_exp, w_exp,
    gbuf, gs1, gs2, gs3, gs4, gs5, gtot, gtwo, gnew,
    send, recv, loc,
):
    net = Net(send, recv)
    m = lax.axis_index("mp")
    core, z = lax.rem(m, 2), m // 2
    seq = lax.axis_index("seq")
    other = 1 - core
    dp = lax.axis_index("dp")
    me = 4 * dp + seq
    hello(
        [("dp", shifted("dp", d)) for d in (1, 2, 3)]
        + [("seq", shifted("seq", d)) for d in (1, 2, 3)]
        + [("mp", shifted("mp", d)) for d in range(1, 8)]
    )
    kv = (kv_a, kv_b)
    kv_sid, kv_rid = (net.send_id(), net.send_id()), net.recv_ids(2)
    dkv_sid, dkv_rid = net.send_id(), net.recv_ids(2)
    fold = Fold(net, acc, rsib, sib, zrec)
    share_one, share_two, share_out, share_grad = Share(net, n2), Share(net, xd), Share(net, out), Share(net, grad)
    gain_sid, gain_rid = [net.send_id() for _ in range(5)], net.recv_ids(5)

    def gain_put(k, ref, count, src, dst, axis, d):
        net.put(gain_sid[k], ref.at[pl.ds(0, count)], gain_rid + k, src, dst, axis, shifted(axis, d))

    def gain_got(k, ref, count):
        net.got(gain_rid + k, ref.at[pl.ds(0, count)])


    def by_col(ref):
        return lambda i, lo, k: ref.at[pl.ds(lo, k), pl.ds(pl.multiple_of(128 * i, 128), 128)]

    all_red = Gather(net, g_red.at[dp, seq], 1024, by_col(f_red), f_red.at[:, pl.ds(0, 1920)], f_red.at[:, pl.ds(0, 256)])
    all_exp = Gather(net, w_exp, 128, lambda i, lo, k: f_exp.at[pl.ds(128 * i + lo, k)], f_exp.at[pl.ds(0, 1920)], f_exp.at[pl.ds(0, 256)])
    all_mrg = Gather(net, g_mrg.at[dp, seq], 256, by_col(f_mrg), f_mrg.at[:, pl.ds(0, 1920)], f_mrg.at[:, pl.ds(0, 256)])
    all_att = Gather(net, g_att.at[dp, seq], 128, lambda i, lo, k: f_att.at[rows(128 * i + lo, k)], f_att.at[pl.ds(0, 1920)], f_att.at[pl.ds(0, 256)])
    s_red = Spread(net, g_red, ra_red, rb_red)
    s_gate = Spread(net, g_gate, ra_gate, rb_gate)
    s_up = Spread(net, g_up, ra_up, rb_up)
    s_mrg = Spread(net, g_mrg, ra_mrg, rb_mrg)
    s_att = Spread(net, g_att, ra_att, rb_att)

    def bring(k, src, dst):
        c = pltpu.make_async_copy(src, dst, loc.at[k])
        c.start()
        return c

    c_x = [bring(0, x_hbm.at[0], xd.at[0])]
    c_wa = bring(2, wa_hbm, wa)
    c_x.append(bring(1, x_hbm.at[1], xd.at[1]))
    c_table = bring(9, table_hbm, stage.at[pl.ds(0, 2)])

    def all_here(ref, k):
        pltpu.make_async_copy(ref, ref, loc.at[k]).wait()

    both_gains = gains[...].astype(F32)
    gain_one, gain_two = both_gains[0:1, :], both_gains[1:2, :]

    def ancestors(t, b):
        p1 = parents[t, b]
        p2 = jnp.where(p1 >= 0, parents[t, jnp.maximum(p1, 0)], -1)
        p3 = jnp.where(p2 >= 0, parents[t, jnp.maximum(p2, 0)], -1)
        return p1, p2, p3

    def turns(t, i):
        ps = ancestors(t, 2 * seq + i)
        depth = sum(jnp.where(p >= 0, 1, 0) for p in ps)

        def pick(k):
            v = stage[k, 0:128]
            for n in (1, 2, 3):
                v = jnp.where(depth == n, stage[k, 128 * n : 128 * n + 128], v)
            return v

        return pick(0), pick(1)

    lower = lanes((128, 128)) < HD

    def own_kv(t, at):
        return kv[t].at[pl.ds(2 * at, 2)]

    for t in (0, 1):
        c_x[t].wait()
        if t == 0:
            c_wa.wait()
            c_table.wait()
        else:
            c_wm = bring(4, wm_hbm, wm)
            c_cot = bring(3, cot_hbm, cot)
            for k in range(16):
                pltpu.make_async_copy(wr_hbm.at[:, pl.ds(128 * k, 128)], g_red.at[k // 4, k % 4], loc.at[10]).start()
            for k in range(4):
                pltpu.make_async_copy(we_hbm.at[0, :, pl.ds(256 * k, 256)], sa.at[k], loc.at[11]).start()
            for k in range(16):
                pltpu.make_async_copy(we_hbm.at[1, pl.ds(128 * k, 128)], g_up.at[k // 4, k % 4], loc.at[12]).start()

        @pl.loop(0, 16, unroll=4)
        def _(i):
            v = xd[t, i // 8, (i // 2) % 4, rows(16 * (i % 2), 16)].astype(F32)
            r = lax.rsqrt(jnp.mean(v * v, axis=-1, keepdims=True) + NORM_EPS)
            n1[t, rows(16 * i, 16)] = (v * r * gain_one).astype(BF16)

        packed = dot(n1[t], wa[...])
        for i in (0, 1):
            c, s = turns(t, i)
            part = packed[128 * i : 128 * i + 128]
            for g in (0, 1):
                v = part[:, 128 * g : 128 * g + 128]
                q[t, i, g] = (v * c + swap_halves(v) * s).astype(BF16)
            v = part[:, 256:384]
            kv[t][2 * seq + i] = jnp.where(lower, v * c + swap_halves(v) * s, v).astype(BF16)
        if t == 0:
            hello_wait(13)
        for d in (1, 2, 3):
            net.put(kv_sid[t], kv[t].at[pl.ds(0, 6)], kv_rid + t, own_kv(t, seq), own_kv(t, seq), "seq", shifted("seq", d))

    def hidden_grad(j):
        w = jnp.concatenate([g_red[k // 4, k % 4, 256 * j : 256 * j + 256] for k in range(16)], axis=1)
        v = dot_nt(cot[...].reshape(512, D), w)
        high = v.astype(BF16)
        low = (v - high.astype(F32)).astype(BF16)
        cols = pl.ds(256 * j, 256)
        g_gate[0, :, :, cols] = high.reshape(4, 128, 256)
        g_gate[1, :, :, cols] = low.reshape(4, 128, 256)

    low_lane = lanes((512, 128)) < HD
    key_col = lanes((128, 512))
    query_row = lax.broadcasted_iota(jnp.int32, (128, 512), 0)

    def key_views(t, ids):
        both = jnp.concatenate([kv[t][jnp.maximum(c, 0)] for c in ids], axis=0).astype(F32)
        turned = pltpu.roll(both, HD, 1)
        zero = jnp.zeros_like(both)
        keys = [jnp.where(low_lane, both, zero).astype(BF16), jnp.where(low_lane, zero, turned).astype(BF16)]
        values = [jnp.where(low_lane, turned, zero).astype(BF16), jnp.where(low_lane, zero, both).astype(BF16)]
        return keys, values

    def attention(t):
        net.got(kv_rid + t, kv[t].at[pl.ds(0, 6)])
        for i in (0, 1):
            b = 2 * seq + i
            ps = ancestors(t, b)
            keys, values = key_views(t, (b, *ps))
            seen = (key_col < 128) & (key_col <= query_row)
            for k, p in enumerate(ps):
                inside = (key_col >= 128 * (k + 1)) & (key_col < 128 * (k + 2))
                seen = seen | (inside & (p >= 0))
            for g in (0, 1):
                total = jnp.zeros((128, 128), F32)
                for h in (0, 1):
                    scores = dot_nt(q[t, i, g], keys[h]) * HD**-0.5
                    scores = jnp.where(seen, scores, MASK_FILL)
                    e = jnp.exp(scores - jnp.max(scores, axis=-1, keepdims=True))
                    p = (e / jnp.sum(e, axis=-1, keepdims=True)).astype(BF16)
                    probs[2 * t + i, 2 * g + h] = p
                    total = total + dot(p, values[h])
                att[t, 128 * i : 128 * i + 128, 128 * g : 128 * g + 128] = total.astype(BF16)

    def mine(p, at):
        return acc[p, at]

    def merge(p):
        for k in range(4):
            cols = pl.ds(512 * k, 512)
            sib[p, :, cols] = dot(att[p, rows(128 * other, 128)], wm[:, cols]).astype(BF16)
        fold.send_rows(p, lambda at: sib.at[p, at])
        for k in range(4):
            cols = pl.ds(512 * k, 512)
            acc[p, :, cols] = dot(att[p, rows(128 * core, 128)], wm[:, cols])

    def to_normed(p, r, v):
        x_own = xd[p, core, z, r : r + 16].astype(F32)
        total = x_own + v
        mid[p, r : r + 16] = total
        rms = lax.rsqrt(jnp.mean(total * total, axis=-1, keepdims=True) + NORM_EPS)
        n2[p, core, z, r : r + 16] = (total * rms * gain_two).astype(BF16)


    def feed_dot(p, j):
        lo = 1024 * (j % 2)
        for k, w in ((0, sa[j]), (1, g_up[:, :, :, 256 * j : 256 * j + 256].reshape(D, 256))):
            v = dot(n2[p].reshape(256, D), w)
            acc[p, :, lo + 256 * k : lo + 256 * k + 256] = v[0:128]
            acc[p, :, lo + 512 + 256 * k : lo + 768 + 256 * k] = v[128:256]

    def feed_rest(p, j):
        cols, cols_up = pl.ds(256 * j, 256), pl.ds(1024 + 256 * j, 256)
        for half in (0, 1):
            lo = 1024 * (j % 2) + 512 * half
            for i in range(4):
                at = pl.ds(32 * i, 32)
                gate, up = acc[p, at, lo : lo + 256], acc[p, at, lo + 256 : lo + 512]
                dh = g_gate[0, 2 * p + half, at, cols].astype(F32) + g_gate[1, 2 * p + half, at, cols].astype(F32)
                sig = 0.5 + 0.5 * jnp.tanh(0.5 * gate)
                act = gate * sig
                to = pl.ds(128 * half + 32 * i, 32)
                hid[p, to, cols] = (act * up).astype(BF16)
                dgu[p, to, cols] = (dh * up * (sig + act * (1.0 - sig))).astype(BF16)
                dgu[p, to, cols_up] = (dh * act).astype(BF16)

    def feed(p, between):
        feed_dot(p, 0)
        for j in (1, 2, 3):
            feed_dot(p, j)
            feed_rest(p, j - 1)
            if j == 1:
                between()
        feed_rest(p, 3)

    attention(0)
    c_wm.wait()
    merge(0)
    attention(1)
    fold.sent(0)
    fold.begin(0, mine, True)
    merge(1)
    c_cot.wait()
    all_here(g_red, 10)
    hidden_grad(0)
    fold.middle(0)
    fold.sent(1)
    fold.begin(1, mine, True)
    hidden_grad(1)
    fold.finish(0, to_normed)
    share_one.begin(0)
    fold.middle(1)
    hidden_grad(2)
    share_one.middle(0)
    fold.finish(1, to_normed)
    share_one.begin(1)
    hidden_grad(3)
    all_here(sa, 11)
    all_here(g_up, 12)
    share_one.later(0)
    share_one.middle(1)
    share_one.finish(0)
    feed(0, lambda: share_one.later(1))
    share_one.finish(1)
    fold.release()
    feed(1, lambda: None)

    def reduce_grad(a):
        @pl.loop(0, 2)
        def _(k):
            cols = pl.ds(pl.multiple_of(512 * a + 256 * k, 256), 256)
            v = dot_tn(hid[...].reshape(512, 1024), cot[:, :, :, :, cols].reshape(512, 256)).astype(BF16)
            g_red[a, 2 * k] = v[:, 0:128]
            g_red[a, 2 * k + 1] = v[:, 128:256]

    reduce_grad(shifted("dp", 2))
    s_red.step0_far(0)

    @pl.loop(0, 2)
    def _(k):
        reduce_grad(lax.rem(dp + 1 + 2 * k, 4))

    s_red.step0_near(0)
    reduce_grad(dp)
    s_red.step0_far(1)
    s_red.step0_near(1)
    def expand_grad(dst, first):
        @pl.loop(0, 4)
        def _(a):
            left = n2[:, :, :, :, pl.ds(pl.multiple_of(512 * a, 512), 512)].reshape(512, 512)
            for k in (0, 1):
                v = dot_tn(left, dgu[:, :, first + 512 * k : first + 512 * k + 512].reshape(512, 512))
                dst[a, :, :, 512 * k : 512 * k + 512] = v.astype(BF16).reshape(4, 128, 512)

    expand_grad(g_gate, 0)
    s_gate.step0()

    def norm_grad(p):
        for k in range(4):
            for j in (2 * k, 2 * k + 1):
                cols = pl.ds(256 * j, 256)
                w_gate = jnp.concatenate([sa[i, 256 * j : 256 * j + 256] for i in range(4)], axis=1)
                w_up = g_up[j // 2, 2 * (j % 2) : 2 * (j % 2) + 2].reshape(256, 1024)
                v = dot_nt(dgu[p], jnp.concatenate([w_gate, w_up], axis=1))
                first, second = v[0:128], v[128:256]
                sib[p, :, cols] = jnp.where(core == 0, second, first).astype(BF16)
                acc[p, :, cols] = jnp.where(core == 0, first, second)
            fold.send_columns(p, k, sib.at[p])

    def to_branch(p, r, v):
        total = mid[p, r : r + 16]
        rms = lax.rsqrt(jnp.mean(total * total, axis=-1, keepdims=True) + NORM_EPS)
        u = v * gain_two
        back_vals = rms * u - total * (rms * rms * rms) * jnp.mean(u * total, axis=-1, keepdims=True)
        full = cot[p, core, z, r : r + 16].astype(F32) + back_vals
        dmid[p, r : r + 16] = full
        xd[p, core, z, r : r + 16] = full.astype(BF16)
        gbuf[1:2, :] = gbuf[1:2, :] + jnp.sum(v * total * rms, axis=0, keepdims=True)

    gbuf[...] = jnp.zeros_like(gbuf)
    norm_grad(0)
    fold.sent(0)
    fold.begin(0, mine, False)
    norm_grad(1)
    s_red.step1()
    for k in range(8):
        half = sa.at[k // 2, pl.ds(1024 * (k % 2), 1024)]
        pltpu.make_async_copy(wr_hbm.at[:, pl.ds(256 * k, 256)], half, loc.at[13]).start()
    expand_grad(g_up, 1024)
    s_up.step0()
    fold.middle(0)
    fold.sent(1)
    fold.begin(1, mine, False)
    s_gate.step1()
    fold.finish(0, to_branch)
    share_two.begin(0)
    fold.middle(1)

    all_here(sa, 13)

    @pl.loop(0, 4)
    def _(j):
        for k in (0, 1):
            v = dot(hid[...].reshape(512, 1024), sa[j, 1024 * k : 1024 * k + 1024])
            dgu[:, :, pl.ds(pl.multiple_of(512 * j + 256 * k, 256), 256)] = v.astype(BF16).reshape(2, 256, 256)

    fold.finish(1, to_branch)
    share_two.begin(1)

    x_slot = lax.rem(z + 1, 4)
    c_xo = [bring(p, x_hbm.at[p, core, z], cot.at[p, core, x_slot]) for p in (0, 1)]
    for k in (0, 1, 2):
        pltpu.make_async_copy(i_exp[k], stage_exp.at[k], loc.at[10]).start()
    share_two.middle(0)
    share_two.middle(1)
    share_two.later(0)
    s_red.step2()
    share_two.finish(0)

    dbr = xd

    def branch_back(t):
        datt[t] = dot_nt(dbr[t].reshape(256, D), wm[...]).astype(BF16)

    branch_back(0)
    share_two.later(1)
    dkv[...] = jnp.zeros_like(dkv)

    def attention_back(t, i):
        u = 2 * t + i
        b = 2 * seq + i
        ps = ancestors(t, b)
        keys, values = key_views(t, (b, *ps))
        c, s = turns(t, i)
        at = rows(128 * i, 128)
        dk = [jnp.zeros((512, 128), F32), jnp.zeros((512, 128), F32)]
        dv = [jnp.zeros((512, 128), F32), jnp.zeros((512, 128), F32)]
        for g in (0, 1):
            dq = jnp.zeros((128, 128), F32)
            da = datt[t, at, 128 * g : 128 * g + 128]
            for h in (0, 1):
                p = probs[u, 2 * g + h]
                pf = p.astype(F32)
                dp = dot_nt(da, values[h])
                inner = jnp.sum(pf * dp, axis=-1, keepdims=True)
                ds = (pf * (dp - inner)).astype(BF16)
                dq = dq + dot(ds, keys[h])
                dk[h] = dk[h] + dot_tn(ds, q[t, i, g])
                dv[h] = dv[h] + dot_tn(p, da)
            dq = dq * HD**-0.5
            dpack[t, at, 128 * g : 128 * g + 128] = (dq * c - swap_halves(dq) * s).astype(BF16)
        both = jnp.where(
            low_lane, (dk[0] + pltpu.roll(dk[1], HD, 1)) * HD**-0.5, pltpu.roll(dv[0], HD, 1) + dv[1]
        )
        dkv[t, b] = dkv[t, b] + both[0:128]
        for blk in range(8):
            v = dkv[t, blk]
            for k, p in enumerate(ps):
                v = v + both[128 * (k + 1) : 128 * (k + 2)] * jnp.where(p == blk, 1.0, 0.0)
            dkv[t, blk] = v

    def send_dkv(t):
        for c in range(8):
            probs[2 * t, c // 4, :, 128 * (c % 4) : 128 * (c % 4) + 128] = dkv[t, c].astype(BF16)
        for d in (1, 2, 3):
            peer = shifted("seq", d)
            src = probs.at[2 * t, peer // 2, :, pl.ds(pl.multiple_of(256 * lax.rem(peer, 2), 256), 256)]
            net.put(dkv_sid, dkv_in, dkv_rid + t, src, dkv_in.at[d - 1, t], "seq", peer)

    def add_dkv(t):
        net.got(dkv_rid + t, dkv_in.at[pl.ds(0, 3), t])
        for i in (0, 1):
            v = dkv[t, 2 * seq + i]
            for d in (0, 1, 2):
                v = v + dkv_in[d, t, :, 128 * i : 128 * i + 128].astype(F32)
            c, s = turns(t, i)
            v = jnp.where(lower, v * c - swap_halves(v) * s, v)
            dpack[t, 128 * i : 128 * i + 128, 256:384] = v.astype(BF16)

    for i in (0, 1):
        attention_back(0, i)
    send_dkv(0)
    share_two.finish(1)
    fold.release()

    def down_rows(p, at):
        return dgu[p, pl.ds(pl.multiple_of(128 * core + at.start, 16), 16)]

    for p in (0, 1):
        fold.send_rows(p, lambda at: dgu.at[p, rows(128 * other + at.start, 32)])
    branch_back(1)
    for i in (0, 1):
        attention_back(1, i)
    send_dkv(1)
    s_up.step1()

    @pl.loop(0, 8)
    def _(j):
        cols = pl.ds(pl.multiple_of(256 * j, 256), 256)
        v = dot_tn(att[...].reshape(512, 256), dbr[:, :, :, :, cols].reshape(512, 256))
        g_mrg[j // 2, 2 * (j % 2)] = v[:, 0:128].astype(BF16)
        g_mrg[j // 2, 2 * (j % 2) + 1] = v[:, 128:256].astype(BF16)

    s_mrg.step0()
    fold.begin(0, down_rows, True)
    fold.begin(1, down_rows, True)
    s_gate.step2()
    add_dkv(0)
    add_dkv(1)

    @pl.loop(0, 4)
    def _(a):
        left = n1[:, :, pl.ds(pl.multiple_of(512 * a, 512), 512)].reshape(512, 512)
        g_att[a] = dot_tn(left, dpack[...].reshape(512, 384)).astype(BF16).reshape(4, 128, 384)

    s_att.step0()
    s_red.step3()
    for k in (0, 1, 2):
        pltpu.make_async_copy(i_mrg[k], dkv.at[0, pl.ds(2 * k, 2)], loc.at[12]).start()
        pltpu.make_async_copy(i_red[k].at[pl.ds(0, 512)], stage.at[k], loc.at[11]).start()
    fold.middle(0)
    fold.middle(1)
    share_one.release()

    @pl.loop(0, 8)
    def _(j):
        v = dot_nt(dpack[...].reshape(512, 384), wa[rows(256 * j, 256)])
        n2[:, :, :, :, pl.ds(pl.multiple_of(256 * j, 256), 256)] = v.astype(BF16).reshape(2, 2, 4, 32, 256)

    def to_out(p, r, v):
        cot[p, core, z, r : r + 16] = (mid[p, r : r + 16] + v).astype(BF16)

    s_mrg.step1()

    def renew(state, at, grads):
        new = adamw(state[0][at], state[1][at], state[2][at], grads)[0]
        state[1][at] = grads
        return new

    flat_stage = [stage.at[k] for k in (0, 1, 2)]

    def use_red(h):
        def use(r, v):
            new = renew(flat_stage, rows(r - 512 * h, 128), v)
            g_red[dp, seq, rows(r, 128)] = new.astype(BF16)

        return use

    all_here(stage, 11)
    s_red.step4(0, use_red(0))
    all_red.begin(0)
    c_red = [bring(4, stage.at[1], o_red.at[pl.ds(0, 512)])]
    local = [bring(14, g_red.at[dp, seq, pl.ds(0, 512)], f_red.at[pl.ds(0, 512), pl.ds(pl.multiple_of(128 * me, 128), 128)])]
    s_up.step2()
    s_att.step1()
    s_gate.step3()
    l_out = []
    for p in (0, 1):
        fold.finish(p, to_out)
        share_out.begin(p, cot.at[p, core, z])
        l_out.append(bring(2 + p, cot.at[p, core, z], out.at[p, core, z]))
    for c in c_red:
        c.wait()
    for k in (0, 1, 2):
        pltpu.make_async_copy(i_red[k].at[pl.ds(512, 512)], stage.at[k], loc.at[11]).start()
    s_mrg.step2()
    all_here(stage, 11)
    s_red.step4(1, use_red(1))
    all_red.begin(1)
    c_red = [bring(4, stage.at[1], o_red.at[pl.ds(512, 512)])]
    local.append(bring(15, g_red.at[dp, seq, pl.ds(512, 512)], f_red.at[pl.ds(512, 512), pl.ds(pl.multiple_of(128 * me, 128), 128)]))
    s_up.step3()
    s_att.step2()
    share_out.middle(0)
    share_out.middle(1)

    def use_expand(j):
        def use(r, v):
            at = rows(r, 16)
            new = adamw(stage_exp[0, at, j, :], stage_exp[1, at, j, :], stage_exp[2, at, j, :], v)[0]
            stage_exp[0, at, j, :] = new
            stage_exp[1, at, j, :] = v

        return use

    all_here(stage_exp, 10)
    s_gate.step4(0, use_expand(0))
    s_gate.step4(1, use_expand(0))
    for c in c_red:
        c.wait()
    for k in (0, 1, 2):
        for a in (0, 1, 2):
            pltpu.make_async_copy(
                i_att[k].at[:, pl.ds(128 * a, 128)], stage.at[k, pl.ds(128 * a, 128)], loc.at[11]
            ).start()

    def norm_rows(p, at):
        return n2[p, core, at.start // 32, pl.ds(pl.multiple_of(at.start % 32, 16), 16)]

    def fold_begin(p):
        fold.begin(p, norm_rows, True)

    all_red.near()
    s_mrg.step3()
    s_att.step3()
    share_out.later(0)
    share_out.later(1)
    for h in (0, 1):
        s_up.step4(h, use_expand(1))
        for i in (0, 1, 2, 3):
            at = rows(64 * h + 16 * i, 16)
            w_exp[at] = stage_exp[0, at].astype(BF16)
        all_exp.begin(h)
    c_exp = [bring(6, stage_exp.at[1], o_exp)]
    local.append(bring(9, w_exp, f_exp.at[pl.ds(128 * me, 128)]))
    def use_mrg(r, v):
        new = renew([dkv.at[0, 2 * k + r // 128] for k in (0, 1, 2)], rows(r % 128, 64), v)
        g_mrg[dp, seq, rows(r, 64)] = new.astype(BF16)

    all_here(dkv.at[0, pl.ds(0, 6)], 12)
    for h in (0, 1):
        s_mrg.step4(h, use_mrg)
        all_mrg.begin(h)
    c_mrg = [bring(7, dkv.at[0, pl.ds(2, 2)], o_mrg)]
    local.append(bring(8, g_mrg.at[dp, seq], f_mrg.at[:, pl.ds(pl.multiple_of(128 * me, 128), 128)]))
    all_here(stage.at[:, pl.ds(0, 384)], 11)

    def use_att(r, v):
        parts = []
        for a in (0, 1, 2):
            parts.append(renew(flat_stage, rows(128 * a + r, 32), v[:, 128 * a : 128 * a + 128]))
        g_att[dp, seq, rows(r, 32)] = jnp.concatenate(parts, axis=1).astype(BF16)

    for h in (0, 1):
        s_att.step4(h, use_att)
        all_att.begin(h)
    c_att = [bring(16 + a, stage.at[1, pl.ds(128 * a, 128)], o_att.at[:, pl.ds(128 * a, 128)]) for a in (0, 1, 2)]
    local.append(bring(5, g_att.at[dp, seq], f_att.at[rows(128 * me, 128)]))
    share_out.finish(0)
    share_out.finish(1)
    fold.release()
    for p in (0, 1):
        fold.send_rows(p, lambda at: n2.at[p, other, at.start // 32])
    all_red.far()
    all_exp.near()
    fold_begin(0)
    fold_begin(1)
    all_red.cross(0)
    all_red.cross(1)
    all_mrg.near()
    all_att.near()
    fold.middle(0)
    fold.middle(1)
    for c in c_xo:
        c.wait()

    def to_grad(p, r, v):
        x = cot[p, core, x_slot, r : r + 16].astype(F32)
        rms = lax.rsqrt(jnp.mean(x * x, axis=-1, keepdims=True) + NORM_EPS)
        u = v * gain_one
        back_vals = rms * u - x * (rms * rms * rms) * jnp.mean(u * x, axis=-1, keepdims=True)
        cot[p, other, z, r : r + 16] = (dmid[p, r : r + 16] + back_vals).astype(BF16)
        gbuf[0:1, :] = gbuf[0:1, :] + jnp.sum(v * x * rms, axis=0, keepdims=True)

    all_exp.far()
    all_red.cross(2)
    for p in (0, 1):
        fold.finish(p, to_grad)
        share_grad.begin(p, cot.at[p, other, z])
    l_grad = [bring(p, cot.at[p, other, z], grad.at[p, core, z]) for p in (0, 1)]
    gs1[m] = gbuf[...]
    for d in range(1, 8):
        gain_put(0, gs1, 7, gbuf, gs1.at[m], "mp", d)
    all_red.cross(3)
    all_exp.cross(0)
    all_mrg.far()
    all_att.far()
    gain_got(0, gs1, 7)
    total = gs1[0]
    for k in range(1, 8):
        total = total + gs1[k]
    gtot[...] = total

    def piece(i, n):
        return pl.ds(pl.multiple_of(i * n, 128), n)

    gs2[dp] = gtot[:, piece(dp, 512)]
    for d in (1, 2, 3):
        gain_put(1, gs2, 3, gtot.at[:, piece(shifted("dp", d), 512)], gs2.at[dp], "dp", d)
    share_grad.middle(0)
    share_grad.middle(1)
    all_exp.cross(1)
    gain_got(1, gs2, 3)
    gtwo[...] = gs2[0] + gs2[1] + gs2[2] + gs2[3]
    gs3[seq] = gtwo[:, piece(seq, 128)]
    for d in (1, 2, 3):
        gain_put(2, gs3, 3, gtwo.at[:, piece(shifted("seq", d), 128)], gs3.at[seq], "seq", d)
    share_grad.later(0)
    share_grad.later(1)
    all_mrg.cross(0)
    all_att.cross(0)
    gain_got(2, gs3, 3)
    shard = gs3[0] + gs3[1] + gs3[2] + gs3[3]
    new = adamw(mg[...], fg[...], sg[...], shard)[0]
    o_gain[...] = shard
    gnew[...] = new
    gs4[seq] = new
    for d in (1, 2, 3):
        gain_put(3, gs4, 3, gnew, gs4.at[seq], "seq", d)
    all_exp.cross(2)
    all_mrg.cross(1)
    all_att.cross(1)
    gain_got(3, gs4, 3)
    gs5[dp] = gs4[...]
    for d in (1, 2, 3):
        gain_put(4, gs5, 3, gs4, gs5.at[dp], "dp", d)
    for k in (2, 3):
        all_mrg.cross(k)
        all_att.cross(k)
    all_exp.cross(3)
    gain_got(4, gs5, 3)
    for a in range(4):
        for b in range(4):
            lo = 128 * (4 * a + b)
            f_gain[:, lo : lo + 128] = gs5[a, b].astype(BF16)
    share_grad.finish(0)
    share_grad.finish(1)
    for g in (all_red, all_exp, all_mrg, all_att):
        g.finish()
    for c in local + l_out + l_grad + c_exp + c_mrg + c_att:
        c.wait()
    net.drain()


def main_call(x, cot, parents, wa, wm, we, wr, gains, table, states, gain_states):
    kinds = [(1024, 128), (128, 1024), (128, 1024), (256, 128), (128, 384)]
    vm, sds = pltpu.VMEM, jax.ShapeDtypeStruct
    scratch = (
        [vm((4, 4, n, c), BF16) for n, c in kinds]
        + [vm((2, 6, 4, n // 4, c), BF16) for n, c in kinds]
        + [vm((2, 6, n // 4, c), BF16) for n, c in kinds]
        + [
            vm((4, 2048, 256), BF16),
            vm((2048, 384), BF16),
            vm((256, 2048), BF16),
            vm((2, 2, 4, 32, D), BF16),
            vm((2, 2, 4, 32, D), BF16),
            vm((2, 256, D), BF16),
            vm((2, 256, D), BF16),
            vm((2, 2, 4, 32, D), BF16),
            vm((2, 256, 1024), BF16),
            vm((2, 128, D), F32),
            vm((2, 128, D), BF16),
            vm((2, 128, D), BF16),
            vm((2, 6, 16, D), BF16),
            vm((4, 4, 128, 512), BF16),
            vm((8, 128, 128), BF16),
            vm((8, 128, 128), BF16),
            vm((2, 2, 2, 128, 128), BF16),
            vm((2, 256, 256), BF16),
            vm((2, 256, 256), BF16),
            vm((2, 8, 128, 128), F32),
            vm((3, 2, 128, 256), BF16),
            vm((2, 256, 384), BF16),
            vm((2, 32, D), F32),
            vm((2, 32, D), F32),
            vm((3, 512, 128), F32),
            vm((3, 128, 2, 1024), F32),
            vm((128, 2, 1024), BF16),
            vm((2, D), F32),
            vm((8, 2, D), F32),
            vm((4, 2, 512), F32),
            vm((4, 2, 128), F32),
            vm((4, 2, 128), F32),
            vm((4, 4, 2, 128), F32),
            vm((2, D), F32),
            vm((2, 512), F32),
            vm((2, 128), F32),
            pltpu.SemaphoreType.DMA((34,)),
            pltpu.SemaphoreType.DMA((234,)),
            pltpu.SemaphoreType.DMA((20,)),
        ]
    )
    rows_out = sds((2, 2, 4, 32, D), BF16)
    shards = [sds((128, 384), F32), sds((2, 128, 128), F32), sds((128, 2, 1024), F32), sds((1024, 128), F32)]
    fulls = [sds((D, 384), BF16), sds((256, D), BF16), sds((D, 2, 1024), BF16), sds((1024, D), BF16)]
    out_shape = [rows_out, rows_out, *shards, *fulls, sds((2, 128), F32), sds((2, D), BF16)]
    vspec = pl.BlockSpec(memory_space=pltpu.VMEM)
    hbm = pl.BlockSpec(memory_space=pl.ANY)
    return pl.pallas_call(
        main_kernel,
        out_shape=out_shape,
        in_specs=[hbm, hbm, pl.BlockSpec(memory_space=pltpu.SMEM), hbm, hbm, hbm, hbm, vspec, hbm]
        + [[hbm] * 3] * 4
        + [vspec] * 3,
        out_specs=[hbm] * 10 + [vspec] * 2,
        scratch_shapes=scratch,
        compiler_params=pltpu.CompilerParams(
            collective_id=1, has_side_effects=True, vmem_limit_bytes=64 * 2**20 - 65536
        ),
    )(x, cot, parents, wa, wm, we, wr, gains, table, *states, *gain_states)


PARTS = (2, 2, 1, 1, 4, 2, 1)


def tail_kernel(*refs):
    groups, copies, refs = refs[:20], refs[20:27], refs[27:]
    outs, copied, refs = refs[:15], refs[15:22], refs[22:]
    held, through, (sem_in, sem_out, sem_a, sem_b) = refs[:20], refs[20:27], refs[27:]
    reads = [pltpu.make_async_copy(src, dst, sem_a.at[k]) for k, (src, dst) in enumerate(zip(groups, held))]
    there, back = [], []
    for k, parts in enumerate(PARTS):
        size = copies[k].shape[0] // parts
        for i in range(parts):
            at, j = pl.ds(size * i, size), len(there)
            there.append(pltpu.make_async_copy(copies[k].at[at], through[k].at[at], sem_in.at[j]))
            back.append(pltpu.make_async_copy(through[k].at[at], copied[k].at[at], sem_out.at[j]))
    writes = []

    def renew(k):
        for c in reads[4 * k : 4 * k + 4]:
            c.wait()
        master, first, second, grads = held[4 * k : 4 * k + 4]
        steps = 8 if k < 4 else 1
        size = master.shape[0] // steps

        @pl.loop(0, steps)
        def _(i):
            at = pl.ds(pl.multiple_of(size * i, size), size)
            master[at], first[at], second[at] = adamw(master[at], first[at], second[at], grads[at])

        for i in range(3):
            c = pltpu.make_async_copy(held[4 * k + i], outs[3 * k + i], sem_b.at[3 * k + i])
            c.start()
            writes.append(c)

    def pass_on(first, last):
        for c, e in zip(there[first:last], back[first:last]):
            c.wait()
            e.start()

    for c in reads[8:12] + there[:4] + reads[:8] + reads[12:] + there[4:]:
        c.start()
    pass_on(0, 4)
    renew(2)
    pass_on(4, 7)
    renew(3)
    pass_on(7, len(there))
    for k in (0, 1, 4):
        renew(k)
    for c in writes + back:
        c.wait()


def tail_call(groups, results):
    flat = [v for g in groups for v in g]
    vm, sds = pltpu.VMEM, jax.ShapeDtypeStruct
    hbm = pl.BlockSpec(memory_space=pl.ANY)
    n = sum(PARTS)
    done = pl.pallas_call(
        tail_kernel,
        in_specs=[hbm] * 27,
        out_specs=[hbm] * 22,
        out_shape=[sds(g[0].shape, F32) for g in groups for _ in range(3)] + [sds(v.shape, v.dtype) for v in results],
        scratch_shapes=[vm(v.shape, F32) for v in flat]
        + [vm(v.shape, v.dtype) for v in results]
        + [pltpu.SemaphoreType.DMA((k,)) for k in (n, n, 20, 15)],
        compiler_params=pltpu.CompilerParams(vmem_limit_bytes=64 * 2**20 - 65536),
    )(*flat, *results)
    return [done[3 * k : 3 * k + 3] for k in range(5)], done[15:]


def rotary_table():
    inv = ROPE_BASE ** (-2.0 * np.arange(HD // 2, dtype=np.float32) / HD)
    angle = np.arange(512, dtype=np.float32)[:, None] * inv.astype(np.float32)[None, :]
    c, s = np.cos(angle), np.sin(angle)
    both = np.stack([np.concatenate([c, c, c, c], 1), np.concatenate([-s, s, -s, s], 1)])
    return both.astype(np.float32)


def on_device(
    inputs, cotangent, parents, weight_attend, weight_merge, weight_expand, weight_reduce, gains,
    master_attend, master_merge, master_expand, master_reduce, master_gains,
    first_attend, first_merge, first_expand, first_reduce, first_gains,
    second_attend, second_merge, second_expand, second_reduce, second_gains,
):
    x = inputs.reshape(2, 2, 4, 32, D)
    cot = cotangent.reshape(2, 2, 4, 32, D)
    we = weight_expand.transpose(1, 0, 2)
    states = [
        [master_attend, first_attend, second_attend],
        [v.reshape(2, 128, 128) for v in (master_merge, first_merge, second_merge)],
        [master_expand, first_expand, second_expand],
        [master_reduce, first_reduce, second_reduce],
    ]
    gain_states = [master_gains, first_gains, second_gains]
    out, grad, g_att, g_mrg, g_exp, g_red, f_att, f_mrg, f_exp, f_red, g_gain, f_gain = main_call(
        x, cot, parents, weight_attend, weight_merge, we, weight_reduce, gains, jnp.asarray(rotary_table()), states, gain_states
    )
    states[1] = [master_merge, first_merge, second_merge]
    sums = (g_att, g_mrg.reshape(256, 128), g_exp, g_red, g_gain)
    results = [out.reshape(512, D), grad.reshape(512, D), f_att, f_mrg, f_exp, f_red, f_gain]
    (s_att, s_mrg, s_exp, s_red, s_gain), results = tail_call(
        [[*v, g] for v, g in zip((*states, gain_states), sums)], results
    )
    out, grad, f_att, f_mrg, f_exp, f_red, f_gain = results
    return (
        out.reshape(2, 256, D), grad.reshape(2, 256, D),
        s_att[0], s_mrg[0], s_exp[0], s_red[0], s_gain[0],
        s_att[1], s_mrg[1], s_exp[1], s_red[1], s_gain[1],
        s_att[2], s_mrg[2], s_exp[2], s_red[2], s_gain[2],
        f_att, f_mrg, f_exp, f_red, f_gain,
    )


def solution(mesh):
    both = ("dp", "seq")
    states = (P(both, "mp"), P("mp", both), P(both, None, "mp"), P("mp", both), P(None, both))
    weights = (P(None, "mp"), P("mp", None), P(None, None, "mp"), P("mp", None), P())
    tokens = P("dp", "seq", None)
    return jax.shard_map(
        on_device,
        mesh=mesh,
        in_specs=(tokens, tokens, P("dp", None), *weights, *states, *states, *states),
        out_specs=(tokens, tokens, *states, *states, *states, *weights),
        check_vma=False,
    )
```
